32 devices in a mesh: rows: 8 (over z, y), dates: 4 (over x, core).
Axes of the slice: x: 2, y: 2, z: 4, core: 2. Of those that a mesh axis runs over, the one named last changes fastest.
Arguments:
- images: bfloat16 [16, 128, 128, 128], P('dates', 'rows'), may hold values from -12 to 12
- day_index: int32 [16], replicated, may hold values from 1 to 365
- valid: int32 [16, 64, 128], P(None, 'rows', 'dates'), may hold values from 0 to 1, as said below
- out_grad: bfloat16 [64, 128, 128], P('rows', 'dates'), may hold values from -6 to 6
- conv_weight: bfloat16 [3, 3, 64, 128], replicated, may hold values from -0.25 to 0.25
- first_gain: float32 [128], replicated, may hold values from 0.1 to 1.9
- first_shift: float32 [128], replicated, may hold values from -3 to 3
- block_weight: bfloat16 [3, 3, 128, 128], replicated, may hold values from -0.1875 to 0.1875
- gn_gain: float32 [128], replicated, may hold values from 0.1 to 1.9
- gn_shift: float32 [128], replicated, may hold values from -3 to 3
- key_weight: bfloat16 [128, 64], replicated, may hold values from -0.5 to 0.5
- queries: float32 [16, 4], replicated, may hold values from -4 to 4
Outputs:
- attended: bfloat16 [64, 128, 128], P('rows', 'dates')
- conv_grad: float32 [3, 3, 64, 128], replicated
- first_gain_grad: float32 [128], replicated
- first_shift_grad: float32 [128], replicated
- block_grad: float32 [3, 3, 128, 128], replicated
- gain_grad: float32 [128], replicated
- shift_grad: float32 [128], replicated
- key_grad: float32 [128, 64], replicated
- query_grad: float32 [16, 4], replicated
The draws below stay inside these ranges and needn't reach their ends.
Inputs may be any that keep to these rules, and one draw needn't show every extreme that they name: Every pixel has at least one valid date.
All inputs are finite; a program needn't handle non-finite values.
Results may differ from the reference program's by a relative error of at most 0.018.
Values may be sent and summed in bfloat16 or wider, within the bound.
No kernel may reach another device: no remote copies, remote signals or barrier semaphores. Data moves between devices by JAX's collectives and lax.ppermute only.
A program may use at most 128 MiB of HBM per device.

```python
import jax
import jax.numpy as jnp
from jax import lax

C_IN = 64
FEAT = 128
HEADS = 16
KEY = 4
GROUPS = 4
COLS = 128
DATES = 16
ROWS_IN = 128
ROWS_OUT = 64


def draw_images(key, part):
    key = jax.random.fold_in(key, 11)
    key_base = jax.random.fold_in(key, 0)
    key_shared = jax.random.fold_in(key, 2)
    key_offset = jax.random.fold_in(key, 3)
    base_shape = (DATES, ROWS_IN, COLS, 2, C_IN)
    shared_shape = (DATES, ROWS_IN, 2 * COLS + 3)
    row_frac = (jnp.arange(ROWS_IN, dtype=jnp.float32) / ROWS_IN)[None, :, None, None, None]
    offsets = jax.random.uniform(key_offset, (C_IN,), jnp.float32, 1.0, 3.0)
    base_noise = jnp.clip(jax.random.normal(key_base, base_shape, jnp.float32), -4.0, 4.0)
    shared_raw = jnp.clip(jax.random.normal(key_shared, shared_shape, jnp.float32), -4.0, 4.0)
    row_scale = jnp.exp(1.09 * row_frac)
    span = 2 * COLS
    smooth = 0.5 * (shared_raw[:, :, 0:span] + shared_raw[:, :, 1:span + 1] + shared_raw[:, :, 2:span + 2] + shared_raw[:, :, 3:span + 3])
    shared = smooth.reshape(DATES, ROWS_IN, COLS, 2)[..., None]
    values = (base_noise + shared) * row_scale + offsets
    return jnp.clip(values, -12.0, 12.0).reshape(DATES, ROWS_IN, COLS, 2 * C_IN).astype(jnp.bfloat16)


def draw_valid(key, part):
    key = jax.random.fold_in(key, 23)
    key_coin, key_pick = jax.random.split(key)
    row_ids = jnp.arange(ROWS_OUT, dtype=jnp.int32)[None, :, None]
    clear_level = 2 + 6 * row_ids // ROWS_OUT
    coin_value = jax.random.randint(key_coin, (DATES, ROWS_OUT, COLS), 0, 8)
    chosen_date = jax.random.randint(key_pick, (1, ROWS_OUT, COLS), 0, DATES)
    date_ids = jnp.arange(DATES, dtype=jnp.int32)[:, None, None]
    return jnp.where((coin_value < clear_level) | (date_ids == chosen_date), 1, 0).astype(jnp.int32)


def set_ends(entries, own_key, least, high):
    longest = entries.shape.index(max(entries.shape))
    spots = []
    for shift in (0, 1):
        where = [jax.random.randint(jax.random.fold_in(own_key, axis), (), 0, length) for axis, length in enumerate(entries.shape)]
        where[longest] = (where[longest] + shift) % entries.shape[longest]
        spots.append(tuple(where))
    return entries.at[spots[0]].set(least).at[spots[1]].set(high)


def block_scale(key, shape, cuts, low, largest):
    def one(dim, blocks):
        steps = jax.random.uniform(jax.random.fold_in(jax.random.fold_in(key, 6), dim), (blocks,), jnp.float32, low / len(cuts), largest / len(cuts))
        return jnp.repeat(jnp.exp(steps), shape[dim] // blocks).reshape((-1,) + (1,) * (len(shape) - dim - 1))

    gain = one(*cuts[0])
    for cut in cuts[1:]:
        gain = gain * one(*cut)
    return gain


def scatter_about(rng, extent, scale, limit, cuts=(), held_as=jnp.bfloat16):
    values = scale * jax.random.normal(rng, extent, jnp.float32)
    if cuts:
        values = values * block_scale(rng, extent, cuts, -0.22, 0.18)
    return jnp.clip(values, -limit, limit).astype(held_as)


def setup_inputs(seed: int = 0) -> dict:
    arg_keys = jax.random.split(jax.random.key(seed), 13)
    return {
        "images": draw_images(jax.random.fold_in(arg_keys[12], 71), 0),
        "day_index": set_ends(jax.random.randint(arg_keys[1], (DATES,), 1, 366), jax.random.fold_in(arg_keys[1], 1), 1, 365).astype(jnp.int32),
        "valid": draw_valid(jax.random.fold_in(arg_keys[12], 71), 0),
        "out_grad": scatter_about(arg_keys[3], (ROWS_OUT, COLS, FEAT), 1.0, 6.0, ((0, 8), (1, 4))),
        "conv_weight": scatter_about(arg_keys[4], (3, 3, C_IN, FEAT), (9 * C_IN) ** -0.5, 0.25),
        "first_gain": jnp.clip(1.0 + 0.18 * jax.random.normal(arg_keys[5], (FEAT,), jnp.float32), 0.1, 1.9),
        "first_shift": scatter_about(arg_keys[6], (FEAT,), 0.5, 3.0, (), jnp.float32),
        "block_weight": scatter_about(arg_keys[7], (3, 3, FEAT, FEAT), (9 * FEAT) ** -0.5, 0.1875),
        "gn_gain": jnp.clip(1.0 + 0.18 * jax.random.normal(arg_keys[8], (FEAT,), jnp.float32), 0.1, 1.9),
        "gn_shift": scatter_about(arg_keys[9], (FEAT,), 0.5, 3.0, (), jnp.float32),
        "key_weight": scatter_about(arg_keys[10], (FEAT, HEADS * KEY), FEAT ** -0.5, 0.5),
        "queries": scatter_about(arg_keys[11], (HEADS, KEY), 1.0, 4.0, (), jnp.float32),
    }


EPS = 1e-05

def silu_slope(values):
    sigmoid_part = jax.nn.sigmoid(values)
    return sigmoid_part * (1.0 + values * (1.0 - sigmoid_part))

def encoding(day_index, feat_width):
    half_range = jnp.arange(feat_width // 2, dtype=jnp.float32)
    frequency = jnp.exp(half_range * (-2.0 * jnp.log(1000.0) / feat_width))
    angles = day_index.astype(jnp.float32)[:, None] * frequency[None, :]
    return jnp.stack([jnp.sin(angles), jnp.cos(angles)], axis=-1).reshape(day_index.shape[0], feat_width)

def convolve(single_date, weight_float):
    natural = single_date.reshape(1, ROWS_IN, 2 * COLS, C_IN).astype(jnp.float32)
    result = lax.conv_general_dilated(natural, weight_float, (2, 2), ((1, 1), (1, 1)), dimension_numbers=('NHWC', 'HWIO', 'NHWC'), precision=lax.Precision.HIGHEST)
    return result[0]

def conv_same(hidden_float, weight_float):
    result = lax.conv_general_dilated(hidden_float[None], weight_float, (1, 1), ((1, 1), (1, 1)), dimension_numbers=('NHWC', 'HWIO', 'NHWC'), precision=lax.Precision.HIGHEST)
    return result[0]

def group_total(values):
    return lax.optimization_barrier(jnp.sum(values.reshape(-1, GROUPS, FEAT // GROUPS), axis=(0, 2)))

def first_block(single_date, weight_float, first_gain, first_shift):
    stored = convolve(single_date, weight_float).astype(jnp.bfloat16)
    stored = lax.optimization_barrier(stored)
    down_values = stored.astype(jnp.float32)
    norm_count = ROWS_OUT * COLS * (FEAT // GROUPS)
    mean_group = group_total(down_values) / norm_count
    inv_group = 1.0 / jnp.sqrt(group_total(down_values * down_values) / norm_count - mean_group * mean_group + EPS)
    mean_full = jnp.repeat(mean_group, FEAT // GROUPS)
    inv_full = jnp.repeat(inv_group, FEAT // GROUPS)
    first_centred = (down_values - mean_full) * inv_full
    first_linear = first_centred * first_gain + first_shift
    hidden = jax.nn.silu(first_linear).astype(jnp.bfloat16)
    return (first_centred, first_linear, inv_full, hidden)

def row_core(conv_row, valid_row, grad_row, norm_mean, norm_inv, gn_gain, gn_shift, key_weight, queries, position_table, grad_scale):
    centred = (conv_row.astype(jnp.float32) - norm_mean[:, None, :]) * norm_inv[:, None, :]
    linear = centred * gn_gain + gn_shift
    features = (jax.nn.silu(linear) + position_table[:, None, :]).astype(jnp.bfloat16)
    date_count, pixel_count, feat_width = features.shape
    score_scale = KEY ** (-0.5)
    feat_float = features.astype(jnp.float32)
    key_vectors = jnp.einsum('tpf,fk->tpk', feat_float, key_weight.astype(jnp.float32)).reshape(date_count, pixel_count, HEADS, KEY)
    scores = jnp.einsum('tphk,hk->tph', key_vectors, queries) * score_scale
    exponent = valid_row.astype(jnp.float32)[:, :, None] * jnp.exp(scores)
    weights = exponent / lax.optimization_barrier(jnp.sum(exponent, axis=0, keepdims=True))
    rounded = weights.astype(jnp.bfloat16).astype(jnp.float32)
    head_values = feat_float.reshape(date_count, pixel_count, HEADS, feat_width // HEADS)
    attended = jnp.einsum('tph,tphe->phe', rounded, head_values).reshape(pixel_count, feat_width)
    upstream = (grad_row.astype(jnp.float32) * grad_scale).reshape(pixel_count, HEADS, feat_width // HEADS)
    attn_grad = jnp.einsum('phe,tphe->tph', upstream, head_values)
    score_grad = weights * (attn_grad - lax.optimization_barrier(jnp.sum(weights * attn_grad, axis=0, keepdims=True)))
    query_part = jnp.einsum('tph,tphk->hk', score_grad, key_vectors) * score_scale
    key_grads = (score_grad[..., None] * queries[None, None] * score_scale).astype(jnp.bfloat16).astype(jnp.float32).reshape(date_count, pixel_count, HEADS * KEY)
    key_part = jnp.einsum('tpf,tpk->fk', feat_float, key_grads)
    feat_grad = (rounded[..., None] * upstream[None]).reshape(date_count, pixel_count, feat_width) + jnp.einsum('tpk,fk->tpf', key_grads, key_weight.astype(jnp.float32))
    linear_grad = feat_grad * silu_slope(linear)
    centred_grad = linear_grad * gn_gain
    return (attended.astype(jnp.bfloat16), centred, linear_grad, centred_grad, key_part, query_part)

def group_sums(values):
    return lax.optimization_barrier(jnp.sum(values.reshape(values.shape[0], -1, GROUPS, FEAT // GROUPS), axis=(1, 3)))

def reference(images, day_index, valid, out_grad, conv_weight, first_gain, first_shift, block_weight, gn_gain, gn_shift, key_weight, queries):
    weight_float = conv_weight.astype(jnp.float32)
    block_float = block_weight.astype(jnp.float32)

    def forward_date(single_date):
        hidden = first_block(single_date, weight_float, first_gain, first_shift)[3]
        return conv_same(hidden.astype(jnp.float32), block_float).astype(jnp.bfloat16)
    block_out = lax.map(forward_date, images)
    norm_count = ROWS_OUT * COLS * (FEAT // GROUPS)

    def date_stats(one_frame):
        grouped = one_frame.astype(jnp.float32).reshape(-1, GROUPS, FEAT // GROUPS)
        return (lax.optimization_barrier(jnp.sum(grouped, axis=(0, 2))), lax.optimization_barrier(jnp.sum(grouped * grouped, axis=(0, 2))))
    sum_first, sum_second = lax.map(date_stats, block_out)
    mean_group = sum_first / norm_count
    inv_group = 1.0 / jnp.sqrt(sum_second / norm_count - mean_group * mean_group + EPS)
    norm_mean = jnp.repeat(mean_group, FEAT // GROUPS, axis=1)
    norm_inv = jnp.repeat(inv_group, FEAT // GROUPS, axis=1)
    position_table = encoding(day_index, FEAT)
    grad_scale = (ROWS_OUT * COLS) ** (-0.5)

    def core_at(row_index):
        conv_row = lax.dynamic_index_in_dim(block_out, row_index, 1, keepdims=False)
        valid_row = lax.dynamic_index_in_dim(valid, row_index, 1, keepdims=False)
        grad_row = lax.dynamic_index_in_dim(out_grad, row_index, 0, keepdims=False)
        return row_core(conv_row, valid_row, grad_row, norm_mean, norm_inv, gn_gain, gn_shift, key_weight, queries, position_table, grad_scale)

    def first_pass(carry_sums, row_index):
        attended, centred, linear_grad, centred_grad, key_part, query_part = core_at(row_index)
        tail_first, tail_second, gain_sum, shift_sum, key_sum, query_sum = carry_sums
        updated = (tail_first + group_sums(centred_grad), tail_second + group_sums(centred_grad * centred), gain_sum + lax.optimization_barrier(jnp.sum(linear_grad * centred, axis=(0, 1))), shift_sum + lax.optimization_barrier(jnp.sum(linear_grad, axis=(0, 1))), key_sum + key_part, query_sum + query_part)
        return (updated, attended)
    zero_groups = jnp.zeros((DATES, GROUPS), jnp.float32)
    start_sums = (zero_groups, zero_groups, jnp.zeros((FEAT,), jnp.float32), jnp.zeros((FEAT,), jnp.float32), jnp.zeros((FEAT, HEADS * KEY), jnp.float32), jnp.zeros((HEADS, KEY), jnp.float32))
    row_indices = jnp.arange(ROWS_OUT).astype(jnp.int32)
    totals, attended = lax.scan(first_pass, start_sums, row_indices)
    tail_first, tail_second, gain_grad, shift_grad, key_grad, query_grad = totals
    first_mean = jnp.repeat(tail_first, FEAT // GROUPS, axis=1) / norm_count
    second_mean = jnp.repeat(tail_second, FEAT // GROUPS, axis=1) / norm_count

    def second_pass(row_index):
        outputs = core_at(row_index)
        centred, centred_grad = (outputs[1], outputs[3])
        return (norm_inv[:, None, :] * (centred_grad - first_mean[:, None, :] - centred * second_mean[:, None, :])).astype(jnp.bfloat16)
    pre_grad = lax.map(second_pass, row_indices)

    def add_date(running, date_index):
        conv_sum, block_sum, gain_sum, shift_sum = running
        single_date = lax.dynamic_index_in_dim(images, date_index, 0, keepdims=False)
        first_centred, first_linear, first_inv, hidden = first_block(single_date, weight_float, first_gain, first_shift)
        cotangent = lax.dynamic_index_in_dim(pre_grad, date_index, 1, keepdims=False).astype(jnp.float32)
        unused, block_pullback = jax.vjp(conv_same, hidden.astype(jnp.float32), block_float)
        hidden_grad, block_part = block_pullback(cotangent)
        first_linear_grad = hidden_grad * silu_slope(first_linear)
        first_centred_grad = first_linear_grad * first_gain
        tail_one = jnp.repeat(group_total(first_centred_grad), FEAT // GROUPS) / norm_count
        tail_two = jnp.repeat(group_total(first_centred_grad * first_centred), FEAT // GROUPS) / norm_count
        down_grad = (first_inv * (first_centred_grad - tail_one - first_centred * tail_two)).astype(jnp.bfloat16)
        unused_down, down_pullback = jax.vjp(lambda weight_arg: convolve(single_date, weight_arg), weight_float)
        conv_part = down_pullback(down_grad.astype(jnp.float32))[0]
        updated = (conv_sum + conv_part, block_sum + block_part, gain_sum + lax.optimization_barrier(jnp.sum(first_linear_grad * first_centred, axis=(0, 1))), shift_sum + lax.optimization_barrier(jnp.sum(first_linear_grad, axis=(0, 1))))
        return (updated, None)
    start_grads = (jnp.zeros_like(weight_float), jnp.zeros_like(block_float), jnp.zeros((FEAT,), jnp.float32), jnp.zeros((FEAT,), jnp.float32))
    grads, unused_out = lax.scan(add_date, start_grads, jnp.arange(DATES).astype(jnp.int32))
    conv_grad, block_grad, first_gain_grad, first_shift_grad = grads
    return (attended, conv_grad, first_gain_grad, first_shift_grad, block_grad, gain_grad, shift_grad, key_grad, query_grad)
```

```python
import functools

import jax
import jax.numpy as jnp
from jax import lax
from jax.experimental import pallas as pl
from jax.experimental.pallas import tpu as pltpu
from jax.sharding import PartitionSpec as P

GROUPS = 4


EPS = 1e-05


MIB = 1 << 20


F32 = jnp.float32


BF16 = jnp.bfloat16


def product(left, right, left_dim, right_dim):
    return lax.dot_general(
        left, right, (((left_dim,), (right_dim,)), ((), ())), preferred_element_type=F32
    )


def group_sum(values):
    width = values.shape[-1]
    lane_group = lax.broadcasted_iota(jnp.int32, values.shape, 1) // (width // GROUPS)
    spread = jnp.zeros_like(values)
    for group in range(GROUPS):
        inside = lane_group == group
        total = jnp.sum(jnp.where(inside, values, 0.0), axis=1, keepdims=True)
        spread = spread + jnp.where(inside, total, 0.0)
    return spread


def sigmoid(values):
    return 0.5 * jnp.tanh(0.5 * values) + 0.5


def from_left(values):
    column = lax.broadcasted_iota(jnp.int32, values.shape, 1)
    return jnp.where(column > 0, pltpu.roll(values, 1, 1), 0.0)


def from_right(values):
    count = values.shape[1]
    column = lax.broadcasted_iota(jnp.int32, values.shape, 1)
    return jnp.where(column < count - 1, pltpu.roll(values, count - 1, 1), 0.0)


def column_sum(values):
    return jnp.sum(jnp.sum(values, axis=0), axis=0, keepdims=True)


def split(values):
    high = values.astype(BF16)
    return high, (values - high.astype(F32)).astype(BF16)


def store_sums(sums_ref, date, dates, first, second):
    for copy in range(sums_ref.shape[0]):
        sums_ref[copy, pl.ds(date, 1), :] = first
        sums_ref[copy, pl.ds(dates + date, 1), :] = second


def norm_table(sums_ref, table_ref, dates, norm_count):
    means = group_sum(jnp.sum(sums_ref[...], axis=0)) / norm_count
    mean = means[:dates]
    table_ref[:dates] = mean
    table_ref[dates:] = 1.0 / jnp.sqrt(means[dates:] - mean * mean + EPS)


def down_kernel(dates, img_ref, above_ref, weight_ref, out_ref, top_ref, low_ref, sums_ref, table):
    date = pl.program_id(0)
    half = weight_ref.shape[2]

    @pl.when(date == 0)
    def _():
        for tap in range(3):
            base = tap * 2 * half
            table[base : base + half, : 2 * half] = weight_ref[tap, 1]
            table[base + half : base + 2 * half, : 2 * half] = weight_ref[tap, 2]
            table[base : base + half, 2 * half :] = jnp.zeros_like(weight_ref[tap, 0])
            table[base + half : base + 2 * half, 2 * half :] = weight_ref[tap, 0]

    even, odd = img_ref[0, :, 0], img_ref[0, :, 1]
    above = jnp.concatenate([above_ref[0][None], odd[:-1]], axis=0)
    rows, cols, width = even.shape
    taps = jnp.concatenate([above, even, odd], axis=-1).reshape(rows * cols, 3 * width)
    both = product(taps, table[...], 1, 0).reshape(rows, cols, 2 * width)
    stored = (both[..., :width] + from_left(both[..., width:])).astype(BF16)
    out_ref[0] = stored
    top_ref[0] = stored[0]
    low_ref[0] = stored[rows - 1]
    values = stored.astype(F32)
    store_sums(sums_ref, date, dates, column_sum(values), column_sum(values * values))


def block_kernel(
    dates,
    norm_count,
    edge_ref,
    conv_ref,
    up_ref,
    down_ref,
    stats_ref,
    gain_ref,
    weight_ref,
    out_ref,
    hidden_ref,
    norm_ref,
    sums_ref,
    table,
):
    date = pl.program_id(0)
    width = conv_ref.shape[-1]

    @pl.when(date == 0)
    def _():
        norm_table(stats_ref, norm_ref, dates, norm_count)
        for row_tap in range(3):
            for col_tap in range(3):
                table[
                    row_tap * width : (row_tap + 1) * width, col_tap * width : (col_tap + 1) * width
                ] = weight_ref[row_tap, col_tap]

    scale = norm_ref[pl.ds(dates + date, 1), :] * gain_ref[0:1]
    shift = gain_ref[1:2] - norm_ref[pl.ds(date, 1), :] * scale

    def activate(values):
        linear = values.astype(F32) * scale + shift
        return linear * sigmoid(linear)

    rows, cols = conv_ref.shape[1:3]
    hidden_ref[0, 0] = (activate(up_ref[0]) * edge_ref[0]).astype(BF16)
    hidden_ref[0, rows + 1] = (activate(down_ref[0]) * edge_ref[1]).astype(BF16)
    hidden_ref[0, 1 : rows + 1] = activate(conv_ref[0]).astype(BF16)
    taps = jnp.concatenate(
        [hidden_ref[0, tap : tap + rows] for tap in range(3)], axis=-1
    ).reshape(rows * cols, 3 * width)
    terms = product(taps, table[...], 1, 0).reshape(rows, cols, 3 * width)
    stored = (
        terms[..., width : 2 * width]
        + from_left(terms[..., :width])
        + from_right(terms[..., 2 * width :])
    ).astype(BF16)
    out_ref[0] = stored
    values = stored.astype(F32)
    store_sums(sums_ref, date, dates, column_sum(values), column_sum(values * values))


def score_kernel(
    dates,
    norm_count,
    grad_scale,
    block_ref,
    stats_ref,
    gain_ref,
    position_ref,
    grad_ref,
    valid_ref,
    score_ref,
    spread_ref,
    feat_ref,
    exp_ref,
    attn_ref,
    norm_ref,
    packed_ref,
    total,
    mean,
):
    date = pl.program_id(0)
    rows, cols, width = block_ref.shape[1:]

    @pl.when(date == 0)
    def _():
        norm_table(stats_ref, norm_ref, dates, norm_count)
        total[...] = jnp.zeros_like(total)
        mean[...] = jnp.zeros_like(mean)

    scale = norm_ref[pl.ds(dates + date, 1), :] * gain_ref[2:3]
    shift = gain_ref[3:4] - norm_ref[pl.ds(date, 1), :] * scale
    linear = block_ref[0].astype(F32) * scale + shift
    features = (linear * sigmoid(linear) + position_ref[pl.ds(date, 1), :]).astype(BF16)
    feat_ref[0] = features
    upstream = grad_ref[...]
    upstream = jnp.stack([upstream[:, row].reshape(cols, width) for row in range(rows)])
    parts = split(upstream.astype(F32) * features.astype(F32))
    parts = jnp.concatenate(parts, axis=-1).reshape(rows * cols, 2 * width)
    attn = product(parts, spread_ref[...], 1, 0).reshape(rows, cols, width) * grad_scale
    both = product(features.reshape(rows * cols, width), score_ref[...], 1, 0)
    scores = (both[:, :width] + both[:, width:]).reshape(rows, cols, width)
    diagonal = lax.broadcasted_iota(jnp.int32, (cols, cols), 0) == lax.broadcasted_iota(
        jnp.int32, (cols, cols), 1
    )
    ones = jnp.ones((cols, width), BF16)
    clear = jnp.concatenate(
        [jnp.where(diagonal, valid_ref[0, row : row + 1], 0.0) for row in range(rows)], axis=0
    ).astype(BF16)
    clear = product(clear, ones, 1, 0).reshape(rows, cols, width)
    exponent = clear * jnp.exp(scores)
    running = total[...] + exponent
    share = jnp.where(running > 0.0, exponent / running, 0.0)
    total[...] = running
    mean[...] += share * (attn - mean[...])
    exp_ref[0] = exponent
    attn_ref[0] = attn

    @pl.when(date == dates - 1)
    def _():
        place = lax.broadcasted_iota(jnp.int32, (cols, width), 1) % rows
        for index, source in enumerate((total, mean)):
            dense = jnp.zeros((cols, width), F32)
            for row in range(rows):
                dense = dense + jnp.where(place == row, source[row], 0.0)
            for copy in range(packed_ref.shape[0]):
                packed_ref[copy, index] = dense


def attend_kernel(
    dates,
    grad_scale,
    packed_ref,
    feat_ref,
    exp_ref,
    attn_ref,
    block_ref,
    norm_ref,
    gain_ref,
    query_ref,
    grad_ref,
    key_ref,
    spread_ref,
    grad_out_ref,
    up_ref,
    down_ref,
    part_ref,
    key_out_ref,
    vector_ref,
    sums_ref,
    inverse,
    average,
    attended,
):
    date = pl.program_id(0)
    rows, cols, width = block_ref.shape[1:]

    @pl.when(date == 0)
    def _():
        denominator = jnp.sum(packed_ref[:, 0], axis=0)
        reciprocal = 1.0 / denominator
        mean = jnp.sum(packed_ref[:, 0] * reciprocal * packed_ref[:, 1], axis=0)
        place = lax.broadcasted_iota(jnp.int32, (cols, width), 1) % rows
        for values, target in ((reciprocal, inverse), (mean, average)):
            parts = jnp.concatenate(split(values), axis=-1)
            wide_place = jnp.concatenate([place, place], axis=-1)
            picked = jnp.concatenate(
                [jnp.where(wide_place == row, parts, jnp.zeros_like(parts)) for row in range(rows)], axis=0
            )
            target[...] = product(picked, spread_ref[...], 1, 0).reshape(rows, cols, width)
        attended[...] = jnp.zeros_like(attended)
        key_out_ref[...] = jnp.zeros_like(key_out_ref)
        vector_ref[...] = jnp.zeros_like(vector_ref)

    features = feat_ref[0]
    weights = exp_ref[0] * inverse[...]
    rounded = weights.astype(BF16).astype(F32)
    attended[...] += rounded * features.astype(F32)
    score_grad = weights * (attn_ref[0] - average[...])
    spread_grad = score_grad * query_ref[0:1]
    rest = spread_grad - spread_grad.astype(BF16).astype(F32)
    lane = lax.broadcasted_iota(jnp.int32, spread_grad.shape, 2) % (width // 16)
    key_grads = jnp.where(lane == 5, rest, spread_grad).astype(BF16).reshape(rows * cols, width)
    key_out_ref[...] += product(features.reshape(rows * cols, width), key_grads, 0, 0)
    upstream = grad_ref[...]
    upstream = jnp.stack([upstream[:, row].reshape(cols, width) for row in range(rows)])
    feat_grad = rounded * (upstream.astype(F32) * grad_scale) + product(
        key_grads, key_ref[...], 1, 1
    ).reshape(rows, cols, width)
    gain = gain_ref[2:3]
    centred = (block_ref[0].astype(F32) - norm_ref[pl.ds(date, 1), :]) * norm_ref[
        pl.ds(dates + date, 1), :
    ]
    linear = centred * gain + gain_ref[3:4]
    part = sigmoid(linear)
    linear_grad = feat_grad * (part * (1.0 + linear * (1.0 - part)))
    first = column_sum(linear_grad)
    second = column_sum(linear_grad * centred)
    vector_ref[0:1] += second
    vector_ref[1:2] += first
    store_sums(sums_ref, date, dates, first * gain, second * gain)
    stored = (linear_grad * gain).astype(BF16)
    grad_out_ref[0] = stored
    up_ref[0, 0] = stored[0]
    up_ref[0, 1] = block_ref[0, 0]
    down_ref[0, 0] = stored[rows - 1]
    down_ref[0, 1] = block_ref[0, rows - 1]

    @pl.when(date == dates - 1)
    def _():
        devices, piece = part_ref.shape[0], part_ref.shape[2]
        for device in range(devices):
            part_ref[device] = attended[:, device * piece : (device + 1) * piece].astype(BF16)
        key_part = key_out_ref[...]
        place = lax.broadcasted_iota(jnp.int32, (width, width), 1) % (width // 16)
        both = pltpu.roll(key_part, width - 4, 1) + pltpu.roll(key_part, width - 5, 1)
        both = jnp.where(place == 0, both, 0.0)
        both = both + pltpu.roll(both, 1, 1)
        both = both + pltpu.roll(both, 2, 1)
        vector_ref[2:3] = 0.5 * jnp.sum(key_ref[...].astype(F32) * both, axis=0, keepdims=True)


def hidden_kernel(
    dates,
    norm_count,
    edge_ref,
    grad_ref,
    block_ref,
    up_ref,
    down_ref,
    tails_ref,
    norm_ref,
    weight_ref,
    conv_ref,
    first_norm_ref,
    gain_ref,
    pre_ref,
    out_ref,
    vector_ref,
    sums_ref,
    table,
    factors,
    padded,
):
    date = pl.program_id(0)
    rows, cols, width = block_ref.shape[1:]

    @pl.when(date == 0)
    def _():
        tails = group_sum(jnp.sum(tails_ref[...], axis=0)) / norm_count
        mean, inverse = norm_ref[:dates], norm_ref[dates:]
        slope = -inverse * inverse * tails[dates:]
        factors[0:dates] = slope
        factors[dates : 2 * dates] = -inverse * tails[:dates] - mean * slope
        vector_ref[...] = jnp.zeros_like(vector_ref)
        for row_tap in range(3):
            for col_tap in range(3):
                table[
                    col_tap * width : (col_tap + 1) * width, row_tap * width : (row_tap + 1) * width
                ] = weight_ref[2 - row_tap, col_tap]

    inverse = norm_ref[pl.ds(dates + date, 1), :]
    slope = factors[pl.ds(date, 1), :]
    constant = factors[pl.ds(dates + date, 1), :]

    def finish(grad, values):
        return grad.astype(F32) * inverse + (values.astype(F32) * slope + constant)

    stored = finish(grad_ref[0], block_ref[0]).astype(BF16)
    pre_ref[0] = stored
    padded[0] = (finish(up_ref[0, 0], up_ref[0, 1]) * edge_ref[0]).astype(BF16)
    padded[rows + 1] = (finish(down_ref[0, 0], down_ref[0, 1]) * edge_ref[1]).astype(BF16)
    padded[1 : rows + 1] = stored
    taps = jnp.concatenate([padded[tap : tap + rows] for tap in range(3)], axis=-1).reshape(
        rows * cols, 3 * width
    )
    terms = product(taps, table[...], 1, 1).reshape(rows, cols, 3 * width)
    hidden_grad = (
        terms[..., width : 2 * width]
        + from_right(terms[..., :width])
        + from_left(terms[..., 2 * width :])
    )
    gain = gain_ref[0:1]
    centred = (conv_ref[0].astype(F32) - first_norm_ref[pl.ds(date, 1), :]) * first_norm_ref[
        pl.ds(dates + date, 1), :
    ]
    linear = centred * gain + gain_ref[1:2]
    part = sigmoid(linear)
    linear_grad = hidden_grad * (part * (1.0 + linear * (1.0 - part)))
    out_ref[0] = linear_grad
    first = column_sum(linear_grad)
    second = column_sum(linear_grad * centred)
    vector_ref[0:1] += second
    vector_ref[1:2] += first
    store_sums(sums_ref, date, dates, first * gain, second * gain)


def block_grad_kernel(dates, hidden_ref, pre_ref, key_ref, vector_ref, out_ref, total):
    date = pl.program_id(0)
    rows, cols, width = pre_ref.shape[1:]

    @pl.when(date == 0)
    def _():
        total[...] = jnp.zeros_like(total)

    grads = pre_ref[0].astype(F32)
    grads = jnp.concatenate(
        [from_right(grads).astype(BF16), pre_ref[0], from_left(grads).astype(BF16)], axis=-1
    ).reshape(rows * cols, 3 * width)
    taps = jnp.concatenate(
        [hidden_ref[0, tap : tap + rows] for tap in range(3)], axis=-1
    ).reshape(rows * cols, 3 * width)
    total[...] += product(taps, grads, 0, 0)

    @pl.when(date == dates - 1)
    def _():
        for row_tap in range(3):
            for col_tap in range(3):
                base = (row_tap * 3 + col_tap) * width
                out_ref[base : base + width] = total[
                    row_tap * width : (row_tap + 1) * width, col_tap * width : (col_tap + 1) * width
                ].astype(BF16)
        high, low = split(key_ref[...])
        out_ref[9 * width : 10 * width] = high
        out_ref[10 * width : 11 * width] = low
        high, low = split(vector_ref[...])
        out_ref[11 * width : 11 * width + 16] = jnp.concatenate([high, low], axis=0)
        out_ref[11 * width + 16 :] = jnp.zeros_like(out_ref[11 * width + 16 :])


def conv_grad_kernel(
    dates,
    norm_count,
    img_ref,
    above_ref,
    conv_ref,
    grad_ref,
    tails_ref,
    norm_ref,
    gain_ref,
    vector_ref,
    out_ref,
    factors,
    total,
):
    date = pl.program_id(0)
    rows, cols, width = conv_ref.shape[1:]
    half = width // 2

    @pl.when(date == 0)
    def _():
        tails = group_sum(jnp.sum(tails_ref[...], axis=0)) / norm_count
        mean, inverse = norm_ref[:dates], norm_ref[dates:]
        slope = -inverse * inverse * tails[dates:]
        factors[0:dates] = slope
        factors[dates : 2 * dates] = -inverse * tails[:dates] - mean * slope
        total[...] = jnp.zeros_like(total)

    scale = norm_ref[pl.ds(dates + date, 1), :] * gain_ref[0:1]
    slope = factors[pl.ds(date, 1), :]
    constant = factors[pl.ds(dates + date, 1), :]
    stored = (grad_ref[0] * scale + (conv_ref[0].astype(F32) * slope + constant)).astype(BF16)
    moved = from_right(stored.astype(F32)).astype(BF16)
    grads = jnp.concatenate([stored, moved], axis=-1).reshape(rows * cols, 2 * width)
    even, odd = img_ref[0, :, 0], img_ref[0, :, 1]
    above = jnp.concatenate([above_ref[0][None], odd[:-1]], axis=0)
    taps = jnp.concatenate([above, even, odd], axis=-1).reshape(rows * cols, 3 * width)
    total[...] += product(taps, grads, 0, 0)

    @pl.when(date == dates - 1)
    def _():
        for tap in range(3):
            base = tap * width
            pair = total[base : base + width, :width].astype(BF16)
            left = total[base + half : base + width, width:].astype(BF16)
            start = tap * 3 * half
            out_ref[start : start + half] = left
            out_ref[start + half : start + 3 * half] = pair
        high, low = split(vector_ref[...])
        out_ref[9 * half : 9 * half + 16] = jnp.concatenate([high, low], axis=0)
        out_ref[9 * half + 16 :] = jnp.zeros_like(out_ref[9 * half + 16 :])


def total_kernel(in_ref, out_ref):
    total = jnp.sum(in_ref[...].astype(F32), axis=0).astype(BF16)
    for copy in range(out_ref.shape[0]):
        out_ref[copy] = total


def per_date(shape):
    zeros = (0,) * (len(shape) - 1)
    return pl.BlockSpec((1,) + tuple(shape[1:]), lambda date: (date,) + zeros)


def whole(shape):
    zeros = (0,) * len(shape)
    return pl.BlockSpec(tuple(shape), lambda date: zeros)


def call(kernel, dates, inputs, outputs, scratch, flops):
    in_specs, arrays = [], []
    for kind, array in inputs:
        arrays.append(array)
        if kind == "scalar":
            in_specs.append(pl.BlockSpec(memory_space=pltpu.SMEM))
        else:
            in_specs.append((per_date if kind == "date" else whole)(array.shape))
    out_specs = [(per_date if kind == "date" else whole)(shape) for kind, shape, _ in outputs]
    moved = sum(array.size * array.dtype.itemsize for array in arrays)
    return pl.pallas_call(
        kernel,
        grid=(dates,),
        in_specs=in_specs,
        out_specs=out_specs,
        out_shape=[jax.ShapeDtypeStruct(shape, dtype) for _, shape, dtype in outputs],
        scratch_shapes=scratch,
        compiler_params=pltpu.CompilerParams(vmem_limit_bytes=48 * MIB),
        cost_estimate=pl.CostEstimate(flops=flops, bytes_accessed=2 * moved, transcendentals=0),
    )(*arrays)


def encoding(day_index, feat_width):
    half_range = jnp.arange(feat_width // 2, dtype=F32)
    frequency = jnp.exp(half_range * (-2.0 * jnp.log(1000.0) / feat_width))
    angles = day_index.astype(F32)[:, None] * frequency[None, :]
    return jnp.stack([jnp.sin(angles), jnp.cos(angles)], axis=-1).reshape(
        day_index.shape[0], feat_width
    )


def neighbours(first_rows, last_rows):
    devices = lax.axis_size("rows")
    down = [(i, i + 1) for i in range(devices - 1)]
    up = [(i + 1, i) for i in range(devices - 1)]
    return lax.ppermute(last_rows, "rows", down), lax.ppermute(first_rows, "rows", up)


def exchange(pieces, axes):
    return lax.all_to_all(pieces, axes, split_axis=0, concat_axis=0, tiled=True)


def sum_over_all(rows_array):
    axes = ("rows", "dates")
    devices = lax.axis_size(axes)
    count, width = rows_array.shape
    pieces = exchange(rows_array.reshape(devices, count // devices, width), axes)
    spread = pl.pallas_call(
        total_kernel,
        out_shape=jax.ShapeDtypeStruct(pieces.shape, BF16),
        compiler_params=pltpu.CompilerParams(vmem_limit_bytes=32 * MIB),
    )(pieces)
    return exchange(spread, axes).reshape(count, width)


def padded_count(count, devices):
    step = 8 * devices
    return -(-count // step) * step


def local(
    images,
    day_index,
    valid,
    out_grad,
    conv_weight,
    first_gain,
    first_shift,
    block_weight,
    gn_gain,
    gn_shift,
    key_weight,
    queries,
):
    dates, rows_here, cols, pair_width = images.shape
    width = conv_weight.shape[-1]
    row_devs, date_devs = lax.axis_size("rows"), lax.axis_size("dates")
    devices = row_devs * date_devs
    rows = rows_here // 2
    heads, depth = queries.shape
    lanes = width // heads
    norm_count = float(rows * row_devs * cols * (width // GROUPS))
    grad_scale = float(rows * row_devs * cols) ** (-0.5)
    row_index = lax.axis_index("rows")
    date_start = lax.axis_index("dates") * dates
    frame = (dates, rows, cols, width)
    edge_rows = (dates, cols, width)
    tile = (row_devs, 2 * dates, width)
    flops = 2 * dates * rows * cols * width * width

    above = lax.ppermute(images[:, -1], "rows", [(i, i + 1) for i in range(row_devs - 1)])
    grads_here = lax.all_gather(out_grad, "dates")
    clear = lax.all_gather(valid.astype(BF16), "dates")
    clear = lax.dynamic_slice_in_dim(clear, date_start, dates, 1)
    clear = clear.transpose(1, 2, 0, 3).reshape(dates, rows, cols).astype(F32)
    edges = jnp.stack([row_index > 0, row_index < row_devs - 1]).astype(F32)
    gains = jnp.stack([first_gain, first_shift, gn_gain, gn_shift] * 2)
    position = lax.dynamic_slice_in_dim(encoding(day_index, width), date_start, dates, 0)
    position = jnp.concatenate([position, position], axis=0)
    half_queries = queries * (depth**-0.5)
    folded = jnp.sum(
        key_weight.astype(F32).reshape(width, heads, depth) * half_queries[None], axis=-1
    )
    folded = jnp.repeat(folded, lanes, axis=1)
    score_weight = jnp.concatenate(split(folded), axis=1)
    key_wide = jnp.pad(
        key_weight.reshape(width, heads, depth), ((0, 0), (0, 0), (0, lanes - depth))
    ).reshape(width, width)
    query_wide = jnp.concatenate(
        [half_queries, jnp.ones((heads, 2), F32), jnp.zeros((heads, lanes - depth - 2), F32)],
        axis=1,
    ).reshape(1, width)
    query_wide = jnp.broadcast_to(query_wide, (8, width))
    head_of = jnp.arange(width) // lanes
    spread = (head_of[:, None] == head_of[None, :]).astype(BF16)
    spread = jnp.concatenate([spread, spread], axis=0)

    paired = images.reshape(dates, rows, 2, cols, pair_width)
    conv_out, top, low, sums = call(
        functools.partial(down_kernel, dates),
        dates,
        [("date", paired), ("date", above), ("all", conv_weight)],
        [
            ("date", frame, BF16),
            ("date", edge_rows, BF16),
            ("date", edge_rows, BF16),
            ("all", tile, F32),
        ],
        [pltpu.VMEM((3 * pair_width, 2 * width), BF16)],
        6 * flops,
    )
    stats = exchange(sums, "rows")
    halo_up, halo_down = neighbours(top, low)
    block_out, hidden, first_norm, sums = call(
        functools.partial(block_kernel, dates, norm_count),
        dates,
        [
            ("scalar", edges),
            ("date", conv_out),
            ("date", halo_up),
            ("date", halo_down),
            ("all", stats),
            ("all", gains),
            ("all", block_weight),
        ],
        [
            ("date", frame, BF16),
            ("date", (dates, rows + 2, cols, width), BF16),
            ("all", (2 * dates, width), F32),
            ("all", tile, F32),
        ],
        [pltpu.VMEM((3 * width, 3 * width), BF16)],
        9 * flops,
    )
    stats = exchange(sums, "rows")
    features, exponent, attn, norm, packed = call(
        functools.partial(score_kernel, dates, norm_count, grad_scale),
        dates,
        [
            ("date", block_out),
            ("all", stats),
            ("all", gains),
            ("all", position),
            ("all", grads_here),
            ("date", clear),
            ("all", score_weight),
            ("all", spread),
        ],
        [
            ("date", frame, BF16),
            ("date", frame, F32),
            ("date", frame, F32),
            ("all", (2 * dates, width), F32),
            ("all", (date_devs, 2, cols, width), F32),
        ],
        [pltpu.VMEM(frame[1:], F32), pltpu.VMEM(frame[1:], F32)],
        5 * flops,
    )
    packed = exchange(packed, "dates")
    block_grad, up, low, attended, key_part, vectors, sums = call(
        functools.partial(attend_kernel, dates, grad_scale),
        dates,
        [
            ("all", packed),
            ("date", features),
            ("date", exponent),
            ("date", attn),
            ("date", block_out),
            ("all", norm),
            ("all", gains),
            ("all", query_wide),
            ("all", grads_here),
            ("all", key_wide),
            ("all", spread),
        ],
        [
            ("date", frame, BF16),
            ("date", (dates, 2, cols, width), BF16),
            ("date", (dates, 2, cols, width), BF16),
            ("all", (date_devs, rows, cols // date_devs, width), BF16),
            ("all", (width, width), F32),
            ("all", (8, width), F32),
            ("all", tile, F32),
        ],
        [pltpu.VMEM(frame[1:], F32)] * 3,
        5 * flops,
    )
    tails = exchange(sums, "rows")
    halo_up, halo_down = neighbours(up, low)
    attended = jnp.sum(exchange(attended, "dates").astype(F32), axis=0).astype(BF16)
    pre_grad, linear_grad, first_vectors, sums = call(
        functools.partial(hidden_kernel, dates, norm_count),
        dates,
        [
            ("scalar", edges),
            ("date", block_grad),
            ("date", block_out),
            ("date", halo_up),
            ("date", halo_down),
            ("all", tails),
            ("all", norm),
            ("all", block_weight),
            ("date", conv_out),
            ("all", first_norm),
            ("all", gains),
        ],
        [
            ("date", frame, BF16),
            ("date", frame, F32),
            ("all", (8, width), F32),
            ("all", tile, F32),
        ],
        [
            pltpu.VMEM((3 * width, 3 * width), BF16),
            pltpu.VMEM((2 * dates, width), F32),
            pltpu.VMEM((rows + 2, cols, width), BF16),
        ],
        9 * flops,
    )
    tails = exchange(sums, "rows")
    (block_rows,) = call(
        functools.partial(block_grad_kernel, dates),
        dates,
        [("date", hidden), ("date", pre_grad), ("all", key_part), ("all", vectors)],
        [("all", (padded_count(11 * width + 16, devices), width), BF16)],
        [pltpu.VMEM((3 * width, 3 * width), F32)],
        9 * flops,
    )
    block_rows = sum_over_all(block_rows)
    (conv_rows,) = call(
        functools.partial(conv_grad_kernel, dates, norm_count),
        dates,
        [
            ("date", paired),
            ("date", above),
            ("date", conv_out),
            ("date", linear_grad),
            ("all", tails),
            ("all", first_norm),
            ("all", gains),
            ("all", first_vectors),
        ],
        [("all", (padded_count(9 * pair_width // 2 + 16, devices), width), BF16)],
        [pltpu.VMEM((2 * dates, width), F32), pltpu.VMEM((3 * pair_width, 2 * width), F32)],
        6 * flops,
    )
    conv_rows = sum_over_all(conv_rows)

    conv_end = 9 * pair_width // 2
    conv_total = conv_rows[:conv_end].astype(F32).reshape(conv_weight.shape)
    first_sums = conv_rows[conv_end : conv_end + 16].astype(F32)
    first_sums = first_sums[:8] + first_sums[8:]
    block_total = block_rows[: 9 * width].astype(F32).reshape(block_weight.shape)
    key_sums = block_rows[9 * width : 11 * width].astype(F32)
    key_sums = key_sums[:width] + key_sums[width:]
    key_total = key_sums.reshape(width, heads, lanes)[:, :, :depth].reshape(width, heads * depth)
    sums = block_rows[11 * width : 11 * width + 16].astype(F32)
    sums = sums[:8] + sums[8:]
    query_total = sums[2].reshape(heads, lanes)[:, :depth]
    return (
        attended,
        conv_total,
        first_sums[0],
        first_sums[1],
        block_total,
        sums[0],
        sums[1],
        key_total,
        query_total,
    )


def solution(mesh):
    return jax.shard_map(
        local,
        mesh=mesh,
        in_specs=(
            P("dates", "rows", None, None),
            P(),
            P(None, "rows", "dates"),
            P("rows", "dates", None),
            P(),
            P(),
            P(),
            P(),
            P(),
            P(),
            P(),
            P(),
        ),
        out_specs=(P("rows", "dates", None), P(), P(), P(), P(), P(), P(), P(), P()),
        check_vma=False,
    )
```

```python
import functools

import jax
import jax.numpy as jnp
from jax import lax
from jax.experimental import pallas as pl
from jax.experimental.pallas import tpu as pltpu
from jax.sharding import PartitionSpec as P

GROUPS = 4


EPS = 1e-05


MIB = 1 << 20


F32 = jnp.float32


BF16 = jnp.bfloat16


def product(left, right, left_dim, right_dim):
    return lax.dot_general(
        left, right, (((left_dim,), (right_dim,)), ((), ())), preferred_element_type=F32
    )


def group_sum(values):
    width = values.shape[-1]
    lane_group = lax.broadcasted_iota(jnp.int32, values.shape, 1) // (width // GROUPS)
    spread = jnp.zeros_like(values)
    for group in range(GROUPS):
        inside = lane_group == group
        total = jnp.sum(jnp.where(inside, values, 0.0), axis=1, keepdims=True)
        spread = spread + jnp.where(inside, total, 0.0)
    return spread


def sigmoid(values):
    return 0.5 * jnp.tanh(0.5 * values) + 0.5


def from_left(values):
    column = lax.broadcasted_iota(jnp.int32, values.shape, 1)
    return jnp.where(column > 0, pltpu.roll(values, 1, 1), 0.0)


def from_right(values):
    count = values.shape[1]
    column = lax.broadcasted_iota(jnp.int32, values.shape, 1)
    return jnp.where(column < count - 1, pltpu.roll(values, count - 1, 1), 0.0)


def column_sum(values):
    return jnp.sum(jnp.sum(values, axis=0), axis=0, keepdims=True)


def split(values):
    high = values.astype(BF16)
    return high, (values - high.astype(F32)).astype(BF16)


def store_sums(sums_ref, date, dates, first, second):
    for copy in range(sums_ref.shape[0]):
        sums_ref[copy, pl.ds(date, 1), :] = first
        sums_ref[copy, pl.ds(dates + date, 1), :] = second


def norm_table(sums_ref, table_ref, dates, norm_count):
    means = group_sum(jnp.sum(sums_ref[...], axis=0)) / norm_count
    mean = means[:dates]
    table_ref[:dates] = mean
    table_ref[dates:] = 1.0 / jnp.sqrt(means[dates:] - mean * mean + EPS)


def down_kernel(dates, img_ref, above_ref, weight_ref, out_ref, top_ref, low_ref, sums_ref, table):
    date = pl.program_id(0)
    half = weight_ref.shape[2]

    @pl.when(date == 0)
    def _():
        for tap in range(3):
            base = tap * 2 * half
            table[base : base + half, : 2 * half] = weight_ref[tap, 1]
            table[base + half : base + 2 * half, : 2 * half] = weight_ref[tap, 2]
            table[base : base + half, 2 * half :] = jnp.zeros_like(weight_ref[tap, 0])
            table[base + half : base + 2 * half, 2 * half :] = weight_ref[tap, 0]

    even, odd = img_ref[0, :, 0], img_ref[0, :, 1]
    above = jnp.concatenate([above_ref[0][None], odd[:-1]], axis=0)
    rows, cols, width = even.shape
    taps = jnp.concatenate([above, even, odd], axis=-1).reshape(rows * cols, 3 * width)
    both = product(taps, table[...], 1, 0).reshape(rows, cols, 2 * width)
    stored = (both[..., :width] + from_left(both[..., width:])).astype(BF16)
    out_ref[0] = stored
    top_ref[0] = stored[0]
    low_ref[0] = stored[rows - 1]
    values = stored.astype(F32)
    store_sums(sums_ref, date, dates, column_sum(values), column_sum(values * values))


def block_kernel(
    dates,
    norm_count,
    edge_ref,
    conv_ref,
    up_ref,
    down_ref,
    stats_ref,
    gain_ref,
    weight_ref,
    out_ref,
    hidden_ref,
    norm_ref,
    sums_ref,
    table,
):
    date = pl.program_id(0)
    width = conv_ref.shape[-1]

    @pl.when(date == 0)
    def _():
        norm_table(stats_ref, norm_ref, dates, norm_count)
        for row_tap in range(3):
            for col_tap in range(3):
                table[
                    row_tap * width : (row_tap + 1) * width, col_tap * width : (col_tap + 1) * width
                ] = weight_ref[row_tap, col_tap]

    scale = norm_ref[pl.ds(dates + date, 1), :] * gain_ref[0:1]
    shift = gain_ref[1:2] - norm_ref[pl.ds(date, 1), :] * scale

    def activate(values):
        linear = values.astype(F32) * scale + shift
        return linear * sigmoid(linear)

    rows, cols = conv_ref.shape[1:3]
    hidden_ref[0, 0] = (activate(up_ref[0]) * edge_ref[0]).astype(BF16)
    hidden_ref[0, rows + 1] = (activate(down_ref[0]) * edge_ref[1]).astype(BF16)
    hidden_ref[0, 1 : rows + 1] = activate(conv_ref[0]).astype(BF16)
    taps = jnp.concatenate(
        [hidden_ref[0, tap : tap + rows] for tap in range(3)], axis=-1
    ).reshape(rows * cols, 3 * width)
    terms = product(taps, table[...], 1, 0).reshape(rows, cols, 3 * width)
    stored = (
        terms[..., width : 2 * width]
        + from_left(terms[..., :width])
        + from_right(terms[..., 2 * width :])
    ).astype(BF16)
    out_ref[0] = stored
    values = stored.astype(F32)
    store_sums(sums_ref, date, dates, column_sum(values), column_sum(values * values))


def score_kernel(
    dates,
    norm_count,
    grad_scale,
    block_ref,
    stats_ref,
    gain_ref,
    position_ref,
    grad_ref,
    valid_ref,
    score_ref,
    spread_ref,
    feat_ref,
    exp_ref,
    attn_ref,
    norm_ref,
    packed_ref,
    total,
    mean,
):
    date = pl.program_id(0)
    rows, cols, width = block_ref.shape[1:]

    @pl.when(date == 0)
    def _():
        norm_table(stats_ref, norm_ref, dates, norm_count)
        total[...] = jnp.zeros_like(total)
        mean[...] = jnp.zeros_like(mean)

    scale = norm_ref[pl.ds(dates + date, 1), :] * gain_ref[2:3]
    shift = gain_ref[3:4] - norm_ref[pl.ds(date, 1), :] * scale
    linear = block_ref[0].astype(F32) * scale + shift
    features = (linear * sigmoid(linear) + position_ref[pl.ds(date, 1), :]).astype(BF16)
    feat_ref[0] = features
    upstream = grad_ref[...]
    upstream = jnp.stack([upstream[:, row].reshape(cols, width) for row in range(rows)])
    parts = split(upstream.astype(F32) * features.astype(F32))
    parts = jnp.concatenate(parts, axis=-1).reshape(rows * cols, 2 * width)
    attn = product(parts, spread_ref[...], 1, 0).reshape(rows, cols, width) * grad_scale
    both = product(features.reshape(rows * cols, width), score_ref[...], 1, 0)
    scores = (both[:, :width] + both[:, width:]).reshape(rows, cols, width)
    diagonal = lax.broadcasted_iota(jnp.int32, (cols, cols), 0) == lax.broadcasted_iota(
        jnp.int32, (cols, cols), 1
    )
    ones = jnp.ones((cols, width), BF16)
    clear = jnp.concatenate(
        [jnp.where(diagonal, valid_ref[0, row : row + 1], 0.0) for row in range(rows)], axis=0
    ).astype(BF16)
    clear = product(clear, ones, 1, 0).reshape(rows, cols, width)
    exponent = clear * jnp.exp(scores)
    running = total[...] + exponent
    share = jnp.where(running > 0.0, exponent / running, 0.0)
    total[...] = running
    mean[...] += share * (attn - mean[...])
    exp_ref[0] = exponent
    attn_ref[0] = attn

    @pl.when(date == dates - 1)
    def _():
        place = lax.broadcasted_iota(jnp.int32, (cols, width), 1) % rows
        for index, source in enumerate((total, mean)):
            dense = jnp.zeros((cols, width), F32)
            for row in range(rows):
                dense = dense + jnp.where(place == row, source[row], 0.0)
            for copy in range(packed_ref.shape[0]):
                packed_ref[copy, index] = dense


def attend_kernel(
    dates,
    grad_scale,
    packed_ref,
    feat_ref,
    exp_ref,
    attn_ref,
    block_ref,
    norm_ref,
    gain_ref,
    query_ref,
    grad_ref,
    key_ref,
    spread_ref,
    grad_out_ref,
    up_ref,
    down_ref,
    part_ref,
    key_out_ref,
    vector_ref,
    sums_ref,
    inverse,
    average,
    attended,
):
    date = pl.program_id(0)
    rows, cols, width = block_ref.shape[1:]

    @pl.when(date == 0)
    def _():
        denominator = jnp.sum(packed_ref[:, 0], axis=0)
        reciprocal = 1.0 / denominator
        mean = jnp.sum(packed_ref[:, 0] * reciprocal * packed_ref[:, 1], axis=0)
        place = lax.broadcasted_iota(jnp.int32, (cols, width), 1) % rows
        for values, target in ((reciprocal, inverse), (mean, average)):
            parts = jnp.concatenate(split(values), axis=-1)
            wide_place = jnp.concatenate([place, place], axis=-1)
            picked = jnp.concatenate(
                [jnp.where(wide_place == row, parts, jnp.zeros_like(parts)) for row in range(rows)], axis=0
            )
            target[...] = product(picked, spread_ref[...], 1, 0).reshape(rows, cols, width)
        attended[...] = jnp.zeros_like(attended)
        key_out_ref[...] = jnp.zeros_like(key_out_ref)
        vector_ref[...] = jnp.zeros_like(vector_ref)

    features = feat_ref[0]
    weights = exp_ref[0] * inverse[...]
    rounded = weights.astype(BF16).astype(F32)
    attended[...] += rounded * features.astype(F32)
    score_grad = weights * (attn_ref[0] - average[...])
    spread_grad = score_grad * query_ref[0:1]
    rest = spread_grad - spread_grad.astype(BF16).astype(F32)
    lane = lax.broadcasted_iota(jnp.int32, spread_grad.shape, 2) % (width // 16)
    key_grads = jnp.where(lane == 5, rest, spread_grad).astype(BF16).reshape(rows * cols, width)
    key_out_ref[...] += product(features.reshape(rows * cols, width), key_grads, 0, 0)
    upstream = grad_ref[...]
    upstream = jnp.stack([upstream[:, row].reshape(cols, width) for row in range(rows)])
    feat_grad = rounded * (upstream.astype(F32) * grad_scale) + product(
        key_grads, key_ref[...], 1, 1
    ).reshape(rows, cols, width)
    gain = gain_ref[2:3]
    centred = (block_ref[0].astype(F32) - norm_ref[pl.ds(date, 1), :]) * norm_ref[
        pl.ds(dates + date, 1), :
    ]
    linear = centred * gain + gain_ref[3:4]
    part = sigmoid(linear)
    linear_grad = feat_grad * (part * (1.0 + linear * (1.0 - part)))
    first = column_sum(linear_grad)
    second = column_sum(linear_grad * centred)
    vector_ref[0:1] += second
    vector_ref[1:2] += first
    store_sums(sums_ref, date, dates, first * gain, second * gain)
    stored = (linear_grad * gain).astype(BF16)
    grad_out_ref[0] = stored
    up_ref[0, 0] = stored[0]
    up_ref[0, 1] = block_ref[0, 0]
    down_ref[0, 0] = stored[rows - 1]
    down_ref[0, 1] = block_ref[0, rows - 1]

    @pl.when(date == dates - 1)
    def _():
        devices, piece = part_ref.shape[0], part_ref.shape[2]
        for device in range(devices):
            part_ref[device] = attended[:, device * piece : (device + 1) * piece].astype(BF16)
        key_part = key_out_ref[...]
        place = lax.broadcasted_iota(jnp.int32, (width, width), 1) % (width // 16)
        both = pltpu.roll(key_part, width - 4, 1) + pltpu.roll(key_part, width - 5, 1)
        both = jnp.where(place == 0, both, 0.0)
        both = both + pltpu.roll(both, 1, 1)
        both = both + pltpu.roll(both, 2, 1)
        vector_ref[2:3] = 0.5 * jnp.sum(key_ref[...].astype(F32) * both, axis=0, keepdims=True)


def hidden_kernel(
    dates,
    norm_count,
    edge_ref,
    grad_ref,
    block_ref,
    up_ref,
    down_ref,
    tails_ref,
    norm_ref,
    weight_ref,
    conv_ref,
    first_norm_ref,
    gain_ref,
    pre_ref,
    out_ref,
    vector_ref,
    sums_ref,
    table,
    factors,
    padded,
):
    date = pl.program_id(0)
    rows, cols, width = block_ref.shape[1:]

    @pl.when(date == 0)
    def _():
        tails = group_sum(jnp.sum(tails_ref[...], axis=0)) / norm_count
        mean, inverse = norm_ref[:dates], norm_ref[dates:]
        slope = -inverse * inverse * tails[dates:]
        factors[0:dates] = slope
        factors[dates : 2 * dates] = -inverse * tails[:dates] - mean * slope
        vector_ref[...] = jnp.zeros_like(vector_ref)
        for row_tap in range(3):
            for col_tap in range(3):
                table[
                    col_tap * width : (col_tap + 1) * width, row_tap * width : (row_tap + 1) * width
                ] = weight_ref[2 - row_tap, col_tap]

    inverse = norm_ref[pl.ds(dates + date, 1), :]
    slope = factors[pl.ds(date, 1), :]
    constant = factors[pl.ds(dates + date, 1), :]

    def finish(grad, values):
        return grad.astype(F32) * inverse + (values.astype(F32) * slope + constant)

    stored = finish(grad_ref[0], block_ref[0]).astype(BF16)
    pre_ref[0] = stored
    padded[0] = (finish(up_ref[0, 0], up_ref[0, 1]) * edge_ref[0]).astype(BF16)
    padded[rows + 1] = (finish(down_ref[0, 0], down_ref[0, 1]) * edge_ref[1]).astype(BF16)
    padded[1 : rows + 1] = stored
    taps = jnp.concatenate([padded[tap : tap + rows] for tap in range(3)], axis=-1).reshape(
        rows * cols, 3 * width
    )
    terms = product(taps, table[...], 1, 1).reshape(rows, cols, 3 * width)
    hidden_grad = (
        terms[..., width : 2 * width]
        + from_right(terms[..., :width])
        + from_left(terms[..., 2 * width :])
    )
    gain = gain_ref[0:1]
    centred = (conv_ref[0].astype(F32) - first_norm_ref[pl.ds(date, 1), :]) * first_norm_ref[
        pl.ds(dates + date, 1), :
    ]
    linear = centred * gain + gain_ref[1:2]
    part = sigmoid(linear)
    linear_grad = hidden_grad * (part * (1.0 + linear * (1.0 - part)))
    out_ref[0] = linear_grad
    first = column_sum(linear_grad)
    second = column_sum(linear_grad * centred)
    vector_ref[0:1] += second
    vector_ref[1:2] += first
    store_sums(sums_ref, date, dates, first * gain, second * gain)


def block_grad_kernel(dates, hidden_ref, pre_ref, key_ref, out_ref, total):
    date = pl.program_id(0)
    rows, cols, width = pre_ref.shape[1:]

    @pl.when(date == 0)
    def _():
        total[...] = jnp.zeros_like(total)

    grads = pre_ref[0].astype(F32)
    grads = jnp.concatenate(
        [from_right(grads).astype(BF16), pre_ref[0], from_left(grads).astype(BF16)], axis=-1
    ).reshape(rows * cols, 3 * width)
    taps = jnp.concatenate(
        [hidden_ref[0, tap : tap + rows] for tap in range(3)], axis=-1
    ).reshape(rows * cols, 3 * width)
    total[...] += product(taps, grads, 0, 0)

    @pl.when(date == dates - 1)
    def _():
        for row_tap in range(3):
            for col_tap in range(3):
                base = (row_tap * 3 + col_tap) * width
                out_ref[base : base + width] = total[
                    row_tap * width : (row_tap + 1) * width, col_tap * width : (col_tap + 1) * width
                ].astype(BF16)
        key_part = key_ref[...]
        rest = key_part - key_part.astype(BF16).astype(F32)
        lanes = width // 16
        place = lax.broadcasted_iota(jnp.int32, key_part.shape, 1) % lanes
        rest = pltpu.roll(rest, lanes // 2, 1)
        key_rows = jnp.where(place < lanes // 2, key_part, rest).astype(BF16)
        out_ref[9 * width : 10 * width] = key_rows
        if out_ref.shape[0] > 10 * width:
            out_ref[10 * width :] = jnp.zeros_like(out_ref[10 * width :])


def conv_grad_kernel(
    dates,
    norm_count,
    img_ref,
    above_ref,
    conv_ref,
    grad_ref,
    tails_ref,
    norm_ref,
    gain_ref,
    vector_ref,
    other_ref,
    out_ref,
    factors,
    total,
):
    date = pl.program_id(0)
    rows, cols, width = conv_ref.shape[1:]
    half = width // 2

    @pl.when(date == 0)
    def _():
        tails = group_sum(jnp.sum(tails_ref[...], axis=0)) / norm_count
        mean, inverse = norm_ref[:dates], norm_ref[dates:]
        slope = -inverse * inverse * tails[dates:]
        factors[0:dates] = slope
        factors[dates : 2 * dates] = -inverse * tails[:dates] - mean * slope
        total[...] = jnp.zeros_like(total)

    scale = norm_ref[pl.ds(dates + date, 1), :] * gain_ref[0:1]
    slope = factors[pl.ds(date, 1), :]
    constant = factors[pl.ds(dates + date, 1), :]
    stored = (grad_ref[0] * scale + (conv_ref[0].astype(F32) * slope + constant)).astype(BF16)
    moved = from_right(stored.astype(F32)).astype(BF16)
    grads = jnp.concatenate([stored, moved], axis=-1).reshape(rows * cols, 2 * width)
    even, odd = img_ref[0, :, 0], img_ref[0, :, 1]
    above = jnp.concatenate([above_ref[0][None], odd[:-1]], axis=0)
    taps = jnp.concatenate([above, even, odd], axis=-1).reshape(rows * cols, 3 * width)
    total[...] += product(taps, grads, 0, 0)

    @pl.when(date == dates - 1)
    def _():
        for tap in range(3):
            base = tap * width
            pair = total[base : base + width, :width].astype(BF16)
            left = total[base + half : base + width, width:].astype(BF16)
            start = tap * 3 * half
            out_ref[start : start + half] = left
            out_ref[start + half : start + 3 * half] = pair
        start = 9 * half
        for source in (vector_ref, other_ref):
            high, low = split(source[...])
            out_ref[start : start + 16] = jnp.concatenate([high, low], axis=0)
            start += 16
        if out_ref.shape[0] > start:
            out_ref[start:] = jnp.zeros_like(out_ref[start:])


def total_kernel(in_ref, out_ref):
    total = jnp.sum(in_ref[...].astype(F32), axis=0).astype(BF16)
    for copy in range(out_ref.shape[0]):
        out_ref[copy] = total


def per_date(shape):
    zeros = (0,) * (len(shape) - 1)
    return pl.BlockSpec((1,) + tuple(shape[1:]), lambda date: (date,) + zeros)


def whole(shape):
    zeros = (0,) * len(shape)
    return pl.BlockSpec(tuple(shape), lambda date: zeros)


def call(kernel, dates, inputs, outputs, scratch, flops):
    in_specs, arrays = [], []
    for kind, array in inputs:
        arrays.append(array)
        if kind == "scalar":
            in_specs.append(pl.BlockSpec(memory_space=pltpu.SMEM))
        else:
            in_specs.append((per_date if kind == "date" else whole)(array.shape))
    out_specs = [(per_date if kind == "date" else whole)(shape) for kind, shape, _ in outputs]
    moved = sum(array.size * array.dtype.itemsize for array in arrays)
    return pl.pallas_call(
        kernel,
        grid=(dates,),
        in_specs=in_specs,
        out_specs=out_specs,
        out_shape=[jax.ShapeDtypeStruct(shape, dtype) for _, shape, dtype in outputs],
        scratch_shapes=scratch,
        compiler_params=pltpu.CompilerParams(vmem_limit_bytes=60 * MIB),
        cost_estimate=pl.CostEstimate(flops=flops, bytes_accessed=2 * moved, transcendentals=0),
    )(*arrays)


def encoding(day_index, feat_width):
    half_range = jnp.arange(feat_width // 2, dtype=F32)
    frequency = jnp.exp(half_range * (-2.0 * jnp.log(1000.0) / feat_width))
    angles = day_index.astype(F32)[:, None] * frequency[None, :]
    return jnp.stack([jnp.sin(angles), jnp.cos(angles)], axis=-1).reshape(
        day_index.shape[0], feat_width
    )


def neighbours(first_rows, last_rows):
    devices = lax.axis_size("rows")
    down = [(i, i + 1) for i in range(devices - 1)]
    up = [(i + 1, i) for i in range(devices - 1)]
    return lax.ppermute(last_rows, "rows", down), lax.ppermute(first_rows, "rows", up)


def exchange(pieces, axes):
    return lax.all_to_all(pieces, axes, split_axis=0, concat_axis=0, tiled=True)


def gather(array, axis):
    return lax.all_gather(array, axis, axis=0, tiled=True)


def scatter(rows_array):
    axes = ("rows", "dates")
    devices = lax.axis_size(axes)
    count, width = rows_array.shape
    return exchange(rows_array.reshape(devices, count // devices, width), axes)


def collect(pieces):
    spread = pl.pallas_call(
        total_kernel,
        out_shape=jax.ShapeDtypeStruct(pieces.shape, BF16),
        compiler_params=pltpu.CompilerParams(vmem_limit_bytes=60 * MIB),
    )(pieces)
    count, rows, width = pieces.shape
    return exchange(spread, ("rows", "dates")).reshape(count * rows, width)


def padded_count(count, devices):
    step = 8 * devices
    return -(-count // step) * step


def local(
    images,
    day_index,
    valid,
    out_grad,
    conv_weight,
    first_gain,
    first_shift,
    block_weight,
    gn_gain,
    gn_shift,
    key_weight,
    queries,
):
    dates, rows_here, cols, pair_width = images.shape
    width = conv_weight.shape[-1]
    row_devs, date_devs = lax.axis_size("rows"), lax.axis_size("dates")
    devices = row_devs * date_devs
    rows = rows_here // 2
    heads, depth = queries.shape
    lanes = width // heads
    norm_count = float(rows * row_devs * cols * (width // GROUPS))
    grad_scale = float(rows * row_devs * cols) ** (-0.5)
    row_index = lax.axis_index("rows")
    date_start = lax.axis_index("dates") * dates
    frame = (dates, rows, cols, width)
    edge_rows = (dates, cols, width)
    tile = (row_devs, 2 * dates, width)
    flops = 2 * dates * rows * cols * width * width

    above = lax.ppermute(images[:, -1], "rows", [(i, i + 1) for i in range(row_devs - 1)])
    paired = images.reshape(dates, rows, 2, cols, pair_width)
    conv_out, top, low, sums = call(
        functools.partial(down_kernel, dates),
        dates,
        [("date", paired), ("date", above), ("all", conv_weight)],
        [
            ("date", frame, BF16),
            ("date", edge_rows, BF16),
            ("date", edge_rows, BF16),
            ("all", (1, 2 * dates, width), F32),
        ],
        [pltpu.VMEM((3 * pair_width, 2 * width), BF16)],
        6 * flops,
    )
    sums, valid, out_grad, day_index, key_weight, queries = lax.optimization_barrier(
        (sums, valid, out_grad, day_index, key_weight, queries)
    )
    halo_up, halo_down = neighbours(top, low)
    stats = gather(sums, "rows")
    grad_rows, valid_rows = out_grad.size // width, valid.size // width
    packed = jnp.concatenate(
        [out_grad.reshape(grad_rows, width), valid.astype(BF16).reshape(valid_rows, width)]
    )
    packed = gather(packed[None], "dates")
    grads_here = packed[:, :grad_rows].reshape((date_devs,) + out_grad.shape)
    clear = packed[:, grad_rows:].reshape((date_devs,) + valid.shape)
    clear = lax.dynamic_slice_in_dim(clear, date_start, dates, 1)
    clear = clear.transpose(1, 2, 0, 3).reshape(dates, rows, cols).astype(F32)
    edges = jnp.stack([row_index > 0, row_index < row_devs - 1]).astype(F32)
    gains = jnp.stack([first_gain, first_shift, gn_gain, gn_shift] * 2)
    position = lax.dynamic_slice_in_dim(encoding(day_index, width), date_start, dates, 0)
    position = jnp.concatenate([position, position], axis=0)
    half_queries = queries * (depth**-0.5)
    folded = jnp.sum(
        key_weight.astype(F32).reshape(width, heads, depth) * half_queries[None], axis=-1
    )
    folded = jnp.repeat(folded, lanes, axis=1)
    score_weight = jnp.concatenate(split(folded), axis=1)
    key_wide = jnp.pad(
        key_weight.reshape(width, heads, depth), ((0, 0), (0, 0), (0, lanes - depth))
    ).reshape(width, width)
    query_wide = jnp.concatenate(
        [half_queries, jnp.ones((heads, 2), F32), jnp.zeros((heads, lanes - depth - 2), F32)],
        axis=1,
    ).reshape(1, width)
    query_wide = jnp.broadcast_to(query_wide, (8, width))
    head_of = jnp.arange(width) // lanes
    spread = (head_of[:, None] == head_of[None, :]).astype(BF16)
    spread = jnp.concatenate([spread, spread], axis=0)

    block_out, hidden, first_norm, sums = call(
        functools.partial(block_kernel, dates, norm_count),
        dates,
        [
            ("scalar", edges),
            ("date", conv_out),
            ("date", halo_up),
            ("date", halo_down),
            ("all", stats),
            ("all", gains),
            ("all", block_weight),
        ],
        [
            ("date", frame, BF16),
            ("date", (dates, rows + 2, cols, width), BF16),
            ("all", (2 * dates, width), F32),
            ("all", tile, F32),
        ],
        [pltpu.VMEM((3 * width, 3 * width), BF16)],
        9 * flops,
    )
    stats = exchange(sums, "rows")
    features, exponent, attn, norm, packed = call(
        functools.partial(score_kernel, dates, norm_count, grad_scale),
        dates,
        [
            ("date", block_out),
            ("all", stats),
            ("all", gains),
            ("all", position),
            ("all", grads_here),
            ("date", clear),
            ("all", score_weight),
            ("all", spread),
        ],
        [
            ("date", frame, BF16),
            ("date", frame, F32),
            ("date", frame, F32),
            ("all", (2 * dates, width), F32),
            ("all", (1, 2, cols, width), F32),
        ],
        [pltpu.VMEM(frame[1:], F32), pltpu.VMEM(frame[1:], F32)],
        5 * flops,
    )
    packed = gather(packed, "dates")
    block_grad, up, low, attended, key_part, vectors, sums = call(
        functools.partial(attend_kernel, dates, grad_scale),
        dates,
        [
            ("all", packed),
            ("date", features),
            ("date", exponent),
            ("date", attn),
            ("date", block_out),
            ("all", norm),
            ("all", gains),
            ("all", query_wide),
            ("all", grads_here),
            ("all", key_wide),
            ("all", spread),
        ],
        [
            ("date", frame, BF16),
            ("date", (dates, 2, cols, width), BF16),
            ("date", (dates, 2, cols, width), BF16),
            ("all", (date_devs, rows, cols // date_devs, width), BF16),
            ("all", (width, width), F32),
            ("all", (8, width), F32),
            ("all", (1, 2 * dates, width), F32),
        ],
        [pltpu.VMEM(frame[1:], F32)] * 3,
        5 * flops,
    )
    halo_up, halo_down = neighbours(up, low)
    tails = gather(sums, "rows")
    pre_grad, linear_grad, first_vectors, sums = call(
        functools.partial(hidden_kernel, dates, norm_count),
        dates,
        [
            ("scalar", edges),
            ("date", block_grad),
            ("date", block_out),
            ("date", halo_up),
            ("date", halo_down),
            ("all", tails),
            ("all", norm),
            ("all", block_weight),
            ("date", conv_out),
            ("all", first_norm),
            ("all", gains),
        ],
        [
            ("date", frame, BF16),
            ("date", frame, F32),
            ("all", (8, width), F32),
            ("all", tile, F32),
        ],
        [
            pltpu.VMEM((3 * width, 3 * width), BF16),
            pltpu.VMEM((2 * dates, width), F32),
            pltpu.VMEM((rows + 2, cols, width), BF16),
        ],
        9 * flops,
    )
    tails = exchange(sums, "rows")
    (block_rows,) = call(
        functools.partial(block_grad_kernel, dates),
        dates,
        [("date", hidden), ("date", pre_grad), ("all", key_part)],
        [("all", (padded_count(10 * width, devices), width), BF16)],
        [pltpu.VMEM((3 * width, 3 * width), F32)],
        9 * flops,
    )
    tails, block_rows = lax.optimization_barrier((tails, block_rows))
    block_pieces = scatter(block_rows)
    (conv_rows,) = call(
        functools.partial(conv_grad_kernel, dates, norm_count),
        dates,
        [
            ("date", paired),
            ("date", above),
            ("date", conv_out),
            ("date", linear_grad),
            ("all", tails),
            ("all", first_norm),
            ("all", gains),
            ("all", first_vectors),
            ("all", vectors),
        ],
        [("all", (padded_count(9 * pair_width // 2 + 32, devices), width), BF16)],
        [pltpu.VMEM((2 * dates, width), F32), pltpu.VMEM((3 * pair_width, 2 * width), F32)],
        6 * flops,
    )
    conv_pieces = scatter(conv_rows)
    conv_rows, attended = lax.optimization_barrier((conv_rows, attended))
    attended = jnp.sum(exchange(attended, "dates").astype(F32), axis=0).astype(BF16)
    block_pieces, conv_rows = lax.optimization_barrier((block_pieces, conv_rows))
    block_rows = collect(block_pieces)
    conv_rows = collect(conv_pieces)

    conv_end = 9 * pair_width // 2
    conv_total = conv_rows[:conv_end].astype(F32).reshape(conv_weight.shape)
    vectors = conv_rows[conv_end : conv_end + 32].astype(F32).reshape(2, 2, 8, width)
    first_sums, sums = vectors[:, 0] + vectors[:, 1]
    block_total = block_rows[: 9 * width].astype(F32).reshape(block_weight.shape)
    key_sums = block_rows[9 * width : 10 * width].astype(F32).reshape(width, heads, lanes)
    key_total = (key_sums[..., :depth] + key_sums[..., depth:]).reshape(width, heads * depth)
    query_total = sums[2].reshape(heads, lanes)[:, :depth]
    return (
        attended,
        conv_total,
        first_sums[0],
        first_sums[1],
        block_total,
        sums[0],
        sums[1],
        key_total,
        query_total,
    )


def solution(mesh):
    return jax.shard_map(
        local,
        mesh=mesh,
        in_specs=(
            P("dates", "rows", None, None),
            P(),
            P(None, "rows", "dates"),
            P("rows", "dates", None),
            P(),
            P(),
            P(),
            P(),
            P(),
            P(),
            P(),
            P(),
        ),
        out_specs=(P("rows", "dates", None), P(), P(), P(), P(), P(), P(), P(), P()),
        check_vma=False,
    )
```

```python
import functools
import math

import jax
import jax.numpy as jnp
from jax import lax
from jax.experimental import pallas as pl
from jax.experimental.pallas import tpu as pltpu
from jax.sharding import PartitionSpec as P

GROUPS = 4


EPS = 1e-05


MIB = 1 << 20


F32 = jnp.float32


BF16 = jnp.bfloat16


def product(left, right, left_dim, right_dim):
    return lax.dot_general(
        left, right, (((left_dim,), (right_dim,)), ((), ())), preferred_element_type=F32
    )


def group_sum(values):
    width = values.shape[-1]
    lane_group = lax.broadcasted_iota(jnp.int32, values.shape, 1) // (width // GROUPS)
    spread = jnp.zeros_like(values)
    for group in range(GROUPS):
        inside = lane_group == group
        total = jnp.sum(jnp.where(inside, values, 0.0), axis=1, keepdims=True)
        spread = spread + jnp.where(inside, total, 0.0)
    return spread


def sigmoid(values):
    return 0.5 * jnp.tanh(0.5 * values) + 0.5


def from_left(values):
    column = lax.broadcasted_iota(jnp.int32, values.shape, 1)
    return jnp.where(column > 0, pltpu.roll(values, 1, 1), 0.0)


def from_right(values):
    count = values.shape[1]
    column = lax.broadcasted_iota(jnp.int32, values.shape, 1)
    return jnp.where(column < count - 1, pltpu.roll(values, count - 1, 1), 0.0)


def column_sum(values):
    return jnp.sum(jnp.sum(values, axis=0), axis=0, keepdims=True)


def edges(place_ref, row_devs):
    place = place_ref[0]
    return (place > 0).astype(F32), (place < row_devs - 1).astype(F32)


def head_spread(width):
    lane = lax.broadcasted_iota(jnp.int32, (2 * width, width), 1) // (width // 16)
    head = lax.broadcasted_iota(jnp.int32, (2 * width, width), 0) % width // (width // 16)
    return (lane == head).astype(F32).astype(BF16)


def split(values):
    high = values.astype(BF16)
    return high, (values - high.astype(F32)).astype(BF16)


def store_sums(sums_ref, date, dates, first, second):
    for copy in range(sums_ref.shape[0]):
        sums_ref[copy, pl.ds(date, 1), :] = first
        sums_ref[copy, pl.ds(dates + date, 1), :] = second


def norm_table(sums_ref, table_ref, dates, norm_count):
    means = group_sum(jnp.sum(sums_ref[...], axis=0)) / norm_count
    mean = means[:dates]
    table_ref[:dates] = mean
    table_ref[dates:] = 1.0 / jnp.sqrt(means[dates:] - mean * mean + EPS)


def down_kernel(dates, img_ref, above_ref, weight_ref, out_ref, top_ref, low_ref, sums_ref, table):
    date = pl.program_id(0)
    half = weight_ref.shape[2]

    @pl.when(date == 0)
    def _():
        for tap in range(3):
            base = tap * 2 * half
            table[base : base + half, : 2 * half] = weight_ref[tap, 1]
            table[base + half : base + 2 * half, : 2 * half] = weight_ref[tap, 2]
            table[base : base + half, 2 * half :] = jnp.zeros_like(weight_ref[tap, 0])
            table[base + half : base + 2 * half, 2 * half :] = weight_ref[tap, 0]

    even, odd = img_ref[0, :, 0], img_ref[0, :, 1]
    above = jnp.concatenate([above_ref[0][None], odd[:-1]], axis=0)
    rows, cols, width = even.shape
    taps = jnp.concatenate([above, even, odd], axis=-1).reshape(rows * cols, 3 * width)
    both = product(taps, table[...], 1, 0).reshape(rows, cols, 2 * width)
    stored = (both[..., :width] + from_left(both[..., width:])).astype(BF16)
    out_ref[0] = stored
    top_ref[0] = stored[0]
    low_ref[0] = stored[rows - 1]
    values = stored.astype(F32)
    store_sums(sums_ref, date, dates, column_sum(values), column_sum(values * values))


def block_kernel(
    dates,
    norm_count,
    row_devs,
    edge_ref,
    conv_ref,
    up_ref,
    down_ref,
    stats_ref,
    gain_ref,
    shift_ref,
    weight_ref,
    out_ref,
    hidden_ref,
    norm_ref,
    sums_ref,
    table,
):
    date = pl.program_id(0)
    width = conv_ref.shape[-1]

    @pl.when(date == 0)
    def _():
        norm_table(stats_ref, norm_ref, dates, norm_count)
        for row_tap in range(3):
            for col_tap in range(3):
                table[
                    row_tap * width : (row_tap + 1) * width, col_tap * width : (col_tap + 1) * width
                ] = weight_ref[row_tap, col_tap]

    scale = norm_ref[pl.ds(dates + date, 1), :] * gain_ref[...]
    shift = shift_ref[...] - norm_ref[pl.ds(date, 1), :] * scale

    def activate(values):
        linear = values.astype(F32) * scale + shift
        return linear * sigmoid(linear)

    rows, cols = conv_ref.shape[1:3]
    above_edge, below_edge = edges(edge_ref, row_devs)
    hidden_ref[0, 0] = (activate(up_ref[0]) * above_edge).astype(BF16)
    hidden_ref[0, rows + 1] = (activate(down_ref[0]) * below_edge).astype(BF16)
    hidden_ref[0, 1 : rows + 1] = activate(conv_ref[0]).astype(BF16)
    taps = jnp.concatenate(
        [hidden_ref[0, tap : tap + rows] for tap in range(3)], axis=-1
    ).reshape(rows * cols, 3 * width)
    terms = product(taps, table[...], 1, 0).reshape(rows, cols, 3 * width)
    stored = (
        terms[..., width : 2 * width]
        + from_left(terms[..., :width])
        + from_right(terms[..., 2 * width :])
    ).astype(BF16)
    out_ref[0] = stored
    values = stored.astype(F32)
    store_sums(sums_ref, date, dates, column_sum(values), column_sum(values * values))


def encoding(day, width):
    lane = lax.broadcasted_iota(jnp.int32, (1, width), 1)
    frequency = jnp.exp((lane // 2).astype(F32) * (-2.0 * math.log(1000.0) / width))
    angles = day.astype(F32) * frequency
    return jnp.where(lane % 2 == 0, jnp.sin(angles), jnp.cos(angles))


def fold_keys(key_ref, query_ref, wide_ref, vector_ref, spread_ref, score_ref):
    heads, depth = query_ref.shape
    width = key_ref.shape[0]
    lanes = width // heads
    spread_ref[...] = head_spread(width)
    row = lax.broadcasted_iota(jnp.int32, (heads * depth, width), 0)
    lane = lax.broadcasted_iota(jnp.int32, (heads * depth, width), 1)
    widen = (row // depth == lane // lanes) & (row % depth == lane % lanes)
    wide = product(key_ref[...], widen.astype(F32).astype(BF16), 1, 0)
    wide_ref[...] = wide.astype(BF16)
    head = lax.broadcasted_iota(jnp.int32, (heads, width), 0)
    lane = lax.broadcasted_iota(jnp.int32, (heads, width), 1)
    queries = jnp.where((lane % lanes == depth) | (lane % lanes == depth + 1), 1.0, 0.0)
    for step in range(depth):
        scaled = query_ref[:, step : step + 1] * depth**-0.5
        queries = queries + jnp.where(lane % lanes == step, scaled, 0.0)
    queries = jnp.sum(jnp.where(lane // lanes == head, queries, 0.0), axis=0, keepdims=True)
    vector_ref[...] = jnp.broadcast_to(queries, vector_ref.shape)
    folded = jnp.concatenate(split(wide * queries), axis=-1)
    folded = product(folded, spread_ref[...], 1, 0)
    score_ref[...] = jnp.concatenate(split(folded), axis=-1)


def score_kernel(
    dates,
    norm_count,
    grad_scale,
    day_ref,
    block_ref,
    stats_ref,
    gain_ref,
    shift_ref,
    grad_ref,
    valid_ref,
    key_ref,
    query_ref,
    feat_ref,
    exp_ref,
    attn_ref,
    norm_ref,
    packed_ref,
    wide_ref,
    vector_ref,
    total,
    mean,
    spread_ref,
    score_ref,
):
    date = pl.program_id(0)
    rows, cols, width = block_ref.shape[1:]

    @pl.when(date == 0)
    def _():
        norm_table(stats_ref, norm_ref, dates, norm_count)
        fold_keys(key_ref, query_ref, wide_ref, vector_ref, spread_ref, score_ref)
        total[...] = jnp.zeros_like(total)
        mean[...] = jnp.zeros_like(mean)

    scale = norm_ref[pl.ds(dates + date, 1), :] * gain_ref[...]
    shift = shift_ref[...] - norm_ref[pl.ds(date, 1), :] * scale
    linear = block_ref[0].astype(F32) * scale + shift
    features = (linear * sigmoid(linear) + encoding(day_ref[date], width)).astype(BF16)
    feat_ref[0] = features
    upstream = grad_ref[...]
    upstream = jnp.stack([upstream[:, row].reshape(cols, width) for row in range(rows)])
    parts = split(upstream.astype(F32) * features.astype(F32))
    parts = jnp.concatenate(parts, axis=-1).reshape(rows * cols, 2 * width)
    attn = product(parts, spread_ref[...], 1, 0).reshape(rows, cols, width) * grad_scale
    both = product(features.reshape(rows * cols, width), score_ref[...], 1, 0)
    scores = (both[:, :width] + both[:, width:]).reshape(rows, cols, width)
    diagonal = lax.broadcasted_iota(jnp.int32, (cols, cols), 0) == lax.broadcasted_iota(
        jnp.int32, (cols, cols), 1
    )
    ones = jnp.ones((cols, width), BF16)
    clear = jnp.concatenate(
        [jnp.where(diagonal, valid_ref[0, row : row + 1], 0.0) for row in range(rows)], axis=0
    ).astype(BF16)
    clear = product(clear, ones, 1, 0).reshape(rows, cols, width)
    exponent = clear * jnp.exp(scores)
    running = total[...] + exponent
    share = jnp.where(running > 0.0, exponent / running, 0.0)
    total[...] = running
    mean[...] += share * (attn - mean[...])
    exp_ref[0] = exponent
    attn_ref[0] = attn

    @pl.when(date == dates - 1)
    def _():
        place = lax.broadcasted_iota(jnp.int32, (cols, width), 1) % rows
        for index, source in enumerate((total, mean)):
            dense = jnp.zeros((cols, width), F32)
            for row in range(rows):
                dense = dense + jnp.where(place == row, source[row], 0.0)
            for copy in range(packed_ref.shape[0]):
                packed_ref[copy, index] = dense


def attend_kernel(
    dates,
    grad_scale,
    packed_ref,
    feat_ref,
    exp_ref,
    attn_ref,
    block_ref,
    norm_ref,
    gain_ref,
    shift_ref,
    query_ref,
    grad_ref,
    key_ref,
    grad_out_ref,
    up_ref,
    down_ref,
    part_ref,
    key_out_ref,
    vector_ref,
    sums_ref,
    inverse,
    average,
    attended,
):
    date = pl.program_id(0)
    rows, cols, width = block_ref.shape[1:]

    @pl.when(date == 0)
    def _():
        denominator = jnp.sum(packed_ref[:, 0], axis=0)
        reciprocal = 1.0 / denominator
        mean = jnp.sum(packed_ref[:, 0] * reciprocal * packed_ref[:, 1], axis=0)
        place = lax.broadcasted_iota(jnp.int32, (cols, width), 1) % rows
        for values, target in ((reciprocal, inverse), (mean, average)):
            parts = jnp.concatenate(split(values), axis=-1)
            wide_place = jnp.concatenate([place, place], axis=-1)
            picked = jnp.concatenate(
                [jnp.where(wide_place == row, parts, jnp.zeros_like(parts)) for row in range(rows)], axis=0
            )
            target[...] = product(picked, head_spread(width), 1, 0).reshape(rows, cols, width)
        attended[...] = jnp.zeros_like(attended)
        key_out_ref[...] = jnp.zeros_like(key_out_ref)
        vector_ref[...] = jnp.zeros_like(vector_ref)

    features = feat_ref[0]
    weights = exp_ref[0] * inverse[...]
    rounded = weights.astype(BF16).astype(F32)
    attended[...] += rounded * features.astype(F32)
    score_grad = weights * (attn_ref[0] - average[...])
    spread_grad = score_grad * query_ref[0:1]
    rest = spread_grad - spread_grad.astype(BF16).astype(F32)
    lane = lax.broadcasted_iota(jnp.int32, spread_grad.shape, 2) % (width // 16)
    key_grads = jnp.where(lane == 5, rest, spread_grad).astype(BF16).reshape(rows * cols, width)
    key_out_ref[...] += product(features.reshape(rows * cols, width), key_grads, 0, 0)
    upstream = grad_ref[...]
    upstream = jnp.stack([upstream[:, row].reshape(cols, width) for row in range(rows)])
    feat_grad = rounded * (upstream.astype(F32) * grad_scale) + product(
        key_grads, key_ref[...], 1, 1
    ).reshape(rows, cols, width)
    gain = gain_ref[...]
    centred = (block_ref[0].astype(F32) - norm_ref[pl.ds(date, 1), :]) * norm_ref[
        pl.ds(dates + date, 1), :
    ]
    linear = centred * gain + shift_ref[...]
    part = sigmoid(linear)
    linear_grad = feat_grad * (part * (1.0 + linear * (1.0 - part)))
    first = column_sum(linear_grad)
    second = column_sum(linear_grad * centred)
    vector_ref[0:1] += second
    vector_ref[1:2] += first
    store_sums(sums_ref, date, dates, first * gain, second * gain)
    stored = (linear_grad * gain).astype(BF16)
    grad_out_ref[0] = stored
    up_ref[0, 0] = stored[0]
    up_ref[0, 1] = block_ref[0, 0]
    down_ref[0, 0] = stored[rows - 1]
    down_ref[0, 1] = block_ref[0, rows - 1]

    @pl.when(date == dates - 1)
    def _():
        devices, piece = part_ref.shape[0], part_ref.shape[2]
        for device in range(devices):
            part_ref[device] = attended[:, device * piece : (device + 1) * piece].astype(BF16)
        key_part = key_out_ref[...]
        place = lax.broadcasted_iota(jnp.int32, (width, width), 1) % (width // 16)
        both = pltpu.roll(key_part, width - 4, 1) + pltpu.roll(key_part, width - 5, 1)
        both = jnp.where(place == 0, both, 0.0)
        both = both + pltpu.roll(both, 1, 1)
        both = both + pltpu.roll(both, 2, 1)
        vector_ref[2:3] = 0.5 * jnp.sum(key_ref[...].astype(F32) * both, axis=0, keepdims=True)


def hidden_kernel(
    dates,
    norm_count,
    row_devs,
    edge_ref,
    grad_ref,
    block_ref,
    up_ref,
    down_ref,
    tails_ref,
    norm_ref,
    weight_ref,
    conv_ref,
    first_norm_ref,
    gain_ref,
    shift_ref,
    pre_ref,
    out_ref,
    vector_ref,
    sums_ref,
    table,
    factors,
    padded,
):
    date = pl.program_id(0)
    rows, cols, width = block_ref.shape[1:]

    @pl.when(date == 0)
    def _():
        tails = group_sum(jnp.sum(tails_ref[...], axis=0)) / norm_count
        mean, inverse = norm_ref[:dates], norm_ref[dates:]
        slope = -inverse * inverse * tails[dates:]
        factors[0:dates] = slope
        factors[dates : 2 * dates] = -inverse * tails[:dates] - mean * slope
        vector_ref[...] = jnp.zeros_like(vector_ref)
        for row_tap in range(3):
            for col_tap in range(3):
                table[
                    col_tap * width : (col_tap + 1) * width, row_tap * width : (row_tap + 1) * width
                ] = weight_ref[2 - row_tap, col_tap]

    inverse = norm_ref[pl.ds(dates + date, 1), :]
    slope = factors[pl.ds(date, 1), :]
    constant = factors[pl.ds(dates + date, 1), :]

    def finish(grad, values):
        return grad.astype(F32) * inverse + (values.astype(F32) * slope + constant)

    above_edge, below_edge = edges(edge_ref, row_devs)
    stored = finish(grad_ref[0], block_ref[0]).astype(BF16)
    pre_ref[0] = stored
    padded[0] = (finish(up_ref[0, 0], up_ref[0, 1]) * above_edge).astype(BF16)
    padded[rows + 1] = (finish(down_ref[0, 0], down_ref[0, 1]) * below_edge).astype(BF16)
    padded[1 : rows + 1] = stored
    taps = jnp.concatenate([padded[tap : tap + rows] for tap in range(3)], axis=-1).reshape(
        rows * cols, 3 * width
    )
    terms = product(taps, table[...], 1, 1).reshape(rows, cols, 3 * width)
    hidden_grad = (
        terms[..., width : 2 * width]
        + from_right(terms[..., :width])
        + from_left(terms[..., 2 * width :])
    )
    gain = gain_ref[...]
    centred = (conv_ref[0].astype(F32) - first_norm_ref[pl.ds(date, 1), :]) * first_norm_ref[
        pl.ds(dates + date, 1), :
    ]
    linear = centred * gain + shift_ref[...]
    part = sigmoid(linear)
    linear_grad = hidden_grad * (part * (1.0 + linear * (1.0 - part)))
    out_ref[0] = linear_grad
    first = column_sum(linear_grad)
    second = column_sum(linear_grad * centred)
    vector_ref[0:1] += second
    vector_ref[1:2] += first
    store_sums(sums_ref, date, dates, first * gain, second * gain)


def block_grad_kernel(dates, hidden_ref, pre_ref, key_ref, out_ref, total):
    date = pl.program_id(0)
    rows, cols, width = pre_ref.shape[1:]

    @pl.when(date == 0)
    def _():
        total[...] = jnp.zeros_like(total)

    grads = pre_ref[0].astype(F32)
    grads = jnp.concatenate(
        [from_right(grads).astype(BF16), pre_ref[0], from_left(grads).astype(BF16)], axis=-1
    ).reshape(rows * cols, 3 * width)
    taps = jnp.concatenate(
        [hidden_ref[0, tap : tap + rows] for tap in range(3)], axis=-1
    ).reshape(rows * cols, 3 * width)
    total[...] += product(taps, grads, 0, 0)

    @pl.when(date == dates - 1)
    def _():
        for row_tap in range(3):
            for col_tap in range(3):
                base = (row_tap * 3 + col_tap) * width
                out_ref[base : base + width] = total[
                    row_tap * width : (row_tap + 1) * width, col_tap * width : (col_tap + 1) * width
                ].astype(BF16)
        key_part = key_ref[...]
        rest = key_part - key_part.astype(BF16).astype(F32)
        lanes = width // 16
        place = lax.broadcasted_iota(jnp.int32, key_part.shape, 1) % lanes
        rest = pltpu.roll(rest, lanes // 2, 1)
        key_rows = jnp.where(place < lanes // 2, key_part, rest).astype(BF16)
        out_ref[9 * width : 10 * width] = key_rows
        if out_ref.shape[0] > 10 * width:
            out_ref[10 * width :] = jnp.zeros_like(out_ref[10 * width :])


def conv_grad_kernel(
    dates,
    norm_count,
    img_ref,
    above_ref,
    conv_ref,
    grad_ref,
    tails_ref,
    norm_ref,
    gain_ref,
    vector_ref,
    other_ref,
    block_rows_ref,
    out_ref,
    factors,
    total,
):
    date = pl.program_id(0)
    rows, cols, width = conv_ref.shape[1:]
    half = width // 2

    @pl.when(date == 0)
    def _():
        tails = group_sum(jnp.sum(tails_ref[...], axis=0)) / norm_count
        mean, inverse = norm_ref[:dates], norm_ref[dates:]
        slope = -inverse * inverse * tails[dates:]
        factors[0:dates] = slope
        factors[dates : 2 * dates] = -inverse * tails[:dates] - mean * slope
        total[...] = jnp.zeros_like(total)

    scale = norm_ref[pl.ds(dates + date, 1), :] * gain_ref[...]
    slope = factors[pl.ds(date, 1), :]
    constant = factors[pl.ds(dates + date, 1), :]
    stored = (grad_ref[0] * scale + (conv_ref[0].astype(F32) * slope + constant)).astype(BF16)
    moved = from_right(stored.astype(F32)).astype(BF16)
    grads = jnp.concatenate([stored, moved], axis=-1).reshape(rows * cols, 2 * width)
    even, odd = img_ref[0, :, 0], img_ref[0, :, 1]
    above = jnp.concatenate([above_ref[0][None], odd[:-1]], axis=0)
    taps = jnp.concatenate([above, even, odd], axis=-1).reshape(rows * cols, 3 * width)
    total[...] += product(taps, grads, 0, 0)

    @pl.when(date == dates - 1)
    def _():
        begin = block_rows_ref.shape[0]
        out_ref[:begin] = block_rows_ref[...]
        for tap in range(3):
            base = tap * width
            pair = total[base : base + width, :width].astype(BF16)
            left = total[base + half : base + width, width:].astype(BF16)
            start = begin + tap * 3 * half
            out_ref[start : start + half] = left
            out_ref[start + half : start + 3 * half] = pair
        start = begin + 9 * half
        for source in (vector_ref, other_ref):
            high, low = split(source[...])
            out_ref[start : start + 16] = jnp.concatenate([high, low], axis=0)
            start += 16
        if out_ref.shape[0] > start:
            out_ref[start:] = jnp.zeros_like(out_ref[start:])


def total_kernel(in_ref, out_ref):
    total = jnp.sum(in_ref[...].astype(F32), axis=0).astype(BF16)
    for copy in range(out_ref.shape[0]):
        out_ref[copy] = total


def final_kernel(depth, rows_ref, conv_ref, block_ref, key_ref, query_ref, *vector_refs):
    conv_end, block_end, width = conv_ref.shape[0], block_ref.shape[0], block_ref.shape[1]
    block_ref[...] = rows_ref[:block_end].astype(F32)
    heads = key_ref.shape[1] // depth
    lanes = width // heads
    row = lax.broadcasted_iota(jnp.int32, (width, heads * depth), 0)
    lane = lax.broadcasted_iota(jnp.int32, (width, heads * depth), 1)
    narrow = (row // lanes == lane // depth) & (row % depth == lane % depth)
    narrow = narrow.astype(F32).astype(BF16)
    key_ref[...] = product(rows_ref[block_end : block_end + width], narrow, 1, 0)
    start = block_end + width
    conv_ref[...] = rows_ref[start : start + conv_end].astype(F32)
    start += conv_end
    for index in range(2):
        both = rows_ref[start : start + 16].astype(F32)
        both = both[:8] + both[8:]
        vector_refs[2 * index][...] = both[0:1]
        vector_refs[2 * index + 1][...] = both[1:2]
        start += 16
    query = product(rows_ref[start - 16 : start], narrow, 1, 0)
    query_ref[...] = query[2:3] + query[10:11]


def per_date(shape):
    zeros = (0,) * (len(shape) - 1)
    return pl.BlockSpec((1,) + tuple(shape[1:]), lambda date: (date,) + zeros)


def whole(shape):
    zeros = (0,) * len(shape)
    return pl.BlockSpec(tuple(shape), lambda date: zeros)


def call(kernel, dates, inputs, outputs, scratch, flops, memory=24):
    in_specs, arrays = [], []
    for kind, array in inputs:
        arrays.append(array)
        if kind == "scalar":
            in_specs.append(pl.BlockSpec(memory_space=pltpu.SMEM))
        else:
            in_specs.append((per_date if kind == "date" else whole)(array.shape))
    out_specs = [(per_date if kind == "date" else whole)(shape) for kind, shape, _ in outputs]
    moved = sum(array.size * array.dtype.itemsize for array in arrays)
    return pl.pallas_call(
        kernel,
        grid=(dates,),
        in_specs=in_specs,
        out_specs=out_specs,
        out_shape=[jax.ShapeDtypeStruct(shape, dtype) for _, shape, dtype in outputs],
        scratch_shapes=scratch,
        compiler_params=pltpu.CompilerParams(vmem_limit_bytes=memory * MIB),
        cost_estimate=pl.CostEstimate(flops=flops, bytes_accessed=2 * moved, transcendentals=0),
    )(*arrays)


def neighbours(first_rows, last_rows):
    devices = lax.axis_size("rows")
    down = [(i, i + 1) for i in range(devices - 1)]
    up = [(i + 1, i) for i in range(devices - 1)]
    return lax.ppermute(last_rows, "rows", down), lax.ppermute(first_rows, "rows", up)


def exchange(pieces, axes):
    return lax.all_to_all(pieces, axes, split_axis=0, concat_axis=0, tiled=True)


def gather(array, axis):
    return lax.all_gather(array, axis, axis=0, tiled=True)


def scatter(rows_array):
    axes = ("rows", "dates")
    devices = lax.axis_size(axes)
    count, width = rows_array.shape
    return exchange(rows_array.reshape(devices, count // devices, width), axes)


def collect(pieces):
    spread = pl.pallas_call(
        total_kernel,
        out_shape=jax.ShapeDtypeStruct(pieces.shape, BF16),
        compiler_params=pltpu.CompilerParams(vmem_limit_bytes=16 * MIB),
    )(pieces)
    count, rows, width = pieces.shape
    return exchange(spread, ("rows", "dates")).reshape(count * rows, width)


def padded_count(count, devices):
    step = 8 * devices
    return -(-count // step) * step


def grouped(array, groups):
    return lax.all_gather(array, "rows", axis_index_groups=groups, axis=0, tiled=True)


def row_totals_by_squares(sums):
    devices = lax.axis_size("rows")
    near = [list(range(start, start + 4)) for start in range(0, devices, 4)]
    far = [list(range(start, devices, 4)) for start in range(4)]
    sums = jnp.sum(grouped(sums, near), axis=0, keepdims=True)
    return grouped(sums, far)


def row_totals_by_pairs(sums):
    devices = lax.axis_size("rows")
    step = 1
    while step < devices:
        pairs = [[i, i + step] for i in range(devices) if i // step % 2 == 0]
        sums = grouped(sums, pairs)
        step *= 2
        if step < devices:
            sums = jnp.sum(sums, axis=0, keepdims=True)
    return sums


def local(
    images,
    day_index,
    valid,
    out_grad,
    conv_weight,
    first_gain,
    first_shift,
    block_weight,
    gn_gain,
    gn_shift,
    key_weight,
    queries,
):
    dates, rows_here, cols, pair_width = images.shape
    width = conv_weight.shape[-1]
    row_devs, date_devs = lax.axis_size("rows"), lax.axis_size("dates")
    devices = row_devs * date_devs
    rows = rows_here // 2
    heads, depth = queries.shape
    norm_count = float(rows * row_devs * cols * (width // GROUPS))
    grad_scale = float(rows * row_devs * cols) ** (-0.5)
    date_start = lax.axis_index("dates") * dates
    frame = (dates, rows, cols, width)
    edge_rows = (dates, cols, width)
    flops = 2 * dates * rows * cols * width * width

    rows_of = lambda vector: vector.reshape(1, width)
    first_gain, first_shift = rows_of(first_gain), rows_of(first_shift)
    gn_gain, gn_shift = rows_of(gn_gain), rows_of(gn_shift)
    above = lax.ppermute(images[:, -1], "rows", [(i, i + 1) for i in range(row_devs - 1)])
    paired = images.reshape(dates, rows, 2, cols, pair_width)
    conv_out, top, low, sums = call(
        functools.partial(down_kernel, dates),
        dates,
        [("date", paired), ("date", above), ("all", conv_weight)],
        [
            ("date", frame, BF16),
            ("date", edge_rows, BF16),
            ("date", edge_rows, BF16),
            ("all", (1, 2 * dates, width), F32),
        ],
        [pltpu.VMEM((3 * pair_width, 2 * width), BF16)],
        6 * flops,
    )
    sums, valid, out_grad = lax.optimization_barrier((sums, valid, out_grad))
    halo_up, halo_down = neighbours(top, low)
    stats = row_totals_by_squares(sums)
    grad_rows, valid_rows = out_grad.size // width, valid.size // width
    packed = jnp.concatenate(
        [out_grad.reshape(grad_rows, width), valid.astype(BF16).reshape(valid_rows, width)]
    )
    packed = gather(packed[None], "dates")
    grads_here = packed[:, :grad_rows].reshape((date_devs,) + out_grad.shape)
    clear = packed[:, grad_rows:].reshape((date_devs,) + valid.shape)
    clear = lax.dynamic_slice_in_dim(clear, date_start, dates, 1)
    clear = clear.transpose(1, 2, 0, 3).reshape(dates, rows, cols).astype(F32)
    days = lax.dynamic_slice_in_dim(day_index, date_start, dates, 0)
    place = lax.axis_index("rows").reshape(1)

    block_out, hidden, first_norm, sums = call(
        functools.partial(block_kernel, dates, norm_count, row_devs),
        dates,
        [
            ("scalar", place),
            ("date", conv_out),
            ("date", halo_up),
            ("date", halo_down),
            ("all", stats),
            ("all", first_gain),
            ("all", first_shift),
            ("all", block_weight),
        ],
        [
            ("date", frame, BF16),
            ("date", (dates, rows + 2, cols, width), BF16),
            ("all", (2 * dates, width), F32),
            ("all", (row_devs, 2 * dates, width), F32),
        ],
        [pltpu.VMEM((3 * width, 3 * width), BF16)],
        9 * flops,
    )
    stats = exchange(sums, "rows")
    features, exponent, attn, norm, packed, key_wide, query_wide = call(
        functools.partial(score_kernel, dates, norm_count, grad_scale),
        dates,
        [
            ("scalar", days),
            ("date", block_out),
            ("all", stats),
            ("all", gn_gain),
            ("all", gn_shift),
            ("all", grads_here),
            ("date", clear),
            ("all", key_weight),
            ("all", queries),
        ],
        [
            ("date", frame, BF16),
            ("date", frame, F32),
            ("date", frame, F32),
            ("all", (2 * dates, width), F32),
            ("all", (1, 2, cols, width), F32),
            ("all", (width, width), BF16),
            ("all", (8, width), F32),
        ],
        [
            pltpu.VMEM(frame[1:], F32),
            pltpu.VMEM(frame[1:], F32),
            pltpu.VMEM((2 * width, width), BF16),
            pltpu.VMEM((width, 2 * width), BF16),
        ],
        5 * flops,
    )
    packed = gather(packed, "dates")
    block_grad, up, low, attended, key_part, vectors, sums = call(
        functools.partial(attend_kernel, dates, grad_scale),
        dates,
        [
            ("all", packed),
            ("date", features),
            ("date", exponent),
            ("date", attn),
            ("date", block_out),
            ("all", norm),
            ("all", gn_gain),
            ("all", gn_shift),
            ("all", query_wide),
            ("all", grads_here),
            ("all", key_wide),
        ],
        [
            ("date", frame, BF16),
            ("date", (dates, 2, cols, width), BF16),
            ("date", (dates, 2, cols, width), BF16),
            ("all", (date_devs, rows, cols // date_devs, width), BF16),
            ("all", (width, width), F32),
            ("all", (8, width), F32),
            ("all", (1, 2 * dates, width), F32),
        ],
        [pltpu.VMEM(frame[1:], F32)] * 3,
        5 * flops,
    )
    halo_up, halo_down = neighbours(up, low)
    tails = row_totals_by_pairs(sums)
    attended, _ = lax.optimization_barrier((attended, tails))
    attended = jnp.sum(exchange(attended, "dates").astype(F32), axis=0).astype(BF16)
    pre_grad, linear_grad, first_vectors, sums = call(
        functools.partial(hidden_kernel, dates, norm_count, row_devs),
        dates,
        [
            ("scalar", place),
            ("date", block_grad),
            ("date", block_out),
            ("date", halo_up),
            ("date", halo_down),
            ("all", tails),
            ("all", norm),
            ("all", block_weight),
            ("date", conv_out),
            ("all", first_norm),
            ("all", first_gain),
            ("all", first_shift),
        ],
        [
            ("date", frame, BF16),
            ("date", frame, F32),
            ("all", (8, width), F32),
            ("all", (row_devs, 2 * dates, width), F32),
        ],
        [
            pltpu.VMEM((3 * width, 3 * width), BF16),
            pltpu.VMEM((2 * dates, width), F32),
            pltpu.VMEM((rows + 2, cols, width), BF16),
        ],
        9 * flops,
    )
    sums, attended = lax.optimization_barrier((sums, attended))
    tails = exchange(sums, "rows")
    (block_rows,) = call(
        functools.partial(block_grad_kernel, dates),
        dates,
        [("date", hidden), ("date", pre_grad), ("all", key_part)],
        [("all", (10 * width, width), BF16)],
        [pltpu.VMEM((3 * width, 3 * width), F32)],
        9 * flops,
    )
    tails, block_rows = lax.optimization_barrier((tails, block_rows))
    conv_count = 9 * pair_width // 2 + 32
    (rows_all,) = call(
        functools.partial(conv_grad_kernel, dates, norm_count),
        dates,
        [
            ("date", paired),
            ("date", above),
            ("date", conv_out),
            ("date", linear_grad),
            ("all", tails),
            ("all", first_norm),
            ("all", first_gain),
            ("all", first_vectors),
            ("all", vectors),
            ("all", block_rows),
        ],
        [("all", (padded_count(10 * width + conv_count, devices), width), BF16)],
        [pltpu.VMEM((2 * dates, width), F32), pltpu.VMEM((3 * pair_width, 2 * width), F32)],
        6 * flops,
    )
    rows_all = collect(scatter(rows_all))
    shapes = [
        (9 * pair_width // 2, width),
        (9 * width, width),
        key_weight.shape,
        (1, heads * depth),
    ] + [(1, width)] * 4
    conv_total, block_total, key_total, query_total, *totals = pl.pallas_call(
        functools.partial(final_kernel, depth),
        out_shape=[jax.ShapeDtypeStruct(shape, F32) for shape in shapes],
        compiler_params=pltpu.CompilerParams(vmem_limit_bytes=16 * MIB),
    )(rows_all)
    totals = [total.reshape(width) for total in totals]
    return (
        attended,
        conv_total.reshape(conv_weight.shape),
        totals[0],
        totals[1],
        block_total.reshape(block_weight.shape),
        totals[2],
        totals[3],
        key_total,
        query_total.reshape(heads, depth),
    )


def solution(mesh):
    return jax.shard_map(
        local,
        mesh=mesh,
        in_specs=(
            P("dates", "rows", None, None),
            P(),
            P(None, "rows", "dates"),
            P("rows", "dates", None),
            P(),
            P(),
            P(),
            P(),
            P(),
            P(),
            P(),
            P(),
        ),
        out_specs=(P("rows", "dates", None), P(), P(), P(), P(), P(), P(), P(), P()),
        check_vma=False,
    )
```

```python
import functools
import math

import jax
import jax.numpy as jnp
from jax import lax
from jax.experimental import pallas as pl
from jax.experimental.pallas import tpu as pltpu
from jax.sharding import PartitionSpec as P

GROUPS = 4


EPS = 1e-05


MIB = 1 << 20


MEMORY = 60


F32 = jnp.float32


BF16 = jnp.bfloat16


def product(left, right, left_dim, right_dim):
    return lax.dot_general(
        left, right, (((left_dim,), (right_dim,)), ((), ())), preferred_element_type=F32
    )


def group_sum(values):
    width = values.shape[-1]
    lane_group = lax.broadcasted_iota(jnp.int32, values.shape, 1) // (width // GROUPS)
    spread = jnp.zeros_like(values)
    for group in range(GROUPS):
        inside = lane_group == group
        total = jnp.sum(jnp.where(inside, values, 0.0), axis=1, keepdims=True)
        spread = spread + jnp.where(inside, total, 0.0)
    return spread


def sigmoid(values):
    return 0.5 * jnp.tanh(0.5 * values) + 0.5


def from_left(values):
    column = lax.broadcasted_iota(jnp.int32, values.shape, 1)
    return jnp.where(column > 0, pltpu.roll(values, 1, 1), 0.0)


def from_right(values):
    count = values.shape[1]
    column = lax.broadcasted_iota(jnp.int32, values.shape, 1)
    return jnp.where(column < count - 1, pltpu.roll(values, count - 1, 1), 0.0)


def column_sum(values):
    return jnp.sum(jnp.sum(values, axis=0), axis=0, keepdims=True)


def edges(place_ref, row_devs):
    place = place_ref[0]
    return (place > 0).astype(F32), (place < row_devs - 1).astype(F32)


def head_spread(width):
    lane = lax.broadcasted_iota(jnp.int32, (2 * width, width), 1) // (width // 16)
    head = lax.broadcasted_iota(jnp.int32, (2 * width, width), 0) % width // (width // 16)
    return (lane == head).astype(F32).astype(BF16)


def split(values):
    high = values.astype(BF16)
    return high, (values - high.astype(F32)).astype(BF16)


def store_sums(sums_ref, date, dates, first, second):
    for copy in range(sums_ref.shape[0]):
        sums_ref[copy, pl.ds(date, 1), :] = first
        sums_ref[copy, pl.ds(dates + date, 1), :] = second


def norm_table(sums_ref, table_ref, dates, norm_count):
    means = group_sum(jnp.sum(sums_ref[...], axis=0)) / norm_count
    mean = means[:dates]
    table_ref[:dates] = mean
    table_ref[dates:] = 1.0 / jnp.sqrt(means[dates:] - mean * mean + EPS)


def down_table(weight_ref, table):
    half = weight_ref.shape[2]
    for tap in range(3):
        base = tap * 2 * half
        table[base : base + half, : 2 * half] = weight_ref[tap, 1]
        table[base + half : base + 2 * half, : 2 * half] = weight_ref[tap, 2]
        table[base : base + half, 2 * half :] = jnp.zeros_like(weight_ref[tap, 0])
        table[base + half : base + 2 * half, 2 * half :] = weight_ref[tap, 0]


def down_rows(taps, table):
    rows, cols, width = taps[0].shape
    taps = jnp.concatenate(taps, axis=-1).reshape(rows * cols, 3 * width)
    both = product(taps, table[...], 1, 0).reshape(rows, cols, 2 * width)
    return (both[..., :width] + from_left(both[..., width:])).astype(BF16)


def down_kernel(dates, img_ref, above_ref, weight_ref, out_ref, sums_ref, table):
    date = pl.program_id(0)

    @pl.when(date == 0)
    def _():
        down_table(weight_ref, table)

    even, odd = img_ref[0, :, 0], img_ref[0, :, 1]
    above = jnp.concatenate([above_ref[0][None], odd[:-1]], axis=0)
    stored = down_rows([above, even, odd], table)
    out_ref[0] = stored
    values = stored.astype(F32)
    store_sums(sums_ref, date, dates, column_sum(values), column_sum(values * values))


def edge_kernel(high_ref, above_ref, last_ref, below_ref, weight_ref, up_ref, down_ref, table):
    dates = above_ref.shape[0]
    down_table(weight_ref, table)
    taps = [
        jnp.concatenate([high_ref[:, 0], last_ref[...]], axis=0),
        jnp.concatenate([high_ref[:, 1], below_ref[:, 0]], axis=0),
        jnp.concatenate([above_ref[...], below_ref[:, 1]], axis=0),
    ]
    stored = down_rows(taps, table)
    up_ref[...] = stored[:dates]
    down_ref[...] = stored[dates:]


def block_kernel(
    dates,
    norm_count,
    row_devs,
    edge_ref,
    conv_ref,
    up_ref,
    down_ref,
    stats_ref,
    gain_ref,
    shift_ref,
    weight_ref,
    out_ref,
    hidden_ref,
    norm_ref,
    sums_ref,
    table,
):
    date = pl.program_id(0)
    width = conv_ref.shape[-1]

    @pl.when(date == 0)
    def _():
        norm_table(stats_ref, norm_ref, dates, norm_count)
        for row_tap in range(3):
            for col_tap in range(3):
                table[
                    row_tap * width : (row_tap + 1) * width, col_tap * width : (col_tap + 1) * width
                ] = weight_ref[row_tap, col_tap]

    scale = norm_ref[pl.ds(dates + date, 1), :] * gain_ref[...]
    shift = shift_ref[...] - norm_ref[pl.ds(date, 1), :] * scale

    def activate(values):
        linear = values.astype(F32) * scale + shift
        return linear * sigmoid(linear)

    rows, cols = conv_ref.shape[1:3]
    above_edge, below_edge = edges(edge_ref, row_devs)
    hidden_ref[0, 0] = (activate(up_ref[0]) * above_edge).astype(BF16)
    hidden_ref[0, rows + 1] = (activate(down_ref[0]) * below_edge).astype(BF16)
    hidden_ref[0, 1 : rows + 1] = activate(conv_ref[0]).astype(BF16)
    taps = jnp.concatenate(
        [hidden_ref[0, tap : tap + rows] for tap in range(3)], axis=-1
    ).reshape(rows * cols, 3 * width)
    terms = product(taps, table[...], 1, 0).reshape(rows, cols, 3 * width)
    stored = (
        terms[..., width : 2 * width]
        + from_left(terms[..., :width])
        + from_right(terms[..., 2 * width :])
    ).astype(BF16)
    out_ref[0] = stored
    values = stored.astype(F32)
    store_sums(sums_ref, date, dates, column_sum(values), column_sum(values * values))


def encoding(day, width):
    lane = lax.broadcasted_iota(jnp.int32, (1, width), 1)
    frequency = jnp.exp((lane // 2).astype(F32) * (-2.0 * math.log(1000.0) / width))
    angles = day.astype(F32) * frequency
    return jnp.where(lane % 2 == 0, jnp.sin(angles), jnp.cos(angles))


def fold_keys(key_ref, query_ref, wide_ref, vector_ref, spread_ref, score_ref):
    depth, heads = query_ref.shape
    width = key_ref.shape[1]
    lanes = width // heads
    spread_ref[...] = head_spread(width)
    row = lax.broadcasted_iota(jnp.int32, (heads * depth, width), 0)
    lane = lax.broadcasted_iota(jnp.int32, (heads * depth, width), 1)
    widen = (row // depth == lane // lanes) & (row % depth == lane % lanes)
    wide = product(key_ref[...], widen.astype(F32).astype(BF16), 0, 0)
    wide_ref[...] = wide.astype(BF16)
    head = lax.broadcasted_iota(jnp.int32, (heads, width), 0)
    lane = lax.broadcasted_iota(jnp.int32, (heads, width), 1)
    inside = (lane // lanes == head).astype(F32).astype(BF16)
    high, low = split(query_ref[...])
    lower = (query_ref[...] - high.astype(F32) - low.astype(F32)).astype(BF16)
    spread = sum(product(part, inside, 1, 0) for part in (high, low, lower))
    step = lax.broadcasted_iota(jnp.int32, (depth, width), 0)
    place = lax.broadcasted_iota(jnp.int32, (depth, width), 1) % lanes
    queries = jnp.sum(jnp.where(step == place, spread * depth**-0.5, 0.0), axis=0, keepdims=True)
    place = lax.broadcasted_iota(jnp.int32, (1, width), 1) % lanes
    queries = queries + jnp.where((place == depth) | (place == depth + 1), 1.0, 0.0)
    vector_ref[...] = jnp.broadcast_to(queries, vector_ref.shape)
    folded = jnp.concatenate(split(wide * queries), axis=-1)
    folded = product(folded, spread_ref[...], 1, 0)
    score_ref[...] = jnp.concatenate(split(folded), axis=-1)


def score_kernel(
    dates,
    norm_count,
    grad_scale,
    day_ref,
    block_ref,
    stats_ref,
    gain_ref,
    shift_ref,
    grad_ref,
    valid_ref,
    key_ref,
    query_ref,
    feat_ref,
    exp_ref,
    attn_ref,
    norm_ref,
    packed_ref,
    wide_ref,
    vector_ref,
    total,
    mean,
    spread_ref,
    score_ref,
):
    date = pl.program_id(0)
    rows, cols, width = block_ref.shape[1:]

    @pl.when(date == 0)
    def _():
        norm_table(stats_ref, norm_ref, dates, norm_count)
        fold_keys(key_ref, query_ref, wide_ref, vector_ref, spread_ref, score_ref)
        total[...] = jnp.zeros_like(total)
        mean[...] = jnp.zeros_like(mean)

    scale = norm_ref[pl.ds(dates + date, 1), :] * gain_ref[...]
    shift = shift_ref[...] - norm_ref[pl.ds(date, 1), :] * scale
    linear = block_ref[0].astype(F32) * scale + shift
    features = (linear * sigmoid(linear) + encoding(day_ref[date], width)).astype(BF16)
    feat_ref[0] = features
    upstream = grad_ref[...]
    upstream = jnp.stack([upstream[:, row].reshape(cols, width) for row in range(rows)])
    parts = split(upstream.astype(F32) * features.astype(F32))
    parts = jnp.concatenate(parts, axis=-1).reshape(rows * cols, 2 * width)
    attn = product(parts, spread_ref[...], 1, 0).reshape(rows, cols, width) * grad_scale
    both = product(features.reshape(rows * cols, width), score_ref[...], 1, 0)
    scores = (both[:, :width] + both[:, width:]).reshape(rows, cols, width)
    diagonal = lax.broadcasted_iota(jnp.int32, (cols, cols), 0) == lax.broadcasted_iota(
        jnp.int32, (cols, cols), 1
    )
    ones = jnp.ones((cols, width), BF16)
    clear = jnp.concatenate(
        [jnp.where(diagonal, valid_ref[0, row : row + 1], 0.0) for row in range(rows)], axis=0
    ).astype(BF16)
    clear = product(clear, ones, 1, 0).reshape(rows, cols, width)
    exponent = clear * jnp.exp(scores)
    running = total[...] + exponent
    share = jnp.where(running > 0.0, exponent / running, 0.0)
    total[...] = running
    mean[...] += share * (attn - mean[...])
    exp_ref[0] = exponent
    attn_ref[0] = attn

    @pl.when(date == dates - 1)
    def _():
        place = lax.broadcasted_iota(jnp.int32, (cols, width), 1) % rows
        for index, source in enumerate((total, mean)):
            dense = jnp.zeros((cols, width), F32)
            for row in range(rows):
                dense = dense + jnp.where(place == row, source[row], 0.0)
            for copy in range(packed_ref.shape[0]):
                packed_ref[copy, index] = dense


def attend_kernel(
    dates,
    grad_scale,
    packed_ref,
    feat_ref,
    exp_ref,
    attn_ref,
    block_ref,
    norm_ref,
    gain_ref,
    shift_ref,
    query_ref,
    grad_ref,
    key_ref,
    grad_out_ref,
    part_ref,
    key_out_ref,
    vector_ref,
    sums_ref,
    inverse,
    average,
    attended,
):
    date = pl.program_id(0)
    rows, cols, width = block_ref.shape[1:]

    @pl.when(date == 0)
    def _():
        denominator = jnp.sum(packed_ref[:, 0], axis=0)
        reciprocal = 1.0 / denominator
        mean = jnp.sum(packed_ref[:, 0] * reciprocal * packed_ref[:, 1], axis=0)
        place = lax.broadcasted_iota(jnp.int32, (cols, width), 1) % rows
        for values, target in ((reciprocal, inverse), (mean, average)):
            parts = jnp.concatenate(split(values), axis=-1)
            wide_place = jnp.concatenate([place, place], axis=-1)
            picked = jnp.concatenate(
                [jnp.where(wide_place == row, parts, jnp.zeros_like(parts)) for row in range(rows)], axis=0
            )
            target[...] = product(picked, head_spread(width), 1, 0).reshape(rows, cols, width)
        attended[...] = jnp.zeros_like(attended)
        key_out_ref[...] = jnp.zeros_like(key_out_ref)
        vector_ref[...] = jnp.zeros_like(vector_ref)

    features = feat_ref[0]
    weights = exp_ref[0] * inverse[...]
    rounded = weights.astype(BF16).astype(F32)
    attended[...] += rounded * features.astype(F32)
    score_grad = weights * (attn_ref[0] - average[...])
    spread_grad = score_grad * query_ref[0:1]
    rest = spread_grad - spread_grad.astype(BF16).astype(F32)
    lane = lax.broadcasted_iota(jnp.int32, spread_grad.shape, 2) % (width // 16)
    key_grads = jnp.where(lane == 5, rest, spread_grad).astype(BF16).reshape(rows * cols, width)
    key_out_ref[...] += product(features.reshape(rows * cols, width), key_grads, 0, 0)
    upstream = grad_ref[...]
    upstream = jnp.stack([upstream[:, row].reshape(cols, width) for row in range(rows)])
    feat_grad = rounded * (upstream.astype(F32) * grad_scale) + product(
        key_grads, key_ref[...], 1, 1
    ).reshape(rows, cols, width)
    gain = gain_ref[...]
    centred = (block_ref[0].astype(F32) - norm_ref[pl.ds(date, 1), :]) * norm_ref[
        pl.ds(dates + date, 1), :
    ]
    linear = centred * gain + shift_ref[...]
    part = sigmoid(linear)
    linear_grad = feat_grad * (part * (1.0 + linear * (1.0 - part)))
    first = column_sum(linear_grad)
    second = column_sum(linear_grad * centred)
    vector_ref[0:1] += second
    vector_ref[1:2] += first
    store_sums(sums_ref, date, dates, first * gain, second * gain)
    grad_out_ref[0] = (linear_grad * gain).astype(BF16)

    @pl.when(date == dates - 1)
    def _():
        devices, piece = part_ref.shape[0], part_ref.shape[2]
        for device in range(devices):
            part_ref[device] = attended[:, device * piece : (device + 1) * piece].astype(BF16)
        key_part = key_out_ref[...]
        place = lax.broadcasted_iota(jnp.int32, (width, width), 1) % (width // 16)
        both = pltpu.roll(key_part, width - 4, 1) + pltpu.roll(key_part, width - 5, 1)
        both = jnp.where(place == 0, both, 0.0)
        both = both + pltpu.roll(both, 1, 1)
        both = both + pltpu.roll(both, 2, 1)
        vector_ref[2:3] = 0.5 * jnp.sum(key_ref[...].astype(F32) * both, axis=0, keepdims=True)


def hidden_kernel(
    dates,
    norm_count,
    row_devs,
    edge_ref,
    grad_ref,
    block_ref,
    tails_ref,
    norm_ref,
    weight_ref,
    conv_ref,
    up_ref,
    down_ref,
    first_norm_ref,
    gain_ref,
    shift_ref,
    pre_ref,
    out_ref,
    vector_ref,
    sums_ref,
    table,
    factors,
    padded,
):
    date = pl.program_id(0)
    rows, cols, width = block_ref.shape[1:]

    @pl.when(date == 0)
    def _():
        tails = group_sum(jnp.sum(tails_ref[...], axis=0)) / norm_count
        mean, inverse = norm_ref[:dates], norm_ref[dates:]
        slope = -inverse * inverse * tails[dates:]
        factors[0:dates] = slope
        factors[dates : 2 * dates] = -inverse * tails[:dates] - mean * slope
        vector_ref[...] = jnp.zeros_like(vector_ref)
        padded[:2] = jnp.zeros_like(padded[:2])
        padded[rows + 2 :] = jnp.zeros_like(padded[rows + 2 :])
        for row_tap in range(3):
            for col_tap in range(3):
                table[
                    col_tap * width : (col_tap + 1) * width, row_tap * width : (row_tap + 1) * width
                ] = weight_ref[2 - row_tap, col_tap]

    inverse = norm_ref[pl.ds(dates + date, 1), :]
    slope = factors[pl.ds(date, 1), :]
    constant = factors[pl.ds(dates + date, 1), :]

    above_edge, below_edge = edges(edge_ref, row_devs)
    stored = (
        grad_ref[0].astype(F32) * inverse + (block_ref[0].astype(F32) * slope + constant)
    ).astype(BF16)
    pre_ref[0] = stored
    padded[2 : rows + 2] = stored
    reach = rows + 2
    taps = jnp.concatenate([padded[tap : tap + reach] for tap in range(3)], axis=-1).reshape(
        reach * cols, 3 * width
    )
    terms = product(taps, table[...], 1, 1).reshape(reach, cols, 3 * width)
    hidden_grad = (
        terms[..., width : 2 * width]
        + from_right(terms[..., :width])
        + from_left(terms[..., 2 * width :])
    )
    gain = gain_ref[...]
    conv = jnp.concatenate([up_ref[0][None], conv_ref[0], down_ref[0][None]], axis=0)
    centred = (conv.astype(F32) - first_norm_ref[pl.ds(date, 1), :]) * first_norm_ref[
        pl.ds(dates + date, 1), :
    ]
    linear = centred * gain + shift_ref[...]
    part = sigmoid(linear)
    linear_grad = hidden_grad * (part * (1.0 + linear * (1.0 - part)))
    linear_grad = jnp.concatenate(
        [
            linear_grad[:1] * above_edge,
            linear_grad[1 : rows + 1],
            linear_grad[rows + 1 :] * below_edge,
        ],
        axis=0,
    )
    out_ref[0] = linear_grad.astype(BF16)
    first = column_sum(linear_grad)
    second = column_sum(linear_grad * centred)
    vector_ref[0:1] += second
    vector_ref[1:2] += first
    store_sums(sums_ref, date, dates, first * gain, second * gain)


def block_grad_kernel(dates, hidden_ref, pre_ref, key_ref, out_ref, total):
    date = pl.program_id(0)
    rows, cols, width = pre_ref.shape[1:]

    @pl.when(date == 0)
    def _():
        total[...] = jnp.zeros_like(total)

    grads = pre_ref[0].astype(F32)
    grads = jnp.concatenate(
        [from_right(grads).astype(BF16), pre_ref[0], from_left(grads).astype(BF16)], axis=-1
    ).reshape(rows * cols, 3 * width)
    taps = jnp.concatenate(
        [hidden_ref[0, tap : tap + rows] for tap in range(3)], axis=-1
    ).reshape(rows * cols, 3 * width)
    total[...] += product(taps, grads, 0, 0)

    @pl.when(date == dates - 1)
    def _():
        for row_tap in range(3):
            for col_tap in range(3):
                base = (row_tap * 3 + col_tap) * width
                out_ref[base : base + width] = total[
                    row_tap * width : (row_tap + 1) * width, col_tap * width : (col_tap + 1) * width
                ].astype(BF16)
        key_part = key_ref[...]
        rest = key_part - key_part.astype(BF16).astype(F32)
        lanes = width // 16
        place = lax.broadcasted_iota(jnp.int32, key_part.shape, 1) % lanes
        rest = pltpu.roll(rest, lanes // 2, 1)
        key_rows = jnp.where(place < lanes // 2, key_part, rest).astype(BF16)
        out_ref[9 * width : 10 * width] = key_rows
        if out_ref.shape[0] > 10 * width:
            out_ref[10 * width :] = jnp.zeros_like(out_ref[10 * width :])


def conv_grad_kernel(
    dates,
    norm_count,
    img_ref,
    above_ref,
    high_ref,
    below_ref,
    conv_ref,
    grad_ref,
    tails_ref,
    norm_ref,
    gain_ref,
    vector_ref,
    other_ref,
    block_rows_ref,
    out_ref,
    factors,
    total,
):
    date = pl.program_id(0)
    rows, cols, width = conv_ref.shape[1:]
    half = width // 2

    @pl.when(date == 0)
    def _():
        tails = group_sum(jnp.sum(tails_ref[...], axis=0)) / norm_count
        mean, inverse = norm_ref[:dates], norm_ref[dates:]
        slope = -inverse * inverse * tails[dates:]
        factors[0:dates] = slope
        factors[dates : 2 * dates] = -inverse * tails[:dates] - mean * slope
        total[...] = jnp.zeros_like(total)

    scale = norm_ref[pl.ds(dates + date, 1), :] * gain_ref[...]
    slope = factors[pl.ds(date, 1), :]
    constant = factors[pl.ds(dates + date, 1), :]
    own = conv_ref[0].astype(F32) * slope + constant
    scaled = grad_ref[0].astype(F32) * scale
    stored = jnp.concatenate(
        [scaled[:1], scaled[1 : rows + 1] + own, scaled[rows + 1 :]], axis=0
    ).astype(BF16)
    moved = from_right(stored.astype(F32)).astype(BF16)
    reach = rows + 2
    grads = jnp.concatenate([stored, moved], axis=-1).reshape(reach * cols, 2 * width)
    even, odd = img_ref[0, :, 0], img_ref[0, :, 1]
    above = above_ref[0][None]
    taps = [
        jnp.concatenate([high_ref[0, :1], above, odd], axis=0),
        jnp.concatenate([high_ref[0, 1:], even, below_ref[0, :1]], axis=0),
        jnp.concatenate([above, odd, below_ref[0, 1:]], axis=0),
    ]
    taps = jnp.concatenate(taps, axis=-1).reshape(reach * cols, 3 * width)
    total[...] += product(taps, grads, 0, 0)

    @pl.when(date == dates - 1)
    def _():
        begin = block_rows_ref.shape[0]
        out_ref[:begin] = block_rows_ref[...]
        for tap in range(3):
            base = tap * width
            pair = total[base : base + width, :width].astype(BF16)
            left = total[base + half : base + width, width:].astype(BF16)
            start = begin + tap * 3 * half
            out_ref[start : start + half] = left
            out_ref[start + half : start + 3 * half] = pair
        start = begin + 9 * half
        for source in (vector_ref, other_ref):
            high, low = split(source[...])
            out_ref[start : start + 16] = jnp.concatenate([high, low], axis=0)
            start += 16
        if out_ref.shape[0] > start:
            out_ref[start:] = jnp.zeros_like(out_ref[start:])


def total_kernel(in_ref, out_ref):
    total = jnp.sum(in_ref[...].astype(F32), axis=0).astype(BF16)
    for copy in range(out_ref.shape[0]):
        out_ref[copy] = total


def final_kernel(depth, rows_ref, conv_ref, block_ref, key_ref, query_ref, *vector_refs):
    conv_end, block_end, width = conv_ref.shape[0], block_ref.shape[0], block_ref.shape[1]
    block_ref[...] = rows_ref[:block_end].astype(F32)
    wide = key_ref.shape[0]
    heads = wide // depth
    lanes = width // heads
    row = lax.broadcasted_iota(jnp.int32, (wide, width), 0)
    lane = lax.broadcasted_iota(jnp.int32, (wide, width), 1)
    narrow = (row // depth == lane // lanes) & (row % depth == lane % depth)
    narrow = narrow.astype(F32).astype(BF16)
    key_ref[...] = product(narrow, rows_ref[block_end : block_end + width], 1, 1)
    start = block_end + width
    conv_ref[...] = rows_ref[start : start + conv_end].astype(F32)
    start += conv_end
    for index in range(2):
        both = rows_ref[start : start + 16].astype(F32)
        both = both[:8] + both[8:]
        vector_refs[2 * index][...] = both[0:1]
        vector_refs[2 * index + 1][...] = both[1:2]
        start += 16
    both = rows_ref[start - 16 : start]
    row = lax.broadcasted_iota(jnp.int32, (heads, width), 0)
    lane = lax.broadcasted_iota(jnp.int32, (heads, width), 1)
    inside = row == lane // lanes
    step = lax.broadcasted_iota(jnp.int32, (8, width), 0)
    place = lax.broadcasted_iota(jnp.int32, (8, width), 1) % lanes
    steps = step == place
    query = jnp.zeros((8, heads), F32)
    for index in (2, 10):
        picked = jnp.where(steps, both[index : index + 1].astype(F32), 0.0).astype(BF16)
        query = query + product(picked, inside.astype(F32).astype(BF16), 1, 1)
    query_ref[...] = query[:depth]


def per_date(shape):
    zeros = (0,) * (len(shape) - 1)
    return pl.BlockSpec((1,) + tuple(shape[1:]), lambda date: (date,) + zeros)


def streamed(kernel, dates, kinds, out_count):
    count = kinds.count("date")

    def body(*refs):
        inputs, rest = list(refs[: len(kinds)]), refs[len(kinds) :]
        outputs, scratch = rest[:out_count], rest[out_count:]
        buffers, ready, scratch = scratch[:count], scratch[count], scratch[count + 1 :]
        date = pl.program_id(0)
        places = [place for place, kind in enumerate(kinds) if kind == "date"]

        def copy(index, step):
            return pltpu.make_async_copy(
                inputs[places[index]].at[step], buffers[index].at[step], ready.at[index, step]
            )

        @pl.when(date == 0)
        def _():
            for step in range(dates):
                for index in range(count):
                    copy(index, step).start()

        for index in range(count):
            copy(index, date).wait()
        views = list(inputs)
        for index, place in enumerate(places):
            views[place] = buffers[index].at[pl.ds(date, 1)]
        kernel(*views, *outputs, *scratch)

    return body


def whole(shape):
    zeros = (0,) * len(shape)
    return pl.BlockSpec(tuple(shape), lambda date: zeros)


def call(kernel, dates, inputs, outputs, scratch, flops, memory=MEMORY):
    in_specs, arrays, buffers = [], [], []
    for kind, array in inputs:
        arrays.append(array)
        if kind == "scalar":
            in_specs.append(pl.BlockSpec(memory_space=pltpu.SMEM))
        elif kind == "date":
            in_specs.append(pl.BlockSpec(memory_space=pl.ANY))
            buffers.append(pltpu.VMEM(array.shape, array.dtype))
        else:
            in_specs.append(whole(array.shape))
    out_specs = [(per_date if kind == "date" else whole)(shape) for kind, shape, _ in outputs]
    moved = sum(array.size * array.dtype.itemsize for array in arrays)
    ready = pltpu.SemaphoreType.DMA((len(buffers), dates))
    return pl.pallas_call(
        streamed(kernel, dates, [kind for kind, _ in inputs], len(outputs)),
        grid=(dates,),
        in_specs=in_specs,
        out_specs=out_specs,
        out_shape=[jax.ShapeDtypeStruct(shape, dtype) for _, shape, dtype in outputs],
        scratch_shapes=buffers + [ready] + scratch,
        compiler_params=pltpu.CompilerParams(vmem_limit_bytes=memory * MIB),
        cost_estimate=pl.CostEstimate(flops=flops, bytes_accessed=2 * moved, transcendentals=0),
    )(*arrays)


def shifted(array, by):
    devices = lax.axis_size("rows")
    pairs = [(i, i + by) for i in range(devices) if 0 <= i + by < devices]
    return lax.ppermute(array, "rows", pairs)


def sum_of_parts(parts):
    devices = lax.axis_size("dates")
    place = lax.axis_index("dates")
    total = lax.dynamic_index_in_dim(parts, place, 0, keepdims=False).astype(F32)
    for step in range(1, devices):
        piece = lax.dynamic_index_in_dim(parts, (place + step) % devices, 0, keepdims=False)
        pairs = [(i, (i + step) % devices) for i in range(devices)]
        total = total + lax.ppermute(piece, "dates", pairs).astype(F32)
    return total.astype(BF16)


def exchange(pieces, axes):
    return lax.all_to_all(pieces, axes, split_axis=0, concat_axis=0, tiled=True)


def gather(array, axis):
    return lax.all_gather(array, axis, axis=0, tiled=True)


def scatter(rows_array):
    axes = ("rows", "dates")
    devices = lax.axis_size(axes)
    count, width = rows_array.shape
    return exchange(rows_array.reshape(devices, count // devices, width), axes)


def collect(pieces):
    spread = pl.pallas_call(
        total_kernel,
        out_shape=jax.ShapeDtypeStruct(pieces.shape, BF16),
        compiler_params=pltpu.CompilerParams(vmem_limit_bytes=MEMORY * MIB),
    )(pieces)
    count, rows, width = pieces.shape
    return exchange(spread, ("rows", "dates")).reshape(count * rows, width)


def padded_count(count, devices):
    step = 8 * devices
    return -(-count // step) * step


def local(
    images,
    day_index,
    valid,
    out_grad,
    conv_weight,
    first_gain,
    first_shift,
    block_weight,
    gn_gain,
    gn_shift,
    key_weight,
    queries,
):
    dates, rows_here, cols, pair_width = images.shape
    width = conv_weight.shape[-1]
    row_devs, date_devs = lax.axis_size("rows"), lax.axis_size("dates")
    devices = row_devs * date_devs
    rows = rows_here // 2
    heads, depth = queries.shape
    norm_count = float(rows * row_devs * cols * (width // GROUPS))
    grad_scale = float(rows * row_devs * cols) ** (-0.5)
    date_start = lax.axis_index("dates") * dates
    frame = (dates, rows, cols, width)
    edge_rows = (dates, cols, width)
    flops = 2 * dates * rows * cols * width * width

    rows_of = lambda vector: vector.reshape(1, width)
    first_gain, first_shift = rows_of(first_gain), rows_of(first_shift)
    gn_gain, gn_shift = rows_of(gn_gain), rows_of(gn_shift)
    last = images[:, -1]
    above = shifted(last, 1)
    high = shifted(images[:, -3:-1], 1)
    below = shifted(images[:, :2], -1)
    paired = images.reshape(dates, rows, 2, cols, pair_width)
    conv_out, sums = call(
        functools.partial(down_kernel, dates),
        dates,
        [("date", paired), ("date", above), ("all", conv_weight)],
        [("date", frame, BF16), ("all", (row_devs, 2 * dates, width), F32)],
        [pltpu.VMEM((3 * pair_width, 2 * width), BF16)],
        6 * flops,
    )
    stats = exchange(sums, "rows")
    high, below, last, _ = lax.optimization_barrier((high, below, last, sums))
    halo_up, halo_down = pl.pallas_call(
        edge_kernel,
        out_shape=[jax.ShapeDtypeStruct(edge_rows, BF16)] * 2,
        scratch_shapes=[pltpu.VMEM((3 * pair_width, 2 * width), BF16)],
        compiler_params=pltpu.CompilerParams(vmem_limit_bytes=MEMORY * MIB),
    )(high, above, last, below, conv_weight)
    days = lax.dynamic_slice_in_dim(day_index, date_start, dates, 0)
    place = lax.axis_index("rows").reshape(1)

    block_out, hidden, first_norm, sums = call(
        functools.partial(block_kernel, dates, norm_count, row_devs),
        dates,
        [
            ("scalar", place),
            ("date", conv_out),
            ("date", halo_up),
            ("date", halo_down),
            ("all", stats),
            ("all", first_gain),
            ("all", first_shift),
            ("all", block_weight),
        ],
        [
            ("date", frame, BF16),
            ("date", (dates, rows + 2, cols, width), BF16),
            ("all", (2 * dates, width), F32),
            ("all", (row_devs, 2 * dates, width), F32),
        ],
        [pltpu.VMEM((3 * width, 3 * width), BF16)],
        9 * flops,
    )
    stats = exchange(sums, "rows")
    sums, valid, out_grad = lax.optimization_barrier((sums, valid, out_grad))
    grad_rows, valid_rows = out_grad.size // width, valid.size // width
    packed = jnp.concatenate(
        [out_grad.reshape(grad_rows, width), valid.astype(BF16).reshape(valid_rows, width)]
    )
    packed = gather(packed[None], "dates")
    grads_here = packed[:, :grad_rows].reshape((date_devs,) + out_grad.shape)
    clear = packed[:, grad_rows:].reshape((date_devs,) + valid.shape)
    clear = lax.dynamic_slice_in_dim(clear, date_start, dates, 1)
    clear = clear.transpose(1, 2, 0, 3).reshape(dates, rows, cols).astype(F32)
    features, exponent, attn, norm, packed, key_wide, query_wide = call(
        functools.partial(score_kernel, dates, norm_count, grad_scale),
        dates,
        [
            ("scalar", days),
            ("date", block_out),
            ("all", stats),
            ("all", gn_gain),
            ("all", gn_shift),
            ("all", grads_here),
            ("date", clear),
            ("all", key_weight.T),
            ("all", queries.T),
        ],
        [
            ("date", frame, BF16),
            ("date", frame, F32),
            ("date", frame, F32),
            ("all", (2 * dates, width), F32),
            ("all", (1, 2, cols, width), F32),
            ("all", (width, width), BF16),
            ("all", (8, width), F32),
        ],
        [
            pltpu.VMEM(frame[1:], F32),
            pltpu.VMEM(frame[1:], F32),
            pltpu.VMEM((2 * width, width), BF16),
            pltpu.VMEM((width, 2 * width), BF16),
        ],
        5 * flops,
        24,
    )
    packed = gather(packed, "dates")
    block_grad, attended, key_part, vectors, sums = call(
        functools.partial(attend_kernel, dates, grad_scale),
        dates,
        [
            ("all", packed),
            ("date", features),
            ("date", exponent),
            ("date", attn),
            ("date", block_out),
            ("all", norm),
            ("all", gn_gain),
            ("all", gn_shift),
            ("all", query_wide),
            ("all", grads_here),
            ("all", key_wide),
        ],
        [
            ("date", frame, BF16),
            ("all", (date_devs, rows, cols // date_devs, width), BF16),
            ("all", (width, width), F32),
            ("all", (8, width), F32),
            ("all", (row_devs, 2 * dates, width), F32),
        ],
        [pltpu.VMEM(frame[1:], F32)] * 3,
        5 * flops,
        24,
    )
    tails = exchange(sums, "rows")
    pre_grad, linear_grad, first_vectors, sums = call(
        functools.partial(hidden_kernel, dates, norm_count, row_devs),
        dates,
        [
            ("scalar", place),
            ("date", block_grad),
            ("date", block_out),
            ("all", tails),
            ("all", norm),
            ("all", block_weight),
            ("date", conv_out),
            ("date", halo_up),
            ("date", halo_down),
            ("all", first_norm),
            ("all", first_gain),
            ("all", first_shift),
        ],
        [
            ("date", frame, BF16),
            ("date", (dates, rows + 2, cols, width), BF16),
            ("all", (8, width), F32),
            ("all", (row_devs, 2 * dates, width), F32),
        ],
        [
            pltpu.VMEM((3 * width, 3 * width), BF16),
            pltpu.VMEM((2 * dates, width), F32),
            pltpu.VMEM((rows + 4, cols, width), BF16),
        ],
        9 * flops,
    )
    tails = exchange(sums, "rows")
    (block_rows,) = call(
        functools.partial(block_grad_kernel, dates),
        dates,
        [("date", hidden), ("date", pre_grad), ("all", key_part)],
        [("all", (10 * width, width), BF16)],
        [pltpu.VMEM((3 * width, 3 * width), F32)],
        9 * flops,
    )
    tails, block_rows = lax.optimization_barrier((tails, block_rows))
    conv_count = 9 * pair_width // 2 + 32
    (rows_all,) = call(
        functools.partial(conv_grad_kernel, dates, norm_count),
        dates,
        [
            ("date", paired),
            ("date", above),
            ("date", high),
            ("date", below),
            ("date", conv_out),
            ("date", linear_grad),
            ("all", tails),
            ("all", first_norm),
            ("all", first_gain),
            ("all", first_vectors),
            ("all", vectors),
            ("all", block_rows),
        ],
        [("all", (padded_count(10 * width + conv_count, devices), width), BF16)],
        [pltpu.VMEM((2 * dates, width), F32), pltpu.VMEM((3 * pair_width, 2 * width), F32)],
        6 * flops,
    )
    pieces = scatter(rows_all)
    attended, _ = lax.optimization_barrier((attended, rows_all))
    attended = sum_of_parts(attended)
    rows_all = collect(pieces)
    shapes = [
        (9 * pair_width // 2, width),
        (9 * width, width),
        (heads * depth, width),
        (depth, heads),
    ] + [(1, width)] * 4
    conv_total, block_total, key_total, query_total, *totals = pl.pallas_call(
        functools.partial(final_kernel, depth),
        out_shape=[jax.ShapeDtypeStruct(shape, F32) for shape in shapes],
        compiler_params=pltpu.CompilerParams(vmem_limit_bytes=MEMORY * MIB),
    )(rows_all)
    totals = [total.reshape(width) for total in totals]
    return (
        attended,
        conv_total.reshape(conv_weight.shape),
        totals[0],
        totals[1],
        block_total.reshape(block_weight.shape),
        totals[2],
        totals[3],
        key_total.T,
        query_total.T,
    )


def solution(mesh):
    return jax.shard_map(
        local,
        mesh=mesh,
        in_specs=(
            P("dates", "rows", None, None),
            P(),
            P(None, "rows", "dates"),
            P("rows", "dates", None),
            P(),
            P(),
            P(),
            P(),
            P(),
            P(),
            P(),
            P(),
        ),
        out_specs=(P("rows", "dates", None), P(), P(), P(), P(), P(), P(), P(), P()),
        check_vma=False,
    )
```

```python
import functools
import math

import jax
import jax.numpy as jnp
from jax import lax
from jax.experimental import pallas as pl
from jax.experimental.pallas import tpu as pltpu
from jax.sharding import PartitionSpec as P

GROUPS = 4


EPS = 1e-05


MIB = 1 << 20


F32 = jnp.float32


BF16 = jnp.bfloat16


def product(left, right, left_dim, right_dim):
    return lax.dot_general(
        left, right, (((left_dim,), (right_dim,)), ((), ())), preferred_element_type=F32
    )


def group_sum(values):
    width = values.shape[-1]
    lane_group = lax.broadcasted_iota(jnp.int32, values.shape, 1) // (width // GROUPS)
    spread = jnp.zeros_like(values)
    for group in range(GROUPS):
        inside = lane_group == group
        total = jnp.sum(jnp.where(inside, values, 0.0), axis=1, keepdims=True)
        spread = spread + jnp.where(inside, total, 0.0)
    return spread


def sigmoid(values):
    return 0.5 * jnp.tanh(0.5 * values) + 0.5


def from_left(values):
    column = lax.broadcasted_iota(jnp.int32, values.shape, 1)
    return jnp.where(column > 0, pltpu.roll(values, 1, 1), 0.0)


def from_right(values):
    count = values.shape[1]
    column = lax.broadcasted_iota(jnp.int32, values.shape, 1)
    return jnp.where(column < count - 1, pltpu.roll(values, count - 1, 1), 0.0)


def column_sum(values):
    return jnp.sum(jnp.sum(values, axis=0), axis=0, keepdims=True)


def edges(place_ref, row_devs):
    place = place_ref[0]
    return (place > 0).astype(F32), (place < row_devs - 1).astype(F32)


def head_spread(width):
    lane = lax.broadcasted_iota(jnp.int32, (2 * width, width), 1) // (width // 16)
    head = lax.broadcasted_iota(jnp.int32, (2 * width, width), 0) % width // (width // 16)
    return (lane == head).astype(F32).astype(BF16)


def split(values):
    high = values.astype(BF16)
    return high, (values - high.astype(F32)).astype(BF16)


def store_sums(sums_ref, date, dates, first, second):
    for copy in range(sums_ref.shape[0]):
        sums_ref[copy, pl.ds(date, 1), :] = first
        sums_ref[copy, pl.ds(dates + date, 1), :] = second


def norm_table(sums_ref, table_ref, dates, norm_count):
    means = group_sum(jnp.sum(sums_ref[...], axis=0)) / norm_count
    mean = means[:dates]
    table_ref[:dates] = mean
    table_ref[dates:] = 1.0 / jnp.sqrt(means[dates:] - mean * mean + EPS)


def down_table(weight_ref, table):
    half = weight_ref.shape[2]
    for tap in range(3):
        base = tap * 2 * half
        table[base : base + half, : 2 * half] = weight_ref[tap, 1]
        table[base + half : base + 2 * half, : 2 * half] = weight_ref[tap, 2]
        table[base : base + half, 2 * half :] = jnp.zeros_like(weight_ref[tap, 0])
        table[base + half : base + 2 * half, 2 * half :] = weight_ref[tap, 0]


def down_rows(taps, table):
    rows, cols, width = taps[0].shape
    taps = jnp.concatenate(taps, axis=-1).reshape(rows * cols, 3 * width)
    both = product(taps, table[...], 1, 0).reshape(rows, cols, 2 * width)
    return (both[..., :width] + from_left(both[..., width:])).astype(BF16)


def down_kernel(dates, img_ref, above_ref, weight_ref, out_ref, sums_ref, table):
    date = pl.program_id(0)

    @pl.when(date == 0)
    def _():
        down_table(weight_ref, table)

    even, odd = img_ref[0, :, 0], img_ref[0, :, 1]
    above = jnp.concatenate([above_ref[0][None], odd[:-1]], axis=0)
    stored = down_rows([above, even, odd], table)
    out_ref[0] = stored
    values = stored.astype(F32)
    store_sums(sums_ref, date, dates, column_sum(values), column_sum(values * values))


def edge_kernel(high_ref, above_ref, last_ref, below_ref, weight_ref, up_ref, down_ref, table):
    dates = above_ref.shape[0]
    down_table(weight_ref, table)
    taps = [
        jnp.concatenate([high_ref[:, 0], last_ref[...]], axis=0),
        jnp.concatenate([high_ref[:, 1], below_ref[:, 0]], axis=0),
        jnp.concatenate([above_ref[...], below_ref[:, 1]], axis=0),
    ]
    stored = down_rows(taps, table)
    up_ref[...] = stored[:dates]
    down_ref[...] = stored[dates:]


def block_kernel(
    dates,
    norm_count,
    row_devs,
    edge_ref,
    conv_ref,
    up_ref,
    down_ref,
    stats_ref,
    gain_ref,
    shift_ref,
    weight_ref,
    out_ref,
    hidden_ref,
    norm_ref,
    sums_ref,
    table,
):
    date = pl.program_id(0)
    width = conv_ref.shape[-1]

    @pl.when(date == 0)
    def _():
        norm_table(stats_ref, norm_ref, dates, norm_count)
        for row_tap in range(3):
            for col_tap in range(3):
                table[
                    row_tap * width : (row_tap + 1) * width, col_tap * width : (col_tap + 1) * width
                ] = weight_ref[row_tap, col_tap]

    scale = norm_ref[pl.ds(dates + date, 1), :] * gain_ref[...]
    shift = shift_ref[...] - norm_ref[pl.ds(date, 1), :] * scale

    def activate(values):
        linear = values.astype(F32) * scale + shift
        return linear * sigmoid(linear)

    rows, cols = conv_ref.shape[1:3]
    above_edge, below_edge = edges(edge_ref, row_devs)
    hidden_ref[0, 0] = (activate(up_ref[0]) * above_edge).astype(BF16)
    hidden_ref[0, rows + 1] = (activate(down_ref[0]) * below_edge).astype(BF16)
    hidden_ref[0, 1 : rows + 1] = activate(conv_ref[0]).astype(BF16)
    taps = jnp.concatenate(
        [hidden_ref[0, tap : tap + rows] for tap in range(3)], axis=-1
    ).reshape(rows * cols, 3 * width)
    terms = product(taps, table[...], 1, 0).reshape(rows, cols, 3 * width)
    stored = (
        terms[..., width : 2 * width]
        + from_left(terms[..., :width])
        + from_right(terms[..., 2 * width :])
    ).astype(BF16)
    out_ref[0] = stored
    values = stored.astype(F32)
    store_sums(sums_ref, date, dates, column_sum(values), column_sum(values * values))


def encoding(day, width):
    lane = lax.broadcasted_iota(jnp.int32, (1, width), 1)
    frequency = jnp.exp((lane // 2).astype(F32) * (-2.0 * math.log(1000.0) / width))
    angles = day.astype(F32) * frequency
    return jnp.where(lane % 2 == 0, jnp.sin(angles), jnp.cos(angles))


def fold_keys(key_ref, query_ref, wide_ref, vector_ref, spread_ref, score_ref):
    depth, heads = query_ref.shape
    width = key_ref.shape[1]
    lanes = width // heads
    spread_ref[...] = head_spread(width)
    row = lax.broadcasted_iota(jnp.int32, (heads * depth, width), 0)
    lane = lax.broadcasted_iota(jnp.int32, (heads * depth, width), 1)
    widen = (row // depth == lane // lanes) & (row % depth == lane % lanes)
    wide = product(key_ref[...], widen.astype(F32).astype(BF16), 0, 0)
    wide_ref[...] = wide.astype(BF16)
    head = lax.broadcasted_iota(jnp.int32, (heads, width), 0)
    lane = lax.broadcasted_iota(jnp.int32, (heads, width), 1)
    inside = (lane // lanes == head).astype(F32).astype(BF16)
    high, low = split(query_ref[...])
    lower = (query_ref[...] - high.astype(F32) - low.astype(F32)).astype(BF16)
    spread = sum(product(part, inside, 1, 0) for part in (high, low, lower))
    step = lax.broadcasted_iota(jnp.int32, (depth, width), 0)
    place = lax.broadcasted_iota(jnp.int32, (depth, width), 1) % lanes
    queries = jnp.sum(jnp.where(step == place, spread * depth**-0.5, 0.0), axis=0, keepdims=True)
    place = lax.broadcasted_iota(jnp.int32, (1, width), 1) % lanes
    queries = queries + jnp.where((place == depth) | (place == depth + 1), 1.0, 0.0)
    vector_ref[...] = jnp.broadcast_to(queries, vector_ref.shape)
    folded = jnp.concatenate(split(wide * queries), axis=-1)
    folded = product(folded, spread_ref[...], 1, 0)
    score_ref[...] = jnp.concatenate(split(folded), axis=-1)


def source_of(turn_ref, device, devices):
    return (device + devices - turn_ref[0]) % devices


def upstream_rows(grad_ref, turn_ref, rows, cols):
    devices = grad_ref.shape[0]
    piece = cols // devices
    parts = [
        grad_ref[source_of(turn_ref, device, devices), : rows * piece].reshape(rows, piece, -1)
        for device in range(devices)
    ]
    return jnp.concatenate(parts, axis=1)


def score_kernel(
    dates,
    norm_count,
    grad_scale,
    day_ref,
    block_ref,
    stats_ref,
    gain_ref,
    shift_ref,
    grad_ref,
    valid_ref,
    turn_ref,
    key_ref,
    query_ref,
    feat_ref,
    exp_ref,
    attn_ref,
    norm_ref,
    packed_ref,
    wide_ref,
    vector_ref,
    total,
    mean,
    spread_ref,
    score_ref,
):
    date = pl.program_id(0)
    rows, cols, width = block_ref.shape[1:]

    @pl.when(date == 0)
    def _():
        norm_table(stats_ref, norm_ref, dates, norm_count)
        fold_keys(key_ref, query_ref, wide_ref, vector_ref, spread_ref, score_ref)
        total[...] = jnp.zeros_like(total)
        mean[...] = jnp.zeros_like(mean)

    scale = norm_ref[pl.ds(dates + date, 1), :] * gain_ref[...]
    shift = shift_ref[...] - norm_ref[pl.ds(date, 1), :] * scale
    linear = block_ref[0].astype(F32) * scale + shift
    features = (linear * sigmoid(linear) + encoding(day_ref[date], width)).astype(BF16)
    feat_ref[0] = features
    upstream = upstream_rows(grad_ref, turn_ref, rows, cols)
    parts = split(upstream.astype(F32) * features.astype(F32))
    parts = jnp.concatenate(parts, axis=-1).reshape(rows * cols, 2 * width)
    attn = product(parts, spread_ref[...], 1, 0).reshape(rows, cols, width) * grad_scale
    both = product(features.reshape(rows * cols, width), score_ref[...], 1, 0)
    scores = (both[:, :width] + both[:, width:]).reshape(rows, cols, width)
    devices = grad_ref.shape[0]
    valid = jnp.zeros((rows, width), F32)
    for device in range(devices):
        piece = valid_ref[
            source_of(turn_ref, device, devices), pl.ds(pl.multiple_of(date * rows, rows), rows), :
        ]
        valid = valid + pltpu.roll(piece, device * (cols // devices), 1)
    diagonal = lax.broadcasted_iota(jnp.int32, (cols, cols), 0) == lax.broadcasted_iota(
        jnp.int32, (cols, cols), 1
    )
    ones = jnp.ones((cols, width), BF16)
    clear = jnp.concatenate(
        [jnp.where(diagonal, valid[row : row + 1], 0.0) for row in range(rows)], axis=0
    ).astype(BF16)
    clear = product(clear, ones, 1, 0).reshape(rows, cols, width)
    exponent = clear * jnp.exp(scores)
    running = total[...] + exponent
    share = jnp.where(running > 0.0, exponent / running, 0.0)
    total[...] = running
    mean[...] += share * (attn - mean[...])
    exp_ref[0] = exponent
    attn_ref[0] = attn

    @pl.when(date == dates - 1)
    def _():
        place = lax.broadcasted_iota(jnp.int32, (cols, width), 1) % rows
        for index, source in enumerate((total, mean)):
            dense = jnp.zeros((cols, width), F32)
            for row in range(rows):
                dense = dense + jnp.where(place == row, source[row], 0.0)
            for copy in range(packed_ref.shape[0]):
                packed_ref[copy, index] = dense


def attend_kernel(
    dates,
    grad_scale,
    packed_ref,
    feat_ref,
    exp_ref,
    attn_ref,
    block_ref,
    norm_ref,
    gain_ref,
    shift_ref,
    query_ref,
    grad_ref,
    turn_ref,
    key_ref,
    grad_out_ref,
    part_ref,
    key_out_ref,
    vector_ref,
    sums_ref,
    inverse,
    average,
    attended,
):
    date = pl.program_id(0)
    rows, cols, width = block_ref.shape[1:]

    @pl.when(date == 0)
    def _():
        denominator = jnp.sum(packed_ref[:, 0], axis=0)
        reciprocal = 1.0 / denominator
        mean = jnp.sum(packed_ref[:, 0] * reciprocal * packed_ref[:, 1], axis=0)
        place = lax.broadcasted_iota(jnp.int32, (cols, width), 1) % rows
        for values, target in ((reciprocal, inverse), (mean, average)):
            parts = jnp.concatenate(split(values), axis=-1)
            wide_place = jnp.concatenate([place, place], axis=-1)
            picked = jnp.concatenate(
                [jnp.where(wide_place == row, parts, jnp.zeros_like(parts)) for row in range(rows)], axis=0
            )
            target[...] = product(picked, head_spread(width), 1, 0).reshape(rows, cols, width)
        attended[...] = jnp.zeros_like(attended)
        key_out_ref[...] = jnp.zeros_like(key_out_ref)
        vector_ref[...] = jnp.zeros_like(vector_ref)

    features = feat_ref[0]
    weights = exp_ref[0] * inverse[...]
    rounded = weights.astype(BF16).astype(F32)
    attended[...] += rounded * features.astype(F32)
    score_grad = weights * (attn_ref[0] - average[...])
    spread_grad = score_grad * query_ref[0:1]
    rest = spread_grad - spread_grad.astype(BF16).astype(F32)
    lane = lax.broadcasted_iota(jnp.int32, spread_grad.shape, 2) % (width // 16)
    key_grads = jnp.where(lane == 5, rest, spread_grad).astype(BF16).reshape(rows * cols, width)
    key_out_ref[...] += product(features.reshape(rows * cols, width), key_grads, 0, 0)
    upstream = upstream_rows(grad_ref, turn_ref, rows, cols)
    feat_grad = rounded * (upstream.astype(F32) * grad_scale) + product(
        key_grads, key_ref[...], 1, 1
    ).reshape(rows, cols, width)
    gain = gain_ref[...]
    centred = (block_ref[0].astype(F32) - norm_ref[pl.ds(date, 1), :]) * norm_ref[
        pl.ds(dates + date, 1), :
    ]
    linear = centred * gain + shift_ref[...]
    part = sigmoid(linear)
    linear_grad = feat_grad * (part * (1.0 + linear * (1.0 - part)))
    first = column_sum(linear_grad)
    second = column_sum(linear_grad * centred)
    vector_ref[0:1] += second
    vector_ref[1:2] += first
    store_sums(sums_ref, date, dates, first * gain, second * gain)
    grad_out_ref[0] = (linear_grad * gain).astype(BF16)

    @pl.when(date == dates - 1)
    def _():
        devices, piece = part_ref.shape[0], part_ref.shape[2]
        for device in range(devices):
            part_ref[device] = attended[:, device * piece : (device + 1) * piece].astype(BF16)
        key_part = key_out_ref[...]
        place = lax.broadcasted_iota(jnp.int32, (width, width), 1) % (width // 16)
        both = pltpu.roll(key_part, width - 4, 1) + pltpu.roll(key_part, width - 5, 1)
        both = jnp.where(place == 0, both, 0.0)
        both = both + pltpu.roll(both, 1, 1)
        both = both + pltpu.roll(both, 2, 1)
        vector_ref[2:3] = 0.5 * jnp.sum(key_ref[...].astype(F32) * both, axis=0, keepdims=True)


def hidden_kernel(
    dates,
    norm_count,
    row_devs,
    edge_ref,
    grad_ref,
    block_ref,
    tails_ref,
    norm_ref,
    weight_ref,
    conv_ref,
    up_ref,
    down_ref,
    first_norm_ref,
    gain_ref,
    shift_ref,
    pre_ref,
    out_ref,
    vector_ref,
    sums_ref,
    table,
    factors,
    padded,
):
    date = pl.program_id(0)
    rows, cols, width = block_ref.shape[1:]

    @pl.when(date == 0)
    def _():
        tails = group_sum(jnp.sum(tails_ref[...], axis=0)) / norm_count
        mean, inverse = norm_ref[:dates], norm_ref[dates:]
        slope = -inverse * inverse * tails[dates:]
        factors[0:dates] = slope
        factors[dates : 2 * dates] = -inverse * tails[:dates] - mean * slope
        vector_ref[...] = jnp.zeros_like(vector_ref)
        padded[:2] = jnp.zeros_like(padded[:2])
        padded[rows + 2 :] = jnp.zeros_like(padded[rows + 2 :])
        for row_tap in range(3):
            for col_tap in range(3):
                table[
                    col_tap * width : (col_tap + 1) * width, row_tap * width : (row_tap + 1) * width
                ] = weight_ref[2 - row_tap, col_tap]

    inverse = norm_ref[pl.ds(dates + date, 1), :]
    slope = factors[pl.ds(date, 1), :]
    constant = factors[pl.ds(dates + date, 1), :]

    above_edge, below_edge = edges(edge_ref, row_devs)
    stored = (
        grad_ref[0].astype(F32) * inverse + (block_ref[0].astype(F32) * slope + constant)
    ).astype(BF16)
    pre_ref[0] = stored
    padded[2 : rows + 2] = stored
    reach = rows + 2
    taps = jnp.concatenate([padded[tap : tap + reach] for tap in range(3)], axis=-1).reshape(
        reach * cols, 3 * width
    )
    terms = product(taps, table[...], 1, 1).reshape(reach, cols, 3 * width)
    hidden_grad = (
        terms[..., width : 2 * width]
        + from_right(terms[..., :width])
        + from_left(terms[..., 2 * width :])
    )
    gain = gain_ref[...]
    conv = jnp.concatenate([up_ref[0][None], conv_ref[0], down_ref[0][None]], axis=0)
    centred = (conv.astype(F32) - first_norm_ref[pl.ds(date, 1), :]) * first_norm_ref[
        pl.ds(dates + date, 1), :
    ]
    linear = centred * gain + shift_ref[...]
    part = sigmoid(linear)
    linear_grad = hidden_grad * (part * (1.0 + linear * (1.0 - part)))
    linear_grad = jnp.concatenate(
        [
            linear_grad[:1] * above_edge,
            linear_grad[1 : rows + 1],
            linear_grad[rows + 1 :] * below_edge,
        ],
        axis=0,
    )
    out_ref[0] = linear_grad.astype(BF16)
    first = column_sum(linear_grad)
    second = column_sum(linear_grad * centred)
    vector_ref[0:1] += second
    vector_ref[1:2] += first
    store_sums(sums_ref, date, dates, first * gain, second * gain)


def block_grad_kernel(dates, hidden_ref, pre_ref, key_ref, out_ref, total):
    date = pl.program_id(0)
    rows, cols, width = pre_ref.shape[1:]

    @pl.when(date == 0)
    def _():
        total[...] = jnp.zeros_like(total)

    grads = pre_ref[0].astype(F32)
    grads = jnp.concatenate(
        [from_right(grads).astype(BF16), pre_ref[0], from_left(grads).astype(BF16)], axis=-1
    ).reshape(rows * cols, 3 * width)
    taps = jnp.concatenate(
        [hidden_ref[0, tap : tap + rows] for tap in range(3)], axis=-1
    ).reshape(rows * cols, 3 * width)
    total[...] += product(taps, grads, 0, 0)

    @pl.when(date == dates - 1)
    def _():
        for row_tap in range(3):
            for col_tap in range(3):
                base = (row_tap * 3 + col_tap) * width
                out_ref[base : base + width] = total[
                    row_tap * width : (row_tap + 1) * width, col_tap * width : (col_tap + 1) * width
                ].astype(BF16)
        key_part = key_ref[...]
        rest = key_part - key_part.astype(BF16).astype(F32)
        lanes = width // 16
        place = lax.broadcasted_iota(jnp.int32, key_part.shape, 1) % lanes
        rest = pltpu.roll(rest, lanes // 2, 1)
        key_rows = jnp.where(place < lanes // 2, key_part, rest).astype(BF16)
        out_ref[9 * width : 10 * width] = key_rows
        if out_ref.shape[0] > 10 * width:
            out_ref[10 * width :] = jnp.zeros_like(out_ref[10 * width :])


def conv_grad_kernel(
    dates,
    norm_count,
    img_ref,
    above_ref,
    high_ref,
    below_ref,
    conv_ref,
    grad_ref,
    tails_ref,
    norm_ref,
    gain_ref,
    vector_ref,
    other_ref,
    block_rows_ref,
    out_ref,
    factors,
    total,
):
    date = pl.program_id(0)
    rows, cols, width = conv_ref.shape[1:]
    half = width // 2

    @pl.when(date == 0)
    def _():
        tails = group_sum(jnp.sum(tails_ref[...], axis=0)) / norm_count
        mean, inverse = norm_ref[:dates], norm_ref[dates:]
        slope = -inverse * inverse * tails[dates:]
        factors[0:dates] = slope
        factors[dates : 2 * dates] = -inverse * tails[:dates] - mean * slope
        total[...] = jnp.zeros_like(total)

    scale = norm_ref[pl.ds(dates + date, 1), :] * gain_ref[...]
    slope = factors[pl.ds(date, 1), :]
    constant = factors[pl.ds(dates + date, 1), :]
    own = conv_ref[0].astype(F32) * slope + constant
    scaled = grad_ref[0].astype(F32) * scale
    stored = jnp.concatenate(
        [scaled[:1], scaled[1 : rows + 1] + own, scaled[rows + 1 :]], axis=0
    ).astype(BF16)
    moved = from_right(stored.astype(F32)).astype(BF16)
    reach = rows + 2
    grads = jnp.concatenate([stored, moved], axis=-1).reshape(reach * cols, 2 * width)
    even, odd = img_ref[0, :, 0], img_ref[0, :, 1]
    above = above_ref[0][None]
    taps = [
        jnp.concatenate([high_ref[0, :1], above, odd], axis=0),
        jnp.concatenate([high_ref[0, 1:], even, below_ref[0, :1]], axis=0),
        jnp.concatenate([above, odd, below_ref[0, 1:]], axis=0),
    ]
    taps = jnp.concatenate(taps, axis=-1).reshape(reach * cols, 3 * width)
    total[...] += product(taps, grads, 0, 0)

    @pl.when(date == dates - 1)
    def _():
        begin = block_rows_ref.shape[0]
        out_ref[:begin] = block_rows_ref[...]
        for tap in range(3):
            base = tap * width
            pair = total[base : base + width, :width].astype(BF16)
            left = total[base + half : base + width, width:].astype(BF16)
            start = begin + tap * 3 * half
            out_ref[start : start + half] = left
            out_ref[start + half : start + 3 * half] = pair
        start = begin + 9 * half
        for source in (vector_ref, other_ref):
            high, low = split(source[...])
            out_ref[start : start + 16] = jnp.concatenate([high, low], axis=0)
            start += 16
        if out_ref.shape[0] > start:
            out_ref[start:] = jnp.zeros_like(out_ref[start:])


def total_kernel(in_ref, out_ref):
    total = jnp.sum(in_ref[...].astype(F32), axis=0).astype(BF16)
    for copy in range(out_ref.shape[0]):
        out_ref[copy] = total


def final_kernel(depth, rows_ref, conv_ref, block_ref, key_ref, query_ref, *vector_refs):
    conv_end, block_end, width = conv_ref.shape[0], block_ref.shape[0], block_ref.shape[1]
    block_ref[...] = rows_ref[:block_end].astype(F32)
    wide = key_ref.shape[0]
    heads = wide // depth
    lanes = width // heads
    row = lax.broadcasted_iota(jnp.int32, (wide, width), 0)
    lane = lax.broadcasted_iota(jnp.int32, (wide, width), 1)
    narrow = (row // depth == lane // lanes) & (row % depth == lane % depth)
    narrow = narrow.astype(F32).astype(BF16)
    key_ref[...] = product(narrow, rows_ref[block_end : block_end + width], 1, 1)
    start = block_end + width
    conv_ref[...] = rows_ref[start : start + conv_end].astype(F32)
    start += conv_end
    for index in range(2):
        both = rows_ref[start : start + 16].astype(F32)
        both = both[:8] + both[8:]
        vector_refs[2 * index][...] = both[0:1]
        vector_refs[2 * index + 1][...] = both[1:2]
        start += 16
    both = rows_ref[start - 16 : start]
    row = lax.broadcasted_iota(jnp.int32, (heads, width), 0)
    lane = lax.broadcasted_iota(jnp.int32, (heads, width), 1)
    inside = row == lane // lanes
    step = lax.broadcasted_iota(jnp.int32, (8, width), 0)
    place = lax.broadcasted_iota(jnp.int32, (8, width), 1) % lanes
    steps = step == place
    query = jnp.zeros((8, heads), F32)
    for index in (2, 10):
        picked = jnp.where(steps, both[index : index + 1].astype(F32), 0.0).astype(BF16)
        query = query + product(picked, inside.astype(F32).astype(BF16), 1, 1)
    query_ref[...] = query[:depth]


def per_date(shape):
    zeros = (0,) * (len(shape) - 1)
    return pl.BlockSpec((1,) + tuple(shape[1:]), lambda date: (date,) + zeros)


def streamed(kernel, dates, kinds, out_count):
    places = [place for place, kind in enumerate(kinds) if kind != "scalar"]

    def body(*refs):
        inputs, rest = list(refs[: len(kinds)]), refs[len(kinds) :]
        outputs, scratch = rest[:out_count], rest[out_count:]
        count = len(places)
        buffers, ready, scratch = scratch[:count], scratch[count], scratch[count + 1 :]
        date = pl.program_id(0)
        views = list(inputs)

        def copy(index, step):
            source, target = inputs[places[index]], buffers[index]
            if kinds[places[index]] == "date":
                source, target = source.at[step], target.at[step]
            return pltpu.make_async_copy(source, target, ready.at[index, step])

        @pl.when(date == 0)
        def _():
            for step in range(dates):
                for index, place in enumerate(places):
                    if step == 0 or kinds[place] == "date":
                        copy(index, step).start()
            for index, place in enumerate(places):
                if kinds[place] == "all":
                    copy(index, 0).wait()

        for index, place in enumerate(places):
            if kinds[place] == "date":
                copy(index, date).wait()
                views[place] = buffers[index].at[pl.ds(date, 1)]
            else:
                views[place] = buffers[index]
        kernel(*views, *outputs, *scratch)

    return body


def whole(shape):
    zeros = (0,) * len(shape)
    return pl.BlockSpec(tuple(shape), lambda date: zeros)


def call(kernel, dates, inputs, outputs, scratch, flops, stream=False):
    in_specs, arrays, buffers = [], [], []
    for kind, array in inputs:
        arrays.append(array)
        if kind == "scalar":
            in_specs.append(pl.BlockSpec(memory_space=pltpu.SMEM))
        elif stream:
            in_specs.append(pl.BlockSpec(memory_space=pl.ANY))
            buffers.append(pltpu.VMEM(array.shape, array.dtype))
        else:
            in_specs.append((per_date if kind == "date" else whole)(array.shape))
    out_specs = [(per_date if kind == "date" else whole)(shape) for kind, shape, _ in outputs]
    moved = sum(array.size * array.dtype.itemsize for array in arrays)
    if stream:
        kernel = streamed(kernel, dates, [kind for kind, _ in inputs], len(outputs))
        scratch = buffers + [pltpu.SemaphoreType.DMA((len(buffers), dates))] + scratch
    return pl.pallas_call(
        kernel,
        grid=(dates,),
        in_specs=in_specs,
        out_specs=out_specs,
        out_shape=[jax.ShapeDtypeStruct(shape, dtype) for _, shape, dtype in outputs],
        scratch_shapes=scratch,
        compiler_params=pltpu.CompilerParams(vmem_limit_bytes=(60 if stream else 24) * MIB),
        cost_estimate=pl.CostEstimate(flops=flops, bytes_accessed=2 * moved, transcendentals=0),
    )(*arrays)


def shifted(array, by):
    devices = lax.axis_size("rows")
    pairs = [(i, i + by) for i in range(devices) if 0 <= i + by < devices]
    return lax.ppermute(array, "rows", pairs)


def turned(array):
    devices = lax.axis_size("dates")
    pieces = [array]
    for step in range(1, devices):
        pairs = [((i + step) % devices, i) for i in range(devices)]
        pieces.append(lax.ppermute(array, "dates", pairs))
    return jnp.stack(pieces)


def sum_of_parts(parts):
    devices = lax.axis_size("dates")
    place = lax.axis_index("dates")
    total = lax.dynamic_index_in_dim(parts, place, 0, keepdims=False).astype(F32)
    for step in range(1, devices):
        piece = lax.dynamic_index_in_dim(parts, (place + step) % devices, 0, keepdims=False)
        pairs = [(i, (i + step) % devices) for i in range(devices)]
        total = total + lax.ppermute(piece, "dates", pairs).astype(F32)
    return total.astype(BF16)


def exchange(pieces, axes):
    return lax.all_to_all(pieces, axes, split_axis=0, concat_axis=0, tiled=True)


def gather(array, axis):
    return lax.all_gather(array, axis, axis=0, tiled=True)


def scatter(rows_array):
    axes = ("rows", "dates")
    devices = lax.axis_size(axes)
    count, width = rows_array.shape
    return exchange(rows_array.reshape(devices, count // devices, width), axes)


def collect(pieces):
    spread = pl.pallas_call(
        total_kernel,
        out_shape=jax.ShapeDtypeStruct(pieces.shape, BF16),
        compiler_params=pltpu.CompilerParams(vmem_limit_bytes=16 * MIB),
    )(pieces)
    count, rows, width = pieces.shape
    return exchange(spread, ("rows", "dates")).reshape(count * rows, width)


def padded_count(count, devices):
    step = 8 * devices
    return -(-count // step) * step


def local(
    images,
    day_index,
    valid,
    out_grad,
    conv_weight,
    first_gain,
    first_shift,
    block_weight,
    gn_gain,
    gn_shift,
    key_weight,
    queries,
):
    dates, rows_here, cols, pair_width = images.shape
    width = conv_weight.shape[-1]
    row_devs, date_devs = lax.axis_size("rows"), lax.axis_size("dates")
    devices = row_devs * date_devs
    rows = rows_here // 2
    heads, depth = queries.shape
    norm_count = float(rows * row_devs * cols * (width // GROUPS))
    grad_scale = float(rows * row_devs * cols) ** (-0.5)
    date_start = lax.axis_index("dates") * dates
    frame = (dates, rows, cols, width)
    edge_rows = (dates, cols, width)
    flops = 2 * dates * rows * cols * width * width

    rows_of = lambda vector: vector.reshape(1, width)
    first_gain, first_shift = rows_of(first_gain), rows_of(first_shift)
    gn_gain, gn_shift = rows_of(gn_gain), rows_of(gn_shift)
    last = images[:, -1]
    above = shifted(last, 1)
    high = shifted(images[:, -3:-1], 1)
    below = shifted(images[:, :2], -1)
    paired = images.reshape(dates, rows, 2, cols, pair_width)
    conv_out, sums = call(
        functools.partial(down_kernel, dates),
        dates,
        [("date", paired), ("date", above), ("all", conv_weight)],
        [("date", frame, BF16), ("all", (row_devs, 2 * dates, width), F32)],
        [pltpu.VMEM((3 * pair_width, 2 * width), BF16)],
        6 * flops,
    )
    stats = exchange(sums, "rows")
    high, below, last, _ = lax.optimization_barrier((high, below, last, sums))
    halo_up, halo_down = pl.pallas_call(
        edge_kernel,
        out_shape=[jax.ShapeDtypeStruct(edge_rows, BF16)] * 2,
        scratch_shapes=[pltpu.VMEM((3 * pair_width, 2 * width), BF16)],
        compiler_params=pltpu.CompilerParams(vmem_limit_bytes=16 * MIB),
    )(high, above, last, below, conv_weight)
    valid, out_grad, _ = lax.optimization_barrier((valid, out_grad, halo_up))
    grad_rows = out_grad.size // width
    valid_rows = valid.astype(BF16).reshape(valid.shape[0] * rows, -1)
    valid_rows = jnp.pad(valid_rows, ((0, 0), (0, width - valid_rows.shape[1])))
    packed = jnp.concatenate([out_grad.reshape(grad_rows, width), valid_rows])
    sources = turned(packed)
    clear = lax.dynamic_slice_in_dim(sources, grad_rows + date_start * rows, dates * rows, 1)
    clear = clear.astype(F32)
    days = lax.dynamic_slice_in_dim(day_index, date_start, dates, 0)
    turn = lax.axis_index("dates").reshape(1)
    place = lax.axis_index("rows").reshape(1)

    block_out, hidden, first_norm, sums = call(
        functools.partial(block_kernel, dates, norm_count, row_devs),
        dates,
        [
            ("scalar", place),
            ("date", conv_out),
            ("date", halo_up),
            ("date", halo_down),
            ("all", stats),
            ("all", first_gain),
            ("all", first_shift),
            ("all", block_weight),
        ],
        [
            ("date", frame, BF16),
            ("date", (dates, rows + 2, cols, width), BF16),
            ("all", (2 * dates, width), F32),
            ("all", (row_devs, 2 * dates, width), F32),
        ],
        [pltpu.VMEM((3 * width, 3 * width), BF16)],
        9 * flops,
    )
    stats = exchange(sums, "rows")
    features, exponent, attn, norm, packed, key_wide, query_wide = call(
        functools.partial(score_kernel, dates, norm_count, grad_scale),
        dates,
        [
            ("scalar", days),
            ("date", block_out),
            ("all", stats),
            ("all", gn_gain),
            ("all", gn_shift),
            ("all", sources),
            ("all", clear),
            ("scalar", turn),
            ("all", key_weight.T),
            ("all", queries.T),
        ],
        [
            ("date", frame, BF16),
            ("date", frame, F32),
            ("date", frame, F32),
            ("all", (2 * dates, width), F32),
            ("all", (1, 2, cols, width), F32),
            ("all", (width, width), BF16),
            ("all", (8, width), F32),
        ],
        [
            pltpu.VMEM(frame[1:], F32),
            pltpu.VMEM(frame[1:], F32),
            pltpu.VMEM((2 * width, width), BF16),
            pltpu.VMEM((width, 2 * width), BF16),
        ],
        5 * flops,
    )
    packed = gather(packed, "dates")
    block_grad, attended, key_part, vectors, sums = call(
        functools.partial(attend_kernel, dates, grad_scale),
        dates,
        [
            ("all", packed),
            ("date", features),
            ("date", exponent),
            ("date", attn),
            ("date", block_out),
            ("all", norm),
            ("all", gn_gain),
            ("all", gn_shift),
            ("all", query_wide),
            ("all", sources),
            ("scalar", turn),
            ("all", key_wide),
        ],
        [
            ("date", frame, BF16),
            ("all", (date_devs, rows, cols // date_devs, width), BF16),
            ("all", (width, width), F32),
            ("all", (8, width), F32),
            ("all", (row_devs, 2 * dates, width), F32),
        ],
        [pltpu.VMEM(frame[1:], F32)] * 3,
        5 * flops,
    )
    tails = exchange(sums, "rows")
    pre_grad, linear_grad, first_vectors, sums = call(
        functools.partial(hidden_kernel, dates, norm_count, row_devs),
        dates,
        [
            ("scalar", place),
            ("date", block_grad),
            ("date", block_out),
            ("all", tails),
            ("all", norm),
            ("all", block_weight),
            ("date", conv_out),
            ("date", halo_up),
            ("date", halo_down),
            ("all", first_norm),
            ("all", first_gain),
            ("all", first_shift),
        ],
        [
            ("date", frame, BF16),
            ("date", (dates, rows + 2, cols, width), BF16),
            ("all", (8, width), F32),
            ("all", (row_devs, 2 * dates, width), F32),
        ],
        [
            pltpu.VMEM((3 * width, 3 * width), BF16),
            pltpu.VMEM((2 * dates, width), F32),
            pltpu.VMEM((rows + 4, cols, width), BF16),
        ],
        9 * flops,
        True,
    )
    tails = exchange(sums, "rows")
    (block_rows,) = call(
        functools.partial(block_grad_kernel, dates),
        dates,
        [("date", hidden), ("date", pre_grad), ("all", key_part)],
        [("all", (10 * width, width), BF16)],
        [pltpu.VMEM((3 * width, 3 * width), F32)],
        9 * flops,
        True,
    )
    tails, block_rows = lax.optimization_barrier((tails, block_rows))
    conv_count = 9 * pair_width // 2 + 32
    (rows_all,) = call(
        functools.partial(conv_grad_kernel, dates, norm_count),
        dates,
        [
            ("date", paired),
            ("date", above),
            ("date", high),
            ("date", below),
            ("date", conv_out),
            ("date", linear_grad),
            ("all", tails),
            ("all", first_norm),
            ("all", first_gain),
            ("all", first_vectors),
            ("all", vectors),
            ("all", block_rows),
        ],
        [("all", (padded_count(10 * width + conv_count, devices), width), BF16)],
        [pltpu.VMEM((2 * dates, width), F32), pltpu.VMEM((3 * pair_width, 2 * width), F32)],
        6 * flops,
        True,
    )
    pieces = scatter(rows_all)
    attended, _ = lax.optimization_barrier((attended, rows_all))
    attended = sum_of_parts(attended)
    rows_all = collect(pieces)
    shapes = [
        (9 * pair_width // 2, width),
        (9 * width, width),
        (heads * depth, width),
        (depth, heads),
    ] + [(1, width)] * 4
    conv_total, block_total, key_total, query_total, *totals = pl.pallas_call(
        functools.partial(final_kernel, depth),
        out_shape=[jax.ShapeDtypeStruct(shape, F32) for shape in shapes],
        compiler_params=pltpu.CompilerParams(vmem_limit_bytes=16 * MIB),
    )(rows_all)
    totals = [total.reshape(width) for total in totals]
    return (
        attended,
        conv_total.reshape(conv_weight.shape),
        totals[0],
        totals[1],
        block_total.reshape(block_weight.shape),
        totals[2],
        totals[3],
        key_total.T,
        query_total.T,
    )


def solution(mesh):
    return jax.shard_map(
        local,
        mesh=mesh,
        in_specs=(
            P("dates", "rows", None, None),
            P(),
            P(None, "rows", "dates"),
            P("rows", "dates", None),
            P(),
            P(),
            P(),
            P(),
            P(),
            P(),
            P(),
            P(),
        ),
        out_specs=(P("rows", "dates", None), P(), P(), P(), P(), P(), P(), P(), P()),
        check_vma=False,
    )
```

```python
import functools
import math

import jax
import jax.numpy as jnp
from jax import lax
from jax.experimental import pallas as pl
from jax.experimental.pallas import tpu as pltpu
from jax.sharding import PartitionSpec as P

GROUPS = 4


EPS = 1e-05


MIB = 1 << 20


F32 = jnp.float32


BF16 = jnp.bfloat16


def product(left, right, left_dim, right_dim):
    return lax.dot_general(
        left, right, (((left_dim,), (right_dim,)), ((), ())), preferred_element_type=F32
    )


def group_sum(values):
    width = values.shape[-1]
    lane_group = lax.broadcasted_iota(jnp.int32, values.shape, 1) // (width // GROUPS)
    spread = jnp.zeros_like(values)
    for group in range(GROUPS):
        inside = lane_group == group
        total = jnp.sum(jnp.where(inside, values, 0.0), axis=1, keepdims=True)
        spread = spread + jnp.where(inside, total, 0.0)
    return spread


def sigmoid(values):
    return 0.5 * jnp.tanh(0.5 * values) + 0.5


def from_left(values):
    column = lax.broadcasted_iota(jnp.int32, values.shape, 1)
    return jnp.where(column > 0, pltpu.roll(values, 1, 1), 0.0)


def from_right(values):
    count = values.shape[1]
    column = lax.broadcasted_iota(jnp.int32, values.shape, 1)
    return jnp.where(column < count - 1, pltpu.roll(values, count - 1, 1), 0.0)


def column_sum(values):
    return jnp.sum(jnp.sum(values, axis=0), axis=0, keepdims=True)


def edges(place_ref, row_devs):
    place = place_ref[0]
    return (place > 0).astype(F32), (place < row_devs - 1).astype(F32)


def head_spread(width):
    lane = lax.broadcasted_iota(jnp.int32, (2 * width, width), 1) // (width // 16)
    head = lax.broadcasted_iota(jnp.int32, (2 * width, width), 0) % width // (width // 16)
    return (lane == head).astype(F32).astype(BF16)


def split(values):
    high = values.astype(BF16)
    return high, (values - high.astype(F32)).astype(BF16)


def store_sums(sums_ref, date, dates, first, second):
    for copy in range(sums_ref.shape[0]):
        sums_ref[copy, pl.ds(date, 1), :] = first
        sums_ref[copy, pl.ds(dates + date, 1), :] = second


def norm_table(sums_ref, table_ref, dates, norm_count):
    means = group_sum(jnp.sum(sums_ref[...], axis=0)) / norm_count
    mean = means[:dates]
    table_ref[:dates] = mean
    table_ref[dates:] = 1.0 / jnp.sqrt(means[dates:] - mean * mean + EPS)


def down_table(weight_ref, table):
    half = weight_ref.shape[2]
    for tap in range(3):
        base = tap * 2 * half
        table[base : base + half, : 2 * half] = weight_ref[tap, 1]
        table[base + half : base + 2 * half, : 2 * half] = weight_ref[tap, 2]
        table[base : base + half, 2 * half :] = jnp.zeros_like(weight_ref[tap, 0])
        table[base + half : base + 2 * half, 2 * half :] = weight_ref[tap, 0]


def down_rows(taps, table):
    rows, cols, width = taps[0].shape
    taps = jnp.concatenate(taps, axis=-1).reshape(rows * cols, 3 * width)
    both = product(taps, table[...], 1, 0).reshape(rows, cols, 2 * width)
    return (both[..., :width] + from_left(both[..., width:])).astype(BF16)


def down_kernel(dates, img_ref, above_ref, weight_ref, out_ref, sums_ref, table):
    date = pl.program_id(0)

    @pl.when(date == 0)
    def _():
        down_table(weight_ref, table)

    even, odd = img_ref[0, :, 0], img_ref[0, :, 1]
    above = jnp.concatenate([above_ref[0][None], odd[:-1]], axis=0)
    stored = down_rows([above, even, odd], table)
    out_ref[0] = stored
    values = stored.astype(F32)
    store_sums(sums_ref, date, dates, column_sum(values), column_sum(values * values))


def edge_kernel(high_ref, above_ref, last_ref, below_ref, weight_ref, up_ref, down_ref, table):
    dates = above_ref.shape[0]
    down_table(weight_ref, table)
    taps = [
        jnp.concatenate([high_ref[:, 0], last_ref[...]], axis=0),
        jnp.concatenate([high_ref[:, 1], below_ref[:, 0]], axis=0),
        jnp.concatenate([above_ref[...], below_ref[:, 1]], axis=0),
    ]
    stored = down_rows(taps, table)
    up_ref[...] = stored[:dates]
    down_ref[...] = stored[dates:]


def block_kernel(
    dates,
    norm_count,
    row_devs,
    edge_ref,
    conv_ref,
    up_ref,
    down_ref,
    stats_ref,
    gain_ref,
    shift_ref,
    weight_ref,
    out_ref,
    hidden_ref,
    norm_ref,
    sums_ref,
    table,
):
    date = pl.program_id(0)
    width = conv_ref.shape[-1]

    @pl.when(date == 0)
    def _():
        norm_table(stats_ref, norm_ref, dates, norm_count)
        for row_tap in range(3):
            for col_tap in range(3):
                table[
                    row_tap * width : (row_tap + 1) * width, col_tap * width : (col_tap + 1) * width
                ] = weight_ref[row_tap, col_tap]

    scale = norm_ref[pl.ds(dates + date, 1), :] * gain_ref[...]
    shift = shift_ref[...] - norm_ref[pl.ds(date, 1), :] * scale

    def activate(values):
        linear = values.astype(F32) * scale + shift
        return linear * sigmoid(linear)

    rows, cols = conv_ref.shape[1:3]
    above_edge, below_edge = edges(edge_ref, row_devs)
    hidden_ref[0, 0] = (activate(up_ref[0]) * above_edge).astype(BF16)
    hidden_ref[0, rows + 1] = (activate(down_ref[0]) * below_edge).astype(BF16)
    hidden_ref[0, 1 : rows + 1] = activate(conv_ref[0]).astype(BF16)
    taps = jnp.concatenate(
        [hidden_ref[0, tap : tap + rows] for tap in range(3)], axis=-1
    ).reshape(rows * cols, 3 * width)
    terms = product(taps, table[...], 1, 0).reshape(rows, cols, 3 * width)
    stored = (
        terms[..., width : 2 * width]
        + from_left(terms[..., :width])
        + from_right(terms[..., 2 * width :])
    ).astype(BF16)
    out_ref[0] = stored
    values = stored.astype(F32)
    store_sums(sums_ref, date, dates, column_sum(values), column_sum(values * values))


def encoding(day, width):
    lane = lax.broadcasted_iota(jnp.int32, (1, width), 1)
    frequency = jnp.exp((lane // 2).astype(F32) * (-2.0 * math.log(1000.0) / width))
    angles = day.astype(F32) * frequency
    return jnp.where(lane % 2 == 0, jnp.sin(angles), jnp.cos(angles))


def fold_keys(key_ref, query_ref, wide_ref, vector_ref, spread_ref, score_ref):
    depth, heads = query_ref.shape
    width = key_ref.shape[1]
    lanes = width // heads
    spread_ref[...] = head_spread(width)
    row = lax.broadcasted_iota(jnp.int32, (heads * depth, width), 0)
    lane = lax.broadcasted_iota(jnp.int32, (heads * depth, width), 1)
    widen = (row // depth == lane // lanes) & (row % depth == lane % lanes)
    wide = product(key_ref[...], widen.astype(F32).astype(BF16), 0, 0)
    wide_ref[...] = wide.astype(BF16)
    head = lax.broadcasted_iota(jnp.int32, (heads, width), 0)
    lane = lax.broadcasted_iota(jnp.int32, (heads, width), 1)
    inside = (lane // lanes == head).astype(F32).astype(BF16)
    high, low = split(query_ref[...])
    lower = (query_ref[...] - high.astype(F32) - low.astype(F32)).astype(BF16)
    spread = sum(product(part, inside, 1, 0) for part in (high, low, lower))
    step = lax.broadcasted_iota(jnp.int32, (depth, width), 0)
    place = lax.broadcasted_iota(jnp.int32, (depth, width), 1) % lanes
    queries = jnp.sum(jnp.where(step == place, spread * depth**-0.5, 0.0), axis=0, keepdims=True)
    place = lax.broadcasted_iota(jnp.int32, (1, width), 1) % lanes
    queries = queries + jnp.where((place == depth) | (place == depth + 1), 1.0, 0.0)
    vector_ref[...] = jnp.broadcast_to(queries, vector_ref.shape)
    folded = jnp.concatenate(split(wide * queries), axis=-1)
    folded = product(folded, spread_ref[...], 1, 0)
    score_ref[...] = jnp.concatenate(split(folded), axis=-1)


def source_of(turn_ref, device, devices):
    return (device + devices - turn_ref[0]) % devices


def upstream_rows(grad_ref, turn_ref, rows, cols):
    devices = grad_ref.shape[0]
    piece = cols // devices
    parts = [
        grad_ref[source_of(turn_ref, device, devices), : rows * piece].reshape(rows, piece, -1)
        for device in range(devices)
    ]
    return jnp.concatenate(parts, axis=1)


def score_kernel(
    dates,
    norm_count,
    grad_scale,
    day_ref,
    block_ref,
    stats_ref,
    gain_ref,
    shift_ref,
    grad_ref,
    valid_ref,
    turn_ref,
    key_ref,
    query_ref,
    feat_ref,
    exp_ref,
    attn_ref,
    norm_ref,
    packed_ref,
    wide_ref,
    vector_ref,
    total,
    mean,
    spread_ref,
    score_ref,
):
    date = pl.program_id(0)
    rows, cols, width = block_ref.shape[1:]

    @pl.when(date == 0)
    def _():
        norm_table(stats_ref, norm_ref, dates, norm_count)
        fold_keys(key_ref, query_ref, wide_ref, vector_ref, spread_ref, score_ref)
        total[...] = jnp.zeros_like(total)
        mean[...] = jnp.zeros_like(mean)

    scale = norm_ref[pl.ds(dates + date, 1), :] * gain_ref[...]
    shift = shift_ref[...] - norm_ref[pl.ds(date, 1), :] * scale
    linear = block_ref[0].astype(F32) * scale + shift
    features = (linear * sigmoid(linear) + encoding(day_ref[date], width)).astype(BF16)
    feat_ref[0] = features
    upstream = upstream_rows(grad_ref, turn_ref, rows, cols)
    parts = split(upstream.astype(F32) * features.astype(F32))
    parts = jnp.concatenate(parts, axis=-1).reshape(rows * cols, 2 * width)
    attn = product(parts, spread_ref[...], 1, 0).reshape(rows, cols, width) * grad_scale
    both = product(features.reshape(rows * cols, width), score_ref[...], 1, 0)
    scores = (both[:, :width] + both[:, width:]).reshape(rows, cols, width)
    devices = grad_ref.shape[0]
    valid = jnp.zeros((rows, width), F32)
    for device in range(devices):
        piece = valid_ref[
            source_of(turn_ref, device, devices), pl.ds(pl.multiple_of(date * rows, rows), rows), :
        ]
        valid = valid + pltpu.roll(piece, device * (cols // devices), 1)
    diagonal = lax.broadcasted_iota(jnp.int32, (cols, cols), 0) == lax.broadcasted_iota(
        jnp.int32, (cols, cols), 1
    )
    ones = jnp.ones((cols, width), BF16)
    clear = jnp.concatenate(
        [jnp.where(diagonal, valid[row : row + 1], 0.0) for row in range(rows)], axis=0
    ).astype(BF16)
    clear = product(clear, ones, 1, 0).reshape(rows, cols, width)
    exponent = clear * jnp.exp(scores)
    running = total[...] + exponent
    share = jnp.where(running > 0.0, exponent / running, 0.0)
    total[...] = running
    mean[...] += share * (attn - mean[...])
    exp_ref[0] = exponent
    attn_ref[0] = attn

    @pl.when(date == dates - 1)
    def _():
        place = lax.broadcasted_iota(jnp.int32, (cols, width), 1) % rows
        for index, source in enumerate((total, mean)):
            dense = jnp.zeros((cols, width), F32)
            for row in range(rows):
                dense = dense + jnp.where(place == row, source[row], 0.0)
            for copy in range(packed_ref.shape[0]):
                packed_ref[copy, index] = dense


def attend_kernel(
    dates,
    grad_scale,
    packed_ref,
    feat_ref,
    exp_ref,
    attn_ref,
    block_ref,
    norm_ref,
    gain_ref,
    shift_ref,
    query_ref,
    grad_ref,
    turn_ref,
    key_ref,
    grad_out_ref,
    part_ref,
    key_out_ref,
    vector_ref,
    sums_ref,
    inverse,
    average,
    attended,
):
    date = pl.program_id(0)
    rows, cols, width = block_ref.shape[1:]

    @pl.when(date == 0)
    def _():
        denominator = jnp.sum(packed_ref[:, 0], axis=0)
        reciprocal = 1.0 / denominator
        mean = jnp.sum(packed_ref[:, 0] * reciprocal * packed_ref[:, 1], axis=0)
        place = lax.broadcasted_iota(jnp.int32, (cols, width), 1) % rows
        for values, target in ((reciprocal, inverse), (mean, average)):
            parts = jnp.concatenate(split(values), axis=-1)
            wide_place = jnp.concatenate([place, place], axis=-1)
            picked = jnp.concatenate(
                [jnp.where(wide_place == row, parts, jnp.zeros_like(parts)) for row in range(rows)], axis=0
            )
            target[...] = product(picked, head_spread(width), 1, 0).reshape(rows, cols, width)
        attended[...] = jnp.zeros_like(attended)
        key_out_ref[...] = jnp.zeros_like(key_out_ref)
        vector_ref[...] = jnp.zeros_like(vector_ref)

    features = feat_ref[0]
    weights = exp_ref[0] * inverse[...]
    rounded = weights.astype(BF16).astype(F32)
    attended[...] += rounded * features.astype(F32)
    score_grad = weights * (attn_ref[0] - average[...])
    spread_grad = score_grad * query_ref[0:1]
    rest = spread_grad - spread_grad.astype(BF16).astype(F32)
    lane = lax.broadcasted_iota(jnp.int32, spread_grad.shape, 2) % (width // 16)
    key_grads = jnp.where(lane == 5, rest, spread_grad).astype(BF16).reshape(rows * cols, width)
    key_out_ref[...] += product(features.reshape(rows * cols, width), key_grads, 0, 0)
    upstream = upstream_rows(grad_ref, turn_ref, rows, cols)
    feat_grad = rounded * (upstream.astype(F32) * grad_scale) + product(
        key_grads, key_ref[...], 1, 1
    ).reshape(rows, cols, width)
    gain = gain_ref[...]
    centred = (block_ref[0].astype(F32) - norm_ref[pl.ds(date, 1), :]) * norm_ref[
        pl.ds(dates + date, 1), :
    ]
    linear = centred * gain + shift_ref[...]
    part = sigmoid(linear)
    linear_grad = feat_grad * (part * (1.0 + linear * (1.0 - part)))
    first = column_sum(linear_grad)
    second = column_sum(linear_grad * centred)
    vector_ref[0:1] += second
    vector_ref[1:2] += first
    store_sums(sums_ref, date, dates, first * gain, second * gain)
    grad_out_ref[0] = (linear_grad * gain).astype(BF16)

    @pl.when(date == dates - 1)
    def _():
        devices, piece = part_ref.shape[0], part_ref.shape[2]
        for device in range(devices):
            part_ref[device] = attended[:, device * piece : (device + 1) * piece].astype(BF16)
        key_part = key_out_ref[...]
        place = lax.broadcasted_iota(jnp.int32, (width, width), 1) % (width // 16)
        both = pltpu.roll(key_part, width - 4, 1) + pltpu.roll(key_part, width - 5, 1)
        both = jnp.where(place == 0, both, 0.0)
        both = both + pltpu.roll(both, 1, 1)
        both = both + pltpu.roll(both, 2, 1)
        vector_ref[2:3] = 0.5 * jnp.sum(key_ref[...].astype(F32) * both, axis=0, keepdims=True)


def hidden_kernel(
    dates,
    norm_count,
    row_devs,
    edge_ref,
    grad_ref,
    block_ref,
    tails_ref,
    norm_ref,
    weight_ref,
    conv_ref,
    up_ref,
    down_ref,
    first_norm_ref,
    gain_ref,
    shift_ref,
    pre_ref,
    out_ref,
    vector_ref,
    sums_ref,
    table,
    factors,
    padded,
):
    date = pl.program_id(0)
    rows, cols, width = block_ref.shape[1:]

    @pl.when(date == 0)
    def _():
        tails = group_sum(jnp.sum(tails_ref[...], axis=0)) / norm_count
        mean, inverse = norm_ref[:dates], norm_ref[dates:]
        slope = -inverse * inverse * tails[dates:]
        factors[0:dates] = slope
        factors[dates : 2 * dates] = -inverse * tails[:dates] - mean * slope
        vector_ref[...] = jnp.zeros_like(vector_ref)
        padded[:2] = jnp.zeros_like(padded[:2])
        padded[rows + 2 :] = jnp.zeros_like(padded[rows + 2 :])
        for row_tap in range(3):
            for col_tap in range(3):
                table[
                    col_tap * width : (col_tap + 1) * width, row_tap * width : (row_tap + 1) * width
                ] = weight_ref[2 - row_tap, col_tap]

    inverse = norm_ref[pl.ds(dates + date, 1), :]
    slope = factors[pl.ds(date, 1), :]
    constant = factors[pl.ds(dates + date, 1), :]

    above_edge, below_edge = edges(edge_ref, row_devs)
    stored = (
        grad_ref[0].astype(F32) * inverse + (block_ref[0].astype(F32) * slope + constant)
    ).astype(BF16)
    pre_ref[0] = stored
    padded[2 : rows + 2] = stored
    reach = rows + 2
    taps = jnp.concatenate([padded[tap : tap + reach] for tap in range(3)], axis=-1).reshape(
        reach * cols, 3 * width
    )
    terms = product(taps, table[...], 1, 1).reshape(reach, cols, 3 * width)
    hidden_grad = (
        terms[..., width : 2 * width]
        + from_right(terms[..., :width])
        + from_left(terms[..., 2 * width :])
    )
    gain = gain_ref[...]
    conv = jnp.concatenate([up_ref[0][None], conv_ref[0], down_ref[0][None]], axis=0)
    centred = (conv.astype(F32) - first_norm_ref[pl.ds(date, 1), :]) * first_norm_ref[
        pl.ds(dates + date, 1), :
    ]
    linear = centred * gain + shift_ref[...]
    part = sigmoid(linear)
    linear_grad = hidden_grad * (part * (1.0 + linear * (1.0 - part)))
    linear_grad = jnp.concatenate(
        [
            linear_grad[:1] * above_edge,
            linear_grad[1 : rows + 1],
            linear_grad[rows + 1 :] * below_edge,
        ],
        axis=0,
    )
    out_ref[0] = linear_grad.astype(BF16)
    first = column_sum(linear_grad)
    second = column_sum(linear_grad * centred)
    vector_ref[0:1] += second
    vector_ref[1:2] += first
    store_sums(sums_ref, date, dates, first * gain, second * gain)


def block_grad_kernel(dates, hidden_ref, pre_ref, key_ref, out_ref, total):
    date = pl.program_id(0)
    rows, cols, width = pre_ref.shape[1:]

    @pl.when(date == 0)
    def _():
        total[...] = jnp.zeros_like(total)

    grads = pre_ref[0].astype(F32)
    grads = jnp.concatenate(
        [from_right(grads).astype(BF16), pre_ref[0], from_left(grads).astype(BF16)], axis=-1
    ).reshape(rows * cols, 3 * width)
    taps = jnp.concatenate(
        [hidden_ref[0, tap : tap + rows] for tap in range(3)], axis=-1
    ).reshape(rows * cols, 3 * width)
    total[...] += product(taps, grads, 0, 0)

    @pl.when(date == dates - 1)
    def _():
        for row_tap in range(3):
            for col_tap in range(3):
                base = (row_tap * 3 + col_tap) * width
                out_ref[base : base + width] = total[
                    row_tap * width : (row_tap + 1) * width, col_tap * width : (col_tap + 1) * width
                ].astype(BF16)
        key_part = key_ref[...]
        rest = key_part - key_part.astype(BF16).astype(F32)
        lanes = width // 16
        place = lax.broadcasted_iota(jnp.int32, key_part.shape, 1) % lanes
        rest = pltpu.roll(rest, lanes // 2, 1)
        key_rows = jnp.where(place < lanes // 2, key_part, rest).astype(BF16)
        out_ref[9 * width : 10 * width] = key_rows
        if out_ref.shape[0] > 10 * width:
            out_ref[10 * width :] = jnp.zeros_like(out_ref[10 * width :])


def conv_grad_kernel(
    dates,
    norm_count,
    img_ref,
    above_ref,
    high_ref,
    below_ref,
    conv_ref,
    grad_ref,
    tails_ref,
    norm_ref,
    gain_ref,
    vector_ref,
    other_ref,
    block_rows_ref,
    turn_ref,
    keep_ref,
    give_ref,
    factors,
    total,
    out_ref,
):
    date = pl.program_id(0)
    rows, cols, width = conv_ref.shape[1:]
    half = width // 2

    @pl.when(date == 0)
    def _():
        tails = group_sum(jnp.sum(tails_ref[...], axis=0)) / norm_count
        mean, inverse = norm_ref[:dates], norm_ref[dates:]
        slope = -inverse * inverse * tails[dates:]
        factors[0:dates] = slope
        factors[dates : 2 * dates] = -inverse * tails[:dates] - mean * slope
        total[...] = jnp.zeros_like(total)

    scale = norm_ref[pl.ds(dates + date, 1), :] * gain_ref[...]
    slope = factors[pl.ds(date, 1), :]
    constant = factors[pl.ds(dates + date, 1), :]
    own = conv_ref[0].astype(F32) * slope + constant
    scaled = grad_ref[0].astype(F32) * scale
    stored = jnp.concatenate(
        [scaled[:1], scaled[1 : rows + 1] + own, scaled[rows + 1 :]], axis=0
    ).astype(BF16)
    moved = from_right(stored.astype(F32)).astype(BF16)
    reach = rows + 2
    grads = jnp.concatenate([stored, moved], axis=-1).reshape(reach * cols, 2 * width)
    even, odd = img_ref[0, :, 0], img_ref[0, :, 1]
    above = above_ref[0][None]
    taps = [
        jnp.concatenate([high_ref[0, :1], above, odd], axis=0),
        jnp.concatenate([high_ref[0, 1:], even, below_ref[0, :1]], axis=0),
        jnp.concatenate([above, odd, below_ref[0, 1:]], axis=0),
    ]
    taps = jnp.concatenate(taps, axis=-1).reshape(reach * cols, 3 * width)
    total[...] += product(taps, grads, 0, 0)

    @pl.when(date == dates - 1)
    def _():
        begin = block_rows_ref.shape[0]
        out_ref[:begin] = block_rows_ref[...]
        for tap in range(3):
            base = tap * width
            pair = total[base : base + width, :width].astype(BF16)
            left = total[base + half : base + width, width:].astype(BF16)
            start = begin + tap * 3 * half
            out_ref[start : start + half] = left
            out_ref[start + half : start + 3 * half] = pair
        start = begin + 9 * half
        for source in (vector_ref, other_ref):
            high, low = split(source[...])
            out_ref[start : start + 16] = jnp.concatenate([high, low], axis=0)
            start += 16
        if out_ref.shape[0] > start:
            out_ref[start:] = jnp.zeros_like(out_ref[start:])
        half_rows = keep_ref.shape[0]
        core = turn_ref[0] % 2
        start = pl.multiple_of(core * half_rows, half_rows)
        keep_ref[...] = out_ref[pl.ds(start, half_rows), :]
        start = pl.multiple_of((1 - core) * half_rows, half_rows)
        give_ref[...] = out_ref[pl.ds(start, half_rows), :]


def total_kernel(in_ref, out_ref):
    total = jnp.sum(in_ref[...].astype(F32), axis=0).astype(BF16)
    for copy in range(out_ref.shape[0]):
        out_ref[copy] = total


def final_kernel(
    depth,
    turn_ref,
    own_ref,
    other_ref,
    conv_ref,
    block_ref,
    key_ref,
    query_ref,
    *refs,
):
    vector_refs, rows_ref = refs[:-1], refs[-1]
    half_rows = own_ref.shape[0]
    core = turn_ref[0] % 2
    rows_ref[pl.ds(pl.multiple_of(core * half_rows, half_rows), half_rows), :] = own_ref[...]
    start = pl.multiple_of((1 - core) * half_rows, half_rows)
    rows_ref[pl.ds(start, half_rows), :] = other_ref[...]
    conv_end, block_end, width = conv_ref.shape[0], block_ref.shape[0], block_ref.shape[1]
    block_ref[...] = rows_ref[:block_end].astype(F32)
    wide = key_ref.shape[0]
    heads = wide // depth
    lanes = width // heads
    row = lax.broadcasted_iota(jnp.int32, (wide, width), 0)
    lane = lax.broadcasted_iota(jnp.int32, (wide, width), 1)
    narrow = (row // depth == lane // lanes) & (row % depth == lane % depth)
    narrow = narrow.astype(F32).astype(BF16)
    key_ref[...] = product(narrow, rows_ref[block_end : block_end + width], 1, 1)
    start = block_end + width
    conv_ref[...] = rows_ref[start : start + conv_end].astype(F32)
    start += conv_end
    for index in range(2):
        both = rows_ref[start : start + 16].astype(F32)
        both = both[:8] + both[8:]
        vector_refs[2 * index][...] = both[0:1]
        vector_refs[2 * index + 1][...] = both[1:2]
        start += 16
    both = rows_ref[start - 16 : start]
    row = lax.broadcasted_iota(jnp.int32, (heads, width), 0)
    lane = lax.broadcasted_iota(jnp.int32, (heads, width), 1)
    inside = row == lane // lanes
    step = lax.broadcasted_iota(jnp.int32, (8, width), 0)
    place = lax.broadcasted_iota(jnp.int32, (8, width), 1) % lanes
    steps = step == place
    query = jnp.zeros((8, heads), F32)
    for index in (2, 10):
        picked = jnp.where(steps, both[index : index + 1].astype(F32), 0.0).astype(BF16)
        query = query + product(picked, inside.astype(F32).astype(BF16), 1, 1)
    query_ref[...] = query[:depth]


def per_date(shape):
    zeros = (0,) * (len(shape) - 1)
    return pl.BlockSpec((1,) + tuple(shape[1:]), lambda date: (date,) + zeros)


def streamed(kernel, dates, kinds, out_kinds, stream):
    loads = [place for place, kind in enumerate(kinds) if stream and kind != "scalar"]
    stores = [place for place, kind in enumerate(out_kinds) if kind == "direct"]

    def body(*refs):
        inputs, rest = list(refs[: len(kinds)]), refs[len(kinds) :]
        outputs, scratch = list(rest[: len(out_kinds)]), rest[len(out_kinds) :]
        loaded, scratch = scratch[: len(loads)], scratch[len(loads) :]
        stored, scratch = scratch[: len(stores)], scratch[len(stores) :]
        ready, done, scratch = scratch[0], scratch[1], scratch[2:]
        date = pl.program_id(0)
        views, results = list(inputs), list(outputs)

        def load(index, step):
            source, target = inputs[loads[index]], loaded[index]
            if kinds[loads[index]] == "date":
                source, target = source.at[step], target.at[step]
            return pltpu.make_async_copy(source, target, ready.at[index, step])

        def store(index, step):
            source, target = stored[index].at[step], outputs[stores[index]].at[step]
            return pltpu.make_async_copy(source, target, done.at[index, step])

        @pl.when(date == 0)
        def _():
            for step in range(dates):
                for index, place in enumerate(loads):
                    if step == 0 or kinds[place] == "date":
                        load(index, step).start()
            for index, place in enumerate(loads):
                if kinds[place] != "date":
                    load(index, 0).wait()

        for index, place in enumerate(loads):
            if kinds[place] == "date":
                load(index, date).wait()
                views[place] = loaded[index].at[pl.ds(date, 1)]
            else:
                views[place] = loaded[index]
        for index, place in enumerate(stores):
            results[place] = stored[index].at[pl.ds(date, 1)]
        kernel(*views, *results, *scratch)
        for index in range(len(stores)):
            store(index, date).start()

        @pl.when(date == dates - 1)
        def _():
            for step in range(dates):
                for index in range(len(stores)):
                    store(index, step).wait()

    return body


def whole(shape):
    zeros = (0,) * len(shape)
    return pl.BlockSpec(tuple(shape), lambda date: zeros)


def call(kernel, dates, inputs, outputs, scratch, flops, stream=False):
    in_specs, arrays, buffers = [], [], []
    for kind, array in inputs:
        large = array.size * array.dtype.itemsize >= MIB // 2
        if kind in ("far", "still") or (stream and kind == "date" and large):
            array = pltpu.with_memory_space_constraint(array, pltpu.HBM)
        arrays.append(array)
        if kind == "scalar":
            in_specs.append(pl.BlockSpec(memory_space=pltpu.SMEM))
        elif stream:
            in_specs.append(pl.BlockSpec(memory_space=pl.ANY))
            buffers.append(pltpu.VMEM(array.shape, array.dtype))
        else:
            in_specs.append((per_date if kind in ("date", "far") else whole)(array.shape))
    out_specs, out_shape = [], []
    for kind, shape, dtype in outputs:
        if kind == "direct":
            out_specs.append(pl.BlockSpec(memory_space=pltpu.HBM))
            buffers.append(pltpu.VMEM(shape, dtype))
        else:
            out_specs.append((per_date if kind == "date" else whole)(shape))
        pinned = kind == "direct" or (stream and kind == "date")
        out_shape.append((pltpu.HBM if pinned else jax.ShapeDtypeStruct)(shape, dtype))
    moved = sum(array.size * array.dtype.itemsize for _, array in inputs)
    if buffers:
        kinds, out_kinds = [kind for kind, _ in inputs], [kind for kind, _, _ in outputs]
        kernel = streamed(kernel, dates, kinds, out_kinds, stream)
        ready = pltpu.SemaphoreType.DMA((max(len(inputs), len(outputs)), dates))
        scratch = buffers + [ready, ready] + scratch
    return pl.pallas_call(
        kernel,
        grid=(dates,),
        in_specs=in_specs,
        out_specs=out_specs,
        out_shape=out_shape,
        scratch_shapes=scratch,
        compiler_params=pltpu.CompilerParams(vmem_limit_bytes=(40 if stream else 24) * MIB),
        cost_estimate=pl.CostEstimate(flops=flops, bytes_accessed=2 * moved, transcendentals=0),
    )(*arrays)


def shifted(array, by):
    devices = lax.axis_size("rows")
    pairs = [(i, i + by) for i in range(devices) if 0 <= i + by < devices]
    return lax.ppermute(array, "rows", pairs)


def turned(array):
    devices = lax.axis_size("dates")
    pieces = [array]
    for step in range(1, devices):
        pairs = [((i + step) % devices, i) for i in range(devices)]
        pieces.append(lax.ppermute(array, "dates", pairs))
    return jnp.stack(pieces)


def sum_of_parts(parts):
    devices = lax.axis_size("dates")
    place = lax.axis_index("dates")
    total = lax.dynamic_index_in_dim(parts, place, 0, keepdims=False).astype(F32)
    for step in range(1, devices):
        piece = lax.dynamic_index_in_dim(parts, (place + step) % devices, 0, keepdims=False)
        pairs = [(i, (i + step) % devices) for i in range(devices)]
        total = total + lax.ppermute(piece, "dates", pairs).astype(F32)
    return total.astype(BF16)


def exchange(pieces, axes):
    return lax.all_to_all(pieces, axes, split_axis=0, concat_axis=0, tiled=True)


def gather(array, axis):
    return lax.all_gather(array, axis, axis=0, tiled=True)


def other_core(array):
    devices = lax.axis_size("dates")
    return lax.ppermute(array, "dates", [(i, i + 1 - 2 * (i % 2)) for i in range(devices)])


def exchange_cores(pieces):
    axes = ("rows", "dates")
    devices = lax.axis_size(axes)
    groups = [list(range(core, devices, 2)) for core in range(2)]
    return lax.all_to_all(
        pieces, axes, split_axis=0, concat_axis=0, axis_index_groups=groups, tiled=True
    )


def scatter(rows_array):
    devices = lax.axis_size(("rows", "dates")) // 2
    count, width = rows_array.shape
    return exchange_cores(rows_array.reshape(devices, count // devices, width))


def collect(pieces):
    spread = pl.pallas_call(
        total_kernel,
        out_shape=jax.ShapeDtypeStruct(pieces.shape, BF16),
        compiler_params=pltpu.CompilerParams(vmem_limit_bytes=16 * MIB),
    )(pieces)
    count, rows, width = pieces.shape
    return exchange_cores(spread).reshape(count * rows, width)


def padded_count(count, devices):
    step = 8 * devices
    return -(-count // step) * step


def local(
    images,
    day_index,
    valid,
    out_grad,
    conv_weight,
    first_gain,
    first_shift,
    block_weight,
    gn_gain,
    gn_shift,
    key_weight,
    queries,
):
    dates, rows_here, cols, pair_width = images.shape
    width = conv_weight.shape[-1]
    row_devs, date_devs = lax.axis_size("rows"), lax.axis_size("dates")
    devices = row_devs * date_devs
    rows = rows_here // 2
    heads, depth = queries.shape
    norm_count = float(rows * row_devs * cols * (width // GROUPS))
    grad_scale = float(rows * row_devs * cols) ** (-0.5)
    date_start = lax.axis_index("dates") * dates
    frame = (dates, rows, cols, width)
    edge_rows = (dates, cols, width)
    flops = 2 * dates * rows * cols * width * width

    rows_of = lambda vector: vector.reshape(1, width)
    first_gain, first_shift = rows_of(first_gain), rows_of(first_shift)
    gn_gain, gn_shift = rows_of(gn_gain), rows_of(gn_shift)
    last = images[:, -1]
    above = shifted(last, 1)
    high, below, above = lax.optimization_barrier((images[:, -3:-1], images[:, :2], above))
    high, below = shifted(high, 1), shifted(below, -1)
    paired = images.reshape(dates, rows, 2, cols, pair_width)
    conv_out, sums = call(
        functools.partial(down_kernel, dates),
        dates,
        [("date", paired), ("date", above), ("still", conv_weight)],
        [("date", frame, BF16), ("all", (row_devs, 2 * dates, width), F32)],
        [pltpu.VMEM((3 * pair_width, 2 * width), BF16)],
        6 * flops,
        True,
    )
    stats = exchange(sums, "rows")
    high, below, last, _ = lax.optimization_barrier((high, below, last, sums))
    halo_up, halo_down = pl.pallas_call(
        edge_kernel,
        out_shape=[jax.ShapeDtypeStruct(edge_rows, BF16)] * 2,
        scratch_shapes=[pltpu.VMEM((3 * pair_width, 2 * width), BF16)],
        compiler_params=pltpu.CompilerParams(vmem_limit_bytes=16 * MIB),
    )(high, above, last, below, conv_weight)
    valid, out_grad, _ = lax.optimization_barrier((valid, out_grad, halo_up))
    grad_rows = out_grad.size // width
    valid_rows = valid.astype(BF16).reshape(valid.shape[0] * rows, -1)
    valid_rows = jnp.pad(valid_rows, ((0, 0), (0, width - valid_rows.shape[1])))
    packed = jnp.concatenate([out_grad.reshape(grad_rows, width), valid_rows])
    sources = turned(packed)
    clear = lax.dynamic_slice_in_dim(sources, grad_rows + date_start * rows, dates * rows, 1)
    clear = clear.astype(F32)
    days = lax.dynamic_slice_in_dim(day_index, date_start, dates, 0)
    turn = lax.axis_index("dates").reshape(1)
    place = lax.axis_index("rows").reshape(1)

    block_out, hidden, first_norm, sums = call(
        functools.partial(block_kernel, dates, norm_count, row_devs),
        dates,
        [
            ("scalar", place),
            ("date", conv_out),
            ("date", halo_up),
            ("date", halo_down),
            ("all", stats),
            ("all", first_gain),
            ("all", first_shift),
            ("still", block_weight),
        ],
        [
            ("date", frame, BF16),
            ("date", (dates, rows + 2, cols, width), BF16),
            ("all", (2 * dates, width), F32),
            ("all", (row_devs, 2 * dates, width), F32),
        ],
        [pltpu.VMEM((3 * width, 3 * width), BF16)],
        9 * flops,
        True,
    )
    stats = exchange(sums, "rows")
    features, exponent, attn, norm, packed, key_wide, query_wide = call(
        functools.partial(score_kernel, dates, norm_count, grad_scale),
        dates,
        [
            ("scalar", days),
            ("far", block_out),
            ("all", stats),
            ("all", gn_gain),
            ("all", gn_shift),
            ("all", sources),
            ("all", clear),
            ("scalar", turn),
            ("all", key_weight.T),
            ("all", queries.T),
        ],
        [
            ("date", frame, BF16),
            ("date", frame, F32),
            ("date", frame, F32),
            ("all", (2 * dates, width), F32),
            ("all", (1, 2, cols, width), F32),
            ("all", (width, width), BF16),
            ("all", (8, width), F32),
        ],
        [
            pltpu.VMEM(frame[1:], F32),
            pltpu.VMEM(frame[1:], F32),
            pltpu.VMEM((2 * width, width), BF16),
            pltpu.VMEM((width, 2 * width), BF16),
        ],
        5 * flops,
    )
    packed = gather(packed, "dates")
    block_grad, attended, key_part, vectors, sums = call(
        functools.partial(attend_kernel, dates, grad_scale),
        dates,
        [
            ("still", packed),
            ("date", features),
            ("date", exponent),
            ("date", attn),
            ("date", block_out),
            ("all", norm),
            ("all", gn_gain),
            ("all", gn_shift),
            ("all", query_wide),
            ("all", sources),
            ("scalar", turn),
            ("all", key_wide),
        ],
        [
            ("direct", frame, BF16),
            ("all", (date_devs, rows, cols // date_devs, width), BF16),
            ("all", (width, width), F32),
            ("all", (8, width), F32),
            ("all", (row_devs, 2 * dates, width), F32),
        ],
        [pltpu.VMEM(frame[1:], F32)] * 3,
        5 * flops,
    )
    tails = exchange(sums, "rows")
    pre_grad, linear_grad, first_vectors, sums = call(
        functools.partial(hidden_kernel, dates, norm_count, row_devs),
        dates,
        [
            ("scalar", place),
            ("date", block_grad),
            ("date", block_out),
            ("all", tails),
            ("all", norm),
            ("still", block_weight),
            ("date", conv_out),
            ("date", halo_up),
            ("date", halo_down),
            ("all", first_norm),
            ("all", first_gain),
            ("all", first_shift),
        ],
        [
            ("date", frame, BF16),
            ("date", (dates, rows + 2, cols, width), BF16),
            ("all", (8, width), F32),
            ("all", (row_devs, 2 * dates, width), F32),
        ],
        [
            pltpu.VMEM((3 * width, 3 * width), BF16),
            pltpu.VMEM((2 * dates, width), F32),
            pltpu.VMEM((rows + 4, cols, width), BF16),
        ],
        9 * flops,
        True,
    )
    tails = exchange(sums, "rows")
    (block_rows,) = call(
        functools.partial(block_grad_kernel, dates),
        dates,
        [("date", hidden), ("date", pre_grad), ("all", key_part)],
        [("all", (10 * width, width), BF16)],
        [pltpu.VMEM((3 * width, 3 * width), F32)],
        9 * flops,
        True,
    )
    tails, block_rows = lax.optimization_barrier((tails, block_rows))
    conv_count = 9 * pair_width // 2 + 32
    half_rows = padded_count(10 * width + conv_count, devices) // 2
    keep, give = call(
        functools.partial(conv_grad_kernel, dates, norm_count),
        dates,
        [
            ("date", paired),
            ("date", above),
            ("date", high),
            ("date", below),
            ("date", conv_out),
            ("date", linear_grad),
            ("all", tails),
            ("all", first_norm),
            ("all", first_gain),
            ("all", first_vectors),
            ("all", vectors),
            ("all", block_rows),
            ("scalar", turn),
        ],
        [("all", (half_rows, width), BF16)] * 2,
        [
            pltpu.VMEM((2 * dates, width), F32),
            pltpu.VMEM((3 * pair_width, 2 * width), F32),
            pltpu.VMEM((2 * half_rows, width), BF16),
        ],
        6 * flops,
        True,
    )
    rows_half = (keep.astype(F32) + other_core(give).astype(F32)).astype(BF16)
    pieces = scatter(rows_half)
    attended, _ = lax.optimization_barrier((attended, rows_half))
    attended = sum_of_parts(attended)
    rows_half = collect(pieces)
    rows_other = other_core(rows_half)
    shapes = [
        (9 * pair_width // 2, width),
        (9 * width, width),
        (heads * depth, width),
        (depth, heads),
    ] + [(1, width)] * 4
    conv_total, block_total, key_total, query_total, *totals = pl.pallas_call(
        functools.partial(final_kernel, depth),
        in_specs=[
            pl.BlockSpec(memory_space=pltpu.SMEM),
            pl.BlockSpec(memory_space=pltpu.VMEM),
            pl.BlockSpec(memory_space=pltpu.VMEM),
        ],
        out_shape=[jax.ShapeDtypeStruct(shape, F32) for shape in shapes],
        scratch_shapes=[pltpu.VMEM((2 * half_rows, width), BF16)],
        compiler_params=pltpu.CompilerParams(vmem_limit_bytes=16 * MIB),
    )(turn, rows_half, rows_other)
    totals = [total.reshape(width) for total in totals]
    return (
        attended,
        conv_total.reshape(conv_weight.shape),
        totals[0],
        totals[1],
        block_total.reshape(block_weight.shape),
        totals[2],
        totals[3],
        key_total.T,
        query_total.T,
    )


def solution(mesh):
    return jax.shard_map(
        local,
        mesh=mesh,
        in_specs=(
            P("dates", "rows", None, None),
            P(),
            P(None, "rows", "dates"),
            P("rows", "dates", None),
            P(),
            P(),
            P(),
            P(),
            P(),
            P(),
            P(),
            P(),
        ),
        out_specs=(P("rows", "dates", None), P(), P(), P(), P(), P(), P(), P(), P()),
        check_vma=False,
    )
```

```python
import functools
import math

import jax
import jax.numpy as jnp
from jax import lax
from jax.experimental import pallas as pl
from jax.experimental.pallas import tpu as pltpu
from jax.sharding import PartitionSpec as P

GROUPS = 4


EPS = 1e-05


MIB = 1 << 20


F32 = jnp.float32


BF16 = jnp.bfloat16


def product(left, right, left_dim, right_dim):
    return lax.dot_general(
        left, right, (((left_dim,), (right_dim,)), ((), ())), preferred_element_type=F32
    )


def group_sum(values):
    width = values.shape[-1]
    lane_group = lax.broadcasted_iota(jnp.int32, values.shape, 1) // (width // GROUPS)
    spread = jnp.zeros_like(values)
    for group in range(GROUPS):
        inside = lane_group == group
        total = jnp.sum(jnp.where(inside, values, 0.0), axis=1, keepdims=True)
        spread = spread + jnp.where(inside, total, 0.0)
    return spread


def sigmoid(values):
    return 0.5 * jnp.tanh(0.5 * values) + 0.5


def from_left(values):
    column = lax.broadcasted_iota(jnp.int32, values.shape, 1)
    return jnp.where(column > 0, pltpu.roll(values, 1, 1), 0.0)


def from_right(values):
    count = values.shape[1]
    column = lax.broadcasted_iota(jnp.int32, values.shape, 1)
    return jnp.where(column < count - 1, pltpu.roll(values, count - 1, 1), 0.0)


def column_sum(values):
    return jnp.sum(jnp.sum(values, axis=0), axis=0, keepdims=True)


def edges(place_ref, row_devs):
    place = place_ref[0]
    return (place > 0).astype(F32), (place < row_devs - 1).astype(F32)


def head_spread(width):
    lane = lax.broadcasted_iota(jnp.int32, (2 * width, width), 1) // (width // 16)
    head = lax.broadcasted_iota(jnp.int32, (2 * width, width), 0) % width // (width // 16)
    return (lane == head).astype(F32).astype(BF16)


def split(values):
    high = values.astype(BF16)
    return high, (values - high.astype(F32)).astype(BF16)


def store_sums(sums_ref, date, dates, first, second):
    for copy in range(sums_ref.shape[0]):
        sums_ref[copy, pl.ds(date, 1), :] = first
        sums_ref[copy, pl.ds(dates + date, 1), :] = second


def norm_table(sums_ref, table_ref, dates, norm_count):
    means = group_sum(jnp.sum(sums_ref[...], axis=0)) / norm_count
    mean = means[:dates]
    table_ref[:dates] = mean
    table_ref[dates:] = 1.0 / jnp.sqrt(means[dates:] - mean * mean + EPS)


def down_table(weight_ref, table):
    half = weight_ref.shape[2]
    for tap in range(3):
        base = tap * 2 * half
        table[base : base + half, : 2 * half] = weight_ref[tap, 1]
        table[base + half : base + 2 * half, : 2 * half] = weight_ref[tap, 2]
        table[base : base + half, 2 * half :] = jnp.zeros_like(weight_ref[tap, 0])
        table[base + half : base + 2 * half, 2 * half :] = weight_ref[tap, 0]


def down_rows(taps, table):
    rows, cols, width = taps[0].shape
    taps = jnp.concatenate(taps, axis=-1).reshape(rows * cols, 3 * width)
    both = product(taps, table[...], 1, 0).reshape(rows, cols, 2 * width)
    return (both[..., :width] + from_left(both[..., width:])).astype(BF16)


def down_kernel(
    date, dates, img_ref, above_ref, weight_ref, out_ref, sums_ref, table
):

    if date == 0:
        down_table(weight_ref, table)

    even, odd = img_ref[0, :, 0], img_ref[0, :, 1]
    above = jnp.concatenate([above_ref[0][None], odd[:-1]], axis=0)
    stored = down_rows([above, even, odd], table)
    out_ref[0] = stored
    values = stored.astype(F32)
    store_sums(sums_ref, date, dates, column_sum(values), column_sum(values * values))


def edge_kernel(
    step, steps, high_ref, above_ref, last_ref, below_ref, weight_ref, up_ref, down_ref, table
):
    dates = above_ref.shape[0]
    down_table(weight_ref, table)
    taps = [
        jnp.concatenate([high_ref[:, 0], last_ref[...]], axis=0),
        jnp.concatenate([high_ref[:, 1], below_ref[:, 0]], axis=0),
        jnp.concatenate([above_ref[...], below_ref[:, 1]], axis=0),
    ]
    stored = down_rows(taps, table)
    up_ref[...] = stored[:dates]
    down_ref[...] = stored[dates:]


def block_kernel(
    date,
    dates,
    edge_ref,
    conv_ref,
    up_ref,
    down_ref,
    stats_ref,
    gain_ref,
    shift_ref,
    weight_ref,
    out_ref,
    hidden_ref,
    norm_ref,
    sums_ref,
    table,
    *,
    norm_count,
    row_devs,
):
    width = conv_ref.shape[-1]

    if date == 0:
        norm_table(stats_ref, norm_ref, dates, norm_count)
        for row_tap in range(3):
            for col_tap in range(3):
                table[
                    row_tap * width : (row_tap + 1) * width, col_tap * width : (col_tap + 1) * width
                ] = weight_ref[row_tap, col_tap]

    scale = norm_ref[pl.ds(dates + date, 1), :] * gain_ref[...]
    shift = shift_ref[...] - norm_ref[pl.ds(date, 1), :] * scale

    def activate(values):
        linear = values.astype(F32) * scale + shift
        return linear * sigmoid(linear)

    rows, cols = conv_ref.shape[1:3]
    above_edge, below_edge = edges(edge_ref, row_devs)
    hidden_ref[0, 0] = (activate(up_ref[0]) * above_edge).astype(BF16)
    hidden_ref[0, rows + 1] = (activate(down_ref[0]) * below_edge).astype(BF16)
    hidden_ref[0, 1 : rows + 1] = activate(conv_ref[0]).astype(BF16)
    taps = jnp.concatenate(
        [hidden_ref[0, tap : tap + rows] for tap in range(3)], axis=-1
    ).reshape(rows * cols, 3 * width)
    terms = product(taps, table[...], 1, 0).reshape(rows, cols, 3 * width)
    stored = (
        terms[..., width : 2 * width]
        + from_left(terms[..., :width])
        + from_right(terms[..., 2 * width :])
    ).astype(BF16)
    out_ref[0] = stored
    values = stored.astype(F32)
    store_sums(sums_ref, date, dates, column_sum(values), column_sum(values * values))


def encoding(day, width):
    lane = lax.broadcasted_iota(jnp.int32, (1, width), 1)
    frequency = jnp.exp((lane // 2).astype(F32) * (-2.0 * math.log(1000.0) / width))
    angles = day.astype(F32) * frequency
    return jnp.where(lane % 2 == 0, jnp.sin(angles), jnp.cos(angles))


def fold_keys(key_ref, query_ref, wide_ref, vector_ref, spread_ref, score_ref):
    depth, heads = query_ref.shape
    width = key_ref.shape[1]
    lanes = width // heads
    spread_ref[...] = head_spread(width)
    row = lax.broadcasted_iota(jnp.int32, (heads * depth, width), 0)
    lane = lax.broadcasted_iota(jnp.int32, (heads * depth, width), 1)
    widen = (row // depth == lane // lanes) & (row % depth == lane % lanes)
    wide = product(key_ref[...], widen.astype(F32).astype(BF16), 0, 0)
    wide_ref[...] = wide.astype(BF16)
    head = lax.broadcasted_iota(jnp.int32, (heads, width), 0)
    lane = lax.broadcasted_iota(jnp.int32, (heads, width), 1)
    inside = (lane // lanes == head).astype(F32).astype(BF16)
    high, low = split(query_ref[...])
    lower = (query_ref[...] - high.astype(F32) - low.astype(F32)).astype(BF16)
    spread = sum(product(part, inside, 1, 0) for part in (high, low, lower))
    step = lax.broadcasted_iota(jnp.int32, (depth, width), 0)
    place = lax.broadcasted_iota(jnp.int32, (depth, width), 1) % lanes
    queries = jnp.sum(jnp.where(step == place, spread * depth**-0.5, 0.0), axis=0, keepdims=True)
    place = lax.broadcasted_iota(jnp.int32, (1, width), 1) % lanes
    queries = queries + jnp.where((place == depth) | (place == depth + 1), 1.0, 0.0)
    vector_ref[...] = jnp.broadcast_to(queries, vector_ref.shape)
    folded = jnp.concatenate(split(wide * queries), axis=-1)
    folded = product(folded, spread_ref[...], 1, 0)
    score_ref[...] = jnp.concatenate(split(folded), axis=-1)


def source_of(turn_ref, device, devices):
    return (device + devices - turn_ref[0]) % devices


def upstream_rows(grad_ref, turn_ref, rows, cols):
    devices = grad_ref.shape[0]
    piece = cols // devices
    parts = [
        grad_ref[source_of(turn_ref, device, devices), : rows * piece].reshape(rows, piece, -1)
        for device in range(devices)
    ]
    return jnp.concatenate(parts, axis=1)


def score_kernel(
    date,
    dates,
    day_ref,
    block_ref,
    stats_ref,
    gain_ref,
    shift_ref,
    grad_ref,
    valid_ref,
    turn_ref,
    key_ref,
    query_ref,
    feat_ref,
    exp_ref,
    attn_ref,
    norm_ref,
    packed_ref,
    wide_ref,
    vector_ref,
    total,
    mean,
    spread_ref,
    score_ref,
    *,
    norm_count,
    grad_scale,
):
    rows, cols, width = block_ref.shape[1:]

    if date == 0:
        norm_table(stats_ref, norm_ref, dates, norm_count)
        fold_keys(key_ref, query_ref, wide_ref, vector_ref, spread_ref, score_ref)
        total[...] = jnp.zeros_like(total)
        mean[...] = jnp.zeros_like(mean)

    scale = norm_ref[pl.ds(dates + date, 1), :] * gain_ref[...]
    shift = shift_ref[...] - norm_ref[pl.ds(date, 1), :] * scale
    linear = block_ref[0].astype(F32) * scale + shift
    features = (linear * sigmoid(linear) + encoding(day_ref[turn_ref[0] * dates + date], width)).astype(BF16)
    feat_ref[0] = features
    upstream = upstream_rows(grad_ref, turn_ref, rows, cols)
    parts = split(upstream.astype(F32) * features.astype(F32))
    parts = jnp.concatenate(parts, axis=-1).reshape(rows * cols, 2 * width)
    attn = product(parts, spread_ref[...], 1, 0).reshape(rows, cols, width) * grad_scale
    both = product(features.reshape(rows * cols, width), score_ref[...], 1, 0)
    scores = (both[:, :width] + both[:, width:]).reshape(rows, cols, width)
    devices = grad_ref.shape[0]
    valid = jnp.zeros((rows, width), F32)
    for device in range(devices):
        piece = valid_ref[
            source_of(turn_ref, device, devices), pl.ds(date * rows, rows), :
        ]
        valid = valid + pltpu.roll(piece, device * (cols // devices), 1)
    diagonal = lax.broadcasted_iota(jnp.int32, (cols, cols), 0) == lax.broadcasted_iota(
        jnp.int32, (cols, cols), 1
    )
    ones = jnp.ones((cols, width), BF16)
    clear = jnp.concatenate(
        [jnp.where(diagonal, valid[row : row + 1], 0.0) for row in range(rows)], axis=0
    ).astype(BF16)
    clear = product(clear, ones, 1, 0).reshape(rows, cols, width)
    exponent = clear * jnp.exp(scores)
    running = total[...] + exponent
    share = jnp.where(running > 0.0, exponent / running, 0.0)
    total[...] = running
    mean[...] += share * (attn - mean[...])
    exp_ref[0] = exponent
    attn_ref[0] = attn

    if date == dates - 1:
        place = lax.broadcasted_iota(jnp.int32, (cols, width), 1) % rows
        for index, source in enumerate((total, mean)):
            dense = jnp.zeros((cols, width), F32)
            for row in range(rows):
                dense = dense + jnp.where(place == row, source[row], 0.0)
            for copy in range(packed_ref.shape[0]):
                packed_ref[copy, index] = dense


def attend_kernel(
    date,
    dates,
    packed_ref,
    feat_ref,
    exp_ref,
    attn_ref,
    block_ref,
    norm_ref,
    gain_ref,
    shift_ref,
    query_ref,
    grad_ref,
    turn_ref,
    key_ref,
    grad_out_ref,
    part_ref,
    key_out_ref,
    vector_ref,
    sums_ref,
    inverse,
    average,
    attended,
    *,
    grad_scale,
):
    rows, cols, width = block_ref.shape[1:]

    if date == 0:
        denominator = jnp.sum(packed_ref[:, 0], axis=0)
        reciprocal = 1.0 / denominator
        mean = jnp.sum(packed_ref[:, 0] * reciprocal * packed_ref[:, 1], axis=0)
        place = lax.broadcasted_iota(jnp.int32, (cols, width), 1) % rows
        for values, target in ((reciprocal, inverse), (mean, average)):
            parts = jnp.concatenate(split(values), axis=-1)
            wide_place = jnp.concatenate([place, place], axis=-1)
            picked = jnp.concatenate(
                [jnp.where(wide_place == row, parts, jnp.zeros_like(parts)) for row in range(rows)], axis=0
            )
            target[...] = product(picked, head_spread(width), 1, 0).reshape(rows, cols, width)
        attended[...] = jnp.zeros_like(attended)
        key_out_ref[...] = jnp.zeros_like(key_out_ref)
        vector_ref[...] = jnp.zeros_like(vector_ref)

    features = feat_ref[0]
    weights = exp_ref[0] * inverse[...]
    rounded = weights.astype(BF16).astype(F32)
    attended[...] += rounded * features.astype(F32)
    score_grad = weights * (attn_ref[0] - average[...])
    spread_grad = score_grad * query_ref[0:1]
    rest = spread_grad - spread_grad.astype(BF16).astype(F32)
    lane = lax.broadcasted_iota(jnp.int32, spread_grad.shape, 2) % (width // 16)
    key_grads = jnp.where(lane == 5, rest, spread_grad).astype(BF16).reshape(rows * cols, width)
    key_out_ref[...] += product(features.reshape(rows * cols, width), key_grads, 0, 0)
    upstream = upstream_rows(grad_ref, turn_ref, rows, cols)
    feat_grad = rounded * (upstream.astype(F32) * grad_scale) + product(
        key_grads, key_ref[...], 1, 1
    ).reshape(rows, cols, width)
    gain = gain_ref[...]
    centred = (block_ref[0].astype(F32) - norm_ref[pl.ds(date, 1), :]) * norm_ref[
        pl.ds(dates + date, 1), :
    ]
    linear = centred * gain + shift_ref[...]
    part = sigmoid(linear)
    linear_grad = feat_grad * (part * (1.0 + linear * (1.0 - part)))
    first = column_sum(linear_grad)
    second = column_sum(linear_grad * centred)
    vector_ref[0:1] += second
    vector_ref[1:2] += first
    store_sums(sums_ref, date, dates, first * gain, second * gain)
    grad_out_ref[0] = (linear_grad * gain).astype(BF16)

    if date == dates - 1:
        devices, piece = part_ref.shape[0], part_ref.shape[2]
        for device in range(devices):
            part_ref[device] = attended[:, device * piece : (device + 1) * piece].astype(BF16)
        key_part = key_out_ref[...]
        place = lax.broadcasted_iota(jnp.int32, (width, width), 1) % (width // 16)
        both = pltpu.roll(key_part, width - 4, 1) + pltpu.roll(key_part, width - 5, 1)
        both = jnp.where(place == 0, both, 0.0)
        both = both + pltpu.roll(both, 1, 1)
        both = both + pltpu.roll(both, 2, 1)
        vector_ref[2:3] = 0.5 * jnp.sum(key_ref[...].astype(F32) * both, axis=0, keepdims=True)


def hidden_kernel(
    date,
    dates,
    edge_ref,
    grad_ref,
    block_ref,
    tails_ref,
    norm_ref,
    weight_ref,
    conv_ref,
    up_ref,
    down_ref,
    first_norm_ref,
    gain_ref,
    shift_ref,
    pre_ref,
    out_ref,
    vector_ref,
    sums_ref,
    table,
    factors,
    padded,
    *,
    norm_count,
    row_devs,
):
    rows, cols, width = block_ref.shape[1:]

    if date == 0:
        tails = group_sum(jnp.sum(tails_ref[...], axis=0)) / norm_count
        mean, inverse = norm_ref[:dates], norm_ref[dates:]
        slope = -inverse * inverse * tails[dates:]
        factors[0:dates] = slope
        factors[dates : 2 * dates] = -inverse * tails[:dates] - mean * slope
        vector_ref[...] = jnp.zeros_like(vector_ref)
        padded[:2] = jnp.zeros_like(padded[:2])
        padded[rows + 2 :] = jnp.zeros_like(padded[rows + 2 :])
        for row_tap in range(3):
            for col_tap in range(3):
                table[
                    col_tap * width : (col_tap + 1) * width, row_tap * width : (row_tap + 1) * width
                ] = weight_ref[2 - row_tap, col_tap]

    inverse = norm_ref[pl.ds(dates + date, 1), :]
    slope = factors[pl.ds(date, 1), :]
    constant = factors[pl.ds(dates + date, 1), :]

    above_edge, below_edge = edges(edge_ref, row_devs)
    stored = (
        grad_ref[0].astype(F32) * inverse + (block_ref[0].astype(F32) * slope + constant)
    ).astype(BF16)
    pre_ref[0] = stored
    padded[2 : rows + 2] = stored
    reach = rows + 2
    taps = jnp.concatenate([padded[tap : tap + reach] for tap in range(3)], axis=-1).reshape(
        reach * cols, 3 * width
    )
    terms = product(taps, table[...], 1, 1).reshape(reach, cols, 3 * width)
    hidden_grad = (
        terms[..., width : 2 * width]
        + from_right(terms[..., :width])
        + from_left(terms[..., 2 * width :])
    )
    gain = gain_ref[...]
    conv = jnp.concatenate([up_ref[0][None], conv_ref[0], down_ref[0][None]], axis=0)
    centred = (conv.astype(F32) - first_norm_ref[pl.ds(date, 1), :]) * first_norm_ref[
        pl.ds(dates + date, 1), :
    ]
    linear = centred * gain + shift_ref[...]
    part = sigmoid(linear)
    linear_grad = hidden_grad * (part * (1.0 + linear * (1.0 - part)))
    linear_grad = jnp.concatenate(
        [
            linear_grad[:1] * above_edge,
            linear_grad[1 : rows + 1],
            linear_grad[rows + 1 :] * below_edge,
        ],
        axis=0,
    )
    out_ref[0] = linear_grad.astype(BF16)
    first = column_sum(linear_grad)
    second = column_sum(linear_grad * centred)
    vector_ref[0:1] += second
    vector_ref[1:2] += first
    store_sums(sums_ref, date, dates, first * gain, second * gain)


def block_grad_kernel(
    date, dates, hidden_ref, pre_ref, key_ref, out_ref, total
):
    rows, cols, width = pre_ref.shape[1:]

    if date == 0:
        total[...] = jnp.zeros_like(total)

    grads = pre_ref[0].astype(F32)
    grads = jnp.concatenate(
        [from_right(grads).astype(BF16), pre_ref[0], from_left(grads).astype(BF16)], axis=-1
    ).reshape(rows * cols, 3 * width)
    taps = jnp.concatenate(
        [hidden_ref[0, tap : tap + rows] for tap in range(3)], axis=-1
    ).reshape(rows * cols, 3 * width)
    total[...] += product(taps, grads, 0, 0)

    if date == dates - 1:
        for row_tap in range(3):
            for col_tap in range(3):
                base = (row_tap * 3 + col_tap) * width
                out_ref[base : base + width] = total[
                    row_tap * width : (row_tap + 1) * width, col_tap * width : (col_tap + 1) * width
                ].astype(BF16)
        key_part = key_ref[...]
        rest = key_part - key_part.astype(BF16).astype(F32)
        lanes = width // 16
        place = lax.broadcasted_iota(jnp.int32, key_part.shape, 1) % lanes
        rest = pltpu.roll(rest, lanes // 2, 1)
        key_rows = jnp.where(place < lanes // 2, key_part, rest).astype(BF16)
        out_ref[9 * width : 10 * width] = key_rows
        if out_ref.shape[0] > 10 * width:
            out_ref[10 * width :] = jnp.zeros_like(out_ref[10 * width :])


def conv_grad_kernel(
    date,
    dates,
    img_ref,
    above_ref,
    high_ref,
    below_ref,
    conv_ref,
    grad_ref,
    tails_ref,
    norm_ref,
    gain_ref,
    vector_ref,
    other_ref,
    block_rows_ref,
    turn_ref,
    keep_ref,
    give_ref,
    factors,
    total,
    out_ref,
    *,
    norm_count,
):
    rows, cols, width = conv_ref.shape[1:]
    half = width // 2

    if date == 0:
        tails = group_sum(jnp.sum(tails_ref[...], axis=0)) / norm_count
        mean, inverse = norm_ref[:dates], norm_ref[dates:]
        slope = -inverse * inverse * tails[dates:]
        factors[0:dates] = slope
        factors[dates : 2 * dates] = -inverse * tails[:dates] - mean * slope
        total[...] = jnp.zeros_like(total)

    scale = norm_ref[pl.ds(dates + date, 1), :] * gain_ref[...]
    slope = factors[pl.ds(date, 1), :]
    constant = factors[pl.ds(dates + date, 1), :]
    own = conv_ref[0].astype(F32) * slope + constant
    scaled = grad_ref[0].astype(F32) * scale
    stored = jnp.concatenate(
        [scaled[:1], scaled[1 : rows + 1] + own, scaled[rows + 1 :]], axis=0
    ).astype(BF16)
    moved = from_right(stored.astype(F32)).astype(BF16)
    reach = rows + 2
    grads = jnp.concatenate([stored, moved], axis=-1).reshape(reach * cols, 2 * width)
    even, odd = img_ref[0, :, 0], img_ref[0, :, 1]
    above = above_ref[0][None]
    taps = [
        jnp.concatenate([high_ref[0, :1], above, odd], axis=0),
        jnp.concatenate([high_ref[0, 1:], even, below_ref[0, :1]], axis=0),
        jnp.concatenate([above, odd, below_ref[0, 1:]], axis=0),
    ]
    taps = jnp.concatenate(taps, axis=-1).reshape(reach * cols, 3 * width)
    total[...] += product(taps, grads, 0, 0)

    if date == dates - 1:
        begin = block_rows_ref.shape[0]
        out_ref[:begin] = block_rows_ref[...]
        for tap in range(3):
            base = tap * width
            pair = total[base : base + width, :width].astype(BF16)
            left = total[base + half : base + width, width:].astype(BF16)
            start = begin + tap * 3 * half
            out_ref[start : start + half] = left
            out_ref[start + half : start + 3 * half] = pair
        start = begin + 9 * half
        for source in (vector_ref, other_ref):
            high, low = split(source[...])
            out_ref[start : start + 16] = jnp.concatenate([high, low], axis=0)
            start += 16
        if out_ref.shape[0] > start:
            out_ref[start:] = jnp.zeros_like(out_ref[start:])
        half_rows = keep_ref.shape[0]
        core = turn_ref[0] % 2
        start = pl.multiple_of(core * half_rows, half_rows)
        keep_ref[...] = out_ref[pl.ds(start, half_rows), :]
        start = pl.multiple_of((1 - core) * half_rows, half_rows)
        give_ref[...] = out_ref[pl.ds(start, half_rows), :]


def total_kernel(in_ref, out_ref):
    total = jnp.sum(in_ref[...].astype(F32), axis=0).astype(BF16)
    for copy in range(out_ref.shape[0]):
        out_ref[copy] = total


def final_kernel(
    depth,
    turn_ref,
    own_ref,
    other_ref,
    conv_ref,
    block_ref,
    key_ref,
    query_ref,
    *refs,
):
    vector_refs, rows_ref = refs[:-1], refs[-1]
    half_rows = own_ref.shape[0]
    core = turn_ref[0] % 2
    rows_ref[pl.ds(pl.multiple_of(core * half_rows, half_rows), half_rows), :] = own_ref[...]
    start = pl.multiple_of((1 - core) * half_rows, half_rows)
    rows_ref[pl.ds(start, half_rows), :] = other_ref[...]
    conv_end, block_end, width = conv_ref.shape[0], block_ref.shape[0], block_ref.shape[1]
    block_ref[...] = rows_ref[:block_end].astype(F32)
    wide = key_ref.shape[0]
    heads = wide // depth
    lanes = width // heads
    row = lax.broadcasted_iota(jnp.int32, (wide, width), 0)
    lane = lax.broadcasted_iota(jnp.int32, (wide, width), 1)
    narrow = (row // depth == lane // lanes) & (row % depth == lane % depth)
    narrow = narrow.astype(F32).astype(BF16)
    key_ref[...] = product(narrow, rows_ref[block_end : block_end + width], 1, 1)
    start = block_end + width
    conv_ref[...] = rows_ref[start : start + conv_end].astype(F32)
    start += conv_end
    for index in range(2):
        both = rows_ref[start : start + 16].astype(F32)
        both = both[:8] + both[8:]
        vector_refs[2 * index][...] = both[0:1]
        vector_refs[2 * index + 1][...] = both[1:2]
        start += 16
    both = rows_ref[start - 16 : start]
    row = lax.broadcasted_iota(jnp.int32, (heads, width), 0)
    lane = lax.broadcasted_iota(jnp.int32, (heads, width), 1)
    inside = row == lane // lanes
    step = lax.broadcasted_iota(jnp.int32, (8, width), 0)
    place = lax.broadcasted_iota(jnp.int32, (8, width), 1) % lanes
    steps = step == place
    query = jnp.zeros((8, heads), F32)
    for index in (2, 10):
        picked = jnp.where(steps, both[index : index + 1].astype(F32), 0.0).astype(BF16)
        query = query + product(picked, inside.astype(F32).astype(BF16), 1, 1)
    query_ref[...] = query[:depth]


def call(kernel, dates, inputs, outputs, scratch, flops):
    in_specs, out_specs, arrays, out_shape, buffers = [], [], [], [], []
    in_vmem, in_hbm = pl.BlockSpec(memory_space=pltpu.VMEM), pl.BlockSpec(memory_space=pltpu.HBM)
    loads, stores = [], []
    for place, (kind, array) in enumerate(inputs):
        if kind == "scalar":
            in_specs.append(pl.BlockSpec(memory_space=pltpu.SMEM))
        elif "far" in kind:
            array = pltpu.with_memory_space_constraint(array, pltpu.HBM)
            in_specs.append(in_hbm)
            loads.append(place)
            buffers.append(pltpu.VMEM(array.shape, array.dtype))
        else:
            in_specs.append(in_vmem)
        arrays.append(array)
    for place, (kind, shape, dtype) in enumerate(outputs):
        if "far" in kind:
            out_shape.append(pltpu.HBM(shape, dtype))
            out_specs.append(in_hbm)
            stores.append(place)
            buffers.append(pltpu.VMEM(shape, dtype))
        else:
            out_shape.append(jax.ShapeDtypeStruct(shape, dtype))
            out_specs.append(in_vmem)
    copies = len(loads) + len(stores)

    def body(*refs):
        views, rest = list(refs[: len(inputs)]), refs[len(inputs) :]
        results, rest = list(rest[: len(outputs)]), rest[len(outputs) :]
        buffer_refs, rest = rest[:copies], rest[copies:]
        started = []
        for index, place in enumerate(loads):
            started.append(
                pltpu.make_async_copy(views[place], buffer_refs[index], rest[0].at[index])
            )
            started[-1].start()
            views[place] = buffer_refs[index]
        sent = []
        for index, place in enumerate(stores):
            buffer = buffer_refs[len(loads) + index]
            sent.append(
                pltpu.make_async_copy(buffer, results[place], rest[0].at[len(loads) + index])
            )
            results[place] = buffer
        for copy in started:
            copy.wait()
        for date in range(dates):
            ins = [
                view.at[pl.ds(date, 1)] if "date" in kind else view
                for view, (kind, _) in zip(views, inputs)
            ]
            outs = [
                result.at[pl.ds(date, 1)] if "date" in kind else result
                for result, (kind, _, _) in zip(results, outputs)
            ]
            kernel(date, dates, *ins, *outs, *rest[1:])
        for copy in sent:
            copy.start()
        for copy in sent:
            copy.wait()

    moved = sum(array.size * array.dtype.itemsize for _, array in inputs)
    return pl.pallas_call(
        body,
        in_specs=in_specs,
        out_specs=out_specs,
        out_shape=out_shape,
        scratch_shapes=buffers + [pltpu.SemaphoreType.DMA((max(copies, 1),))] + scratch,
        compiler_params=pltpu.CompilerParams(vmem_limit_bytes=40 * MIB),
        cost_estimate=pl.CostEstimate(flops=flops, bytes_accessed=2 * moved, transcendentals=0),
    )(*arrays)


def shifted(array, by):
    devices = lax.axis_size("rows")
    pairs = [(i, i + by) for i in range(devices) if 0 <= i + by < devices]
    return lax.ppermute(array, "rows", pairs)


def turned(array):
    devices = lax.axis_size("dates")
    pieces = [array]
    for step in range(1, devices):
        pairs = [((i + step) % devices, i) for i in range(devices)]
        pieces.append(lax.ppermute(array, "dates", pairs))
    return jnp.stack(pieces)


def row_totals(sums):
    devices = lax.axis_size("rows")
    step = 1
    while step < devices:
        pairs = [(i, i ^ step) for i in range(devices)]
        sums = sums + lax.ppermute(sums, "rows", pairs)
        step *= 2
    return sums


def sum_of_parts(parts):
    devices = lax.axis_size("dates")
    place = lax.axis_index("dates")
    total = lax.dynamic_index_in_dim(parts, place, 0, keepdims=False).astype(F32)
    for step in range(1, devices):
        piece = lax.dynamic_index_in_dim(parts, (place + step) % devices, 0, keepdims=False)
        pairs = [(i, (i + step) % devices) for i in range(devices)]
        total = total + lax.ppermute(piece, "dates", pairs).astype(F32)
    return total.astype(BF16)


def exchange(pieces, axes):
    return lax.all_to_all(pieces, axes, split_axis=0, concat_axis=0, tiled=True)


def gather(array, axis):
    return lax.all_gather(array, axis, axis=0, tiled=True)


def other_core(array):
    devices = lax.axis_size("dates")
    return lax.ppermute(array, "dates", [(i, i + 1 - 2 * (i % 2)) for i in range(devices)])


def exchange_cores(pieces):
    axes = ("rows", "dates")
    devices = lax.axis_size(axes)
    groups = [list(range(core, devices, 2)) for core in range(2)]
    return lax.all_to_all(
        pieces, axes, split_axis=0, concat_axis=0, axis_index_groups=groups, tiled=True
    )


def scatter(rows_array):
    devices = lax.axis_size(("rows", "dates")) // 2
    count, width = rows_array.shape
    return exchange_cores(rows_array.reshape(devices, count // devices, width))


def collect(pieces):
    spread = pl.pallas_call(
        total_kernel,
        out_shape=jax.ShapeDtypeStruct(pieces.shape, BF16),
        compiler_params=pltpu.CompilerParams(vmem_limit_bytes=16 * MIB),
    )(pieces)
    count, rows, width = pieces.shape
    return exchange_cores(spread).reshape(count * rows, width)


def padded_count(count, devices):
    step = 8 * devices
    return -(-count // step) * step


def local(
    images,
    day_index,
    valid,
    out_grad,
    conv_weight,
    first_gain,
    first_shift,
    block_weight,
    gn_gain,
    gn_shift,
    key_weight,
    queries,
):
    dates, rows_here, cols, pair_width = images.shape
    width = conv_weight.shape[-1]
    row_devs, date_devs = lax.axis_size("rows"), lax.axis_size("dates")
    devices = row_devs * date_devs
    rows = rows_here // 2
    heads, depth = queries.shape
    norm_count = float(rows * row_devs * cols * (width // GROUPS))
    grad_scale = float(rows * row_devs * cols) ** (-0.5)
    date_start = lax.axis_index("dates") * dates
    frame = (dates, rows, cols, width)
    edge_rows = (dates, cols, width)
    flops = 2 * dates * rows * cols * width * width

    rows_of = lambda vector: vector.reshape(1, width)
    first_gain, first_shift = rows_of(first_gain), rows_of(first_shift)
    gn_gain, gn_shift = rows_of(gn_gain), rows_of(gn_shift)
    last = images[:, -1]
    above = shifted(last, 1)
    grad_rows = out_grad.size // width
    valid_rows = valid.astype(BF16).reshape(valid.shape[0] * rows, -1)
    valid_rows = jnp.pad(valid_rows, ((0, 0), (0, width - valid_rows.shape[1])))
    packed = jnp.concatenate([out_grad.reshape(grad_rows, width), valid_rows])
    high, below, above, packed = lax.optimization_barrier(
        (images[:, -3:-1], images[:, :2], above, packed)
    )
    high, below = shifted(high, 1), shifted(below, -1)
    paired = images.reshape(dates, rows, 2, cols, pair_width)
    conv_out, sums = call(
        down_kernel,
        dates,
        [("date far", paired), ("date", above), ("all far", conv_weight)],
        [("date far", frame, BF16), ("all", (row_devs, 2 * dates, width), F32)],
        [pltpu.VMEM((3 * pair_width, 2 * width), BF16)],
        6 * flops,
    )
    stats = exchange(sums, "rows")
    high, below, last, _ = lax.optimization_barrier((high, below, last, sums))
    halo_up, halo_down = call(
        edge_kernel,
        1,
        [("all", high), ("all", above), ("all", last), ("all", below), ("all far", conv_weight)],
        [("all far", edge_rows, BF16)] * 2,
        [pltpu.VMEM((3 * pair_width, 2 * width), BF16)],
        6 * flops // rows,
    )
    packed, _ = lax.optimization_barrier((packed, halo_up))
    sources = turned(packed)
    clear = lax.dynamic_slice_in_dim(sources, grad_rows + date_start * rows, dates * rows, 1)
    clear = clear.astype(F32)
    turn = lax.axis_index("dates").reshape(1)
    place = lax.axis_index("rows").reshape(1)

    block_out, hidden, first_norm, sums = call(
        functools.partial(block_kernel, norm_count=norm_count, row_devs=row_devs),
        dates,
        [
            ("scalar", place),
            ("date far", conv_out),
            ("date far", halo_up),
            ("date far", halo_down),
            ("all", stats),
            ("all", first_gain),
            ("all", first_shift),
            ("all far", block_weight),
        ],
        [
            ("date far", frame, BF16),
            ("date far", (dates, rows + 2, cols, width), BF16),
            ("all", (2 * dates, width), F32),
            ("all", (row_devs, 2 * dates, width), F32),
        ],
        [pltpu.VMEM((3 * width, 3 * width), BF16)],
        9 * flops,
    )
    stats = exchange(sums, "rows")
    features, exponent, attn, norm, packed, key_wide, query_wide = call(
        functools.partial(score_kernel, norm_count=norm_count, grad_scale=grad_scale),
        dates,
        [
            ("scalar", day_index),
            ("date far", block_out),
            ("all", stats),
            ("all", gn_gain),
            ("all", gn_shift),
            ("all", sources),
            ("all", clear),
            ("scalar", turn),
            ("all", key_weight.T),
            ("all", queries.T),
        ],
        [
            ("date", frame, BF16),
            ("date", frame, F32),
            ("date", frame, F32),
            ("all", (2 * dates, width), F32),
            ("all", (1, 2, cols, width), F32),
            ("all", (width, width), BF16),
            ("all", (8, width), F32),
        ],
        [
            pltpu.VMEM(frame[1:], F32),
            pltpu.VMEM(frame[1:], F32),
            pltpu.VMEM((2 * width, width), BF16),
            pltpu.VMEM((width, 2 * width), BF16),
        ],
        5 * flops,
    )
    packed = gather(packed, "dates")
    block_grad, attended, key_part, vectors, sums = call(
        functools.partial(attend_kernel, grad_scale=grad_scale),
        dates,
        [
            ("all", packed),
            ("date", features),
            ("date", exponent),
            ("date", attn),
            ("date", block_out),
            ("all", norm),
            ("all", gn_gain),
            ("all", gn_shift),
            ("all", query_wide),
            ("all", sources),
            ("scalar", turn),
            ("all", key_wide),
        ],
        [
            ("date far", frame, BF16),
            ("all far", (date_devs, rows, cols // date_devs, width), BF16),
            ("all far", (width, width), F32),
            ("all", (8, width), F32),
            ("all", (1, 2 * dates, width), F32),
        ],
        [pltpu.VMEM(frame[1:], F32)] * 3,
        5 * flops,
    )
    tails = row_totals(sums)
    pre_grad, linear_grad, first_vectors, sums = call(
        functools.partial(hidden_kernel, norm_count=norm_count, row_devs=row_devs),
        dates,
        [
            ("scalar", place),
            ("date far", block_grad),
            ("date far", block_out),
            ("all", tails),
            ("all", norm),
            ("all far", block_weight),
            ("date far", conv_out),
            ("date far", halo_up),
            ("date far", halo_down),
            ("all", first_norm),
            ("all", first_gain),
            ("all", first_shift),
        ],
        [
            ("date far", frame, BF16),
            ("date far", (dates, rows + 2, cols, width), BF16),
            ("all", (8, width), F32),
            ("all", (row_devs, 2 * dates, width), F32),
        ],
        [
            pltpu.VMEM((3 * width, 3 * width), BF16),
            pltpu.VMEM((2 * dates, width), F32),
            pltpu.VMEM((rows + 4, cols, width), BF16),
        ],
        9 * flops,
    )
    tails = exchange(sums, "rows")
    (block_rows,) = call(
        block_grad_kernel,
        dates,
        [("date far", hidden), ("date far", pre_grad), ("all far", key_part)],
        [("all far", (10 * width, width), BF16)],
        [pltpu.VMEM((3 * width, 3 * width), F32)],
        9 * flops,
    )
    tails, block_rows = lax.optimization_barrier((tails, block_rows))
    conv_count = 9 * pair_width // 2 + 32
    half_rows = padded_count(10 * width + conv_count, devices) // 2
    keep, give = call(
        functools.partial(conv_grad_kernel, norm_count=norm_count),
        dates,
        [
            ("date far", paired),
            ("date", above),
            ("date", high),
            ("date", below),
            ("date far", conv_out),
            ("date far", linear_grad),
            ("all", tails),
            ("all", first_norm),
            ("all", first_gain),
            ("all", first_vectors),
            ("all", vectors),
            ("all far", block_rows),
            ("scalar", turn),
        ],
        [("all", (half_rows, width), BF16)] * 2,
        [
            pltpu.VMEM((2 * dates, width), F32),
            pltpu.VMEM((3 * pair_width, 2 * width), F32),
            pltpu.VMEM((2 * half_rows, width), BF16),
        ],
        6 * flops,
    )
    rows_half = (keep.astype(F32) + other_core(give).astype(F32)).astype(BF16)
    pieces = scatter(rows_half)
    attended, _ = lax.optimization_barrier((attended, rows_half))
    attended = sum_of_parts(attended)
    rows_half = collect(pieces)
    rows_other = other_core(rows_half)
    shapes = [
        (9 * pair_width // 2, width),
        (9 * width, width),
        (heads * depth, width),
        (depth, heads),
    ] + [(1, width)] * 4
    conv_total, block_total, key_total, query_total, *totals = pl.pallas_call(
        functools.partial(final_kernel, depth),
        in_specs=[
            pl.BlockSpec(memory_space=pltpu.SMEM),
            pl.BlockSpec(memory_space=pltpu.VMEM),
            pl.BlockSpec(memory_space=pltpu.VMEM),
        ],
        out_shape=[jax.ShapeDtypeStruct(shape, F32) for shape in shapes],
        scratch_shapes=[pltpu.VMEM((2 * half_rows, width), BF16)],
        compiler_params=pltpu.CompilerParams(vmem_limit_bytes=16 * MIB),
    )(turn, rows_half, rows_other)
    totals = [total.reshape(width) for total in totals]
    return (
        attended,
        conv_total.reshape(conv_weight.shape),
        totals[0],
        totals[1],
        block_total.reshape(block_weight.shape),
        totals[2],
        totals[3],
        key_total.T,
        query_total.T,
    )


def solution(mesh):
    return jax.shard_map(
        local,
        mesh=mesh,
        in_specs=(
            P("dates", "rows", None, None),
            P(),
            P(None, "rows", "dates"),
            P("rows", "dates", None),
            P(),
            P(),
            P(),
            P(),
            P(),
            P(),
            P(),
            P(),
        ),
        out_specs=(P("rows", "dates", None), P(), P(), P(), P(), P(), P(), P(), P()),
        check_vma=False,
    )
```

```python
import functools
import math

import jax
import jax.numpy as jnp
from jax import lax
from jax.experimental import pallas as pl
from jax.experimental.pallas import tpu as pltpu
from jax.sharding import PartitionSpec as P

GROUPS = 4


EPS = 1e-05


MIB = 1 << 20


F32 = jnp.float32


BF16 = jnp.bfloat16


def product(left, right, left_dim, right_dim):
    return lax.dot_general(
        left, right, (((left_dim,), (right_dim,)), ((), ())), preferred_element_type=F32
    )


def group_sum(values):
    width = values.shape[-1]
    lane_group = lax.broadcasted_iota(jnp.int32, values.shape, 1) // (width // GROUPS)
    spread = jnp.zeros_like(values)
    for group in range(GROUPS):
        inside = lane_group == group
        total = jnp.sum(jnp.where(inside, values, 0.0), axis=1, keepdims=True)
        spread = spread + jnp.where(inside, total, 0.0)
    return spread


def sigmoid(values):
    return 0.5 * jnp.tanh(0.5 * values) + 0.5


def from_left(values):
    column = lax.broadcasted_iota(jnp.int32, values.shape, 1)
    return jnp.where(column > 0, pltpu.roll(values, 1, 1), 0.0)


def from_right(values):
    count = values.shape[1]
    column = lax.broadcasted_iota(jnp.int32, values.shape, 1)
    return jnp.where(column < count - 1, pltpu.roll(values, count - 1, 1), 0.0)


def column_sum(values):
    return jnp.sum(jnp.sum(values, axis=0), axis=0, keepdims=True)


def edges(place_ref, row_devs):
    place = place_ref[0]
    return (place > 0).astype(F32), (place < row_devs - 1).astype(F32)


def head_spread(width):
    lane = lax.broadcasted_iota(jnp.int32, (2 * width, width), 1) // (width // 16)
    head = lax.broadcasted_iota(jnp.int32, (2 * width, width), 0) % width // (width // 16)
    return (lane == head).astype(F32).astype(BF16)


def split(values):
    high = values.astype(BF16)
    return high, (values - high.astype(F32)).astype(BF16)


def store_sums(sums_ref, date, dates, first, second):
    for copy in range(sums_ref.shape[0]):
        sums_ref[copy, pl.ds(date, 1), :] = first
        sums_ref[copy, pl.ds(dates + date, 1), :] = second


def norm_table(sums_ref, table_ref, dates, norm_count):
    means = group_sum(jnp.sum(sums_ref[...], axis=0)) / norm_count
    mean = means[:dates]
    table_ref[:dates] = mean
    table_ref[dates:] = 1.0 / jnp.sqrt(means[dates:] - mean * mean + EPS)


def down_table(weight_ref, table):
    half = weight_ref.shape[2]
    for tap in range(3):
        base = tap * 2 * half
        table[base : base + half, : 2 * half] = weight_ref[tap, 1]
        table[base + half : base + 2 * half, : 2 * half] = weight_ref[tap, 2]
        table[base : base + half, 2 * half :] = jnp.zeros_like(weight_ref[tap, 0])
        table[base + half : base + 2 * half, 2 * half :] = weight_ref[tap, 0]


def down_rows(taps, table):
    rows, cols, width = taps[0].shape
    taps = jnp.concatenate(taps, axis=-1).reshape(rows * cols, 3 * width)
    both = product(taps, table[...], 1, 0).reshape(rows, cols, 2 * width)
    return (both[..., :width] + from_left(both[..., width:])).astype(BF16)


def down_kernel(
    date, dates, img_ref, above_ref, weight_ref, out_ref, sums_ref, table
):

    if date == 0:
        down_table(weight_ref, table)

    even, odd = img_ref[0, :, 0], img_ref[0, :, 1]
    above = jnp.concatenate([above_ref[0][None], odd[:-1]], axis=0)
    stored = down_rows([above, even, odd], table)
    out_ref[0] = stored
    values = stored.astype(F32)
    store_sums(sums_ref, date, dates, column_sum(values), column_sum(values * values))


def sort_halos(place_ref, inner_ref, outer_ref, high_ref, below_ref):
    odd = place_ref[0] % 2 == 1

    @pl.when(odd)
    def _():
        high_ref[...] = inner_ref[...]
        below_ref[...] = outer_ref[...]

    @pl.when(jnp.logical_not(odd))
    def _():
        high_ref[...] = outer_ref[...]
        below_ref[...] = inner_ref[...]


def edge_kernel(
    step,
    steps,
    place_ref,
    inner_ref,
    outer_ref,
    above_ref,
    last_ref,
    weight_ref,
    up_ref,
    down_ref,
    table,
    high_ref,
    below_ref,
):
    dates = above_ref.shape[0]
    sort_halos(place_ref, inner_ref, outer_ref, high_ref, below_ref)
    down_table(weight_ref, table)
    taps = [
        jnp.concatenate([high_ref[:, 0], last_ref[...]], axis=0),
        jnp.concatenate([high_ref[:, 1], below_ref[:, 0]], axis=0),
        jnp.concatenate([above_ref[...], below_ref[:, 1]], axis=0),
    ]
    stored = down_rows(taps, table)
    up_ref[...] = stored[:dates]
    down_ref[...] = stored[dates:]


def block_kernel(
    date,
    dates,
    edge_ref,
    conv_ref,
    up_ref,
    down_ref,
    stats_ref,
    gain_ref,
    shift_ref,
    weight_ref,
    out_ref,
    hidden_ref,
    norm_ref,
    sums_ref,
    table,
    *,
    norm_count,
    row_devs,
):
    width = conv_ref.shape[-1]

    if date == 0:
        norm_table(stats_ref, norm_ref, dates, norm_count)
        for row_tap in range(3):
            for col_tap in range(3):
                table[
                    row_tap * width : (row_tap + 1) * width, col_tap * width : (col_tap + 1) * width
                ] = weight_ref[row_tap, col_tap]

    scale = norm_ref[pl.ds(dates + date, 1), :] * gain_ref[...]
    shift = shift_ref[...] - norm_ref[pl.ds(date, 1), :] * scale

    def activate(values):
        linear = values.astype(F32) * scale + shift
        return linear * sigmoid(linear)

    rows, cols = conv_ref.shape[1:3]
    above_edge, below_edge = edges(edge_ref, row_devs)
    hidden_ref[0, 0] = (activate(up_ref[0]) * above_edge).astype(BF16)
    hidden_ref[0, rows + 1] = (activate(down_ref[0]) * below_edge).astype(BF16)
    hidden_ref[0, 1 : rows + 1] = activate(conv_ref[0]).astype(BF16)
    taps = jnp.concatenate(
        [hidden_ref[0, tap : tap + rows] for tap in range(3)], axis=-1
    ).reshape(rows * cols, 3 * width)
    terms = product(taps, table[...], 1, 0).reshape(rows, cols, 3 * width)
    stored = (
        terms[..., width : 2 * width]
        + from_left(terms[..., :width])
        + from_right(terms[..., 2 * width :])
    ).astype(BF16)
    out_ref[0] = stored
    values = stored.astype(F32)
    store_sums(sums_ref, date, dates, column_sum(values), column_sum(values * values))


def encoding(day, width):
    lane = lax.broadcasted_iota(jnp.int32, (1, width), 1)
    frequency = jnp.exp((lane // 2).astype(F32) * (-2.0 * math.log(1000.0) / width))
    angles = day.astype(F32) * frequency
    return jnp.where(lane % 2 == 0, jnp.sin(angles), jnp.cos(angles))


def fold_keys(key_ref, query_ref, wide_ref, vector_ref, spread_ref, score_ref):
    depth, heads = query_ref.shape
    width = key_ref.shape[1]
    lanes = width // heads
    spread_ref[...] = head_spread(width)
    row = lax.broadcasted_iota(jnp.int32, (heads * depth, width), 0)
    lane = lax.broadcasted_iota(jnp.int32, (heads * depth, width), 1)
    widen = (row // depth == lane // lanes) & (row % depth == lane % lanes)
    wide = product(key_ref[...], widen.astype(F32).astype(BF16), 0, 0)
    wide_ref[...] = wide.astype(BF16)
    head = lax.broadcasted_iota(jnp.int32, (heads, width), 0)
    lane = lax.broadcasted_iota(jnp.int32, (heads, width), 1)
    inside = (lane // lanes == head).astype(F32).astype(BF16)
    high, low = split(query_ref[...])
    lower = (query_ref[...] - high.astype(F32) - low.astype(F32)).astype(BF16)
    spread = sum(product(part, inside, 1, 0) for part in (high, low, lower))
    step = lax.broadcasted_iota(jnp.int32, (depth, width), 0)
    place = lax.broadcasted_iota(jnp.int32, (depth, width), 1) % lanes
    queries = jnp.sum(jnp.where(step == place, spread * depth**-0.5, 0.0), axis=0, keepdims=True)
    place = lax.broadcasted_iota(jnp.int32, (1, width), 1) % lanes
    queries = queries + jnp.where((place == depth) | (place == depth + 1), 1.0, 0.0)
    vector_ref[...] = jnp.broadcast_to(queries, vector_ref.shape)
    folded = jnp.concatenate(split(wide * queries), axis=-1)
    folded = product(folded, spread_ref[...], 1, 0)
    score_ref[...] = jnp.concatenate(split(folded), axis=-1)


def source_of(turn_ref, device, devices):
    half = devices // 2
    core = (device + turn_ref[0]) % 2
    return core * half + (device // 2 + half - turn_ref[0] // 2) % half


def upstream_rows(grad_ref, turn_ref, rows, cols):
    devices = grad_ref.shape[0]
    piece = cols // devices
    parts = [
        grad_ref[source_of(turn_ref, device, devices), : rows * piece].reshape(rows, piece, -1)
        for device in range(devices)
    ]
    return jnp.concatenate(parts, axis=1)


def score_kernel(
    date,
    dates,
    day_ref,
    block_ref,
    stats_ref,
    gain_ref,
    shift_ref,
    grad_ref,
    valid_ref,
    turn_ref,
    key_ref,
    query_ref,
    feat_ref,
    exp_ref,
    attn_ref,
    norm_ref,
    packed_ref,
    own_ref,
    wide_ref,
    vector_ref,
    total,
    mean,
    spread_ref,
    score_ref,
    *,
    norm_count,
    grad_scale,
):
    rows, cols, width = block_ref.shape[1:]

    if date == 0:
        norm_table(stats_ref, norm_ref, dates, norm_count)
        fold_keys(key_ref, query_ref, wide_ref, vector_ref, spread_ref, score_ref)
        total[...] = jnp.zeros_like(total)
        mean[...] = jnp.zeros_like(mean)

    scale = norm_ref[pl.ds(dates + date, 1), :] * gain_ref[...]
    shift = shift_ref[...] - norm_ref[pl.ds(date, 1), :] * scale
    linear = block_ref[0].astype(F32) * scale + shift
    features = (linear * sigmoid(linear) + encoding(day_ref[turn_ref[0] * dates + date], width)).astype(BF16)
    feat_ref[0] = features
    upstream = upstream_rows(grad_ref, turn_ref, rows, cols)
    parts = split(upstream.astype(F32) * features.astype(F32))
    parts = jnp.concatenate(parts, axis=-1).reshape(rows * cols, 2 * width)
    attn = product(parts, spread_ref[...], 1, 0).reshape(rows, cols, width) * grad_scale
    both = product(features.reshape(rows * cols, width), score_ref[...], 1, 0)
    scores = (both[:, :width] + both[:, width:]).reshape(rows, cols, width)
    devices = grad_ref.shape[0]
    valid = jnp.zeros((rows, width), F32)
    for device in range(devices):
        piece = valid_ref[
            source_of(turn_ref, device, devices), pl.ds(date * rows, rows), :
        ]
        valid = valid + pltpu.roll(piece, device * (cols // devices), 1)
    diagonal = lax.broadcasted_iota(jnp.int32, (cols, cols), 0) == lax.broadcasted_iota(
        jnp.int32, (cols, cols), 1
    )
    ones = jnp.ones((cols, width), BF16)
    clear = jnp.concatenate(
        [jnp.where(diagonal, valid[row : row + 1], 0.0) for row in range(rows)], axis=0
    ).astype(BF16)
    clear = product(clear, ones, 1, 0).reshape(rows, cols, width)
    exponent = clear * jnp.exp(scores)
    running = total[...] + exponent
    share = jnp.where(running > 0.0, exponent / running, 0.0)
    total[...] = running
    mean[...] += share * (attn - mean[...])
    exp_ref[0] = exponent
    attn_ref[0] = attn

    if date == dates - 1:
        place = lax.broadcasted_iota(jnp.int32, (cols, width), 1) % rows
        for index, source in enumerate((total, mean)):
            dense = jnp.zeros((cols, width), F32)
            for row in range(rows):
                dense = dense + jnp.where(place == row, source[row], 0.0)
            if index == 0:
                packed_ref[0, 0] = dense.astype(BF16)
                own_ref[...] = dense
            else:
                packed_ref[0, 1], packed_ref[0, 2] = split(dense)


def attend_kernel(
    date,
    dates,
    packed_ref,
    own_ref,
    feat_ref,
    exp_ref,
    attn_ref,
    block_ref,
    norm_ref,
    gain_ref,
    shift_ref,
    query_ref,
    grad_ref,
    turn_ref,
    key_ref,
    grad_out_ref,
    part_ref,
    key_out_ref,
    vector_ref,
    sums_ref,
    inverse,
    average,
    attended,
    *,
    grad_scale,
):
    rows, cols, width = block_ref.shape[1:]

    if date == 0:
        totals = packed_ref[:, 0].astype(F32)
        reciprocal = 1.0 / jnp.sum(totals, axis=0)
        means = packed_ref[:, 1].astype(F32) + packed_ref[:, 2].astype(F32)
        mean = jnp.sum(totals * reciprocal * means, axis=0)
        own = own_ref[...]
        sent = own.astype(BF16).astype(F32)
        reciprocal = reciprocal * jnp.where(own > 0.0, sent / own, 0.0)
        place = lax.broadcasted_iota(jnp.int32, (cols, width), 1) % rows
        for values, target in ((reciprocal, inverse), (mean, average)):
            parts = jnp.concatenate(split(values), axis=-1)
            wide_place = jnp.concatenate([place, place], axis=-1)
            picked = jnp.concatenate(
                [jnp.where(wide_place == row, parts, jnp.zeros_like(parts)) for row in range(rows)], axis=0
            )
            target[...] = product(picked, head_spread(width), 1, 0).reshape(rows, cols, width)
        attended[...] = jnp.zeros_like(attended)
        key_out_ref[...] = jnp.zeros_like(key_out_ref)
        vector_ref[...] = jnp.zeros_like(vector_ref)

    features = feat_ref[0]
    weights = exp_ref[0] * inverse[...]
    rounded = weights.astype(BF16).astype(F32)
    attended[...] += rounded * features.astype(F32)
    score_grad = weights * (attn_ref[0] - average[...])
    spread_grad = score_grad * query_ref[0:1]
    rest = spread_grad - spread_grad.astype(BF16).astype(F32)
    lane = lax.broadcasted_iota(jnp.int32, spread_grad.shape, 2) % (width // 16)
    key_grads = jnp.where(lane == 5, rest, spread_grad).astype(BF16).reshape(rows * cols, width)
    key_out_ref[...] += product(features.reshape(rows * cols, width), key_grads, 0, 0)
    upstream = upstream_rows(grad_ref, turn_ref, rows, cols)
    feat_grad = rounded * (upstream.astype(F32) * grad_scale) + product(
        key_grads, key_ref[...], 1, 1
    ).reshape(rows, cols, width)
    gain = gain_ref[...]
    centred = (block_ref[0].astype(F32) - norm_ref[pl.ds(date, 1), :]) * norm_ref[
        pl.ds(dates + date, 1), :
    ]
    linear = centred * gain + shift_ref[...]
    part = sigmoid(linear)
    linear_grad = feat_grad * (part * (1.0 + linear * (1.0 - part)))
    first = column_sum(linear_grad)
    second = column_sum(linear_grad * centred)
    vector_ref[0:1] += second
    vector_ref[1:2] += first
    store_sums(sums_ref, date, dates, first * gain, second * gain)
    grad_out_ref[0] = (linear_grad * gain).astype(BF16)

    if date == dates - 1:
        devices, piece = part_ref.shape[0], part_ref.shape[2]
        for device in range(devices):
            part_ref[device] = attended[:, device * piece : (device + 1) * piece].astype(BF16)
        key_part = key_out_ref[...]
        place = lax.broadcasted_iota(jnp.int32, (width, width), 1) % (width // 16)
        both = pltpu.roll(key_part, width - 4, 1) + pltpu.roll(key_part, width - 5, 1)
        both = jnp.where(place == 0, both, 0.0)
        both = both + pltpu.roll(both, 1, 1)
        both = both + pltpu.roll(both, 2, 1)
        vector_ref[2:3] = 0.5 * jnp.sum(key_ref[...].astype(F32) * both, axis=0, keepdims=True)


def hidden_kernel(
    date,
    dates,
    edge_ref,
    grad_ref,
    block_ref,
    tails_ref,
    norm_ref,
    weight_ref,
    conv_ref,
    up_ref,
    down_ref,
    first_norm_ref,
    gain_ref,
    shift_ref,
    pre_ref,
    out_ref,
    vector_ref,
    sums_ref,
    table,
    factors,
    padded,
    *,
    norm_count,
    row_devs,
):
    rows, cols, width = block_ref.shape[1:]

    if date == 0:
        tails = group_sum(jnp.sum(tails_ref[...], axis=0)) / norm_count
        mean, inverse = norm_ref[:dates], norm_ref[dates:]
        slope = -inverse * inverse * tails[dates:]
        factors[0:dates] = slope
        factors[dates : 2 * dates] = -inverse * tails[:dates] - mean * slope
        vector_ref[...] = jnp.zeros_like(vector_ref)
        padded[:2] = jnp.zeros_like(padded[:2])
        padded[rows + 2 :] = jnp.zeros_like(padded[rows + 2 :])
        for row_tap in range(3):
            for col_tap in range(3):
                table[
                    col_tap * width : (col_tap + 1) * width, row_tap * width : (row_tap + 1) * width
                ] = weight_ref[2 - row_tap, col_tap]

    inverse = norm_ref[pl.ds(dates + date, 1), :]
    slope = factors[pl.ds(date, 1), :]
    constant = factors[pl.ds(dates + date, 1), :]

    above_edge, below_edge = edges(edge_ref, row_devs)
    stored = (
        grad_ref[0].astype(F32) * inverse + (block_ref[0].astype(F32) * slope + constant)
    ).astype(BF16)
    pre_ref[0] = stored
    padded[2 : rows + 2] = stored
    reach = rows + 2
    taps = jnp.concatenate([padded[tap : tap + reach] for tap in range(3)], axis=-1).reshape(
        reach * cols, 3 * width
    )
    terms = product(taps, table[...], 1, 1).reshape(reach, cols, 3 * width)
    hidden_grad = (
        terms[..., width : 2 * width]
        + from_right(terms[..., :width])
        + from_left(terms[..., 2 * width :])
    )
    gain = gain_ref[...]
    conv = jnp.concatenate([up_ref[0][None], conv_ref[0], down_ref[0][None]], axis=0)
    centred = (conv.astype(F32) - first_norm_ref[pl.ds(date, 1), :]) * first_norm_ref[
        pl.ds(dates + date, 1), :
    ]
    linear = centred * gain + shift_ref[...]
    part = sigmoid(linear)
    linear_grad = hidden_grad * (part * (1.0 + linear * (1.0 - part)))
    linear_grad = jnp.concatenate(
        [
            linear_grad[:1] * above_edge,
            linear_grad[1 : rows + 1],
            linear_grad[rows + 1 :] * below_edge,
        ],
        axis=0,
    )
    out_ref[0] = linear_grad.astype(BF16)
    first = column_sum(linear_grad)
    second = column_sum(linear_grad * centred)
    vector_ref[0:1] += second
    vector_ref[1:2] += first
    store_sums(sums_ref, date, dates, first * gain, second * gain)


def block_grad_kernel(
    date, dates, hidden_ref, pre_ref, key_ref, out_ref, total
):
    rows, cols, width = pre_ref.shape[1:]

    if date == 0:
        total[...] = jnp.zeros_like(total)

    grads = pre_ref[0].astype(F32)
    grads = jnp.concatenate(
        [from_right(grads).astype(BF16), pre_ref[0], from_left(grads).astype(BF16)], axis=-1
    ).reshape(rows * cols, 3 * width)
    taps = jnp.concatenate(
        [hidden_ref[0, tap : tap + rows] for tap in range(3)], axis=-1
    ).reshape(rows * cols, 3 * width)
    total[...] += product(taps, grads, 0, 0)

    if date == dates - 1:
        for row_tap in range(3):
            for col_tap in range(3):
                base = (row_tap * 3 + col_tap) * width
                out_ref[base : base + width] = total[
                    row_tap * width : (row_tap + 1) * width, col_tap * width : (col_tap + 1) * width
                ].astype(BF16)
        key_part = key_ref[...]
        rest = key_part - key_part.astype(BF16).astype(F32)
        lanes = width // 16
        place = lax.broadcasted_iota(jnp.int32, key_part.shape, 1) % lanes
        rest = pltpu.roll(rest, lanes // 2, 1)
        key_rows = jnp.where(place < lanes // 2, key_part, rest).astype(BF16)
        out_ref[9 * width : 10 * width] = key_rows
        if out_ref.shape[0] > 10 * width:
            out_ref[10 * width :] = jnp.zeros_like(out_ref[10 * width :])


def conv_grad_kernel(
    date,
    dates,
    img_ref,
    above_ref,
    inner_ref,
    outer_ref,
    place_ref,
    conv_ref,
    grad_ref,
    tails_ref,
    norm_ref,
    gain_ref,
    vector_ref,
    other_ref,
    block_rows_ref,
    turn_ref,
    keep_ref,
    give_ref,
    factors,
    total,
    out_ref,
    high_ref,
    below_ref,
    *,
    norm_count,
):
    rows, cols, width = conv_ref.shape[1:]
    half = width // 2

    if date == 0:
        sort_halos(place_ref, inner_ref, outer_ref, high_ref, below_ref)
        tails = group_sum(jnp.sum(tails_ref[...], axis=0)) / norm_count
        mean, inverse = norm_ref[:dates], norm_ref[dates:]
        slope = -inverse * inverse * tails[dates:]
        factors[0:dates] = slope
        factors[dates : 2 * dates] = -inverse * tails[:dates] - mean * slope
        total[...] = jnp.zeros_like(total)

    scale = norm_ref[pl.ds(dates + date, 1), :] * gain_ref[...]
    slope = factors[pl.ds(date, 1), :]
    constant = factors[pl.ds(dates + date, 1), :]
    own = conv_ref[0].astype(F32) * slope + constant
    scaled = grad_ref[0].astype(F32) * scale
    stored = jnp.concatenate(
        [scaled[:1], scaled[1 : rows + 1] + own, scaled[rows + 1 :]], axis=0
    ).astype(BF16)
    moved = from_right(stored.astype(F32)).astype(BF16)
    reach = rows + 2
    grads = jnp.concatenate([stored, moved], axis=-1).reshape(reach * cols, 2 * width)
    even, odd = img_ref[0, :, 0], img_ref[0, :, 1]
    above = above_ref[0][None]
    taps = [
        jnp.concatenate([high_ref[date, :1], above, odd], axis=0),
        jnp.concatenate([high_ref[date, 1:], even, below_ref[date, :1]], axis=0),
        jnp.concatenate([above, odd, below_ref[date, 1:]], axis=0),
    ]
    taps = jnp.concatenate(taps, axis=-1).reshape(reach * cols, 3 * width)
    total[...] += product(taps, grads, 0, 0)

    if date == dates - 1:
        begin = block_rows_ref.shape[0]
        out_ref[:begin] = block_rows_ref[...]
        for tap in range(3):
            base = tap * width
            pair = total[base : base + width, :width].astype(BF16)
            left = total[base + half : base + width, width:].astype(BF16)
            start = begin + tap * 3 * half
            out_ref[start : start + half] = left
            out_ref[start + half : start + 3 * half] = pair
        start = begin + 9 * half
        for source in (vector_ref, other_ref):
            high, low = split(source[...])
            out_ref[start : start + 16] = jnp.concatenate([high, low], axis=0)
            start += 16
        if out_ref.shape[0] > start:
            out_ref[start:] = jnp.zeros_like(out_ref[start:])
        half_rows = keep_ref.shape[0]
        core = turn_ref[0] % 2
        start = pl.multiple_of(core * half_rows, half_rows)
        keep_ref[...] = out_ref[pl.ds(start, half_rows), :]
        start = pl.multiple_of((1 - core) * half_rows, half_rows)
        give_ref[...] = out_ref[pl.ds(start, half_rows), :]


def total_kernel(in_ref, out_ref):
    total = jnp.sum(in_ref[...].astype(F32), axis=0).astype(BF16)
    for copy in range(out_ref.shape[0]):
        out_ref[copy] = total


def final_kernel(
    depth,
    turn_ref,
    own_ref,
    other_ref,
    conv_ref,
    block_ref,
    key_ref,
    query_ref,
    *refs,
):
    vector_refs, rows_ref = refs[:-1], refs[-1]
    half_rows = own_ref.shape[0]
    core = turn_ref[0] % 2
    rows_ref[pl.ds(pl.multiple_of(core * half_rows, half_rows), half_rows), :] = own_ref[...]
    start = pl.multiple_of((1 - core) * half_rows, half_rows)
    rows_ref[pl.ds(start, half_rows), :] = other_ref[...]
    conv_end, block_end, width = conv_ref.shape[0], block_ref.shape[0], block_ref.shape[1]
    block_ref[...] = rows_ref[:block_end].astype(F32)
    wide = key_ref.shape[0]
    heads = wide // depth
    lanes = width // heads
    row = lax.broadcasted_iota(jnp.int32, (wide, width), 0)
    lane = lax.broadcasted_iota(jnp.int32, (wide, width), 1)
    narrow = (row // depth == lane // lanes) & (row % depth == lane % depth)
    narrow = narrow.astype(F32).astype(BF16)
    key_ref[...] = product(narrow, rows_ref[block_end : block_end + width], 1, 1)
    start = block_end + width
    conv_ref[...] = rows_ref[start : start + conv_end].astype(F32)
    start += conv_end
    for index in range(2):
        both = rows_ref[start : start + 16].astype(F32)
        both = both[:8] + both[8:]
        vector_refs[2 * index][...] = both[0:1]
        vector_refs[2 * index + 1][...] = both[1:2]
        start += 16
    both = rows_ref[start - 16 : start]
    row = lax.broadcasted_iota(jnp.int32, (heads, width), 0)
    lane = lax.broadcasted_iota(jnp.int32, (heads, width), 1)
    inside = row == lane // lanes
    step = lax.broadcasted_iota(jnp.int32, (8, width), 0)
    place = lax.broadcasted_iota(jnp.int32, (8, width), 1) % lanes
    steps = step == place
    query = jnp.zeros((8, heads), F32)
    for index in (2, 10):
        picked = jnp.where(steps, both[index : index + 1].astype(F32), 0.0).astype(BF16)
        query = query + product(picked, inside.astype(F32).astype(BF16), 1, 1)
    query_ref[...] = query[:depth]


def call(kernel, dates, inputs, outputs, scratch, flops):
    in_specs, out_specs, arrays, out_shape, buffers = [], [], [], [], []
    in_vmem, in_hbm = pl.BlockSpec(memory_space=pltpu.VMEM), pl.BlockSpec(memory_space=pltpu.HBM)
    loads, stores = [], []
    for place, (kind, array) in enumerate(inputs):
        if kind == "scalar":
            in_specs.append(pl.BlockSpec(memory_space=pltpu.SMEM))
        elif "far" in kind:
            array = pltpu.with_memory_space_constraint(array, pltpu.HBM)
            in_specs.append(in_hbm)
            loads.append(place)
            buffers.append(pltpu.VMEM(array.shape, array.dtype))
        else:
            in_specs.append(in_vmem)
        arrays.append(array)
    for place, (kind, shape, dtype) in enumerate(outputs):
        if "far" in kind:
            out_shape.append(pltpu.HBM(shape, dtype))
            out_specs.append(in_hbm)
            stores.append(place)
            buffers.append(pltpu.VMEM(shape, dtype))
        else:
            out_shape.append(jax.ShapeDtypeStruct(shape, dtype))
            out_specs.append(in_vmem)
    copies = len(loads) + len(stores)
    kinds = [kind for kind, _ in inputs] + [kind for kind, _, _ in outputs]

    def body(*refs):
        views, rest = list(refs[: len(kinds)]), refs[len(kinds) :]
        buffer_refs, ready, rest = rest[:copies], rest[copies], rest[copies + 1 :]

        def copies_of(place, index, inward):
            outside, inside = views[place], buffer_refs[index]
            made = []
            for date in range(dates if "date" in kinds[place] else 1):
                here = pl.ds(date, 1) if "date" in kinds[place] else slice(None)
                pair = (outside.at[here], inside.at[here])
                source, target = pair if inward else pair[::-1]
                made.append(pltpu.make_async_copy(source, target, ready.at[index, date]))
            return made

        incoming = [copies_of(place, index, True) for index, place in enumerate(loads)]
        outgoing = [
            copies_of(len(inputs) + place, len(loads) + index, False)
            for index, place in enumerate(stores)
        ]
        for date in range(dates):
            for moves in incoming:
                if date < len(moves):
                    moves[date].start()
        for index, place in enumerate(loads):
            views[place] = buffer_refs[index]
        for index, place in enumerate(stores):
            views[len(inputs) + place] = buffer_refs[len(loads) + index]
        for date in range(dates):
            for moves in incoming:
                if date < len(moves):
                    moves[date].wait()
            here = [
                view.at[pl.ds(date, 1)] if "date" in kind else view
                for view, kind in zip(views, kinds)
            ]
            kernel(date, dates, *here, *rest)
            for moves in outgoing:
                if len(moves) == dates:
                    moves[date].start()
                elif date == dates - 1:
                    moves[0].start()
        for moves in outgoing:
            for move in moves:
                move.wait()

    moved = sum(array.size * array.dtype.itemsize for _, array in inputs)
    return pl.pallas_call(
        body,
        in_specs=in_specs,
        out_specs=out_specs,
        out_shape=out_shape,
        scratch_shapes=buffers + [pltpu.SemaphoreType.DMA((max(copies, 1), dates))] + scratch,
        compiler_params=pltpu.CompilerParams(vmem_limit_bytes=40 * MIB),
        cost_estimate=pl.CostEstimate(flops=flops, bytes_accessed=2 * moved, transcendentals=0),
    )(*arrays)


def shifted(array, by):
    devices = lax.axis_size("rows")
    pairs = [(i, i + by) for i in range(devices) if 0 <= i + by < devices]
    return lax.ppermute(array, "rows", pairs)


def turned(array):
    devices = lax.axis_size("dates")
    pieces = [array]
    for step in range(2, devices, 2):
        pairs = [((i + step) % devices, i) for i in range(devices)]
        pieces.append(lax.ppermute(array, "dates", pairs))
    return jnp.stack(pieces + [other_core(piece) for piece in pieces])


def sum_of_parts(parts):
    devices = lax.axis_size("dates")
    place = lax.axis_index("dates")
    total = lax.dynamic_index_in_dim(parts, place, 0, keepdims=False).astype(F32)
    for step in range(1, devices):
        piece = lax.dynamic_index_in_dim(parts, (place + step) % devices, 0, keepdims=False)
        pairs = [(i, (i + step) % devices) for i in range(devices)]
        total = total + lax.ppermute(piece, "dates", pairs).astype(F32)
    return total.astype(BF16)


def exchange(pieces, axes):
    return lax.all_to_all(pieces, axes, split_axis=0, concat_axis=0, tiled=True)


def gather(array, axis):
    return lax.all_gather(array, axis, axis=0, tiled=True)


def other_core(array):
    devices = lax.axis_size("dates")
    return lax.ppermute(array, "dates", [(i, i + 1 - 2 * (i % 2)) for i in range(devices)])


def exchange_cores(pieces):
    axes = ("rows", "dates")
    devices = lax.axis_size(axes)
    groups = [list(range(core, devices, 2)) for core in range(2)]
    return lax.all_to_all(
        pieces, axes, split_axis=0, concat_axis=0, axis_index_groups=groups, tiled=True
    )


def scatter(rows_array):
    devices = lax.axis_size(("rows", "dates")) // 2
    count, width = rows_array.shape
    return exchange_cores(rows_array.reshape(devices, count // devices, width))


def collect(pieces):
    spread = pl.pallas_call(
        total_kernel,
        out_shape=jax.ShapeDtypeStruct(pieces.shape, BF16),
        compiler_params=pltpu.CompilerParams(vmem_limit_bytes=16 * MIB),
    )(pieces)
    count, rows, width = pieces.shape
    return exchange_cores(spread).reshape(count * rows, width)


def padded_count(count, devices):
    step = 8 * devices
    return -(-count // step) * step


def local(
    images,
    day_index,
    valid,
    out_grad,
    conv_weight,
    first_gain,
    first_shift,
    block_weight,
    gn_gain,
    gn_shift,
    key_weight,
    queries,
):
    dates, rows_here, cols, pair_width = images.shape
    width = conv_weight.shape[-1]
    row_devs, date_devs = lax.axis_size("rows"), lax.axis_size("dates")
    devices = row_devs * date_devs
    rows = rows_here // 2
    heads, depth = queries.shape
    norm_count = float(rows * row_devs * cols * (width // GROUPS))
    grad_scale = float(rows * row_devs * cols) ** (-0.5)
    date_start = lax.axis_index("dates") * dates
    frame = (dates, rows, cols, width)
    edge_rows = (dates, cols, width)
    flops = 2 * dates * rows * cols * width * width

    rows_of = lambda vector: vector.reshape(1, width)
    first_gain, first_shift = rows_of(first_gain), rows_of(first_shift)
    gn_gain, gn_shift = rows_of(gn_gain), rows_of(gn_shift)
    last = images[:, -1]
    above = shifted(last, 1)
    grad_rows = out_grad.size // width
    valid_rows = valid.astype(BF16).reshape(valid.shape[0] * rows, -1)
    valid_rows = jnp.pad(valid_rows, ((0, 0), (0, width - valid_rows.shape[1])))
    packed = jnp.concatenate([out_grad.reshape(grad_rows, width), valid_rows])
    row_place = lax.axis_index("rows")
    odd = row_place % 2 == 1
    inner = jnp.where(odd, images[:, :2], images[:, -3:-1])
    outer = jnp.where(odd, images[:, -3:-1], images[:, :2])
    inner, outer, above, packed = lax.optimization_barrier((inner, outer, above, packed))
    inner = lax.ppermute(inner, "rows", [(i, i ^ 1) for i in range(row_devs)])
    pairs = [(i, i + 1) for i in range(1, row_devs - 1, 2)]
    outer = lax.ppermute(outer, "rows", pairs + [(j, i) for i, j in pairs])
    paired = images.reshape(dates, rows, 2, cols, pair_width)
    conv_out, sums = call(
        down_kernel,
        dates,
        [("date far", paired), ("date", above), ("all far", conv_weight)],
        [("date far", frame, BF16), ("all", (row_devs, 2 * dates, width), F32)],
        [pltpu.VMEM((3 * pair_width, 2 * width), BF16)],
        6 * flops,
    )
    stats = exchange(sums, "rows")
    inner, outer, last, _ = lax.optimization_barrier((inner, outer, last, sums))
    place = row_place.reshape(1)
    halo_up, halo_down = call(
        edge_kernel,
        1,
        [
            ("scalar", place),
            ("all", inner),
            ("all", outer),
            ("all", above),
            ("all", last),
            ("all", conv_weight),
        ],
        [("all", edge_rows, BF16)] * 2,
        [
            pltpu.VMEM((3 * pair_width, 2 * width), BF16),
            pltpu.VMEM(inner.shape, BF16),
            pltpu.VMEM(inner.shape, BF16),
        ],
        6 * flops // rows,
    )
    packed, _ = lax.optimization_barrier((packed, halo_up))
    sources = turned(packed)
    clear = lax.dynamic_slice_in_dim(sources, grad_rows + date_start * rows, dates * rows, 1)
    clear = clear.astype(F32)
    turn = lax.axis_index("dates").reshape(1)
    block_out, hidden, first_norm, sums = call(
        functools.partial(block_kernel, norm_count=norm_count, row_devs=row_devs),
        dates,
        [
            ("scalar", place),
            ("date far", conv_out),
            ("date", halo_up),
            ("date", halo_down),
            ("all", stats),
            ("all", first_gain),
            ("all", first_shift),
            ("all far", block_weight),
        ],
        [
            ("date far", frame, BF16),
            ("date far", (dates, rows + 2, cols, width), BF16),
            ("all", (2 * dates, width), F32),
            ("all", (row_devs, 2 * dates, width), F32),
        ],
        [pltpu.VMEM((3 * width, 3 * width), BF16)],
        9 * flops,
    )
    stats = exchange(sums, "rows")
    features, exponent, attn, norm, packed, own_total, key_wide, query_wide = call(
        functools.partial(score_kernel, norm_count=norm_count, grad_scale=grad_scale),
        dates,
        [
            ("scalar", day_index),
            ("date far", block_out),
            ("all", stats),
            ("all", gn_gain),
            ("all", gn_shift),
            ("all", sources),
            ("all", clear),
            ("scalar", turn),
            ("all", key_weight.T),
            ("all", queries.T),
        ],
        [
            ("date", frame, BF16),
            ("date", frame, F32),
            ("date", frame, F32),
            ("all", (2 * dates, width), F32),
            ("all", (1, 3, cols, width), BF16),
            ("all", (cols, width), F32),
            ("all", (width, width), BF16),
            ("all", (8, width), F32),
        ],
        [
            pltpu.VMEM(frame[1:], F32),
            pltpu.VMEM(frame[1:], F32),
            pltpu.VMEM((2 * width, width), BF16),
            pltpu.VMEM((width, 2 * width), BF16),
        ],
        5 * flops,
    )
    packed = gather(packed, "dates")
    block_grad, attended, key_part, vectors, sums = call(
        functools.partial(attend_kernel, grad_scale=grad_scale),
        dates,
        [
            ("all", packed),
            ("all", own_total),
            ("date", features),
            ("date", exponent),
            ("date", attn),
            ("date", block_out),
            ("all", norm),
            ("all", gn_gain),
            ("all", gn_shift),
            ("all", query_wide),
            ("all", sources),
            ("scalar", turn),
            ("all", key_wide),
        ],
        [
            ("date far", frame, BF16),
            ("all far", (date_devs, rows, cols // date_devs, width), BF16),
            ("all far", (width, width), F32),
            ("all", (8, width), F32),
            ("all", (row_devs, 2 * dates, width), F32),
        ],
        [pltpu.VMEM(frame[1:], F32)] * 3,
        5 * flops,
    )
    tails = exchange(sums, "rows")
    pre_grad, linear_grad, first_vectors, sums = call(
        functools.partial(hidden_kernel, norm_count=norm_count, row_devs=row_devs),
        dates,
        [
            ("scalar", place),
            ("date far", block_grad),
            ("date far", block_out),
            ("all", tails),
            ("all", norm),
            ("all far", block_weight),
            ("date far", conv_out),
            ("date", halo_up),
            ("date", halo_down),
            ("all", first_norm),
            ("all", first_gain),
            ("all", first_shift),
        ],
        [
            ("date far", frame, BF16),
            ("date far", (dates, rows + 2, cols, width), BF16),
            ("all", (8, width), F32),
            ("all", (row_devs, 2 * dates, width), F32),
        ],
        [
            pltpu.VMEM((3 * width, 3 * width), BF16),
            pltpu.VMEM((2 * dates, width), F32),
            pltpu.VMEM((rows + 4, cols, width), BF16),
        ],
        9 * flops,
    )
    tails = exchange(sums, "rows")
    (block_rows,) = call(
        block_grad_kernel,
        dates,
        [("date far", hidden), ("date far", pre_grad), ("all far", key_part)],
        [("all far", (10 * width, width), BF16)],
        [pltpu.VMEM((3 * width, 3 * width), F32)],
        9 * flops,
    )
    tails, block_rows = lax.optimization_barrier((tails, block_rows))
    conv_count = 9 * pair_width // 2 + 32
    half_rows = padded_count(10 * width + conv_count, devices) // 2
    keep, give = call(
        functools.partial(conv_grad_kernel, norm_count=norm_count),
        dates,
        [
            ("date far", paired),
            ("date", above),
            ("all", inner),
            ("all", outer),
            ("scalar", place),
            ("date far", conv_out),
            ("date far", linear_grad),
            ("all", tails),
            ("all", first_norm),
            ("all", first_gain),
            ("all", first_vectors),
            ("all", vectors),
            ("all far", block_rows),
            ("scalar", turn),
        ],
        [("all", (half_rows, width), BF16)] * 2,
        [
            pltpu.VMEM((2 * dates, width), F32),
            pltpu.VMEM((3 * pair_width, 2 * width), F32),
            pltpu.VMEM((2 * half_rows, width), BF16),
            pltpu.VMEM(inner.shape, BF16),
            pltpu.VMEM(inner.shape, BF16),
        ],
        6 * flops,
    )
    rows_half = (keep.astype(F32) + other_core(give).astype(F32)).astype(BF16)
    pieces = scatter(rows_half)
    attended, _ = lax.optimization_barrier((attended, rows_half))
    attended = sum_of_parts(attended)
    rows_half = collect(pieces)
    rows_other = other_core(rows_half)
    shapes = [
        (9 * pair_width // 2, width),
        (9 * width, width),
        (heads * depth, width),
        (depth, heads),
    ] + [(1, width)] * 4
    conv_total, block_total, key_total, query_total, *totals = pl.pallas_call(
        functools.partial(final_kernel, depth),
        in_specs=[
            pl.BlockSpec(memory_space=pltpu.SMEM),
            pl.BlockSpec(memory_space=pltpu.VMEM),
            pl.BlockSpec(memory_space=pltpu.VMEM),
        ],
        out_shape=[jax.ShapeDtypeStruct(shape, F32) for shape in shapes],
        scratch_shapes=[pltpu.VMEM((2 * half_rows, width), BF16)],
        compiler_params=pltpu.CompilerParams(vmem_limit_bytes=16 * MIB),
    )(turn, rows_half, rows_other)
    totals = [total.reshape(width) for total in totals]
    return (
        attended,
        conv_total.reshape(conv_weight.shape),
        totals[0],
        totals[1],
        block_total.reshape(block_weight.shape),
        totals[2],
        totals[3],
        key_total.T,
        query_total.T,
    )


def solution(mesh):
    return jax.shard_map(
        local,
        mesh=mesh,
        in_specs=(
            P("dates", "rows", None, None),
            P(),
            P(None, "rows", "dates"),
            P("rows", "dates", None),
            P(),
            P(),
            P(),
            P(),
            P(),
            P(),
            P(),
            P(),
        ),
        out_specs=(P("rows", "dates", None), P(), P(), P(), P(), P(), P(), P(), P()),
        check_vma=False,
    )
```

```python
import functools
import math

import jax
import jax.numpy as jnp
from jax import lax
from jax.experimental import pallas as pl
from jax.experimental.pallas import tpu as pltpu
from jax.sharding import PartitionSpec as P

GROUPS = 4


EPS = 1e-05


MIB = 1 << 20


F32 = jnp.float32


BF16 = jnp.bfloat16


def product(left, right, left_dim, right_dim):
    return lax.dot_general(
        left, right, (((left_dim,), (right_dim,)), ((), ())), preferred_element_type=F32
    )


def group_sum(values):
    width = values.shape[-1]
    lane_group = lax.broadcasted_iota(jnp.int32, values.shape, 1) // (width // GROUPS)
    spread = jnp.zeros_like(values)
    for group in range(GROUPS):
        inside = lane_group == group
        total = jnp.sum(jnp.where(inside, values, 0.0), axis=1, keepdims=True)
        spread = spread + jnp.where(inside, total, 0.0)
    return spread


def sigmoid(values):
    return 0.5 * jnp.tanh(0.5 * values) + 0.5


def from_left(values):
    column = lax.broadcasted_iota(jnp.int32, values.shape, 1)
    return jnp.where(column > 0, pltpu.roll(values, 1, 1), 0.0)


def from_right(values):
    count = values.shape[1]
    column = lax.broadcasted_iota(jnp.int32, values.shape, 1)
    return jnp.where(column < count - 1, pltpu.roll(values, count - 1, 1), 0.0)


def column_sum(values):
    return jnp.sum(jnp.sum(values, axis=0), axis=0, keepdims=True)


def edges(place_ref, row_devs):
    place = place_ref[0]
    return (place > 0).astype(F32), (place < row_devs - 1).astype(F32)


def head_spread(width):
    lane = lax.broadcasted_iota(jnp.int32, (2 * width, width), 1) // (width // 16)
    head = lax.broadcasted_iota(jnp.int32, (2 * width, width), 0) % width // (width // 16)
    return (lane == head).astype(F32).astype(BF16)


def split(values):
    high = values.astype(BF16)
    return high, (values - high.astype(F32)).astype(BF16)


def store_sums(sums_ref, date, dates, first, second):
    for copy in range(sums_ref.shape[0]):
        sums_ref[copy, pl.ds(date, 1), :] = first
        sums_ref[copy, pl.ds(dates + date, 1), :] = second


def norm_table(sums_ref, table_ref, dates, norm_count):
    means = group_sum(jnp.sum(sums_ref[...], axis=0)) / norm_count
    mean = means[:dates]
    table_ref[:dates] = mean
    table_ref[dates:] = 1.0 / jnp.sqrt(means[dates:] - mean * mean + EPS)


def down_table(weight_ref, table):
    half = weight_ref.shape[2]
    for tap in range(3):
        base = tap * 2 * half
        table[base : base + half, : 2 * half] = weight_ref[tap, 1]
        table[base + half : base + 2 * half, : 2 * half] = weight_ref[tap, 2]
        table[base : base + half, 2 * half :] = jnp.zeros_like(weight_ref[tap, 0])
        table[base + half : base + 2 * half, 2 * half :] = weight_ref[tap, 0]


def down_rows(taps, table):
    rows, cols, width = taps[0].shape
    taps = jnp.concatenate(taps, axis=-1).reshape(rows * cols, 3 * width)
    both = product(taps, table[...], 1, 0).reshape(rows, cols, 2 * width)
    return (both[..., :width] + from_left(both[..., width:])).astype(BF16)


def down_kernel(
    date, dates, img_ref, above_ref, weight_ref, out_ref, sums_ref, table
):

    if date == 0:
        down_table(weight_ref, table)

    even, odd = img_ref[0, :, 0], img_ref[0, :, 1]
    above = jnp.concatenate([above_ref[0][None], odd[:-1]], axis=0)
    stored = down_rows([above, even, odd], table)
    out_ref[0] = stored
    values = stored.astype(F32)
    store_sums(sums_ref, date, dates, column_sum(values), column_sum(values * values))


def sort_halos(place_ref, inner_ref, outer_ref, high_ref, below_ref):
    odd = place_ref[0] % 2 == 1

    @pl.when(odd)
    def _():
        high_ref[...] = inner_ref[...]
        below_ref[...] = outer_ref[...]

    @pl.when(jnp.logical_not(odd))
    def _():
        high_ref[...] = outer_ref[...]
        below_ref[...] = inner_ref[...]


def load_kernel(
    place_ref,
    last_ref,
    img_hbm,
    grad_hbm,
    valid_hbm,
    img_ref,
    inner_ref,
    outer_ref,
    packed_ref,
    valid_ref,
    ready,
):
    blocks = grad_hbm.shape[0]
    moves = [
        pltpu.make_async_copy(grad_hbm, packed_ref.at[pl.ds(0, blocks)], ready.at[0]),
        pltpu.make_async_copy(valid_hbm, valid_ref, ready.at[1]),
        pltpu.make_async_copy(img_hbm, img_ref, ready.at[2]),
    ]
    for move in moves:
        move.start()
    for move in moves:
        move.wait()
    rows = img_ref.shape[1]
    odd = place_ref[0] % 2 == 1

    @pl.when(odd)
    def _():
        inner_ref[...] = img_ref[:, :2]
        outer_ref[...] = img_ref[:, rows - 3 : rows - 1]

    @pl.when(jnp.logical_not(odd))
    def _():
        inner_ref[...] = img_ref[:, rows - 3 : rows - 1]
        outer_ref[...] = img_ref[:, :2]

    piece, width = packed_ref.shape[1:]
    dates, rows, cols = valid_ref.shape
    values = valid_ref[...].astype(F32).reshape(dates * rows, cols)
    values = jnp.concatenate([values, jnp.zeros((dates * rows, width - cols), F32)], axis=1)
    packed_ref[blocks:] = values.astype(BF16).reshape(-1, piece, width)


def edge_kernel(
    step,
    steps,
    place_ref,
    inner_ref,
    outer_ref,
    above_ref,
    last_ref,
    weight_ref,
    up_ref,
    down_ref,
    table,
    high_ref,
    below_ref,
):
    dates = above_ref.shape[0]
    sort_halos(place_ref, inner_ref, outer_ref, high_ref, below_ref)
    down_table(weight_ref, table)
    taps = [
        jnp.concatenate([high_ref[:, 0], last_ref[...]], axis=0),
        jnp.concatenate([high_ref[:, 1], below_ref[:, 0]], axis=0),
        jnp.concatenate([above_ref[...], below_ref[:, 1]], axis=0),
    ]
    stored = down_rows(taps, table)
    up_ref[...] = stored[:dates]
    down_ref[...] = stored[dates:]


def activate_rows(date, dates, edge_flags, conv_refs, norm_refs, hidden_ref):
    conv_ref, up_ref, down_ref = conv_refs
    norm_ref, gain_ref, shift_ref = norm_refs
    scale = norm_ref[pl.ds(dates + date, 1), :] * gain_ref[...]
    shift = shift_ref[...] - norm_ref[pl.ds(date, 1), :] * scale

    def activate(values):
        linear = values.astype(F32) * scale + shift
        return linear * sigmoid(linear)

    rows = conv_ref.shape[1]
    hidden_ref[0, 0] = (activate(up_ref[0]) * edge_flags[0]).astype(BF16)
    hidden_ref[0, rows + 1] = (activate(down_ref[0]) * edge_flags[1]).astype(BF16)
    hidden_ref[0, 1 : rows + 1] = activate(conv_ref[0]).astype(BF16)


def block_kernel(
    date,
    dates,
    edge_ref,
    conv_ref,
    up_ref,
    down_ref,
    stats_ref,
    gain_ref,
    shift_ref,
    weight_ref,
    out_ref,
    norm_ref,
    sums_ref,
    table,
    hidden_ref,
    *,
    norm_count,
    row_devs,
):
    width = conv_ref.shape[-1]

    if date == 0:
        norm_table(stats_ref, norm_ref, dates, norm_count)
        for row_tap in range(3):
            for col_tap in range(3):
                table[
                    row_tap * width : (row_tap + 1) * width, col_tap * width : (col_tap + 1) * width
                ] = weight_ref[row_tap, col_tap]

    rows, cols = conv_ref.shape[1:3]
    activate_rows(
        date,
        dates,
        edges(edge_ref, row_devs),
        (conv_ref, up_ref, down_ref),
        (norm_ref, gain_ref, shift_ref),
        hidden_ref,
    )
    taps = jnp.concatenate(
        [hidden_ref[0, tap : tap + rows] for tap in range(3)], axis=-1
    ).reshape(rows * cols, 3 * width)
    terms = product(taps, table[...], 1, 0).reshape(rows, cols, 3 * width)
    stored = (
        terms[..., width : 2 * width]
        + from_left(terms[..., :width])
        + from_right(terms[..., 2 * width :])
    ).astype(BF16)
    out_ref[0] = stored
    values = stored.astype(F32)
    store_sums(sums_ref, date, dates, column_sum(values), column_sum(values * values))


def encoding(day, width):
    lane = lax.broadcasted_iota(jnp.int32, (1, width), 1)
    frequency = jnp.exp((lane // 2).astype(F32) * (-2.0 * math.log(1000.0) / width))
    angles = day.astype(F32) * frequency
    return jnp.where(lane % 2 == 0, jnp.sin(angles), jnp.cos(angles))


def fold_keys(key_ref, query_ref, wide_ref, vector_ref, spread_ref, score_ref):
    depth, heads = query_ref.shape
    width = key_ref.shape[1]
    lanes = width // heads
    spread_ref[...] = head_spread(width)
    row = lax.broadcasted_iota(jnp.int32, (heads * depth, width), 0)
    lane = lax.broadcasted_iota(jnp.int32, (heads * depth, width), 1)
    widen = (row // depth == lane // lanes) & (row % depth == lane % lanes)
    wide = product(key_ref[...], widen.astype(F32).astype(BF16), 0, 0)
    wide_ref[...] = wide.astype(BF16)
    head = lax.broadcasted_iota(jnp.int32, (heads, width), 0)
    lane = lax.broadcasted_iota(jnp.int32, (heads, width), 1)
    inside = (lane // lanes == head).astype(F32).astype(BF16)
    high, low = split(query_ref[...])
    lower = (query_ref[...] - high.astype(F32) - low.astype(F32)).astype(BF16)
    spread = sum(product(part, inside, 1, 0) for part in (high, low, lower))
    step = lax.broadcasted_iota(jnp.int32, (depth, width), 0)
    place = lax.broadcasted_iota(jnp.int32, (depth, width), 1) % lanes
    queries = jnp.sum(jnp.where(step == place, spread * depth**-0.5, 0.0), axis=0, keepdims=True)
    place = lax.broadcasted_iota(jnp.int32, (1, width), 1) % lanes
    queries = queries + jnp.where((place == depth) | (place == depth + 1), 1.0, 0.0)
    vector_ref[...] = jnp.broadcast_to(queries, vector_ref.shape)
    folded = jnp.concatenate(split(wide * queries), axis=-1)
    folded = product(folded, spread_ref[...], 1, 0)
    score_ref[...] = jnp.concatenate(split(folded), axis=-1)


def source_of(turn_ref, device, devices):
    half = devices // 2
    core = (device + turn_ref[0]) % 2
    return core * half + (device // 2 + half - turn_ref[0] // 2) % half


def upstream_rows(grad_ref, turn_ref, rows, cols):
    devices = grad_ref.shape[0]
    piece = cols // devices
    parts = [
        grad_ref[source_of(turn_ref, device, devices), : rows * piece].reshape(rows, piece, -1)
        for device in range(devices)
    ]
    return jnp.concatenate(parts, axis=1)


def score_kernel(
    date,
    dates,
    day_ref,
    block_ref,
    stats_ref,
    gain_ref,
    shift_ref,
    grad_ref,
    valid_ref,
    turn_ref,
    key_ref,
    query_ref,
    feat_ref,
    exp_ref,
    attn_ref,
    norm_ref,
    packed_ref,
    own_ref,
    wide_ref,
    vector_ref,
    total,
    mean,
    spread_ref,
    score_ref,
    *,
    norm_count,
    grad_scale,
):
    rows, cols, width = block_ref.shape[1:]

    if date == 0:
        norm_table(stats_ref, norm_ref, dates, norm_count)
        fold_keys(key_ref, query_ref, wide_ref, vector_ref, spread_ref, score_ref)
        total[...] = jnp.zeros_like(total)
        mean[...] = jnp.zeros_like(mean)

    scale = norm_ref[pl.ds(dates + date, 1), :] * gain_ref[...]
    shift = shift_ref[...] - norm_ref[pl.ds(date, 1), :] * scale
    linear = block_ref[0].astype(F32) * scale + shift
    features = (linear * sigmoid(linear) + encoding(day_ref[turn_ref[0] * dates + date], width)).astype(BF16)
    feat_ref[0] = features
    upstream = upstream_rows(grad_ref, turn_ref, rows, cols)
    parts = split(upstream.astype(F32) * features.astype(F32))
    parts = jnp.concatenate(parts, axis=-1).reshape(rows * cols, 2 * width)
    attn = product(parts, spread_ref[...], 1, 0).reshape(rows, cols, width) * grad_scale
    both = product(features.reshape(rows * cols, width), score_ref[...], 1, 0)
    scores = (both[:, :width] + both[:, width:]).reshape(rows, cols, width)
    devices = grad_ref.shape[0]
    valid = jnp.zeros((rows, width), F32)
    for device in range(devices):
        piece = valid_ref[
            source_of(turn_ref, device, devices), pl.ds(date * rows, rows), :
        ]
        valid = valid + pltpu.roll(piece, device * (cols // devices), 1)
    diagonal = lax.broadcasted_iota(jnp.int32, (cols, cols), 0) == lax.broadcasted_iota(
        jnp.int32, (cols, cols), 1
    )
    ones = jnp.ones((cols, width), BF16)
    clear = jnp.concatenate(
        [jnp.where(diagonal, valid[row : row + 1], 0.0) for row in range(rows)], axis=0
    ).astype(BF16)
    clear = product(clear, ones, 1, 0).reshape(rows, cols, width)
    exponent = clear * jnp.exp(scores)
    running = total[...] + exponent
    share = jnp.where(running > 0.0, exponent / running, 0.0)
    total[...] = running
    mean[...] += share * (attn - mean[...])
    exp_ref[0] = exponent
    attn_ref[0] = attn

    if date == dates - 1:
        place = lax.broadcasted_iota(jnp.int32, (cols, width), 1) % rows
        for index, source in enumerate((total, mean)):
            dense = jnp.zeros((cols, width), F32)
            for row in range(rows):
                dense = dense + jnp.where(place == row, source[row], 0.0)
            if index == 0:
                packed_ref[0, 0] = dense.astype(BF16)
                own_ref[...] = dense
            else:
                packed_ref[0, 1], packed_ref[0, 2] = split(dense)


def attend_kernel(
    date,
    dates,
    packed_ref,
    own_ref,
    feat_ref,
    exp_ref,
    attn_ref,
    block_ref,
    norm_ref,
    gain_ref,
    shift_ref,
    query_ref,
    grad_ref,
    turn_ref,
    key_ref,
    grad_out_ref,
    part_ref,
    key_out_ref,
    vector_ref,
    sums_ref,
    inverse,
    average,
    attended,
    *,
    grad_scale,
):
    rows, cols, width = block_ref.shape[1:]

    if date == 0:
        totals = packed_ref[:, 0].astype(F32)
        reciprocal = 1.0 / jnp.sum(totals, axis=0)
        means = packed_ref[:, 1].astype(F32) + packed_ref[:, 2].astype(F32)
        mean = jnp.sum(totals * reciprocal * means, axis=0)
        own = own_ref[...]
        sent = own.astype(BF16).astype(F32)
        reciprocal = reciprocal * jnp.where(own > 0.0, sent / own, 0.0)
        place = lax.broadcasted_iota(jnp.int32, (cols, width), 1) % rows
        for values, target in ((reciprocal, inverse), (mean, average)):
            parts = jnp.concatenate(split(values), axis=-1)
            wide_place = jnp.concatenate([place, place], axis=-1)
            picked = jnp.concatenate(
                [jnp.where(wide_place == row, parts, jnp.zeros_like(parts)) for row in range(rows)], axis=0
            )
            target[...] = product(picked, head_spread(width), 1, 0).reshape(rows, cols, width)
        attended[...] = jnp.zeros_like(attended)
        key_out_ref[...] = jnp.zeros_like(key_out_ref)
        vector_ref[...] = jnp.zeros_like(vector_ref)

    features = feat_ref[0]
    weights = exp_ref[0] * inverse[...]
    rounded = weights.astype(BF16).astype(F32)
    attended[...] += rounded * features.astype(F32)
    score_grad = weights * (attn_ref[0] - average[...])
    spread_grad = score_grad * query_ref[0:1]
    rest = spread_grad - spread_grad.astype(BF16).astype(F32)
    lane = lax.broadcasted_iota(jnp.int32, spread_grad.shape, 2) % (width // 16)
    key_grads = jnp.where(lane == 5, rest, spread_grad).astype(BF16).reshape(rows * cols, width)
    key_out_ref[...] += product(features.reshape(rows * cols, width), key_grads, 0, 0)
    upstream = upstream_rows(grad_ref, turn_ref, rows, cols)
    feat_grad = rounded * (upstream.astype(F32) * grad_scale) + product(
        key_grads, key_ref[...], 1, 1
    ).reshape(rows, cols, width)
    gain = gain_ref[...]
    centred = (block_ref[0].astype(F32) - norm_ref[pl.ds(date, 1), :]) * norm_ref[
        pl.ds(dates + date, 1), :
    ]
    linear = centred * gain + shift_ref[...]
    part = sigmoid(linear)
    linear_grad = feat_grad * (part * (1.0 + linear * (1.0 - part)))
    first = column_sum(linear_grad)
    second = column_sum(linear_grad * centred)
    vector_ref[0:1] += second
    vector_ref[1:2] += first
    store_sums(sums_ref, date, dates, first * gain, second * gain)
    grad_out_ref[0] = (linear_grad * gain).astype(BF16)

    if date == dates - 1:
        devices, piece = part_ref.shape[0], part_ref.shape[2]
        for device in range(devices):
            part_ref[device] = attended[:, device * piece : (device + 1) * piece].astype(BF16)
        key_part = key_out_ref[...]
        place = lax.broadcasted_iota(jnp.int32, (width, width), 1) % (width // 16)
        both = pltpu.roll(key_part, width - 4, 1) + pltpu.roll(key_part, width - 5, 1)
        both = jnp.where(place == 0, both, 0.0)
        both = both + pltpu.roll(both, 1, 1)
        both = both + pltpu.roll(both, 2, 1)
        vector_ref[2:3] = 0.5 * jnp.sum(key_ref[...].astype(F32) * both, axis=0, keepdims=True)


def hidden_kernel(
    date,
    dates,
    edge_ref,
    grad_ref,
    block_ref,
    tails_ref,
    norm_ref,
    weight_ref,
    conv_ref,
    up_ref,
    down_ref,
    first_norm_ref,
    gain_ref,
    shift_ref,
    pre_ref,
    out_ref,
    vector_ref,
    sums_ref,
    table,
    factors,
    padded,
    *,
    norm_count,
    row_devs,
):
    rows, cols, width = block_ref.shape[1:]

    if date == 0:
        tails = group_sum(jnp.sum(tails_ref[...], axis=0)) / norm_count
        mean, inverse = norm_ref[:dates], norm_ref[dates:]
        slope = -inverse * inverse * tails[dates:]
        factors[0:dates] = slope
        factors[dates : 2 * dates] = -inverse * tails[:dates] - mean * slope
        vector_ref[...] = jnp.zeros_like(vector_ref)
        padded[:2] = jnp.zeros_like(padded[:2])
        padded[rows + 2 :] = jnp.zeros_like(padded[rows + 2 :])
        for row_tap in range(3):
            for col_tap in range(3):
                table[
                    col_tap * width : (col_tap + 1) * width, row_tap * width : (row_tap + 1) * width
                ] = weight_ref[2 - row_tap, col_tap]

    inverse = norm_ref[pl.ds(dates + date, 1), :]
    slope = factors[pl.ds(date, 1), :]
    constant = factors[pl.ds(dates + date, 1), :]

    above_edge, below_edge = edges(edge_ref, row_devs)
    stored = (
        grad_ref[0].astype(F32) * inverse + (block_ref[0].astype(F32) * slope + constant)
    ).astype(BF16)
    pre_ref[0] = stored
    padded[2 : rows + 2] = stored
    reach = rows + 2
    taps = jnp.concatenate([padded[tap : tap + reach] for tap in range(3)], axis=-1).reshape(
        reach * cols, 3 * width
    )
    terms = product(taps, table[...], 1, 1).reshape(reach, cols, 3 * width)
    hidden_grad = (
        terms[..., width : 2 * width]
        + from_right(terms[..., :width])
        + from_left(terms[..., 2 * width :])
    )
    gain = gain_ref[...]
    conv = jnp.concatenate([up_ref[0][None], conv_ref[0], down_ref[0][None]], axis=0)
    centred = (conv.astype(F32) - first_norm_ref[pl.ds(date, 1), :]) * first_norm_ref[
        pl.ds(dates + date, 1), :
    ]
    linear = centred * gain + shift_ref[...]
    part = sigmoid(linear)
    linear_grad = hidden_grad * (part * (1.0 + linear * (1.0 - part)))
    linear_grad = jnp.concatenate(
        [
            linear_grad[:1] * above_edge,
            linear_grad[1 : rows + 1],
            linear_grad[rows + 1 :] * below_edge,
        ],
        axis=0,
    )
    out_ref[0] = linear_grad.astype(BF16)
    first = column_sum(linear_grad)
    second = column_sum(linear_grad * centred)
    vector_ref[0:1] += second
    vector_ref[1:2] += first
    store_sums(sums_ref, date, dates, first * gain, second * gain)


def block_grad_kernel(
    date,
    dates,
    edge_ref,
    conv_ref,
    up_ref,
    down_ref,
    norm_ref,
    gain_ref,
    shift_ref,
    pre_ref,
    key_ref,
    out_ref,
    total,
    hidden_ref,
    *,
    row_devs,
):
    rows, cols, width = pre_ref.shape[1:]

    if date == 0:
        total[...] = jnp.zeros_like(total)

    activate_rows(
        date,
        dates,
        edges(edge_ref, row_devs),
        (conv_ref, up_ref, down_ref),
        (norm_ref, gain_ref, shift_ref),
        hidden_ref,
    )
    grads = pre_ref[0].astype(F32)
    grads = jnp.concatenate(
        [from_right(grads).astype(BF16), pre_ref[0], from_left(grads).astype(BF16)], axis=-1
    ).reshape(rows * cols, 3 * width)
    taps = jnp.concatenate(
        [hidden_ref[0, tap : tap + rows] for tap in range(3)], axis=-1
    ).reshape(rows * cols, 3 * width)
    total[...] += product(taps, grads, 0, 0)

    if date == dates - 1:
        for row_tap in range(3):
            for col_tap in range(3):
                base = (row_tap * 3 + col_tap) * width
                out_ref[base : base + width] = total[
                    row_tap * width : (row_tap + 1) * width, col_tap * width : (col_tap + 1) * width
                ].astype(BF16)
        key_part = key_ref[...]
        rest = key_part - key_part.astype(BF16).astype(F32)
        lanes = width // 16
        place = lax.broadcasted_iota(jnp.int32, key_part.shape, 1) % lanes
        rest = pltpu.roll(rest, lanes // 2, 1)
        key_rows = jnp.where(place < lanes // 2, key_part, rest).astype(BF16)
        out_ref[9 * width : 10 * width] = key_rows
        if out_ref.shape[0] > 10 * width:
            out_ref[10 * width :] = jnp.zeros_like(out_ref[10 * width :])


def conv_grad_kernel(
    date,
    dates,
    img_ref,
    above_ref,
    inner_ref,
    outer_ref,
    place_ref,
    conv_ref,
    grad_ref,
    tails_ref,
    norm_ref,
    gain_ref,
    vector_ref,
    other_ref,
    block_rows_ref,
    turn_ref,
    keep_ref,
    give_ref,
    factors,
    total,
    out_ref,
    high_ref,
    below_ref,
    *,
    norm_count,
):
    rows, cols, width = conv_ref.shape[1:]
    half = width // 2

    if date == 0:
        sort_halos(place_ref, inner_ref, outer_ref, high_ref, below_ref)
        tails = group_sum(jnp.sum(tails_ref[...], axis=0)) / norm_count
        mean, inverse = norm_ref[:dates], norm_ref[dates:]
        slope = -inverse * inverse * tails[dates:]
        factors[0:dates] = slope
        factors[dates : 2 * dates] = -inverse * tails[:dates] - mean * slope
        total[...] = jnp.zeros_like(total)

    scale = norm_ref[pl.ds(dates + date, 1), :] * gain_ref[...]
    slope = factors[pl.ds(date, 1), :]
    constant = factors[pl.ds(dates + date, 1), :]
    own = conv_ref[0].astype(F32) * slope + constant
    scaled = grad_ref[0].astype(F32) * scale
    stored = jnp.concatenate(
        [scaled[:1], scaled[1 : rows + 1] + own, scaled[rows + 1 :]], axis=0
    ).astype(BF16)
    moved = from_right(stored.astype(F32)).astype(BF16)
    reach = rows + 2
    grads = jnp.concatenate([stored, moved], axis=-1).reshape(reach * cols, 2 * width)
    even, odd = img_ref[0, :, 0], img_ref[0, :, 1]
    above = above_ref[0][None]
    taps = [
        jnp.concatenate([high_ref[date, :1], above, odd], axis=0),
        jnp.concatenate([high_ref[date, 1:], even, below_ref[date, :1]], axis=0),
        jnp.concatenate([above, odd, below_ref[date, 1:]], axis=0),
    ]
    taps = jnp.concatenate(taps, axis=-1).reshape(reach * cols, 3 * width)
    total[...] += product(taps, grads, 0, 0)

    if date == dates - 1:
        begin = block_rows_ref.shape[0]
        out_ref[:begin] = block_rows_ref[...]
        for tap in range(3):
            base = tap * width
            pair = total[base : base + width, :width].astype(BF16)
            left = total[base + half : base + width, width:].astype(BF16)
            start = begin + tap * 3 * half
            out_ref[start : start + half] = left
            out_ref[start + half : start + 3 * half] = pair
        start = begin + 9 * half
        for source in (vector_ref, other_ref):
            high, low = split(source[...])
            out_ref[start : start + 16] = jnp.concatenate([high, low], axis=0)
            start += 16
        if out_ref.shape[0] > start:
            out_ref[start:] = jnp.zeros_like(out_ref[start:])
        half_rows = keep_ref.shape[0]
        core = turn_ref[0] % 2
        start = pl.multiple_of(core * half_rows, half_rows)
        keep_ref[...] = out_ref[pl.ds(start, half_rows), :]
        start = pl.multiple_of((1 - core) * half_rows, half_rows)
        give_ref[...] = out_ref[pl.ds(start, half_rows), :]


def total_kernel(in_ref, out_ref):
    total = jnp.sum(in_ref[...].astype(F32), axis=0).astype(BF16)
    for copy in range(out_ref.shape[0]):
        out_ref[copy] = total


def final_kernel(
    depth,
    turn_ref,
    own_ref,
    other_ref,
    conv_ref,
    block_ref,
    key_ref,
    query_ref,
    *refs,
):
    vector_refs, rows_ref = refs[:-1], refs[-1]
    half_rows = own_ref.shape[0]
    core = turn_ref[0] % 2
    rows_ref[pl.ds(pl.multiple_of(core * half_rows, half_rows), half_rows), :] = own_ref[...]
    start = pl.multiple_of((1 - core) * half_rows, half_rows)
    rows_ref[pl.ds(start, half_rows), :] = other_ref[...]
    conv_end, block_end, width = conv_ref.shape[0], block_ref.shape[0], block_ref.shape[1]
    block_ref[...] = rows_ref[:block_end].astype(F32)
    wide = key_ref.shape[0]
    heads = wide // depth
    lanes = width // heads
    row = lax.broadcasted_iota(jnp.int32, (wide, width), 0)
    lane = lax.broadcasted_iota(jnp.int32, (wide, width), 1)
    narrow = (row // depth == lane // lanes) & (row % depth == lane % depth)
    narrow = narrow.astype(F32).astype(BF16)
    key_ref[...] = product(narrow, rows_ref[block_end : block_end + width], 1, 1)
    start = block_end + width
    conv_ref[...] = rows_ref[start : start + conv_end].astype(F32)
    start += conv_end
    for index in range(2):
        both = rows_ref[start : start + 16].astype(F32)
        both = both[:8] + both[8:]
        vector_refs[2 * index][...] = both[0:1]
        vector_refs[2 * index + 1][...] = both[1:2]
        start += 16
    both = rows_ref[start - 16 : start]
    row = lax.broadcasted_iota(jnp.int32, (heads, width), 0)
    lane = lax.broadcasted_iota(jnp.int32, (heads, width), 1)
    inside = row == lane // lanes
    step = lax.broadcasted_iota(jnp.int32, (8, width), 0)
    place = lax.broadcasted_iota(jnp.int32, (8, width), 1) % lanes
    steps = step == place
    query = jnp.zeros((8, heads), F32)
    for index in (2, 10):
        picked = jnp.where(steps, both[index : index + 1].astype(F32), 0.0).astype(BF16)
        query = query + product(picked, inside.astype(F32).astype(BF16), 1, 1)
    query_ref[...] = query[:depth]


def call(kernel, dates, inputs, outputs, scratch, flops):
    in_specs, out_specs, arrays, out_shape, buffers = [], [], [], [], []
    in_vmem, in_hbm = pl.BlockSpec(memory_space=pltpu.VMEM), pl.BlockSpec(memory_space=pltpu.HBM)
    loads, stores = [], []
    for place, (kind, array) in enumerate(inputs):
        if kind == "scalar":
            in_specs.append(pl.BlockSpec(memory_space=pltpu.SMEM))
        elif "far" in kind:
            array = pltpu.with_memory_space_constraint(array, pltpu.HBM)
            in_specs.append(in_hbm)
            loads.append(place)
            buffers.append(pltpu.VMEM(array.shape, array.dtype))
        else:
            in_specs.append(in_vmem)
        arrays.append(array)
    for place, (kind, shape, dtype) in enumerate(outputs):
        if "far" in kind:
            out_shape.append(pltpu.HBM(shape, dtype))
            out_specs.append(in_hbm)
            stores.append(place)
            buffers.append(pltpu.VMEM(shape, dtype))
        else:
            out_shape.append(jax.ShapeDtypeStruct(shape, dtype))
            out_specs.append(in_vmem)
    copies = len(loads) + len(stores)
    kinds = [kind for kind, _ in inputs] + [kind for kind, _, _ in outputs]

    def body(*refs):
        views, rest = list(refs[: len(kinds)]), refs[len(kinds) :]
        buffer_refs, ready, rest = rest[:copies], rest[copies], rest[copies + 1 :]

        def copies_of(place, index, inward):
            outside, inside = views[place], buffer_refs[index]
            made = []
            for date in range(dates if "date" in kinds[place] else 1):
                here = pl.ds(date, 1) if "date" in kinds[place] else slice(None)
                pair = (outside.at[here], inside.at[here])
                source, target = pair if inward else pair[::-1]
                made.append(pltpu.make_async_copy(source, target, ready.at[index, date]))
            return made

        incoming = [copies_of(place, index, True) for index, place in enumerate(loads)]
        outgoing = [
            copies_of(len(inputs) + place, len(loads) + index, False)
            for index, place in enumerate(stores)
        ]
        for date in range(dates):
            for moves in incoming:
                if date < len(moves):
                    moves[date].start()
        for index, place in enumerate(loads):
            views[place] = buffer_refs[index]
        for index, place in enumerate(stores):
            views[len(inputs) + place] = buffer_refs[len(loads) + index]
        for date in range(dates):
            for moves in incoming:
                if date < len(moves):
                    moves[date].wait()
            here = [
                view.at[pl.ds(date, 1)] if "date" in kind else view
                for view, kind in zip(views, kinds)
            ]
            kernel(date, dates, *here, *rest)
            for moves in outgoing:
                if len(moves) == dates:
                    moves[date].start()
                elif date == dates - 1:
                    moves[0].start()
        for moves in outgoing:
            for move in moves:
                move.wait()

    moved = sum(array.size * array.dtype.itemsize for _, array in inputs)
    return pl.pallas_call(
        body,
        in_specs=in_specs,
        out_specs=out_specs,
        out_shape=out_shape,
        scratch_shapes=buffers + [pltpu.SemaphoreType.DMA((max(copies, 1), dates))] + scratch,
        compiler_params=pltpu.CompilerParams(vmem_limit_bytes=40 * MIB),
        cost_estimate=pl.CostEstimate(flops=flops, bytes_accessed=2 * moved, transcendentals=0),
    )(*arrays)


def shifted(array, by):
    devices = lax.axis_size("rows")
    pairs = [(i, i + by) for i in range(devices) if 0 <= i + by < devices]
    return lax.ppermute(array, "rows", pairs)


def same_core(array):
    devices = lax.axis_size("dates")
    pieces = [array]
    for step in range(2, devices, 2):
        pairs = [((i + step) % devices, i) for i in range(devices)]
        pieces.append(lax.ppermute(array, "dates", pairs))
    return pieces


def sum_of_parts(parts):
    devices = lax.axis_size("dates")
    place = lax.axis_index("dates")
    total = lax.dynamic_index_in_dim(parts, place, 0, keepdims=False).astype(F32)
    for step in range(1, devices):
        piece = lax.dynamic_index_in_dim(parts, (place + step) % devices, 0, keepdims=False)
        pairs = [(i, (i + step) % devices) for i in range(devices)]
        total = total + lax.ppermute(piece, "dates", pairs).astype(F32)
    return total.astype(BF16)


def exchange(pieces, axes):
    return lax.all_to_all(pieces, axes, split_axis=0, concat_axis=0, tiled=True)


def gather(array, axis):
    return lax.all_gather(array, axis, axis=0, tiled=True)


def other_core(array):
    devices = lax.axis_size("dates")
    return lax.ppermute(array, "dates", [(i, i + 1 - 2 * (i % 2)) for i in range(devices)])


def exchange_cores(pieces):
    axes = ("rows", "dates")
    devices = lax.axis_size(axes)
    groups = [list(range(core, devices, 2)) for core in range(2)]
    return lax.all_to_all(
        pieces, axes, split_axis=0, concat_axis=0, axis_index_groups=groups, tiled=True
    )


def scatter(rows_array):
    devices = lax.axis_size(("rows", "dates")) // 2
    count, width = rows_array.shape
    return exchange_cores(rows_array.reshape(devices, count // devices, width))


def collect(pieces):
    spread = pl.pallas_call(
        total_kernel,
        out_shape=jax.ShapeDtypeStruct(pieces.shape, BF16),
        compiler_params=pltpu.CompilerParams(vmem_limit_bytes=16 * MIB),
    )(pieces)
    count, rows, width = pieces.shape
    return exchange_cores(spread).reshape(count * rows, width)


def padded_count(count, devices):
    step = 8 * devices
    return -(-count // step) * step


def local(
    images,
    day_index,
    valid,
    out_grad,
    conv_weight,
    first_gain,
    first_shift,
    block_weight,
    gn_gain,
    gn_shift,
    key_weight,
    queries,
):
    dates, rows_here, cols, pair_width = images.shape
    width = conv_weight.shape[-1]
    row_devs, date_devs = lax.axis_size("rows"), lax.axis_size("dates")
    devices = row_devs * date_devs
    rows = rows_here // 2
    heads, depth = queries.shape
    norm_count = float(rows * row_devs * cols * (width // GROUPS))
    grad_scale = float(rows * row_devs * cols) ** (-0.5)
    date_start = lax.axis_index("dates") * dates
    frame = (dates, rows, cols, width)
    edge_rows = (dates, cols, width)
    flops = 2 * dates * rows * cols * width * width

    rows_of = lambda vector: vector.reshape(1, width)
    first_gain, first_shift = rows_of(first_gain), rows_of(first_shift)
    gn_gain, gn_shift = rows_of(gn_gain), rows_of(gn_shift)
    last = images[:, -1]
    above = shifted(last, 1)
    grad_rows = out_grad.size // width
    row_place = lax.axis_index("rows")
    place = row_place.reshape(1)
    valid_count = valid.shape[0] * rows
    piece = out_grad.shape[1]
    packed_shape = ((grad_rows + valid_count) // piece, piece, width)
    in_hbm, in_vmem = pl.BlockSpec(memory_space=pltpu.HBM), pl.BlockSpec(memory_space=pltpu.VMEM)
    images_near, inner, outer, packed = pl.pallas_call(
        load_kernel,
        in_specs=[pl.BlockSpec(memory_space=pltpu.SMEM), in_vmem, in_hbm, in_hbm, in_hbm],
        out_specs=[in_vmem] * 4,
        out_shape=[
            jax.ShapeDtypeStruct(shape, BF16)
            for shape in (images.shape,) + ((dates, 2, cols, pair_width),) * 2 + (packed_shape,)
        ],
        scratch_shapes=[pltpu.VMEM(valid.shape, valid.dtype), pltpu.SemaphoreType.DMA((3,))],
        compiler_params=pltpu.CompilerParams(vmem_limit_bytes=16 * MIB),
    )(
        place,
        last,
        *[pltpu.with_memory_space_constraint(x, pltpu.HBM) for x in (images, out_grad, valid)],
    )
    packed = packed.reshape(grad_rows + valid_count, width)
    inner, outer, above, packed = lax.optimization_barrier((inner, outer, above, packed))
    inner = lax.ppermute(inner, "rows", [(i, i ^ 1) for i in range(row_devs)])
    pairs = [(i, i + 1) for i in range(1, row_devs - 1, 2)]
    outer = lax.ppermute(outer, "rows", pairs + [(j, i) for i, j in pairs])
    paired = images.reshape(dates, rows, 2, cols, pair_width)
    conv_out, sums = call(
        down_kernel,
        dates,
        [
            ("date", images_near.reshape(paired.shape)),
            ("date", above),
            ("all far", conv_weight),
        ],
        [("date far", frame, BF16), ("all", (row_devs, 2 * dates, width), F32)],
        [pltpu.VMEM((3 * pair_width, 2 * width), BF16)],
        6 * flops,
    )
    stats = exchange(sums, "rows")
    inner, outer, last, _ = lax.optimization_barrier((inner, outer, last, sums))
    halo_up, halo_down = call(
        edge_kernel,
        1,
        [
            ("scalar", place),
            ("all", inner),
            ("all", outer),
            ("all", above),
            ("all", last),
            ("all", conv_weight),
        ],
        [("all", edge_rows, BF16)] * 2,
        [
            pltpu.VMEM((3 * pair_width, 2 * width), BF16),
            pltpu.VMEM(inner.shape, BF16),
            pltpu.VMEM(inner.shape, BF16),
        ],
        6 * flops // rows,
    )
    turn = lax.axis_index("dates").reshape(1)
    packed, _ = lax.optimization_barrier((packed, halo_up))
    pieces = same_core(packed)
    block_out, first_norm, sums = call(
        functools.partial(block_kernel, norm_count=norm_count, row_devs=row_devs),
        dates,
        [
            ("scalar", place),
            ("date far", conv_out),
            ("date", halo_up),
            ("date", halo_down),
            ("all", stats),
            ("all", first_gain),
            ("all", first_shift),
            ("all far", block_weight),
        ],
        [
            ("date far", frame, BF16),
            ("all", (2 * dates, width), F32),
            ("all", (row_devs, 2 * dates, width), F32),
        ],
        [
            pltpu.VMEM((3 * width, 3 * width), BF16),
            pltpu.VMEM((1, rows + 2, cols, width), BF16),
        ],
        9 * flops,
    )
    stats = exchange(sums, "rows")
    pieces, _ = lax.optimization_barrier((pieces, sums))
    sources = jnp.stack(pieces + [other_core(piece) for piece in pieces])
    clear = lax.dynamic_slice_in_dim(sources, grad_rows + date_start * rows, dates * rows, 1)
    clear = clear.astype(F32)
    features, exponent, attn, norm, packed, own_total, key_wide, query_wide = call(
        functools.partial(score_kernel, norm_count=norm_count, grad_scale=grad_scale),
        dates,
        [
            ("scalar", day_index),
            ("date far", block_out),
            ("all", stats),
            ("all", gn_gain),
            ("all", gn_shift),
            ("all", sources),
            ("all", clear),
            ("scalar", turn),
            ("all", key_weight.T),
            ("all", queries.T),
        ],
        [
            ("date", frame, BF16),
            ("date", frame, F32),
            ("date", frame, F32),
            ("all", (2 * dates, width), F32),
            ("all", (1, 3, cols, width), BF16),
            ("all", (cols, width), F32),
            ("all", (width, width), BF16),
            ("all", (8, width), F32),
        ],
        [
            pltpu.VMEM(frame[1:], F32),
            pltpu.VMEM(frame[1:], F32),
            pltpu.VMEM((2 * width, width), BF16),
            pltpu.VMEM((width, 2 * width), BF16),
        ],
        5 * flops,
    )
    packed = gather(packed, "dates")
    block_grad, attended, key_part, vectors, sums = call(
        functools.partial(attend_kernel, grad_scale=grad_scale),
        dates,
        [
            ("all", packed),
            ("all", own_total),
            ("date", features),
            ("date", exponent),
            ("date", attn),
            ("date", block_out),
            ("all", norm),
            ("all", gn_gain),
            ("all", gn_shift),
            ("all", query_wide),
            ("all", sources),
            ("scalar", turn),
            ("all", key_wide),
        ],
        [
            ("date far", frame, BF16),
            ("all far", (date_devs, rows, cols // date_devs, width), BF16),
            ("all far", (width, width), F32),
            ("all", (8, width), F32),
            ("all", (row_devs, 2 * dates, width), F32),
        ],
        [pltpu.VMEM(frame[1:], F32)] * 3,
        5 * flops,
    )
    tails = exchange(sums, "rows")
    pre_grad, linear_grad, first_vectors, sums = call(
        functools.partial(hidden_kernel, norm_count=norm_count, row_devs=row_devs),
        dates,
        [
            ("scalar", place),
            ("date far", block_grad),
            ("date far", block_out),
            ("all", tails),
            ("all", norm),
            ("all far", block_weight),
            ("date far", conv_out),
            ("date", halo_up),
            ("date", halo_down),
            ("all", first_norm),
            ("all", first_gain),
            ("all", first_shift),
        ],
        [
            ("date far", frame, BF16),
            ("date far", (dates, rows + 2, cols, width), BF16),
            ("all", (8, width), F32),
            ("all", (row_devs, 2 * dates, width), F32),
        ],
        [
            pltpu.VMEM((3 * width, 3 * width), BF16),
            pltpu.VMEM((2 * dates, width), F32),
            pltpu.VMEM((rows + 4, cols, width), BF16),
        ],
        9 * flops,
    )
    tails = exchange(sums, "rows")
    (block_rows,) = call(
        functools.partial(block_grad_kernel, row_devs=row_devs),
        dates,
        [
            ("scalar", place),
            ("date far", conv_out),
            ("date", halo_up),
            ("date", halo_down),
            ("all", first_norm),
            ("all", first_gain),
            ("all", first_shift),
            ("date far", pre_grad),
            ("all far", key_part),
        ],
        [("all far", (10 * width, width), BF16)],
        [
            pltpu.VMEM((3 * width, 3 * width), F32),
            pltpu.VMEM((1, rows + 2, cols, width), BF16),
        ],
        9 * flops,
    )
    tails, block_rows = lax.optimization_barrier((tails, block_rows))
    conv_count = 9 * pair_width // 2 + 32
    half_rows = padded_count(10 * width + conv_count, devices) // 2
    keep, give = call(
        functools.partial(conv_grad_kernel, norm_count=norm_count),
        dates,
        [
            ("date far", paired),
            ("date", above),
            ("all", inner),
            ("all", outer),
            ("scalar", place),
            ("date far", conv_out),
            ("date far", linear_grad),
            ("all", tails),
            ("all", first_norm),
            ("all", first_gain),
            ("all", first_vectors),
            ("all", vectors),
            ("all far", block_rows),
            ("scalar", turn),
        ],
        [("all", (half_rows, width), BF16)] * 2,
        [
            pltpu.VMEM((2 * dates, width), F32),
            pltpu.VMEM((3 * pair_width, 2 * width), F32),
            pltpu.VMEM((2 * half_rows, width), BF16),
            pltpu.VMEM(inner.shape, BF16),
            pltpu.VMEM(inner.shape, BF16),
        ],
        6 * flops,
    )
    rows_half = (keep.astype(F32) + other_core(give).astype(F32)).astype(BF16)
    pieces = scatter(rows_half)
    attended, _ = lax.optimization_barrier((attended, rows_half))
    attended = sum_of_parts(attended)
    rows_half = collect(pieces)
    rows_other = other_core(rows_half)
    shapes = [
        (9 * pair_width // 2, width),
        (9 * width, width),
        (heads * depth, width),
        (depth, heads),
    ] + [(1, width)] * 4
    conv_total, block_total, key_total, query_total, *totals = pl.pallas_call(
        functools.partial(final_kernel, depth),
        in_specs=[
            pl.BlockSpec(memory_space=pltpu.SMEM),
            pl.BlockSpec(memory_space=pltpu.VMEM),
            pl.BlockSpec(memory_space=pltpu.VMEM),
        ],
        out_shape=[jax.ShapeDtypeStruct(shape, F32) for shape in shapes],
        scratch_shapes=[pltpu.VMEM((2 * half_rows, width), BF16)],
        compiler_params=pltpu.CompilerParams(vmem_limit_bytes=16 * MIB),
    )(turn, rows_half, rows_other)
    totals = [total.reshape(width) for total in totals]
    return (
        attended,
        conv_total.reshape(conv_weight.shape),
        totals[0],
        totals[1],
        block_total.reshape(block_weight.shape),
        totals[2],
        totals[3],
        key_total.T,
        query_total.T,
    )


def solution(mesh):
    return jax.shard_map(
        local,
        mesh=mesh,
        in_specs=(
            P("dates", "rows", None, None),
            P(),
            P(None, "rows", "dates"),
            P("rows", "dates", None),
            P(),
            P(),
            P(),
            P(),
            P(),
            P(),
            P(),
            P(),
        ),
        out_specs=(P("rows", "dates", None), P(), P(), P(), P(), P(), P(), P(), P()),
        check_vma=False,
    )
```

```python
import functools
import math

import jax
import jax.numpy as jnp
from jax import lax
from jax.experimental import pallas as pl
from jax.experimental.pallas import tpu as pltpu
from jax.sharding import PartitionSpec as P

GROUPS = 4


EPS = 1e-05


MIB = 1 << 20


F32 = jnp.float32


BF16 = jnp.bfloat16


def product(left, right, left_dim, right_dim):
    return lax.dot_general(
        left, right, (((left_dim,), (right_dim,)), ((), ())), preferred_element_type=F32
    )


def group_sum(values):
    width = values.shape[-1]
    lane_group = lax.broadcasted_iota(jnp.int32, values.shape, 1) // (width // GROUPS)
    spread = jnp.zeros_like(values)
    for group in range(GROUPS):
        inside = lane_group == group
        total = jnp.sum(jnp.where(inside, values, 0.0), axis=1, keepdims=True)
        spread = spread + jnp.where(inside, total, 0.0)
    return spread


def sigmoid(values):
    return 0.5 * jnp.tanh(0.5 * values) + 0.5


def from_left(values):
    column = lax.broadcasted_iota(jnp.int32, values.shape, 1)
    return jnp.where(column > 0, pltpu.roll(values, 1, 1), 0.0)


def from_right(values):
    count = values.shape[1]
    column = lax.broadcasted_iota(jnp.int32, values.shape, 1)
    return jnp.where(column < count - 1, pltpu.roll(values, count - 1, 1), 0.0)


def column_sum(values):
    return jnp.sum(jnp.sum(values, axis=0), axis=0, keepdims=True)


def edges(place_ref, row_devs):
    place = place_ref[0]
    return (place > 0).astype(F32), (place < row_devs - 1).astype(F32)


def head_spread(width):
    lane = lax.broadcasted_iota(jnp.int32, (2 * width, width), 1) // (width // 16)
    head = lax.broadcasted_iota(jnp.int32, (2 * width, width), 0) % width // (width // 16)
    return (lane == head).astype(F32).astype(BF16)


def split(values):
    high = values.astype(BF16)
    return high, (values - high.astype(F32)).astype(BF16)


def store_sums(sums_ref, date, dates, first, second):
    for copy in range(sums_ref.shape[0]):
        sums_ref[copy, pl.ds(date, 1), :] = first
        sums_ref[copy, pl.ds(dates + date, 1), :] = second


def norm_table(sums_ref, table_ref, dates, norm_count):
    means = group_sum(jnp.sum(sums_ref[...], axis=0)) / norm_count
    mean = means[:dates]
    table_ref[:dates] = mean
    table_ref[dates:] = 1.0 / jnp.sqrt(means[dates:] - mean * mean + EPS)


def down_table(weight_ref, table):
    half = weight_ref.shape[2]
    for tap in range(3):
        base = tap * 2 * half
        table[base : base + half, : 2 * half] = weight_ref[tap, 1]
        table[base + half : base + 2 * half, : 2 * half] = weight_ref[tap, 2]
        table[base : base + half, 2 * half :] = jnp.zeros_like(weight_ref[tap, 0])
        table[base + half : base + 2 * half, 2 * half :] = weight_ref[tap, 0]


def down_rows(taps, table):
    rows, cols, width = taps[0].shape
    taps = jnp.concatenate(taps, axis=-1).reshape(rows * cols, 3 * width)
    both = product(taps, table[...], 1, 0).reshape(rows, cols, 2 * width)
    return (both[..., :width] + from_left(both[..., width:])).astype(BF16)


def down_kernel(
    date, dates, img_ref, above_ref, weight_ref, out_ref, sums_ref, table
):

    if date == 0:
        down_table(weight_ref, table)

    even, odd = img_ref[0, :, 0], img_ref[0, :, 1]
    above = jnp.concatenate([above_ref[0][None], odd[:-1]], axis=0)
    stored = down_rows([above, even, odd], table)
    out_ref[0] = stored
    values = stored.astype(F32)
    store_sums(sums_ref, date, dates, column_sum(values), column_sum(values * values))


def sort_halos(place_ref, inner_ref, outer_ref, high_ref, below_ref):
    odd = place_ref[0] % 2 == 1

    @pl.when(odd)
    def _():
        high_ref[...] = inner_ref[...]
        below_ref[...] = outer_ref[...]

    @pl.when(jnp.logical_not(odd))
    def _():
        high_ref[...] = outer_ref[...]
        below_ref[...] = inner_ref[...]


def load_kernel(
    place_ref,
    last_ref,
    img_hbm,
    grad_hbm,
    valid_hbm,
    img_ref,
    inner_ref,
    outer_ref,
    packed_ref,
    valid_ref,
    ready,
):
    blocks = grad_hbm.shape[0]
    moves = [
        pltpu.make_async_copy(grad_hbm, packed_ref.at[pl.ds(0, blocks)], ready.at[0]),
        pltpu.make_async_copy(valid_hbm, valid_ref, ready.at[1]),
        pltpu.make_async_copy(img_hbm, img_ref, ready.at[2]),
    ]
    for move in moves:
        move.start()
    for move in moves:
        move.wait()
    rows = img_ref.shape[1]
    odd = place_ref[0] % 2 == 1

    @pl.when(odd)
    def _():
        inner_ref[...] = img_ref[:, :2]
        outer_ref[...] = img_ref[:, rows - 3 : rows - 1]

    @pl.when(jnp.logical_not(odd))
    def _():
        inner_ref[...] = img_ref[:, rows - 3 : rows - 1]
        outer_ref[...] = img_ref[:, :2]

    piece, width = packed_ref.shape[1:]
    dates, rows, cols = valid_ref.shape
    values = valid_ref[...].astype(F32).reshape(dates * rows, cols)
    values = jnp.concatenate([values, jnp.zeros((dates * rows, width - cols), F32)], axis=1)
    packed_ref[blocks:] = values.astype(BF16).reshape(-1, piece, width)


def edge_kernel(
    step,
    steps,
    place_ref,
    inner_ref,
    outer_ref,
    above_ref,
    last_ref,
    weight_ref,
    up_ref,
    down_ref,
    table,
    high_ref,
    below_ref,
):
    dates = above_ref.shape[0]
    sort_halos(place_ref, inner_ref, outer_ref, high_ref, below_ref)
    down_table(weight_ref, table)
    taps = [
        jnp.concatenate([high_ref[:, 0], last_ref[...]], axis=0),
        jnp.concatenate([high_ref[:, 1], below_ref[:, 0]], axis=0),
        jnp.concatenate([above_ref[...], below_ref[:, 1]], axis=0),
    ]
    stored = down_rows(taps, table)
    up_ref[...] = stored[:dates]
    down_ref[...] = stored[dates:]


def activate_rows(date, dates, edge_flags, conv_refs, norm_refs, hidden_ref):
    conv_ref, up_ref, down_ref = conv_refs
    norm_ref, gain_ref, shift_ref = norm_refs
    scale = norm_ref[pl.ds(dates + date, 1), :] * gain_ref[...]
    shift = shift_ref[...] - norm_ref[pl.ds(date, 1), :] * scale

    def activate(values):
        linear = values.astype(F32) * scale + shift
        return linear * sigmoid(linear)

    rows = conv_ref.shape[1]
    hidden_ref[0, 0] = (activate(up_ref[0]) * edge_flags[0]).astype(BF16)
    hidden_ref[0, rows + 1] = (activate(down_ref[0]) * edge_flags[1]).astype(BF16)
    hidden_ref[0, 1 : rows + 1] = activate(conv_ref[0]).astype(BF16)


def block_kernel(
    date,
    dates,
    edge_ref,
    conv_ref,
    up_ref,
    down_ref,
    stats_ref,
    gain_ref,
    shift_ref,
    weight_ref,
    out_ref,
    norm_ref,
    sums_ref,
    table,
    hidden_ref,
    *,
    norm_count,
    row_devs,
):
    width = conv_ref.shape[-1]

    if date == 0:
        norm_table(stats_ref, norm_ref, dates, norm_count)
        for row_tap in range(3):
            for col_tap in range(3):
                table[
                    row_tap * width : (row_tap + 1) * width, col_tap * width : (col_tap + 1) * width
                ] = weight_ref[row_tap, col_tap]

    rows, cols = conv_ref.shape[1:3]
    activate_rows(
        date,
        dates,
        edges(edge_ref, row_devs),
        (conv_ref, up_ref, down_ref),
        (norm_ref, gain_ref, shift_ref),
        hidden_ref,
    )
    taps = jnp.concatenate(
        [hidden_ref[0, tap : tap + rows] for tap in range(3)], axis=-1
    ).reshape(rows * cols, 3 * width)
    terms = product(taps, table[...], 1, 0).reshape(rows, cols, 3 * width)
    stored = (
        terms[..., width : 2 * width]
        + from_left(terms[..., :width])
        + from_right(terms[..., 2 * width :])
    ).astype(BF16)
    out_ref[0] = stored
    values = stored.astype(F32)
    store_sums(sums_ref, date, dates, column_sum(values), column_sum(values * values))


def encoding(day, width):
    lane = lax.broadcasted_iota(jnp.int32, (1, width), 1)
    frequency = jnp.exp((lane // 2).astype(F32) * (-2.0 * math.log(1000.0) / width))
    angles = day.astype(F32) * frequency
    return jnp.where(lane % 2 == 0, jnp.sin(angles), jnp.cos(angles))


def fold_keys(key_ref, query_ref, wide_ref, vector_ref, spread_ref, score_ref):
    depth, heads = query_ref.shape
    width = key_ref.shape[1]
    lanes = width // heads
    spread_ref[...] = head_spread(width)
    row = lax.broadcasted_iota(jnp.int32, (heads * depth, width), 0)
    lane = lax.broadcasted_iota(jnp.int32, (heads * depth, width), 1)
    widen = (row // depth == lane // lanes) & (row % depth == lane % lanes)
    wide = product(key_ref[...], widen.astype(F32).astype(BF16), 0, 0)
    wide_ref[...] = wide.astype(BF16)
    head = lax.broadcasted_iota(jnp.int32, (heads, width), 0)
    lane = lax.broadcasted_iota(jnp.int32, (heads, width), 1)
    inside = (lane // lanes == head).astype(F32).astype(BF16)
    high, low = split(query_ref[...])
    lower = (query_ref[...] - high.astype(F32) - low.astype(F32)).astype(BF16)
    spread = sum(product(part, inside, 1, 0) for part in (high, low, lower))
    step = lax.broadcasted_iota(jnp.int32, (depth, width), 0)
    place = lax.broadcasted_iota(jnp.int32, (depth, width), 1) % lanes
    queries = jnp.sum(jnp.where(step == place, spread * depth**-0.5, 0.0), axis=0, keepdims=True)
    place = lax.broadcasted_iota(jnp.int32, (1, width), 1) % lanes
    queries = queries + jnp.where((place == depth) | (place == depth + 1), 1.0, 0.0)
    vector_ref[...] = jnp.broadcast_to(queries, vector_ref.shape)
    folded = jnp.concatenate(split(wide * queries), axis=-1)
    folded = product(folded, spread_ref[...], 1, 0)
    score_ref[...] = jnp.concatenate(split(folded), axis=-1)


def source_of(turn_ref, device, devices):
    half = devices // 2
    core = (device + turn_ref[0]) % 2
    return core * half + (device // 2 + half - turn_ref[0] // 2) % half


def upstream_rows(grad_ref, turn_ref, rows, cols):
    devices = grad_ref.shape[0]
    piece = cols // devices
    parts = [
        grad_ref[source_of(turn_ref, device, devices), : rows * piece].reshape(rows, piece, -1)
        for device in range(devices)
    ]
    return jnp.concatenate(parts, axis=1)


def score_kernel(
    date,
    dates,
    day_ref,
    block_ref,
    stats_ref,
    gain_ref,
    shift_ref,
    grad_ref,
    valid_ref,
    turn_ref,
    key_ref,
    query_ref,
    feat_ref,
    exp_ref,
    attn_ref,
    norm_ref,
    packed_ref,
    own_ref,
    wide_ref,
    vector_ref,
    total,
    mean,
    spread_ref,
    score_ref,
    *,
    norm_count,
    grad_scale,
):
    rows, cols, width = block_ref.shape[1:]

    if date == 0:
        norm_table(stats_ref, norm_ref, dates, norm_count)
        fold_keys(key_ref, query_ref, wide_ref, vector_ref, spread_ref, score_ref)
        total[...] = jnp.zeros_like(total)
        mean[...] = jnp.zeros_like(mean)

    scale = norm_ref[pl.ds(dates + date, 1), :] * gain_ref[...]
    shift = shift_ref[...] - norm_ref[pl.ds(date, 1), :] * scale
    linear = block_ref[0].astype(F32) * scale + shift
    features = (linear * sigmoid(linear) + encoding(day_ref[turn_ref[0] * dates + date], width)).astype(BF16)
    feat_ref[0] = features
    upstream = upstream_rows(grad_ref, turn_ref, rows, cols)
    parts = split(upstream.astype(F32) * features.astype(F32))
    parts = jnp.concatenate(parts, axis=-1).reshape(rows * cols, 2 * width)
    attn = product(parts, spread_ref[...], 1, 0).reshape(rows, cols, width) * grad_scale
    both = product(features.reshape(rows * cols, width), score_ref[...], 1, 0)
    scores = (both[:, :width] + both[:, width:]).reshape(rows, cols, width)
    devices = grad_ref.shape[0]
    valid = jnp.zeros((rows, width), F32)
    for device in range(devices):
        piece = valid_ref[
            source_of(turn_ref, device, devices), pl.ds(date * rows, rows), :
        ]
        valid = valid + pltpu.roll(piece, device * (cols // devices), 1)
    diagonal = lax.broadcasted_iota(jnp.int32, (cols, cols), 0) == lax.broadcasted_iota(
        jnp.int32, (cols, cols), 1
    )
    ones = jnp.ones((cols, width), BF16)
    clear = jnp.concatenate(
        [jnp.where(diagonal, valid[row : row + 1], 0.0) for row in range(rows)], axis=0
    ).astype(BF16)
    clear = product(clear, ones, 1, 0).reshape(rows, cols, width)
    exponent = clear * jnp.exp(scores)
    running = total[...] + exponent
    share = jnp.where(running > 0.0, exponent / running, 0.0)
    total[...] = running
    mean[...] += share * (attn - mean[...])
    exp_ref[0] = exponent
    attn_ref[0] = attn

    if date == dates - 1:
        place = lax.broadcasted_iota(jnp.int32, (cols, width), 1) % rows
        for index, source in enumerate((total, mean)):
            dense = jnp.zeros((cols, width), F32)
            for row in range(rows):
                dense = dense + jnp.where(place == row, source[row], 0.0)
            if index == 0:
                packed_ref[0, 0] = dense.astype(BF16)
                own_ref[...] = dense
            else:
                packed_ref[0, 1], packed_ref[0, 2] = split(dense)


def attend_kernel(
    date,
    dates,
    packed_ref,
    own_ref,
    feat_ref,
    exp_ref,
    attn_ref,
    block_ref,
    norm_ref,
    gain_ref,
    shift_ref,
    query_ref,
    grad_ref,
    turn_ref,
    key_ref,
    grad_out_ref,
    part_ref,
    key_out_ref,
    vector_ref,
    sums_ref,
    inverse,
    average,
    attended,
    *,
    grad_scale,
):
    rows, cols, width = block_ref.shape[1:]

    if date == 0:
        totals = packed_ref[:, 0].astype(F32)
        reciprocal = 1.0 / jnp.sum(totals, axis=0)
        means = packed_ref[:, 1].astype(F32) + packed_ref[:, 2].astype(F32)
        mean = jnp.sum(totals * reciprocal * means, axis=0)
        own = own_ref[...]
        sent = own.astype(BF16).astype(F32)
        reciprocal = reciprocal * jnp.where(own > 0.0, sent / own, 0.0)
        place = lax.broadcasted_iota(jnp.int32, (cols, width), 1) % rows
        for values, target in ((reciprocal, inverse), (mean, average)):
            parts = jnp.concatenate(split(values), axis=-1)
            wide_place = jnp.concatenate([place, place], axis=-1)
            picked = jnp.concatenate(
                [jnp.where(wide_place == row, parts, jnp.zeros_like(parts)) for row in range(rows)], axis=0
            )
            target[...] = product(picked, head_spread(width), 1, 0).reshape(rows, cols, width)
        attended[...] = jnp.zeros_like(attended)
        key_out_ref[...] = jnp.zeros_like(key_out_ref)
        vector_ref[...] = jnp.zeros_like(vector_ref)

    features = feat_ref[0]
    weights = exp_ref[0] * inverse[...]
    rounded = weights.astype(BF16).astype(F32)
    attended[...] += rounded * features.astype(F32)
    score_grad = weights * (attn_ref[0] - average[...])
    spread_grad = score_grad * query_ref[0:1]
    rest = spread_grad - spread_grad.astype(BF16).astype(F32)
    lane = lax.broadcasted_iota(jnp.int32, spread_grad.shape, 2) % (width // 16)
    key_grads = jnp.where(lane == 5, rest, spread_grad).astype(BF16).reshape(rows * cols, width)
    key_out_ref[...] += product(features.reshape(rows * cols, width), key_grads, 0, 0)
    upstream = upstream_rows(grad_ref, turn_ref, rows, cols)
    feat_grad = rounded * (upstream.astype(F32) * grad_scale) + product(
        key_grads, key_ref[...], 1, 1
    ).reshape(rows, cols, width)
    gain = gain_ref[...]
    centred = (block_ref[0].astype(F32) - norm_ref[pl.ds(date, 1), :]) * norm_ref[
        pl.ds(dates + date, 1), :
    ]
    linear = centred * gain + shift_ref[...]
    part = sigmoid(linear)
    linear_grad = feat_grad * (part * (1.0 + linear * (1.0 - part)))
    first = column_sum(linear_grad)
    second = column_sum(linear_grad * centred)
    vector_ref[0:1] += second
    vector_ref[1:2] += first
    store_sums(sums_ref, date, dates, first * gain, second * gain)
    grad_out_ref[0] = (linear_grad * gain).astype(BF16)

    if date == dates - 1:
        devices, piece = part_ref.shape[0], part_ref.shape[2]
        for device in range(devices):
            part_ref[device] = attended[:, device * piece : (device + 1) * piece].astype(BF16)
        key_part = key_out_ref[...]
        place = lax.broadcasted_iota(jnp.int32, (width, width), 1) % (width // 16)
        both = pltpu.roll(key_part, width - 4, 1) + pltpu.roll(key_part, width - 5, 1)
        both = jnp.where(place == 0, both, 0.0)
        both = both + pltpu.roll(both, 1, 1)
        both = both + pltpu.roll(both, 2, 1)
        vector_ref[2:3] = 0.5 * jnp.sum(key_ref[...].astype(F32) * both, axis=0, keepdims=True)


def hidden_kernel(
    date,
    dates,
    edge_ref,
    grad_ref,
    block_ref,
    tails_ref,
    norm_ref,
    weight_ref,
    conv_ref,
    up_ref,
    down_ref,
    first_norm_ref,
    gain_ref,
    shift_ref,
    pre_ref,
    out_ref,
    vector_ref,
    sums_ref,
    table,
    factors,
    padded,
    *,
    norm_count,
    row_devs,
):
    rows, cols, width = block_ref.shape[1:]

    if date == 0:
        tails = group_sum(jnp.sum(tails_ref[...], axis=0)) / norm_count
        mean, inverse = norm_ref[:dates], norm_ref[dates:]
        slope = -inverse * inverse * tails[dates:]
        factors[0:dates] = slope
        factors[dates : 2 * dates] = -inverse * tails[:dates] - mean * slope
        vector_ref[...] = jnp.zeros_like(vector_ref)
        padded[:2] = jnp.zeros_like(padded[:2])
        padded[rows + 2 :] = jnp.zeros_like(padded[rows + 2 :])
        for row_tap in range(3):
            for col_tap in range(3):
                table[
                    col_tap * width : (col_tap + 1) * width, row_tap * width : (row_tap + 1) * width
                ] = weight_ref[2 - row_tap, col_tap]

    inverse = norm_ref[pl.ds(dates + date, 1), :]
    slope = factors[pl.ds(date, 1), :]
    constant = factors[pl.ds(dates + date, 1), :]

    above_edge, below_edge = edges(edge_ref, row_devs)
    stored = (
        grad_ref[0].astype(F32) * inverse + (block_ref[0].astype(F32) * slope + constant)
    ).astype(BF16)
    pre_ref[0] = stored
    padded[2 : rows + 2] = stored
    reach = rows + 2
    taps = jnp.concatenate([padded[tap : tap + reach] for tap in range(3)], axis=-1).reshape(
        reach * cols, 3 * width
    )
    terms = product(taps, table[...], 1, 1).reshape(reach, cols, 3 * width)
    hidden_grad = (
        terms[..., width : 2 * width]
        + from_right(terms[..., :width])
        + from_left(terms[..., 2 * width :])
    )
    gain = gain_ref[...]
    conv = jnp.concatenate([up_ref[0][None], conv_ref[0], down_ref[0][None]], axis=0)
    centred = (conv.astype(F32) - first_norm_ref[pl.ds(date, 1), :]) * first_norm_ref[
        pl.ds(dates + date, 1), :
    ]
    linear = centred * gain + shift_ref[...]
    part = sigmoid(linear)
    linear_grad = hidden_grad * (part * (1.0 + linear * (1.0 - part)))
    linear_grad = jnp.concatenate(
        [
            linear_grad[:1] * above_edge,
            linear_grad[1 : rows + 1],
            linear_grad[rows + 1 :] * below_edge,
        ],
        axis=0,
    )
    out_ref[0] = linear_grad.astype(BF16)
    first = column_sum(linear_grad)
    second = column_sum(linear_grad * centred)
    vector_ref[0:1] += second
    vector_ref[1:2] += first
    store_sums(sums_ref, date, dates, first * gain, second * gain)


def block_grad_kernel(
    date,
    dates,
    edge_ref,
    conv_ref,
    up_ref,
    down_ref,
    norm_ref,
    gain_ref,
    shift_ref,
    pre_ref,
    key_ref,
    out_ref,
    total,
    hidden_ref,
    *,
    row_devs,
):
    rows, cols, width = pre_ref.shape[1:]

    if date == 0:
        total[...] = jnp.zeros_like(total)

    activate_rows(
        date,
        dates,
        edges(edge_ref, row_devs),
        (conv_ref, up_ref, down_ref),
        (norm_ref, gain_ref, shift_ref),
        hidden_ref,
    )
    grads = pre_ref[0].astype(F32)
    grads = jnp.concatenate(
        [from_right(grads).astype(BF16), pre_ref[0], from_left(grads).astype(BF16)], axis=-1
    ).reshape(rows * cols, 3 * width)
    taps = jnp.concatenate(
        [hidden_ref[0, tap : tap + rows] for tap in range(3)], axis=-1
    ).reshape(rows * cols, 3 * width)
    total[...] += product(taps, grads, 0, 0)

    if date == dates - 1:
        for row_tap in range(3):
            for col_tap in range(3):
                base = (row_tap * 3 + col_tap) * width
                out_ref[base : base + width] = total[
                    row_tap * width : (row_tap + 1) * width, col_tap * width : (col_tap + 1) * width
                ].astype(BF16)
        key_part = key_ref[...]
        rest = key_part - key_part.astype(BF16).astype(F32)
        lanes = width // 16
        place = lax.broadcasted_iota(jnp.int32, key_part.shape, 1) % lanes
        rest = pltpu.roll(rest, lanes // 2, 1)
        key_rows = jnp.where(place < lanes // 2, key_part, rest).astype(BF16)
        out_ref[9 * width : 10 * width] = key_rows
        if out_ref.shape[0] > 10 * width:
            out_ref[10 * width :] = jnp.zeros_like(out_ref[10 * width :])


def conv_grad_kernel(
    date,
    dates,
    img_ref,
    above_ref,
    inner_ref,
    outer_ref,
    place_ref,
    conv_ref,
    grad_ref,
    tails_ref,
    norm_ref,
    gain_ref,
    vector_ref,
    other_ref,
    block_rows_ref,
    turn_ref,
    keep_ref,
    give_ref,
    factors,
    total,
    out_ref,
    high_ref,
    below_ref,
    *,
    norm_count,
):
    rows, cols, width = conv_ref.shape[1:]
    half = width // 2

    if date == 0:
        sort_halos(place_ref, inner_ref, outer_ref, high_ref, below_ref)
        tails = group_sum(jnp.sum(tails_ref[...], axis=0)) / norm_count
        mean, inverse = norm_ref[:dates], norm_ref[dates:]
        slope = -inverse * inverse * tails[dates:]
        factors[0:dates] = slope
        factors[dates : 2 * dates] = -inverse * tails[:dates] - mean * slope
        total[...] = jnp.zeros_like(total)

    scale = norm_ref[pl.ds(dates + date, 1), :] * gain_ref[...]
    slope = factors[pl.ds(date, 1), :]
    constant = factors[pl.ds(dates + date, 1), :]
    own = conv_ref[0].astype(F32) * slope + constant
    scaled = grad_ref[0].astype(F32) * scale
    stored = jnp.concatenate(
        [scaled[:1], scaled[1 : rows + 1] + own, scaled[rows + 1 :]], axis=0
    ).astype(BF16)
    moved = from_right(stored.astype(F32)).astype(BF16)
    reach = rows + 2
    grads = jnp.concatenate([stored, moved], axis=-1).reshape(reach * cols, 2 * width)
    even, odd = img_ref[0, :, 0], img_ref[0, :, 1]
    above = above_ref[0][None]
    taps = [
        jnp.concatenate([high_ref[date, :1], above, odd], axis=0),
        jnp.concatenate([high_ref[date, 1:], even, below_ref[date, :1]], axis=0),
        jnp.concatenate([above, odd, below_ref[date, 1:]], axis=0),
    ]
    taps = jnp.concatenate(taps, axis=-1).reshape(reach * cols, 3 * width)
    total[...] += product(taps, grads, 0, 0)

    if date == dates - 1:
        begin = block_rows_ref.shape[0]
        out_ref[:begin] = block_rows_ref[...]
        for tap in range(3):
            base = tap * width
            pair = total[base : base + width, :width].astype(BF16)
            left = total[base + half : base + width, width:].astype(BF16)
            start = begin + tap * 3 * half
            out_ref[start : start + half] = left
            out_ref[start + half : start + 3 * half] = pair
        start = begin + 9 * half
        for source in (vector_ref, other_ref):
            high, low = split(source[...])
            out_ref[start : start + 16] = jnp.concatenate([high, low], axis=0)
            start += 16
        if out_ref.shape[0] > start:
            out_ref[start:] = jnp.zeros_like(out_ref[start:])
        half_rows = keep_ref.shape[0]
        core = turn_ref[0] % 2
        start = pl.multiple_of(core * half_rows, half_rows)
        keep_ref[...] = out_ref[pl.ds(start, half_rows), :]
        start = pl.multiple_of((1 - core) * half_rows, half_rows)
        give_ref[...] = out_ref[pl.ds(start, half_rows), :]


def total_kernel(in_ref, out_ref):
    total = jnp.sum(in_ref[...].astype(F32), axis=0).astype(BF16)
    for copy in range(out_ref.shape[0]):
        out_ref[copy] = total


def final_kernel(
    depth,
    turn_ref,
    own_ref,
    other_ref,
    conv_ref,
    block_ref,
    key_ref,
    query_ref,
    *refs,
):
    vector_refs, rows_ref = refs[:-1], refs[-1]
    half_rows = own_ref.shape[0]
    core = turn_ref[0] % 2
    rows_ref[pl.ds(pl.multiple_of(core * half_rows, half_rows), half_rows), :] = own_ref[...]
    start = pl.multiple_of((1 - core) * half_rows, half_rows)
    rows_ref[pl.ds(start, half_rows), :] = other_ref[...]
    conv_end, block_end, width = conv_ref.shape[0], block_ref.shape[0], block_ref.shape[1]
    block_ref[...] = rows_ref[:block_end].astype(F32)
    wide = key_ref.shape[0]
    heads = wide // depth
    lanes = width // heads
    row = lax.broadcasted_iota(jnp.int32, (wide, width), 0)
    lane = lax.broadcasted_iota(jnp.int32, (wide, width), 1)
    narrow = (row // depth == lane // lanes) & (row % depth == lane % depth)
    narrow = narrow.astype(F32).astype(BF16)
    key_ref[...] = product(narrow, rows_ref[block_end : block_end + width], 1, 1)
    start = block_end + width
    conv_ref[...] = rows_ref[start : start + conv_end].astype(F32)
    start += conv_end
    for index in range(2):
        both = rows_ref[start : start + 16].astype(F32)
        both = both[:8] + both[8:]
        vector_refs[2 * index][...] = both[0:1]
        vector_refs[2 * index + 1][...] = both[1:2]
        start += 16
    both = rows_ref[start - 16 : start]
    row = lax.broadcasted_iota(jnp.int32, (heads, width), 0)
    lane = lax.broadcasted_iota(jnp.int32, (heads, width), 1)
    inside = row == lane // lanes
    step = lax.broadcasted_iota(jnp.int32, (8, width), 0)
    place = lax.broadcasted_iota(jnp.int32, (8, width), 1) % lanes
    steps = step == place
    query = jnp.zeros((8, heads), F32)
    for index in (2, 10):
        picked = jnp.where(steps, both[index : index + 1].astype(F32), 0.0).astype(BF16)
        query = query + product(picked, inside.astype(F32).astype(BF16), 1, 1)
    query_ref[...] = query[:depth]


def call(kernel, dates, inputs, outputs, scratch, flops):
    in_specs, out_specs, arrays, out_shape, buffers = [], [], [], [], []
    in_vmem, in_hbm = pl.BlockSpec(memory_space=pltpu.VMEM), pl.BlockSpec(memory_space=pltpu.HBM)
    loads, stores = [], []
    for place, (kind, array) in enumerate(inputs):
        if kind == "scalar":
            in_specs.append(pl.BlockSpec(memory_space=pltpu.SMEM))
        elif "far" in kind:
            array = pltpu.with_memory_space_constraint(array, pltpu.HBM)
            in_specs.append(in_hbm)
            loads.append(place)
            buffers.append(pltpu.VMEM(array.shape, array.dtype))
        else:
            in_specs.append(in_vmem)
        arrays.append(array)
    for place, (kind, shape, dtype) in enumerate(outputs):
        if "far" in kind:
            out_shape.append(pltpu.HBM(shape, dtype))
            out_specs.append(in_hbm)
            stores.append(place)
            buffers.append(pltpu.VMEM(shape, dtype))
        else:
            out_shape.append(jax.ShapeDtypeStruct(shape, dtype))
            out_specs.append(in_vmem)
    copies = len(loads) + len(stores)
    kinds = [kind for kind, _ in inputs] + [kind for kind, _, _ in outputs]

    def body(*refs):
        views, rest = list(refs[: len(kinds)]), refs[len(kinds) :]
        buffer_refs, ready, rest = rest[:copies], rest[copies], rest[copies + 1 :]

        def copies_of(place, index, inward):
            outside, inside = views[place], buffer_refs[index]
            made = []
            for date in range(dates if "date" in kinds[place] else 1):
                here = pl.ds(date, 1) if "date" in kinds[place] else slice(None)
                pair = (outside.at[here], inside.at[here])
                source, target = pair if inward else pair[::-1]
                made.append(pltpu.make_async_copy(source, target, ready.at[index, date]))
            return made

        incoming = [copies_of(place, index, True) for index, place in enumerate(loads)]
        outgoing = [
            copies_of(len(inputs) + place, len(loads) + index, False)
            for index, place in enumerate(stores)
        ]
        for date in range(dates):
            for moves in incoming:
                if date < len(moves):
                    moves[date].start()
        for index, place in enumerate(loads):
            views[place] = buffer_refs[index]
        for index, place in enumerate(stores):
            views[len(inputs) + place] = buffer_refs[len(loads) + index]
        for date in range(dates):
            for moves in incoming:
                if date < len(moves):
                    moves[date].wait()
            here = [
                view.at[pl.ds(date, 1)] if "date" in kind else view
                for view, kind in zip(views, kinds)
            ]
            kernel(date, dates, *here, *rest)
            for moves in outgoing:
                if len(moves) == dates:
                    moves[date].start()
                elif date == dates - 1:
                    moves[0].start()
        for moves in outgoing:
            for move in moves:
                move.wait()

    moved = sum(array.size * array.dtype.itemsize for _, array in inputs)
    return pl.pallas_call(
        body,
        in_specs=in_specs,
        out_specs=out_specs,
        out_shape=out_shape,
        scratch_shapes=buffers + [pltpu.SemaphoreType.DMA((max(copies, 1), dates))] + scratch,
        compiler_params=pltpu.CompilerParams(vmem_limit_bytes=40 * MIB),
        cost_estimate=pl.CostEstimate(flops=flops, bytes_accessed=2 * moved, transcendentals=0),
    )(*arrays)


def shifted(array, by):
    devices = lax.axis_size("rows")
    pairs = [(i, i + by) for i in range(devices) if 0 <= i + by < devices]
    return lax.ppermute(array, "rows", pairs)


def same_core(array):
    devices = lax.axis_size("dates")
    pieces = [array]
    for step in range(2, devices, 2):
        pairs = [((i + step) % devices, i) for i in range(devices)]
        pieces.append(lax.ppermute(array, "dates", pairs))
    return pieces


def sum_of_parts(parts):
    devices = lax.axis_size("dates")
    place = lax.axis_index("dates")
    total = lax.dynamic_index_in_dim(parts, place, 0, keepdims=False).astype(F32)
    for step in range(1, devices):
        piece = lax.dynamic_index_in_dim(parts, (place + step) % devices, 0, keepdims=False)
        pairs = [(i, (i + step) % devices) for i in range(devices)]
        total = total + lax.ppermute(piece, "dates", pairs).astype(F32)
    return total.astype(BF16)


def exchange(pieces, axes):
    return lax.all_to_all(pieces, axes, split_axis=0, concat_axis=0, tiled=True)


def gather(array, axis):
    return lax.all_gather(array, axis, axis=0, tiled=True)


def other_core(array):
    devices = lax.axis_size("dates")
    return lax.ppermute(array, "dates", [(i, i + 1 - 2 * (i % 2)) for i in range(devices)])


def exchange_cores(pieces):
    axes = ("rows", "dates")
    devices = lax.axis_size(axes)
    groups = [list(range(core, devices, 2)) for core in range(2)]
    return lax.all_to_all(
        pieces, axes, split_axis=0, concat_axis=0, axis_index_groups=groups, tiled=True
    )


def scatter(rows_array):
    devices = lax.axis_size(("rows", "dates")) // 2
    count, width = rows_array.shape
    return exchange_cores(rows_array.reshape(devices, count // devices, width))


def collect(pieces):
    spread = pl.pallas_call(
        total_kernel,
        out_shape=jax.ShapeDtypeStruct(pieces.shape, BF16),
        compiler_params=pltpu.CompilerParams(vmem_limit_bytes=16 * MIB),
    )(pieces)
    count, rows, width = pieces.shape
    return exchange_cores(spread).reshape(count * rows, width)


def padded_count(count, devices):
    step = 8 * devices
    return -(-count // step) * step


def local(
    images,
    day_index,
    valid,
    out_grad,
    conv_weight,
    first_gain,
    first_shift,
    block_weight,
    gn_gain,
    gn_shift,
    key_weight,
    queries,
):
    dates, rows_here, cols, pair_width = images.shape
    width = conv_weight.shape[-1]
    row_devs, date_devs = lax.axis_size("rows"), lax.axis_size("dates")
    devices = row_devs * date_devs
    rows = rows_here // 2
    heads, depth = queries.shape
    norm_count = float(rows * row_devs * cols * (width // GROUPS))
    grad_scale = float(rows * row_devs * cols) ** (-0.5)
    date_start = lax.axis_index("dates") * dates
    frame = (dates, rows, cols, width)
    edge_rows = (dates, cols, width)
    flops = 2 * dates * rows * cols * width * width

    rows_of = lambda vector: vector.reshape(1, width)
    first_gain, first_shift = rows_of(first_gain), rows_of(first_shift)
    gn_gain, gn_shift = rows_of(gn_gain), rows_of(gn_shift)
    last = images[:, -1]
    above = shifted(last, 1)
    grad_rows = out_grad.size // width
    row_place = lax.axis_index("rows")
    place = row_place.reshape(1)
    valid_count = valid.shape[0] * rows
    piece = out_grad.shape[1]
    packed_shape = ((grad_rows + valid_count) // piece, piece, width)
    in_hbm, in_vmem = pl.BlockSpec(memory_space=pltpu.HBM), pl.BlockSpec(memory_space=pltpu.VMEM)
    images_near, inner, outer, packed = pl.pallas_call(
        load_kernel,
        in_specs=[pl.BlockSpec(memory_space=pltpu.SMEM), in_vmem, in_hbm, in_hbm, in_hbm],
        out_specs=[in_vmem] * 4,
        out_shape=[
            jax.ShapeDtypeStruct(shape, BF16)
            for shape in (images.shape,) + ((dates, 2, cols, pair_width),) * 2 + (packed_shape,)
        ],
        scratch_shapes=[pltpu.VMEM(valid.shape, valid.dtype), pltpu.SemaphoreType.DMA((3,))],
        compiler_params=pltpu.CompilerParams(vmem_limit_bytes=16 * MIB),
    )(
        place,
        last,
        *[pltpu.with_memory_space_constraint(x, pltpu.HBM) for x in (images, out_grad, valid)],
    )
    packed = packed.reshape(grad_rows + valid_count, width)
    inner = lax.ppermute(inner, "rows", [(i, i ^ 1) for i in range(row_devs)])
    pairs = [(i, i + 1) for i in range(1, row_devs - 1, 2)]
    outer = lax.ppermute(outer, "rows", pairs + [(j, i) for i, j in pairs])
    paired = images.reshape(dates, rows, 2, cols, pair_width)
    conv_out, sums = call(
        down_kernel,
        dates,
        [
            ("date", images_near.reshape(paired.shape)),
            ("date", above),
            ("all", conv_weight),
        ],
        [("date far", frame, BF16), ("all", (row_devs, 2 * dates, width), F32)],
        [pltpu.VMEM((3 * pair_width, 2 * width), BF16)],
        6 * flops,
    )
    stats = exchange(sums, "rows")
    inner, outer, last, _ = lax.optimization_barrier((inner, outer, last, sums))
    halo_up, halo_down = call(
        edge_kernel,
        1,
        [
            ("scalar", place),
            ("all", inner),
            ("all", outer),
            ("all", above),
            ("all", last),
            ("all", conv_weight),
        ],
        [("all", edge_rows, BF16)] * 2,
        [
            pltpu.VMEM((3 * pair_width, 2 * width), BF16),
            pltpu.VMEM(inner.shape, BF16),
            pltpu.VMEM(inner.shape, BF16),
        ],
        6 * flops // rows,
    )
    turn = lax.axis_index("dates").reshape(1)
    packed, _ = lax.optimization_barrier((packed, halo_up))
    pieces = same_core(packed)
    block_out, first_norm, sums = call(
        functools.partial(block_kernel, norm_count=norm_count, row_devs=row_devs),
        dates,
        [
            ("scalar", place),
            ("date far", conv_out),
            ("date", halo_up),
            ("date", halo_down),
            ("all", stats),
            ("all", first_gain),
            ("all", first_shift),
            ("all far", block_weight),
        ],
        [
            ("date far", frame, BF16),
            ("all", (2 * dates, width), F32),
            ("all", (row_devs, 2 * dates, width), F32),
        ],
        [
            pltpu.VMEM((3 * width, 3 * width), BF16),
            pltpu.VMEM((1, rows + 2, cols, width), BF16),
        ],
        9 * flops,
    )
    stats = exchange(sums, "rows")
    pieces, _ = lax.optimization_barrier((pieces, sums))
    sources = jnp.stack(pieces + [other_core(piece) for piece in pieces])
    clear = lax.dynamic_slice_in_dim(sources, grad_rows + date_start * rows, dates * rows, 1)
    clear = clear.astype(F32)
    features, exponent, attn, norm, packed, own_total, key_wide, query_wide = call(
        functools.partial(score_kernel, norm_count=norm_count, grad_scale=grad_scale),
        dates,
        [
            ("scalar", day_index),
            ("date far", block_out),
            ("all", stats),
            ("all", gn_gain),
            ("all", gn_shift),
            ("all", sources),
            ("all", clear),
            ("scalar", turn),
            ("all", key_weight.T),
            ("all", queries.T),
        ],
        [
            ("date", frame, BF16),
            ("date", frame, F32),
            ("date", frame, F32),
            ("all", (2 * dates, width), F32),
            ("all", (1, 3, cols, width), BF16),
            ("all", (cols, width), F32),
            ("all", (width, width), BF16),
            ("all", (8, width), F32),
        ],
        [
            pltpu.VMEM(frame[1:], F32),
            pltpu.VMEM(frame[1:], F32),
            pltpu.VMEM((2 * width, width), BF16),
            pltpu.VMEM((width, 2 * width), BF16),
        ],
        5 * flops,
    )
    packed = gather(packed, "dates")
    block_grad, attended, key_part, vectors, sums = call(
        functools.partial(attend_kernel, grad_scale=grad_scale),
        dates,
        [
            ("all", packed),
            ("all", own_total),
            ("date", features),
            ("date", exponent),
            ("date", attn),
            ("date", block_out),
            ("all", norm),
            ("all", gn_gain),
            ("all", gn_shift),
            ("all", query_wide),
            ("all", sources),
            ("scalar", turn),
            ("all", key_wide),
        ],
        [
            ("date far", frame, BF16),
            ("all far", (date_devs, rows, cols // date_devs, width), BF16),
            ("all far", (width, width), F32),
            ("all", (8, width), F32),
            ("all", (row_devs, 2 * dates, width), F32),
        ],
        [pltpu.VMEM(frame[1:], F32)] * 3,
        5 * flops,
    )
    tails = exchange(sums, "rows")
    pre_grad, linear_grad, first_vectors, sums = call(
        functools.partial(hidden_kernel, norm_count=norm_count, row_devs=row_devs),
        dates,
        [
            ("scalar", place),
            ("date far", block_grad),
            ("date far", block_out),
            ("all", tails),
            ("all", norm),
            ("all far", block_weight),
            ("date far", conv_out),
            ("date", halo_up),
            ("date", halo_down),
            ("all", first_norm),
            ("all", first_gain),
            ("all", first_shift),
        ],
        [
            ("date far", frame, BF16),
            ("date far", (dates, rows + 2, cols, width), BF16),
            ("all", (8, width), F32),
            ("all", (row_devs, 2 * dates, width), F32),
        ],
        [
            pltpu.VMEM((3 * width, 3 * width), BF16),
            pltpu.VMEM((2 * dates, width), F32),
            pltpu.VMEM((rows + 4, cols, width), BF16),
        ],
        9 * flops,
    )
    tails = exchange(sums, "rows")
    (block_rows,) = call(
        functools.partial(block_grad_kernel, row_devs=row_devs),
        dates,
        [
            ("scalar", place),
            ("date far", conv_out),
            ("date", halo_up),
            ("date", halo_down),
            ("all", first_norm),
            ("all", first_gain),
            ("all", first_shift),
            ("date far", pre_grad),
            ("all far", key_part),
        ],
        [("all far", (10 * width, width), BF16)],
        [
            pltpu.VMEM((3 * width, 3 * width), F32),
            pltpu.VMEM((1, rows + 2, cols, width), BF16),
        ],
        9 * flops,
    )
    tails, block_rows = lax.optimization_barrier((tails, block_rows))
    conv_count = 9 * pair_width // 2 + 32
    half_rows = padded_count(10 * width + conv_count, devices) // 2
    keep, give = call(
        functools.partial(conv_grad_kernel, norm_count=norm_count),
        dates,
        [
            ("date far", paired),
            ("date", above),
            ("all", inner),
            ("all", outer),
            ("scalar", place),
            ("date far", conv_out),
            ("date far", linear_grad),
            ("all", tails),
            ("all", first_norm),
            ("all", first_gain),
            ("all", first_vectors),
            ("all", vectors),
            ("all far", block_rows),
            ("scalar", turn),
        ],
        [("all", (half_rows, width), BF16)] * 2,
        [
            pltpu.VMEM((2 * dates, width), F32),
            pltpu.VMEM((3 * pair_width, 2 * width), F32),
            pltpu.VMEM((2 * half_rows, width), BF16),
            pltpu.VMEM(inner.shape, BF16),
            pltpu.VMEM(inner.shape, BF16),
        ],
        6 * flops,
    )
    rows_half = (keep.astype(F32) + other_core(give).astype(F32)).astype(BF16)
    pieces = scatter(rows_half)
    attended, _ = lax.optimization_barrier((attended, rows_half))
    attended = sum_of_parts(attended)
    rows_half = collect(pieces)
    rows_other = other_core(rows_half)
    shapes = [
        (9 * pair_width // 2, width),
        (9 * width, width),
        (heads * depth, width),
        (depth, heads),
    ] + [(1, width)] * 4
    conv_total, block_total, key_total, query_total, *totals = pl.pallas_call(
        functools.partial(final_kernel, depth),
        in_specs=[
            pl.BlockSpec(memory_space=pltpu.SMEM),
            pl.BlockSpec(memory_space=pltpu.VMEM),
            pl.BlockSpec(memory_space=pltpu.VMEM),
        ],
        out_shape=[jax.ShapeDtypeStruct(shape, F32) for shape in shapes],
        scratch_shapes=[pltpu.VMEM((2 * half_rows, width), BF16)],
        compiler_params=pltpu.CompilerParams(vmem_limit_bytes=16 * MIB),
    )(turn, rows_half, rows_other)
    totals = [total.reshape(width) for total in totals]
    return (
        attended,
        conv_total.reshape(conv_weight.shape),
        totals[0],
        totals[1],
        block_total.reshape(block_weight.shape),
        totals[2],
        totals[3],
        key_total.T,
        query_total.T,
    )


def solution(mesh):
    return jax.shard_map(
        local,
        mesh=mesh,
        in_specs=(
            P("dates", "rows", None, None),
            P(),
            P(None, "rows", "dates"),
            P("rows", "dates", None),
            P(),
            P(),
            P(),
            P(),
            P(),
            P(),
            P(),
            P(),
        ),
        out_specs=(P("rows", "dates", None), P(), P(), P(), P(), P(), P(), P(), P()),
        check_vma=False,
    )
```

```python
import functools
import math

import jax
import jax.numpy as jnp
from jax import lax
from jax.experimental import pallas as pl
from jax.experimental.pallas import tpu as pltpu
from jax.sharding import PartitionSpec as P

GROUPS = 4


EPS = 1e-05


MIB = 1 << 20


F32 = jnp.float32


BF16 = jnp.bfloat16


def product(left, right, left_dim, right_dim):
    return lax.dot_general(
        left, right, (((left_dim,), (right_dim,)), ((), ())), preferred_element_type=F32
    )


def group_sum(values):
    width = values.shape[-1]
    lane_group = lax.broadcasted_iota(jnp.int32, values.shape, 1) // (width // GROUPS)
    spread = jnp.zeros_like(values)
    for group in range(GROUPS):
        inside = lane_group == group
        total = jnp.sum(jnp.where(inside, values, 0.0), axis=1, keepdims=True)
        spread = spread + jnp.where(inside, total, 0.0)
    return spread


def sigmoid(values):
    return 0.5 * jnp.tanh(0.5 * values) + 0.5


def from_left(values):
    moved = pltpu.roll(values, 1, 1)
    first = moved[:, :8]
    column = lax.broadcasted_iota(jnp.int32, first.shape, 1)
    return jnp.concatenate([jnp.where(column > 0, first, 0.0), moved[:, 8:]], axis=1)


def from_right(values):
    count = values.shape[1]
    moved = pltpu.roll(values, count - 1, 1)
    last = moved[:, count - 8 :]
    column = lax.broadcasted_iota(jnp.int32, last.shape, 1)
    return jnp.concatenate([moved[:, : count - 8], jnp.where(column < 7, last, 0.0)], axis=1)


def pair_table(weight_ref, table, backward):
    width = weight_ref.shape[-1]
    for row in range(4):
        for parity in range(2):
            for col_tap in range(3):
                deep = slice(row * width, (row + 1) * width)
                start = (col_tap * 2 + parity) * width
                wide = slice(start, start + width)
                tap = row - parity
                inside = 0 <= tap <= 2
                if backward:
                    block = weight_ref[2 - tap, col_tap] if inside else None
                    where = (wide, deep)
                else:
                    block = weight_ref[tap, col_tap] if inside else None
                    where = (deep, wide)
                table[where] = block if inside else jnp.zeros((width, width), BF16)


def pair_rows(padded, table, backward):
    rows, cols, width = padded.shape
    pairs = padded.reshape(rows // 2, 2, cols, width)
    count = rows // 2 - 1
    taps = [pairs[:count, 0], pairs[:count, 1], pairs[1:, 0], pairs[1:, 1]]
    taps = jnp.concatenate(taps, axis=-1).reshape(count * cols, 4 * width)
    terms = product(taps, table[...], 1, 1 if backward else 0).reshape(count, cols, 6 * width)
    parts = [terms[..., place * width : (place + 1) * width] for place in range(6)]
    first, last = (from_right, from_left) if backward else (from_left, from_right)
    results = [
        parts[2 + parity] + first(parts[parity]) + last(parts[4 + parity]) for parity in range(2)
    ]
    return jnp.stack(results, axis=1).reshape(2 * count, cols, width)


def column_sum(values):
    return jnp.sum(jnp.sum(values, axis=0), axis=0, keepdims=True)


def edges(place_ref, row_devs):
    place = place_ref[0]
    return (place > 0).astype(F32), (place < row_devs - 1).astype(F32)


def head_spread(width):
    lane = lax.broadcasted_iota(jnp.int32, (2 * width, width), 1) // (width // 16)
    head = lax.broadcasted_iota(jnp.int32, (2 * width, width), 0) % width // (width // 16)
    return (lane == head).astype(F32).astype(BF16)


def split(values):
    high = values.astype(BF16)
    return high, (values - high.astype(F32)).astype(BF16)


def store_sums(sums_ref, date, dates, first, second):
    for copy in range(sums_ref.shape[0]):
        sums_ref[copy, pl.ds(date, 1), :] = first
        sums_ref[copy, pl.ds(dates + date, 1), :] = second


def norm_table(sums_ref, table_ref, dates, norm_count):
    means = group_sum(jnp.sum(sums_ref[...], axis=0)) / norm_count
    mean = means[:dates]
    table_ref[:dates] = mean
    table_ref[dates:] = 1.0 / jnp.sqrt(means[dates:] - mean * mean + EPS)


def down_table(weight_ref, table):
    half = weight_ref.shape[2]
    for tap in range(3):
        base = tap * 2 * half
        table[base : base + half, : 2 * half] = weight_ref[tap, 1]
        table[base + half : base + 2 * half, : 2 * half] = weight_ref[tap, 2]
        table[base : base + half, 2 * half :] = jnp.zeros_like(weight_ref[tap, 0])
        table[base + half : base + 2 * half, 2 * half :] = weight_ref[tap, 0]


def down_rows(taps, table):
    rows, cols, width = taps[0].shape
    taps = jnp.concatenate(taps, axis=-1).reshape(rows * cols, 3 * width)
    both = product(taps, table[...], 1, 0).reshape(rows, cols, 2 * width)
    return (both[..., :width] + from_left(both[..., width:])).astype(BF16)


def down_kernel(
    date, dates, img_ref, above_ref, weight_ref, out_ref, sums_ref, table
):

    if date == 0:
        down_table(weight_ref, table)

    even, odd = img_ref[0, :, 0], img_ref[0, :, 1]
    above = jnp.concatenate([above_ref[0][None], odd[:-1]], axis=0)
    stored = down_rows([above, even, odd], table)
    out_ref[0] = stored
    values = stored.astype(F32)
    store_sums(sums_ref, date, dates, column_sum(values), column_sum(values * values))


def sort_halos(place_ref, inner_ref, outer_ref, high_ref, below_ref):
    odd = place_ref[0] % 2 == 1

    @pl.when(odd)
    def _():
        high_ref[...] = inner_ref[...]
        below_ref[...] = outer_ref[...]

    @pl.when(jnp.logical_not(odd))
    def _():
        high_ref[...] = outer_ref[...]
        below_ref[...] = inner_ref[...]


def load_kernel(
    place_ref,
    last_ref,
    img_hbm,
    grad_hbm,
    valid_hbm,
    img_ref,
    inner_ref,
    outer_ref,
    packed_ref,
    valid_ref,
    ready,
):
    blocks = grad_hbm.shape[0]
    moves = [
        pltpu.make_async_copy(grad_hbm, packed_ref.at[pl.ds(0, blocks)], ready.at[0]),
        pltpu.make_async_copy(valid_hbm, valid_ref, ready.at[1]),
        pltpu.make_async_copy(img_hbm, img_ref, ready.at[2]),
    ]
    for move in moves:
        move.start()
    for move in moves:
        move.wait()
    rows = img_ref.shape[1]
    odd = place_ref[0] % 2 == 1

    @pl.when(odd)
    def _():
        inner_ref[...] = img_ref[:, :2]
        outer_ref[...] = img_ref[:, rows - 3 : rows - 1]

    @pl.when(jnp.logical_not(odd))
    def _():
        inner_ref[...] = img_ref[:, rows - 3 : rows - 1]
        outer_ref[...] = img_ref[:, :2]

    piece, width = packed_ref.shape[1:]
    dates, rows, cols = valid_ref.shape
    values = valid_ref[...].astype(F32).reshape(dates * rows, cols)
    values = jnp.concatenate([values, jnp.zeros((dates * rows, width - cols), F32)], axis=1)
    packed_ref[blocks:] = values.astype(BF16).reshape(-1, piece, width)


def edge_kernel(
    step,
    steps,
    place_ref,
    inner_ref,
    outer_ref,
    above_ref,
    last_ref,
    weight_ref,
    up_ref,
    down_ref,
    table,
    high_ref,
    below_ref,
):
    dates = above_ref.shape[0]
    sort_halos(place_ref, inner_ref, outer_ref, high_ref, below_ref)
    down_table(weight_ref, table)
    taps = [
        jnp.concatenate([high_ref[:, 0], last_ref[...]], axis=0),
        jnp.concatenate([high_ref[:, 1], below_ref[:, 0]], axis=0),
        jnp.concatenate([above_ref[...], below_ref[:, 1]], axis=0),
    ]
    stored = down_rows(taps, table)
    up_ref[...] = stored[:dates]
    down_ref[...] = stored[dates:]


def activate_rows(date, dates, edge_flags, conv_refs, norm_refs, hidden_ref):
    conv_ref, up_ref, down_ref = conv_refs
    norm_ref, gain_ref, shift_ref = norm_refs
    scale = norm_ref[pl.ds(dates + date, 1), :] * gain_ref[...]
    shift = shift_ref[...] - norm_ref[pl.ds(date, 1), :] * scale

    def activate(values):
        linear = values.astype(F32) * scale + shift
        return linear * sigmoid(linear)

    rows = conv_ref.shape[1]
    hidden_ref[0, 0] = (activate(up_ref[0]) * edge_flags[0]).astype(BF16)
    hidden_ref[0, rows + 1] = (activate(down_ref[0]) * edge_flags[1]).astype(BF16)
    hidden_ref[0, 1 : rows + 1] = activate(conv_ref[0]).astype(BF16)


def block_kernel(
    date,
    dates,
    edge_ref,
    conv_ref,
    up_ref,
    down_ref,
    stats_ref,
    gain_ref,
    shift_ref,
    weight_ref,
    out_ref,
    norm_ref,
    sums_ref,
    table,
    hidden_ref,
    *,
    norm_count,
    row_devs,
):

    if date == 0:
        norm_table(stats_ref, norm_ref, dates, norm_count)
        pair_table(weight_ref, table, False)

    activate_rows(
        date,
        dates,
        edges(edge_ref, row_devs),
        (conv_ref, up_ref, down_ref),
        (norm_ref, gain_ref, shift_ref),
        hidden_ref,
    )
    stored = pair_rows(hidden_ref[0], table, False).astype(BF16)
    out_ref[0] = stored
    values = stored.astype(F32)
    store_sums(sums_ref, date, dates, column_sum(values), column_sum(values * values))


def encoding(day, width):
    lane = lax.broadcasted_iota(jnp.int32, (1, width), 1)
    frequency = jnp.exp((lane // 2).astype(F32) * (-2.0 * math.log(1000.0) / width))
    angles = day.astype(F32) * frequency
    return jnp.where(lane % 2 == 0, jnp.sin(angles), jnp.cos(angles))


def fold_keys(key_ref, query_ref, wide_ref, vector_ref, spread_ref, score_ref):
    depth, heads = query_ref.shape
    width = key_ref.shape[1]
    lanes = width // heads
    spread_ref[...] = head_spread(width)
    row = lax.broadcasted_iota(jnp.int32, (heads * depth, width), 0)
    lane = lax.broadcasted_iota(jnp.int32, (heads * depth, width), 1)
    widen = (row // depth == lane // lanes) & (row % depth == lane % lanes)
    wide = product(key_ref[...], widen.astype(F32).astype(BF16), 0, 0)
    wide_ref[...] = wide.astype(BF16)
    head = lax.broadcasted_iota(jnp.int32, (heads, width), 0)
    lane = lax.broadcasted_iota(jnp.int32, (heads, width), 1)
    inside = (lane // lanes == head).astype(F32).astype(BF16)
    high, low = split(query_ref[...])
    lower = (query_ref[...] - high.astype(F32) - low.astype(F32)).astype(BF16)
    spread = sum(product(part, inside, 1, 0) for part in (high, low, lower))
    step = lax.broadcasted_iota(jnp.int32, (depth, width), 0)
    place = lax.broadcasted_iota(jnp.int32, (depth, width), 1) % lanes
    queries = jnp.sum(jnp.where(step == place, spread * depth**-0.5, 0.0), axis=0, keepdims=True)
    place = lax.broadcasted_iota(jnp.int32, (1, width), 1) % lanes
    queries = queries + jnp.where((place == depth) | (place == depth + 1), 1.0, 0.0)
    vector_ref[...] = jnp.broadcast_to(queries, vector_ref.shape)
    folded = jnp.concatenate(split(wide * queries), axis=-1)
    folded = product(folded, spread_ref[...], 1, 0)
    score_ref[...] = jnp.concatenate(split(folded), axis=-1)


def source_of(turn_ref, device, devices):
    half = devices // 2
    core = (device + turn_ref[0]) % 2
    return core * half + (device // 2 + half - turn_ref[0] // 2) % half


def upstream_rows(grad_ref, turn_ref, rows, cols):
    devices = grad_ref.shape[0]
    piece = cols // devices
    parts = [
        grad_ref[source_of(turn_ref, device, devices), : rows * piece].reshape(rows, piece, -1)
        for device in range(devices)
    ]
    return jnp.concatenate(parts, axis=1)


def score_kernel(
    date,
    dates,
    day_ref,
    block_ref,
    stats_ref,
    gain_ref,
    shift_ref,
    grad_ref,
    valid_ref,
    turn_ref,
    key_ref,
    query_ref,
    feat_ref,
    exp_ref,
    attn_ref,
    norm_ref,
    packed_ref,
    own_ref,
    wide_ref,
    vector_ref,
    total,
    mean,
    spread_ref,
    score_ref,
    *,
    norm_count,
    grad_scale,
):
    rows, cols, width = block_ref.shape[1:]

    if date == 0:
        norm_table(stats_ref, norm_ref, dates, norm_count)
        fold_keys(key_ref, query_ref, wide_ref, vector_ref, spread_ref, score_ref)
        total[...] = jnp.zeros_like(total)
        mean[...] = jnp.zeros_like(mean)

    scale = norm_ref[pl.ds(dates + date, 1), :] * gain_ref[...]
    shift = shift_ref[...] - norm_ref[pl.ds(date, 1), :] * scale
    linear = block_ref[0].astype(F32) * scale + shift
    features = (linear * sigmoid(linear) + encoding(day_ref[turn_ref[0] * dates + date], width)).astype(BF16)
    feat_ref[0] = features
    upstream = upstream_rows(grad_ref, turn_ref, rows, cols)
    parts = split(upstream.astype(F32) * features.astype(F32))
    parts = jnp.concatenate(parts, axis=-1).reshape(rows * cols, 2 * width)
    attn = product(parts, spread_ref[...], 1, 0).reshape(rows, cols, width) * grad_scale
    both = product(features.reshape(rows * cols, width), score_ref[...], 1, 0)
    scores = (both[:, :width] + both[:, width:]).reshape(rows, cols, width)
    devices = grad_ref.shape[0]
    valid = jnp.zeros((rows, width), F32)
    for device in range(devices):
        piece = valid_ref[
            source_of(turn_ref, device, devices), pl.ds(date * rows, rows), :
        ]
        valid = valid + pltpu.roll(piece, device * (cols // devices), 1)
    diagonal = lax.broadcasted_iota(jnp.int32, (cols, cols), 0) == lax.broadcasted_iota(
        jnp.int32, (cols, cols), 1
    )
    ones = jnp.ones((cols, width), BF16)
    clear = jnp.concatenate(
        [jnp.where(diagonal, valid[row : row + 1], 0.0) for row in range(rows)], axis=0
    ).astype(BF16)
    clear = product(clear, ones, 1, 0).reshape(rows, cols, width)
    exponent = clear * jnp.exp(scores)
    running = total[...] + exponent
    share = jnp.where(running > 0.0, exponent / running, 0.0)
    total[...] = running
    mean[...] += share * (attn - mean[...])
    exp_ref[0] = exponent
    attn_ref[0] = attn

    if date == dates - 1:
        place = lax.broadcasted_iota(jnp.int32, (cols, width), 1) % rows
        for index, source in enumerate((total, mean)):
            dense = jnp.zeros((cols, width), F32)
            for row in range(rows):
                dense = dense + jnp.where(place == row, source[row], 0.0)
            if index == 0:
                packed_ref[0, 0] = dense.astype(BF16)
                own_ref[...] = dense
            else:
                packed_ref[0, 1], packed_ref[0, 2] = split(dense)


def attend_kernel(
    date,
    dates,
    packed_ref,
    own_ref,
    feat_ref,
    exp_ref,
    attn_ref,
    block_ref,
    norm_ref,
    gain_ref,
    shift_ref,
    query_ref,
    grad_ref,
    turn_ref,
    key_ref,
    grad_out_ref,
    part_ref,
    key_out_ref,
    vector_ref,
    sums_ref,
    inverse,
    average,
    attended,
    *,
    grad_scale,
):
    rows, cols, width = block_ref.shape[1:]

    if date == 0:
        totals = packed_ref[:, 0].astype(F32)
        reciprocal = 1.0 / jnp.sum(totals, axis=0)
        means = packed_ref[:, 1].astype(F32) + packed_ref[:, 2].astype(F32)
        mean = jnp.sum(totals * reciprocal * means, axis=0)
        own = own_ref[...]
        sent = own.astype(BF16).astype(F32)
        reciprocal = reciprocal * jnp.where(own > 0.0, sent / own, 0.0)
        place = lax.broadcasted_iota(jnp.int32, (cols, width), 1) % rows
        for values, target in ((reciprocal, inverse), (mean, average)):
            parts = jnp.concatenate(split(values), axis=-1)
            wide_place = jnp.concatenate([place, place], axis=-1)
            picked = jnp.concatenate(
                [jnp.where(wide_place == row, parts, jnp.zeros_like(parts)) for row in range(rows)], axis=0
            )
            target[...] = product(picked, head_spread(width), 1, 0).reshape(rows, cols, width)
        attended[...] = jnp.zeros_like(attended)
        key_out_ref[...] = jnp.zeros_like(key_out_ref)
        vector_ref[...] = jnp.zeros_like(vector_ref)

    features = feat_ref[0]
    weights = exp_ref[0] * inverse[...]
    rounded = weights.astype(BF16).astype(F32)
    attended[...] += rounded * features.astype(F32)
    score_grad = weights * (attn_ref[0] - average[...])
    spread_grad = score_grad * query_ref[0:1]
    rest = spread_grad - spread_grad.astype(BF16).astype(F32)
    lane = lax.broadcasted_iota(jnp.int32, spread_grad.shape, 2) % (width // 16)
    key_grads = jnp.where(lane == 5, rest, spread_grad).astype(BF16).reshape(rows * cols, width)
    key_out_ref[...] += product(features.reshape(rows * cols, width), key_grads, 0, 0)
    upstream = upstream_rows(grad_ref, turn_ref, rows, cols)
    feat_grad = rounded * (upstream.astype(F32) * grad_scale) + product(
        key_grads, key_ref[...], 1, 1
    ).reshape(rows, cols, width)
    gain = gain_ref[...]
    centred = (block_ref[0].astype(F32) - norm_ref[pl.ds(date, 1), :]) * norm_ref[
        pl.ds(dates + date, 1), :
    ]
    linear = centred * gain + shift_ref[...]
    part = sigmoid(linear)
    linear_grad = feat_grad * (part * (1.0 + linear * (1.0 - part)))
    first = column_sum(linear_grad)
    second = column_sum(linear_grad * centred)
    vector_ref[0:1] += second
    vector_ref[1:2] += first
    store_sums(sums_ref, date, dates, first * gain, second * gain)
    grad_out_ref[0] = (linear_grad * gain).astype(BF16)

    if date == dates - 1:
        devices, piece = part_ref.shape[0], part_ref.shape[2]
        for device in range(devices):
            part_ref[device] = attended[:, device * piece : (device + 1) * piece].astype(BF16)
        key_part = key_out_ref[...]
        place = lax.broadcasted_iota(jnp.int32, (width, width), 1) % (width // 16)
        both = pltpu.roll(key_part, width - 4, 1) + pltpu.roll(key_part, width - 5, 1)
        both = jnp.where(place == 0, both, 0.0)
        both = both + pltpu.roll(both, 1, 1)
        both = both + pltpu.roll(both, 2, 1)
        vector_ref[2:3] = 0.5 * jnp.sum(key_ref[...].astype(F32) * both, axis=0, keepdims=True)


def hidden_kernel(
    date,
    dates,
    edge_ref,
    grad_ref,
    block_ref,
    tails_ref,
    norm_ref,
    weight_ref,
    conv_ref,
    up_ref,
    down_ref,
    first_norm_ref,
    gain_ref,
    shift_ref,
    pre_ref,
    out_ref,
    vector_ref,
    sums_ref,
    table,
    factors,
    padded,
    *,
    norm_count,
    row_devs,
):
    rows, cols, width = block_ref.shape[1:]

    if date == 0:
        tails = group_sum(jnp.sum(tails_ref[...], axis=0)) / norm_count
        mean, inverse = norm_ref[:dates], norm_ref[dates:]
        slope = -inverse * inverse * tails[dates:]
        factors[0:dates] = slope
        factors[dates : 2 * dates] = -inverse * tails[:dates] - mean * slope
        vector_ref[...] = jnp.zeros_like(vector_ref)
        padded[:2] = jnp.zeros_like(padded[:2])
        padded[rows + 2 :] = jnp.zeros_like(padded[rows + 2 :])
        pair_table(weight_ref, table, True)

    inverse = norm_ref[pl.ds(dates + date, 1), :]
    slope = factors[pl.ds(date, 1), :]
    constant = factors[pl.ds(dates + date, 1), :]

    above_edge, below_edge = edges(edge_ref, row_devs)
    stored = (
        grad_ref[0].astype(F32) * inverse + (block_ref[0].astype(F32) * slope + constant)
    ).astype(BF16)
    pre_ref[0] = stored
    padded[2 : rows + 2] = stored
    hidden_grad = pair_rows(padded[...], table, True)
    gain = gain_ref[...]
    conv = jnp.concatenate([up_ref[0][None], conv_ref[0], down_ref[0][None]], axis=0)
    centred = (conv.astype(F32) - first_norm_ref[pl.ds(date, 1), :]) * first_norm_ref[
        pl.ds(dates + date, 1), :
    ]
    linear = centred * gain + shift_ref[...]
    part = sigmoid(linear)
    linear_grad = hidden_grad * (part * (1.0 + linear * (1.0 - part)))
    linear_grad = jnp.concatenate(
        [
            linear_grad[:1] * above_edge,
            linear_grad[1 : rows + 1],
            linear_grad[rows + 1 :] * below_edge,
        ],
        axis=0,
    )
    out_ref[0] = linear_grad.astype(BF16)
    first = column_sum(linear_grad)
    second = column_sum(linear_grad * centred)
    vector_ref[0:1] += second
    vector_ref[1:2] += first
    store_sums(sums_ref, date, dates, first * gain, second * gain)


def block_grad_kernel(
    date,
    dates,
    edge_ref,
    conv_ref,
    up_ref,
    down_ref,
    norm_ref,
    gain_ref,
    shift_ref,
    pre_ref,
    key_ref,
    out_ref,
    total,
    hidden_ref,
    *,
    row_devs,
):
    rows, cols, width = pre_ref.shape[1:]

    if date == 0:
        total[...] = jnp.zeros_like(total)

    activate_rows(
        date,
        dates,
        edges(edge_ref, row_devs),
        (conv_ref, up_ref, down_ref),
        (norm_ref, gain_ref, shift_ref),
        hidden_ref,
    )
    grads = pre_ref[0].astype(F32)
    grads = jnp.concatenate(
        [from_right(grads).astype(BF16), pre_ref[0], from_left(grads).astype(BF16)], axis=-1
    ).reshape(rows * cols, 3 * width)
    taps = jnp.concatenate(
        [hidden_ref[0, tap : tap + rows] for tap in range(3)], axis=-1
    ).reshape(rows * cols, 3 * width)
    total[...] += product(taps, grads, 0, 0)

    if date == dates - 1:
        for row_tap in range(3):
            for col_tap in range(3):
                base = (row_tap * 3 + col_tap) * width
                out_ref[base : base + width] = total[
                    row_tap * width : (row_tap + 1) * width, col_tap * width : (col_tap + 1) * width
                ].astype(BF16)
        key_part = key_ref[...]
        rest = key_part - key_part.astype(BF16).astype(F32)
        lanes = width // 16
        place = lax.broadcasted_iota(jnp.int32, key_part.shape, 1) % lanes
        rest = pltpu.roll(rest, lanes // 2, 1)
        key_rows = jnp.where(place < lanes // 2, key_part, rest).astype(BF16)
        out_ref[9 * width : 10 * width] = key_rows
        if out_ref.shape[0] > 10 * width:
            out_ref[10 * width :] = jnp.zeros_like(out_ref[10 * width :])


def conv_grad_kernel(
    date,
    dates,
    img_ref,
    above_ref,
    inner_ref,
    outer_ref,
    place_ref,
    conv_ref,
    grad_ref,
    tails_ref,
    norm_ref,
    gain_ref,
    vector_ref,
    other_ref,
    block_rows_ref,
    turn_ref,
    keep_ref,
    give_ref,
    factors,
    total,
    out_ref,
    high_ref,
    below_ref,
    *,
    norm_count,
):
    rows, cols, width = conv_ref.shape[1:]
    half = width // 2

    if date == 0:
        sort_halos(place_ref, inner_ref, outer_ref, high_ref, below_ref)
        tails = group_sum(jnp.sum(tails_ref[...], axis=0)) / norm_count
        mean, inverse = norm_ref[:dates], norm_ref[dates:]
        slope = -inverse * inverse * tails[dates:]
        factors[0:dates] = slope
        factors[dates : 2 * dates] = -inverse * tails[:dates] - mean * slope
        total[...] = jnp.zeros_like(total)

    scale = norm_ref[pl.ds(dates + date, 1), :] * gain_ref[...]
    slope = factors[pl.ds(date, 1), :]
    constant = factors[pl.ds(dates + date, 1), :]
    own = conv_ref[0].astype(F32) * slope + constant
    scaled = grad_ref[0].astype(F32) * scale
    stored = jnp.concatenate(
        [scaled[:1], scaled[1 : rows + 1] + own, scaled[rows + 1 :]], axis=0
    ).astype(BF16)
    moved = from_right(stored.astype(F32)).astype(BF16)
    reach = rows + 2
    grads = jnp.concatenate([stored, moved], axis=-1).reshape(reach * cols, 2 * width)
    even, odd = img_ref[0, :, 0], img_ref[0, :, 1]
    above = above_ref[0][None]
    taps = [
        jnp.concatenate([high_ref[date, :1], above, odd], axis=0),
        jnp.concatenate([high_ref[date, 1:], even, below_ref[date, :1]], axis=0),
        jnp.concatenate([above, odd, below_ref[date, 1:]], axis=0),
    ]
    taps = jnp.concatenate(taps, axis=-1).reshape(reach * cols, 3 * width)
    total[...] += product(taps, grads, 0, 0)

    if date == dates - 1:
        begin = block_rows_ref.shape[0]
        out_ref[:begin] = block_rows_ref[...]
        for tap in range(3):
            base = tap * width
            pair = total[base : base + width, :width].astype(BF16)
            left = total[base + half : base + width, width:].astype(BF16)
            start = begin + tap * 3 * half
            out_ref[start : start + half] = left
            out_ref[start + half : start + 3 * half] = pair
        start = begin + 9 * half
        for source in (vector_ref, other_ref):
            high, low = split(source[...])
            out_ref[start : start + 16] = jnp.concatenate([high, low], axis=0)
            start += 16
        if out_ref.shape[0] > start:
            out_ref[start:] = jnp.zeros_like(out_ref[start:])
        half_rows = keep_ref.shape[0]
        core = turn_ref[0] % 2
        start = pl.multiple_of(core * half_rows, half_rows)
        keep_ref[...] = out_ref[pl.ds(start, half_rows), :]
        start = pl.multiple_of((1 - core) * half_rows, half_rows)
        give_ref[...] = out_ref[pl.ds(start, half_rows), :]


def total_kernel(in_ref, out_ref):
    total = jnp.sum(in_ref[...].astype(F32), axis=0).astype(BF16)
    for copy in range(out_ref.shape[0]):
        out_ref[copy] = total


def final_kernel(
    depth,
    turn_ref,
    own_ref,
    other_ref,
    conv_ref,
    block_ref,
    key_ref,
    query_ref,
    *refs,
):
    vector_refs, rows_ref = refs[:-1], refs[-1]
    half_rows = own_ref.shape[0]
    core = turn_ref[0] % 2
    rows_ref[pl.ds(pl.multiple_of(core * half_rows, half_rows), half_rows), :] = own_ref[...]
    start = pl.multiple_of((1 - core) * half_rows, half_rows)
    rows_ref[pl.ds(start, half_rows), :] = other_ref[...]
    conv_end, block_end, width = conv_ref.shape[0], block_ref.shape[0], block_ref.shape[1]
    block_ref[...] = rows_ref[:block_end].astype(F32)
    wide = key_ref.shape[0]
    heads = wide // depth
    lanes = width // heads
    row = lax.broadcasted_iota(jnp.int32, (wide, width), 0)
    lane = lax.broadcasted_iota(jnp.int32, (wide, width), 1)
    narrow = (row // depth == lane // lanes) & (row % depth == lane % depth)
    narrow = narrow.astype(F32).astype(BF16)
    key_ref[...] = product(narrow, rows_ref[block_end : block_end + width], 1, 1)
    start = block_end + width
    conv_ref[...] = rows_ref[start : start + conv_end].astype(F32)
    start += conv_end
    for index in range(2):
        both = rows_ref[start : start + 16].astype(F32)
        both = both[:8] + both[8:]
        vector_refs[2 * index][...] = both[0:1]
        vector_refs[2 * index + 1][...] = both[1:2]
        start += 16
    both = rows_ref[start - 16 : start]
    row = lax.broadcasted_iota(jnp.int32, (heads, width), 0)
    lane = lax.broadcasted_iota(jnp.int32, (heads, width), 1)
    inside = row == lane // lanes
    step = lax.broadcasted_iota(jnp.int32, (8, width), 0)
    place = lax.broadcasted_iota(jnp.int32, (8, width), 1) % lanes
    steps = step == place
    query = jnp.zeros((8, heads), F32)
    for index in (2, 10):
        picked = jnp.where(steps, both[index : index + 1].astype(F32), 0.0).astype(BF16)
        query = query + product(picked, inside.astype(F32).astype(BF16), 1, 1)
    query_ref[...] = query[:depth]


def call(kernel, dates, inputs, outputs, scratch, flops):
    in_specs, out_specs, arrays, out_shape, buffers = [], [], [], [], []
    in_vmem, in_hbm = pl.BlockSpec(memory_space=pltpu.VMEM), pl.BlockSpec(memory_space=pltpu.HBM)
    loads, stores = [], []
    for place, (kind, array) in enumerate(inputs):
        if kind == "scalar":
            in_specs.append(pl.BlockSpec(memory_space=pltpu.SMEM))
        elif "far" in kind:
            array = pltpu.with_memory_space_constraint(array, pltpu.HBM)
            in_specs.append(in_hbm)
            loads.append(place)
            buffers.append(pltpu.VMEM(array.shape, array.dtype))
        else:
            in_specs.append(in_vmem)
        arrays.append(array)
    for place, (kind, shape, dtype) in enumerate(outputs):
        if "far" in kind:
            out_shape.append(pltpu.HBM(shape, dtype))
            out_specs.append(in_hbm)
            stores.append(place)
            buffers.append(pltpu.VMEM(shape, dtype))
        else:
            out_shape.append(jax.ShapeDtypeStruct(shape, dtype))
            out_specs.append(in_vmem)
    copies = len(loads) + len(stores)
    kinds = [kind for kind, _ in inputs] + [kind for kind, _, _ in outputs]

    def body(*refs):
        views, rest = list(refs[: len(kinds)]), refs[len(kinds) :]
        buffer_refs, ready, rest = rest[:copies], rest[copies], rest[copies + 1 :]

        def copies_of(place, index, inward):
            outside, inside = views[place], buffer_refs[index]
            made = []
            for date in range(dates if "date" in kinds[place] else 1):
                here = pl.ds(date, 1) if "date" in kinds[place] else slice(None)
                pair = (outside.at[here], inside.at[here])
                source, target = pair if inward else pair[::-1]
                made.append(pltpu.make_async_copy(source, target, ready.at[index, date]))
            return made

        incoming = [copies_of(place, index, True) for index, place in enumerate(loads)]
        outgoing = [
            copies_of(len(inputs) + place, len(loads) + index, False)
            for index, place in enumerate(stores)
        ]
        for date in range(dates):
            for moves in incoming:
                if date < len(moves):
                    moves[date].start()
        for index, place in enumerate(loads):
            views[place] = buffer_refs[index]
        for index, place in enumerate(stores):
            views[len(inputs) + place] = buffer_refs[len(loads) + index]
        for date in range(dates):
            for moves in incoming:
                if date < len(moves):
                    moves[date].wait()
            here = [
                view.at[pl.ds(date, 1)] if "date" in kind else view
                for view, kind in zip(views, kinds)
            ]
            kernel(date, dates, *here, *rest)
            for moves in outgoing:
                if len(moves) == dates:
                    moves[date].start()
                elif date == dates - 1:
                    moves[0].start()
        for moves in outgoing:
            for move in moves:
                move.wait()

    moved = sum(array.size * array.dtype.itemsize for _, array in inputs)
    return pl.pallas_call(
        body,
        in_specs=in_specs,
        out_specs=out_specs,
        out_shape=out_shape,
        scratch_shapes=buffers + [pltpu.SemaphoreType.DMA((max(copies, 1), dates))] + scratch,
        compiler_params=pltpu.CompilerParams(vmem_limit_bytes=40 * MIB),
        cost_estimate=pl.CostEstimate(flops=flops, bytes_accessed=2 * moved, transcendentals=0),
    )(*arrays)


def shifted(array, by):
    devices = lax.axis_size("rows")
    pairs = [(i, i + by) for i in range(devices) if 0 <= i + by < devices]
    return lax.ppermute(array, "rows", pairs)


def same_core(array):
    devices = lax.axis_size("dates")
    pieces = [array]
    for step in range(2, devices, 2):
        pairs = [((i + step) % devices, i) for i in range(devices)]
        pieces.append(lax.ppermute(array, "dates", pairs))
    return pieces


def sum_of_parts(parts):
    devices = lax.axis_size("dates")
    place = lax.axis_index("dates")
    total = lax.dynamic_index_in_dim(parts, place, 0, keepdims=False).astype(F32)
    for step in range(1, devices):
        piece = lax.dynamic_index_in_dim(parts, (place + step) % devices, 0, keepdims=False)
        pairs = [(i, (i + step) % devices) for i in range(devices)]
        total = total + lax.ppermute(piece, "dates", pairs).astype(F32)
    return total.astype(BF16)


def exchange(pieces, axes):
    return lax.all_to_all(pieces, axes, split_axis=0, concat_axis=0, tiled=True)


def gather(array, axis):
    return lax.all_gather(array, axis, axis=0, tiled=True)


def other_core(array):
    devices = lax.axis_size("dates")
    return lax.ppermute(array, "dates", [(i, i + 1 - 2 * (i % 2)) for i in range(devices)])


def exchange_cores(pieces):
    axes = ("rows", "dates")
    devices = lax.axis_size(axes)
    groups = [list(range(core, devices, 2)) for core in range(2)]
    return lax.all_to_all(
        pieces, axes, split_axis=0, concat_axis=0, axis_index_groups=groups, tiled=True
    )


def scatter(rows_array):
    devices = lax.axis_size(("rows", "dates")) // 2
    count, width = rows_array.shape
    return exchange_cores(rows_array.reshape(devices, count // devices, width))


def collect(pieces):
    spread = pl.pallas_call(
        total_kernel,
        out_shape=jax.ShapeDtypeStruct(pieces.shape, BF16),
        compiler_params=pltpu.CompilerParams(vmem_limit_bytes=16 * MIB),
    )(pieces)
    count, rows, width = pieces.shape
    return exchange_cores(spread).reshape(count * rows, width)


def padded_count(count, devices):
    step = 8 * devices
    return -(-count // step) * step


def local(
    images,
    day_index,
    valid,
    out_grad,
    conv_weight,
    first_gain,
    first_shift,
    block_weight,
    gn_gain,
    gn_shift,
    key_weight,
    queries,
):
    dates, rows_here, cols, pair_width = images.shape
    width = conv_weight.shape[-1]
    row_devs, date_devs = lax.axis_size("rows"), lax.axis_size("dates")
    devices = row_devs * date_devs
    rows = rows_here // 2
    heads, depth = queries.shape
    norm_count = float(rows * row_devs * cols * (width // GROUPS))
    grad_scale = float(rows * row_devs * cols) ** (-0.5)
    date_start = lax.axis_index("dates") * dates
    frame = (dates, rows, cols, width)
    edge_rows = (dates, cols, width)
    flops = 2 * dates * rows * cols * width * width

    rows_of = lambda vector: vector.reshape(1, width)
    first_gain, first_shift = rows_of(first_gain), rows_of(first_shift)
    gn_gain, gn_shift = rows_of(gn_gain), rows_of(gn_shift)
    last = images[:, -1]
    above = shifted(last, 1)
    grad_rows = out_grad.size // width
    row_place = lax.axis_index("rows")
    place = row_place.reshape(1)
    valid_count = valid.shape[0] * rows
    piece = out_grad.shape[1]
    packed_shape = ((grad_rows + valid_count) // piece, piece, width)
    in_hbm, in_vmem = pl.BlockSpec(memory_space=pltpu.HBM), pl.BlockSpec(memory_space=pltpu.VMEM)
    images_near, inner, outer, packed = pl.pallas_call(
        load_kernel,
        in_specs=[pl.BlockSpec(memory_space=pltpu.SMEM), in_vmem, in_hbm, in_hbm, in_hbm],
        out_specs=[in_vmem] * 4,
        out_shape=[
            jax.ShapeDtypeStruct(shape, BF16)
            for shape in (images.shape,) + ((dates, 2, cols, pair_width),) * 2 + (packed_shape,)
        ],
        scratch_shapes=[pltpu.VMEM(valid.shape, valid.dtype), pltpu.SemaphoreType.DMA((3,))],
        compiler_params=pltpu.CompilerParams(vmem_limit_bytes=16 * MIB),
    )(
        place,
        last,
        *[pltpu.with_memory_space_constraint(x, pltpu.HBM) for x in (images, out_grad, valid)],
    )
    packed = packed.reshape(grad_rows + valid_count, width)
    inner, outer, above, packed = lax.optimization_barrier((inner, outer, above, packed))
    inner = lax.ppermute(inner, "rows", [(i, i ^ 1) for i in range(row_devs)])
    pairs = [(i, i + 1) for i in range(1, row_devs - 1, 2)]
    outer = lax.ppermute(outer, "rows", pairs + [(j, i) for i, j in pairs])
    paired = images.reshape(dates, rows, 2, cols, pair_width)
    conv_out, sums = call(
        down_kernel,
        dates,
        [
            ("date", images_near.reshape(paired.shape)),
            ("date", above),
            ("all", conv_weight),
        ],
        [("date far", frame, BF16), ("all", (row_devs, 2 * dates, width), F32)],
        [pltpu.VMEM((3 * pair_width, 2 * width), BF16)],
        6 * flops,
    )
    stats = exchange(sums, "rows")
    inner, outer, last, _ = lax.optimization_barrier((inner, outer, last, sums))
    halo_up, halo_down = call(
        edge_kernel,
        1,
        [
            ("scalar", place),
            ("all", inner),
            ("all", outer),
            ("all", above),
            ("all", last),
            ("all", conv_weight),
        ],
        [("all", edge_rows, BF16)] * 2,
        [
            pltpu.VMEM((3 * pair_width, 2 * width), BF16),
            pltpu.VMEM(inner.shape, BF16),
            pltpu.VMEM(inner.shape, BF16),
        ],
        6 * flops // rows,
    )
    turn = lax.axis_index("dates").reshape(1)
    packed, _ = lax.optimization_barrier((packed, halo_up))
    pieces = same_core(packed)
    block_out, first_norm, sums = call(
        functools.partial(block_kernel, norm_count=norm_count, row_devs=row_devs),
        dates,
        [
            ("scalar", place),
            ("date far", conv_out),
            ("date", halo_up),
            ("date", halo_down),
            ("all", stats),
            ("all", first_gain),
            ("all", first_shift),
            ("all far", block_weight),
        ],
        [
            ("date far", frame, BF16),
            ("all", (2 * dates, width), F32),
            ("all", (row_devs, 2 * dates, width), F32),
        ],
        [
            pltpu.VMEM((4 * width, 6 * width), BF16),
            pltpu.VMEM((1, rows + 2, cols, width), BF16),
        ],
        9 * flops,
    )
    stats = exchange(sums, "rows")
    pieces, _ = lax.optimization_barrier((pieces, sums))
    sources = jnp.stack(pieces + [other_core(piece) for piece in pieces])
    clear = lax.dynamic_slice_in_dim(sources, grad_rows + date_start * rows, dates * rows, 1)
    clear = clear.astype(F32)
    features, exponent, attn, norm, packed, own_total, key_wide, query_wide = call(
        functools.partial(score_kernel, norm_count=norm_count, grad_scale=grad_scale),
        dates,
        [
            ("scalar", day_index),
            ("date far", block_out),
            ("all", stats),
            ("all", gn_gain),
            ("all", gn_shift),
            ("all", sources),
            ("all", clear),
            ("scalar", turn),
            ("all", key_weight.T),
            ("all", queries.T),
        ],
        [
            ("date", frame, BF16),
            ("date", frame, F32),
            ("date", frame, F32),
            ("all", (2 * dates, width), F32),
            ("all", (1, 3, cols, width), BF16),
            ("all", (cols, width), F32),
            ("all", (width, width), BF16),
            ("all", (8, width), F32),
        ],
        [
            pltpu.VMEM(frame[1:], F32),
            pltpu.VMEM(frame[1:], F32),
            pltpu.VMEM((2 * width, width), BF16),
            pltpu.VMEM((width, 2 * width), BF16),
        ],
        5 * flops,
    )
    packed = gather(packed, "dates")
    block_grad, attended, key_part, vectors, sums = call(
        functools.partial(attend_kernel, grad_scale=grad_scale),
        dates,
        [
            ("all", packed),
            ("all", own_total),
            ("date", features),
            ("date", exponent),
            ("date", attn),
            ("date", block_out),
            ("all", norm),
            ("all", gn_gain),
            ("all", gn_shift),
            ("all", query_wide),
            ("all", sources),
            ("scalar", turn),
            ("all", key_wide),
        ],
        [
            ("date far", frame, BF16),
            ("all far", (date_devs, rows, cols // date_devs, width), BF16),
            ("all far", (width, width), F32),
            ("all", (8, width), F32),
            ("all", (row_devs, 2 * dates, width), F32),
        ],
        [pltpu.VMEM(frame[1:], F32)] * 3,
        5 * flops,
    )
    tails = exchange(sums, "rows")
    pre_grad, linear_grad, first_vectors, sums = call(
        functools.partial(hidden_kernel, norm_count=norm_count, row_devs=row_devs),
        dates,
        [
            ("scalar", place),
            ("date far", block_grad),
            ("date far", block_out),
            ("all", tails),
            ("all", norm),
            ("all far", block_weight),
            ("date far", conv_out),
            ("date", halo_up),
            ("date", halo_down),
            ("all", first_norm),
            ("all", first_gain),
            ("all", first_shift),
        ],
        [
            ("date far", frame, BF16),
            ("date far", (dates, rows + 2, cols, width), BF16),
            ("all", (8, width), F32),
            ("all", (row_devs, 2 * dates, width), F32),
        ],
        [
            pltpu.VMEM((6 * width, 4 * width), BF16),
            pltpu.VMEM((2 * dates, width), F32),
            pltpu.VMEM((rows + 4, cols, width), BF16),
        ],
        9 * flops,
    )
    tails = exchange(sums, "rows")
    (block_rows,) = call(
        functools.partial(block_grad_kernel, row_devs=row_devs),
        dates,
        [
            ("scalar", place),
            ("date far", conv_out),
            ("date", halo_up),
            ("date", halo_down),
            ("all", first_norm),
            ("all", first_gain),
            ("all", first_shift),
            ("date far", pre_grad),
            ("all far", key_part),
        ],
        [("all far", (10 * width, width), BF16)],
        [
            pltpu.VMEM((3 * width, 3 * width), F32),
            pltpu.VMEM((1, rows + 2, cols, width), BF16),
        ],
        9 * flops,
    )
    tails, block_rows = lax.optimization_barrier((tails, block_rows))
    conv_count = 9 * pair_width // 2 + 32
    half_rows = padded_count(10 * width + conv_count, devices) // 2
    keep, give = call(
        functools.partial(conv_grad_kernel, norm_count=norm_count),
        dates,
        [
            ("date far", paired),
            ("date", above),
            ("all", inner),
            ("all", outer),
            ("scalar", place),
            ("date far", conv_out),
            ("date far", linear_grad),
            ("all", tails),
            ("all", first_norm),
            ("all", first_gain),
            ("all", first_vectors),
            ("all", vectors),
            ("all far", block_rows),
            ("scalar", turn),
        ],
        [("all", (half_rows, width), BF16)] * 2,
        [
            pltpu.VMEM((2 * dates, width), F32),
            pltpu.VMEM((3 * pair_width, 2 * width), F32),
            pltpu.VMEM((2 * half_rows, width), BF16),
            pltpu.VMEM(inner.shape, BF16),
            pltpu.VMEM(inner.shape, BF16),
        ],
        6 * flops,
    )
    rows_half = (keep.astype(F32) + other_core(give).astype(F32)).astype(BF16)
    pieces = scatter(rows_half)
    attended, _ = lax.optimization_barrier((attended, rows_half))
    attended = sum_of_parts(attended)
    rows_half = collect(pieces)
    rows_other = other_core(rows_half)
    shapes = [
        (9 * pair_width // 2, width),
        (9 * width, width),
        (heads * depth, width),
        (depth, heads),
    ] + [(1, width)] * 4
    conv_total, block_total, key_total, query_total, *totals = pl.pallas_call(
        functools.partial(final_kernel, depth),
        in_specs=[
            pl.BlockSpec(memory_space=pltpu.SMEM),
            pl.BlockSpec(memory_space=pltpu.VMEM),
            pl.BlockSpec(memory_space=pltpu.VMEM),
        ],
        out_shape=[jax.ShapeDtypeStruct(shape, F32) for shape in shapes],
        scratch_shapes=[pltpu.VMEM((2 * half_rows, width), BF16)],
        compiler_params=pltpu.CompilerParams(vmem_limit_bytes=16 * MIB),
    )(turn, rows_half, rows_other)
    totals = [total.reshape(width) for total in totals]
    return (
        attended,
        conv_total.reshape(conv_weight.shape),
        totals[0],
        totals[1],
        block_total.reshape(block_weight.shape),
        totals[2],
        totals[3],
        key_total.T,
        query_total.T,
    )


def solution(mesh):
    return jax.shard_map(
        local,
        mesh=mesh,
        in_specs=(
            P("dates", "rows", None, None),
            P(),
            P(None, "rows", "dates"),
            P("rows", "dates", None),
            P(),
            P(),
            P(),
            P(),
            P(),
            P(),
            P(),
            P(),
        ),
        out_specs=(P("rows", "dates", None), P(), P(), P(), P(), P(), P(), P(), P()),
        check_vma=False,
    )
```

```python
import functools
import math

import jax
import jax.numpy as jnp
from jax import lax
from jax.experimental import pallas as pl
from jax.experimental.pallas import tpu as pltpu
from jax.sharding import PartitionSpec as P

GROUPS = 4


EPS = 1e-05


MIB = 1 << 20


F32 = jnp.float32


BF16 = jnp.bfloat16


def product(left, right, left_dim, right_dim):
    return lax.dot_general(
        left, right, (((left_dim,), (right_dim,)), ((), ())), preferred_element_type=F32
    )


def group_sum(values):
    width = values.shape[-1]
    lane_group = lax.broadcasted_iota(jnp.int32, values.shape, 1) // (width // GROUPS)
    spread = jnp.zeros_like(values)
    for group in range(GROUPS):
        inside = lane_group == group
        total = jnp.sum(jnp.where(inside, values, 0.0), axis=1, keepdims=True)
        spread = spread + jnp.where(inside, total, 0.0)
    return spread


def sigmoid(values):
    return 0.5 * jnp.tanh(0.5 * values) + 0.5


def from_left(values):
    moved = pltpu.roll(values, 1, 1)
    first = moved[:, :8]
    column = lax.broadcasted_iota(jnp.int32, first.shape, 1)
    return jnp.concatenate([jnp.where(column > 0, first, 0.0), moved[:, 8:]], axis=1)


def from_right(values):
    count = values.shape[1]
    moved = pltpu.roll(values, count - 1, 1)
    last = moved[:, count - 8 :]
    column = lax.broadcasted_iota(jnp.int32, last.shape, 1)
    return jnp.concatenate([moved[:, : count - 8], jnp.where(column < 7, last, 0.0)], axis=1)


def tap_table(weight_ref, table, backward):
    width = weight_ref.shape[-1]
    for row_tap in range(3):
        for col_tap in range(3):
            deep = slice(row_tap * width, (row_tap + 1) * width)
            wide = slice(col_tap * width, (col_tap + 1) * width)
            if backward:
                table[wide, deep] = weight_ref[2 - row_tap, col_tap]
            else:
                table[deep, wide] = weight_ref[row_tap, col_tap]


def tap_rows(padded, table, backward):
    rows, cols, width = padded.shape[0] - 2, *padded.shape[1:]
    taps = jnp.concatenate([padded[tap : tap + rows] for tap in range(3)], axis=-1)
    taps = taps.reshape(rows * cols, 3 * width)
    terms = product(taps, table[...], 1, 1 if backward else 0).reshape(rows, cols, 3 * width)
    first, last = (from_right, from_left) if backward else (from_left, from_right)
    return (
        terms[..., width : 2 * width]
        + first(terms[..., :width])
        + last(terms[..., 2 * width :])
    )


def column_sum(values):
    return jnp.sum(jnp.sum(values, axis=0), axis=0, keepdims=True)


def edges(place_ref, row_devs):
    place = place_ref[0]
    return (place > 0).astype(F32), (place < row_devs - 1).astype(F32)


def head_spread(width):
    lane = lax.broadcasted_iota(jnp.int32, (2 * width, width), 1) // (width // 16)
    head = lax.broadcasted_iota(jnp.int32, (2 * width, width), 0) % width // (width // 16)
    return (lane == head).astype(F32).astype(BF16)


def split(values):
    high = values.astype(BF16)
    return high, (values - high.astype(F32)).astype(BF16)


def store_sums(sums_ref, date, dates, first, second):
    for copy in range(sums_ref.shape[0]):
        sums_ref[copy, pl.ds(date, 1), :] = first
        sums_ref[copy, pl.ds(dates + date, 1), :] = second


def norm_table(sums_ref, table_ref, dates, norm_count):
    means = group_sum(jnp.sum(sums_ref[...], axis=0)) / norm_count
    mean = means[:dates]
    table_ref[:dates] = mean
    table_ref[dates:] = 1.0 / jnp.sqrt(means[dates:] - mean * mean + EPS)


def down_table(weight_ref, table):
    half = weight_ref.shape[2]
    for tap in range(3):
        base = tap * 2 * half
        table[base : base + half, : 2 * half] = weight_ref[tap, 1]
        table[base + half : base + 2 * half, : 2 * half] = weight_ref[tap, 2]
        table[base : base + half, 2 * half :] = jnp.zeros_like(weight_ref[tap, 0])
        table[base + half : base + 2 * half, 2 * half :] = weight_ref[tap, 0]


def down_rows(taps, table):
    rows, cols, width = taps[0].shape
    taps = jnp.concatenate(taps, axis=-1).reshape(rows * cols, 3 * width)
    both = product(taps, table[...], 1, 0).reshape(rows, cols, 2 * width)
    return (both[..., :width] + from_left(both[..., width:])).astype(BF16)


def down_kernel(
    date, dates, img_ref, above_ref, weight_ref, out_ref, sums_ref, table
):

    if date == 0:
        down_table(weight_ref, table)

    even, odd = img_ref[0, :, 0], img_ref[0, :, 1]
    above = jnp.concatenate([above_ref[0][None], odd[:-1]], axis=0)
    stored = down_rows([above, even, odd], table)
    out_ref[0] = stored
    values = stored.astype(F32)
    store_sums(sums_ref, date, dates, column_sum(values), column_sum(values * values))


def sort_halos(place_ref, inner_ref, outer_ref, high_ref, below_ref):
    odd = place_ref[0] % 2 == 1

    @pl.when(odd)
    def _():
        high_ref[...] = inner_ref[...]
        below_ref[...] = outer_ref[...]

    @pl.when(jnp.logical_not(odd))
    def _():
        high_ref[...] = outer_ref[...]
        below_ref[...] = inner_ref[...]


def load_kernel(
    place_ref,
    last_ref,
    img_hbm,
    grad_hbm,
    valid_hbm,
    img_ref,
    inner_ref,
    outer_ref,
    packed_ref,
    valid_ref,
    ready,
):
    blocks = grad_hbm.shape[0]
    moves = [
        pltpu.make_async_copy(grad_hbm, packed_ref.at[pl.ds(0, blocks)], ready.at[0]),
        pltpu.make_async_copy(valid_hbm, valid_ref, ready.at[1]),
        pltpu.make_async_copy(img_hbm, img_ref, ready.at[2]),
    ]
    for move in moves:
        move.start()
    for move in moves:
        move.wait()
    rows = img_ref.shape[1]
    odd = place_ref[0] % 2 == 1

    @pl.when(odd)
    def _():
        inner_ref[...] = img_ref[:, :2]
        outer_ref[...] = img_ref[:, rows - 3 : rows - 1]

    @pl.when(jnp.logical_not(odd))
    def _():
        inner_ref[...] = img_ref[:, rows - 3 : rows - 1]
        outer_ref[...] = img_ref[:, :2]

    piece, width = packed_ref.shape[1:]
    dates, rows, cols = valid_ref.shape
    values = valid_ref[...].astype(F32).reshape(dates * rows, cols)
    values = jnp.concatenate([values, jnp.zeros((dates * rows, width - cols), F32)], axis=1)
    packed_ref[blocks:] = values.astype(BF16).reshape(-1, piece, width)


def edge_kernel(
    step,
    steps,
    place_ref,
    inner_ref,
    outer_ref,
    above_ref,
    last_ref,
    weight_ref,
    up_ref,
    down_ref,
    table,
    high_ref,
    below_ref,
):
    dates = above_ref.shape[0]
    sort_halos(place_ref, inner_ref, outer_ref, high_ref, below_ref)
    down_table(weight_ref, table)
    taps = [
        jnp.concatenate([high_ref[:, 0], last_ref[...]], axis=0),
        jnp.concatenate([high_ref[:, 1], below_ref[:, 0]], axis=0),
        jnp.concatenate([above_ref[...], below_ref[:, 1]], axis=0),
    ]
    stored = down_rows(taps, table)
    up_ref[...] = stored[:dates]
    down_ref[...] = stored[dates:]


def activate_rows(date, dates, edge_flags, conv_refs, norm_refs, hidden_ref):
    conv_ref, up_ref, down_ref = conv_refs
    norm_ref, gain_ref, shift_ref = norm_refs
    scale = norm_ref[pl.ds(dates + date, 1), :] * gain_ref[...]
    shift = shift_ref[...] - norm_ref[pl.ds(date, 1), :] * scale

    def activate(values):
        linear = values.astype(F32) * scale + shift
        return linear * sigmoid(linear)

    rows = conv_ref.shape[1]
    hidden_ref[0, 0] = (activate(up_ref[0]) * edge_flags[0]).astype(BF16)
    hidden_ref[0, rows + 1] = (activate(down_ref[0]) * edge_flags[1]).astype(BF16)
    hidden_ref[0, 1 : rows + 1] = activate(conv_ref[0]).astype(BF16)


def block_kernel(
    date,
    dates,
    edge_ref,
    conv_ref,
    up_ref,
    down_ref,
    stats_ref,
    gain_ref,
    shift_ref,
    weight_ref,
    out_ref,
    norm_ref,
    sums_ref,
    table,
    hidden_ref,
    *,
    norm_count,
    row_devs,
):

    if date == 0:
        norm_table(stats_ref, norm_ref, dates, norm_count)
        tap_table(weight_ref, table, False)

    activate_rows(
        date,
        dates,
        edges(edge_ref, row_devs),
        (conv_ref, up_ref, down_ref),
        (norm_ref, gain_ref, shift_ref),
        hidden_ref,
    )
    stored = tap_rows(hidden_ref[0], table, False).astype(BF16)
    out_ref[0] = stored
    values = stored.astype(F32)
    store_sums(sums_ref, date, dates, column_sum(values), column_sum(values * values))


def encoding(day, width):
    lane = lax.broadcasted_iota(jnp.int32, (1, width), 1)
    frequency = jnp.exp((lane // 2).astype(F32) * (-2.0 * math.log(1000.0) / width))
    angles = day.astype(F32) * frequency
    return jnp.where(lane % 2 == 0, jnp.sin(angles), jnp.cos(angles))


def fold_keys(key_ref, query_ref, wide_ref, vector_ref, spread_ref, score_ref):
    depth, heads = query_ref.shape
    width = key_ref.shape[1]
    lanes = width // heads
    spread_ref[...] = head_spread(width)
    row = lax.broadcasted_iota(jnp.int32, (heads * depth, width), 0)
    lane = lax.broadcasted_iota(jnp.int32, (heads * depth, width), 1)
    widen = (row // depth == lane // lanes) & (row % depth == lane % lanes)
    wide = product(key_ref[...], widen.astype(F32).astype(BF16), 0, 0)
    wide_ref[...] = wide.astype(BF16)
    head = lax.broadcasted_iota(jnp.int32, (heads, width), 0)
    lane = lax.broadcasted_iota(jnp.int32, (heads, width), 1)
    inside = (lane // lanes == head).astype(F32).astype(BF16)
    high, low = split(query_ref[...])
    lower = (query_ref[...] - high.astype(F32) - low.astype(F32)).astype(BF16)
    spread = sum(product(part, inside, 1, 0) for part in (high, low, lower))
    step = lax.broadcasted_iota(jnp.int32, (depth, width), 0)
    place = lax.broadcasted_iota(jnp.int32, (depth, width), 1) % lanes
    queries = jnp.sum(jnp.where(step == place, spread * depth**-0.5, 0.0), axis=0, keepdims=True)
    place = lax.broadcasted_iota(jnp.int32, (1, width), 1) % lanes
    queries = queries + jnp.where((place == depth) | (place == depth + 1), 1.0, 0.0)
    vector_ref[...] = jnp.broadcast_to(queries, vector_ref.shape)
    folded = jnp.concatenate(split(wide * queries), axis=-1)
    folded = product(folded, spread_ref[...], 1, 0)
    score_ref[...] = jnp.concatenate(split(folded), axis=-1)


def source_of(turn_ref, device, devices):
    half = devices // 2
    core = (device + turn_ref[0]) % 2
    return core * half + (device // 2 + half - turn_ref[0] // 2) % half


def upstream_rows(grad_ref, turn_ref, rows, cols):
    devices = grad_ref.shape[0]
    piece = cols // devices
    parts = [
        grad_ref[source_of(turn_ref, device, devices), : rows * piece].reshape(rows, piece, -1)
        for device in range(devices)
    ]
    return jnp.concatenate(parts, axis=1)


def score_kernel(
    date,
    dates,
    day_ref,
    block_ref,
    stats_ref,
    gain_ref,
    shift_ref,
    grad_ref,
    valid_ref,
    turn_ref,
    key_ref,
    query_ref,
    feat_ref,
    exp_ref,
    attn_ref,
    norm_ref,
    packed_ref,
    own_ref,
    wide_ref,
    vector_ref,
    total,
    mean,
    spread_ref,
    score_ref,
    *,
    norm_count,
    grad_scale,
):
    rows, cols, width = block_ref.shape[1:]

    if date == 0:
        norm_table(stats_ref, norm_ref, dates, norm_count)
        fold_keys(key_ref, query_ref, wide_ref, vector_ref, spread_ref, score_ref)
        total[...] = jnp.zeros_like(total)
        mean[...] = jnp.zeros_like(mean)

    scale = norm_ref[pl.ds(dates + date, 1), :] * gain_ref[...]
    shift = shift_ref[...] - norm_ref[pl.ds(date, 1), :] * scale
    linear = block_ref[0].astype(F32) * scale + shift
    features = (linear * sigmoid(linear) + encoding(day_ref[turn_ref[0] * dates + date], width)).astype(BF16)
    feat_ref[0] = features
    upstream = upstream_rows(grad_ref, turn_ref, rows, cols)
    parts = split(upstream.astype(F32) * features.astype(F32))
    parts = jnp.concatenate(parts, axis=-1).reshape(rows * cols, 2 * width)
    attn = product(parts, spread_ref[...], 1, 0).reshape(rows, cols, width) * grad_scale
    both = product(features.reshape(rows * cols, width), score_ref[...], 1, 0)
    scores = (both[:, :width] + both[:, width:]).reshape(rows, cols, width)
    devices = grad_ref.shape[0]
    valid = jnp.zeros((rows, width), F32)
    for device in range(devices):
        piece = valid_ref[
            source_of(turn_ref, device, devices), pl.ds(date * rows, rows), :
        ]
        valid = valid + pltpu.roll(piece, device * (cols // devices), 1)
    diagonal = lax.broadcasted_iota(jnp.int32, (cols, cols), 0) == lax.broadcasted_iota(
        jnp.int32, (cols, cols), 1
    )
    ones = jnp.ones((cols, width), BF16)
    clear = jnp.concatenate(
        [jnp.where(diagonal, valid[row : row + 1], 0.0) for row in range(rows)], axis=0
    ).astype(BF16)
    clear = product(clear, ones, 1, 0).reshape(rows, cols, width)
    exponent = clear * jnp.exp(scores)
    running = total[...] + exponent
    share = jnp.where(running > 0.0, exponent / running, 0.0)
    total[...] = running
    mean[...] += share * (attn - mean[...])
    exp_ref[0] = exponent
    attn_ref[0] = attn

    if date == dates - 1:
        place = lax.broadcasted_iota(jnp.int32, (cols, width), 1) % rows
        for index, source in enumerate((total, mean)):
            dense = jnp.zeros((cols, width), F32)
            for row in range(rows):
                dense = dense + jnp.where(place == row, source[row], 0.0)
            if index == 0:
                packed_ref[0, 0] = dense.astype(BF16)
                own_ref[...] = dense
            else:
                packed_ref[0, 1], packed_ref[0, 2] = split(dense)


def attend_kernel(
    date,
    dates,
    packed_ref,
    own_ref,
    feat_ref,
    exp_ref,
    attn_ref,
    block_ref,
    norm_ref,
    gain_ref,
    shift_ref,
    query_ref,
    grad_ref,
    turn_ref,
    key_ref,
    grad_out_ref,
    part_ref,
    key_out_ref,
    vector_ref,
    sums_ref,
    inverse,
    average,
    attended,
    *,
    grad_scale,
):
    rows, cols, width = block_ref.shape[1:]

    if date == 0:
        totals = packed_ref[:, 0].astype(F32)
        reciprocal = 1.0 / jnp.sum(totals, axis=0)
        means = packed_ref[:, 1].astype(F32) + packed_ref[:, 2].astype(F32)
        mean = jnp.sum(totals * reciprocal * means, axis=0)
        own = own_ref[...]
        sent = own.astype(BF16).astype(F32)
        reciprocal = reciprocal * jnp.where(own > 0.0, sent / own, 0.0)
        place = lax.broadcasted_iota(jnp.int32, (cols, width), 1) % rows
        for values, target in ((reciprocal, inverse), (mean, average)):
            parts = jnp.concatenate(split(values), axis=-1)
            wide_place = jnp.concatenate([place, place], axis=-1)
            picked = jnp.concatenate(
                [jnp.where(wide_place == row, parts, jnp.zeros_like(parts)) for row in range(rows)], axis=0
            )
            target[...] = product(picked, head_spread(width), 1, 0).reshape(rows, cols, width)
        attended[...] = jnp.zeros_like(attended)
        key_out_ref[...] = jnp.zeros_like(key_out_ref)
        vector_ref[...] = jnp.zeros_like(vector_ref)

    features = feat_ref[0]
    weights = exp_ref[0] * inverse[...]
    rounded = weights.astype(BF16).astype(F32)
    attended[...] += rounded * features.astype(F32)
    score_grad = weights * (attn_ref[0] - average[...])
    spread_grad = score_grad * query_ref[0:1]
    rest = spread_grad - spread_grad.astype(BF16).astype(F32)
    lane = lax.broadcasted_iota(jnp.int32, spread_grad.shape, 2) % (width // 16)
    key_grads = jnp.where(lane == 5, rest, spread_grad).astype(BF16).reshape(rows * cols, width)
    key_out_ref[...] += product(features.reshape(rows * cols, width), key_grads, 0, 0)
    upstream = upstream_rows(grad_ref, turn_ref, rows, cols)
    feat_grad = rounded * (upstream.astype(F32) * grad_scale) + product(
        key_grads, key_ref[...], 1, 1
    ).reshape(rows, cols, width)
    gain = gain_ref[...]
    centred = (block_ref[0].astype(F32) - norm_ref[pl.ds(date, 1), :]) * norm_ref[
        pl.ds(dates + date, 1), :
    ]
    linear = centred * gain + shift_ref[...]
    part = sigmoid(linear)
    linear_grad = feat_grad * (part * (1.0 + linear * (1.0 - part)))
    first = column_sum(linear_grad)
    second = column_sum(linear_grad * centred)
    vector_ref[0:1] += second
    vector_ref[1:2] += first
    store_sums(sums_ref, date, dates, first * gain, second * gain)
    grad_out_ref[0] = (linear_grad * gain).astype(BF16)

    if date == dates - 1:
        devices, piece = part_ref.shape[0], part_ref.shape[2]
        for device in range(devices):
            part_ref[device] = attended[:, device * piece : (device + 1) * piece].astype(BF16)
        key_part = key_out_ref[...]
        place = lax.broadcasted_iota(jnp.int32, (width, width), 1) % (width // 16)
        both = pltpu.roll(key_part, width - 4, 1) + pltpu.roll(key_part, width - 5, 1)
        both = jnp.where(place == 0, both, 0.0)
        both = both + pltpu.roll(both, 1, 1)
        both = both + pltpu.roll(both, 2, 1)
        vector_ref[2:3] = 0.5 * jnp.sum(key_ref[...].astype(F32) * both, axis=0, keepdims=True)


def hidden_kernel(
    date,
    dates,
    edge_ref,
    grad_ref,
    block_ref,
    tails_ref,
    norm_ref,
    weight_ref,
    conv_ref,
    up_ref,
    down_ref,
    first_norm_ref,
    gain_ref,
    shift_ref,
    pre_ref,
    out_ref,
    vector_ref,
    sums_ref,
    table,
    factors,
    padded,
    *,
    norm_count,
    row_devs,
):
    rows, cols, width = block_ref.shape[1:]

    if date == 0:
        tails = group_sum(jnp.sum(tails_ref[...], axis=0)) / norm_count
        mean, inverse = norm_ref[:dates], norm_ref[dates:]
        slope = -inverse * inverse * tails[dates:]
        factors[0:dates] = slope
        factors[dates : 2 * dates] = -inverse * tails[:dates] - mean * slope
        vector_ref[...] = jnp.zeros_like(vector_ref)
        padded[:2] = jnp.zeros_like(padded[:2])
        padded[rows + 2 :] = jnp.zeros_like(padded[rows + 2 :])
        tap_table(weight_ref, table, True)

    inverse = norm_ref[pl.ds(dates + date, 1), :]
    slope = factors[pl.ds(date, 1), :]
    constant = factors[pl.ds(dates + date, 1), :]

    above_edge, below_edge = edges(edge_ref, row_devs)
    stored = (
        grad_ref[0].astype(F32) * inverse + (block_ref[0].astype(F32) * slope + constant)
    ).astype(BF16)
    pre_ref[0] = stored
    padded[2 : rows + 2] = stored
    hidden_grad = tap_rows(padded[...], table, True)
    gain = gain_ref[...]
    conv = jnp.concatenate([up_ref[0][None], conv_ref[0], down_ref[0][None]], axis=0)
    centred = (conv.astype(F32) - first_norm_ref[pl.ds(date, 1), :]) * first_norm_ref[
        pl.ds(dates + date, 1), :
    ]
    linear = centred * gain + shift_ref[...]
    part = sigmoid(linear)
    linear_grad = hidden_grad * (part * (1.0 + linear * (1.0 - part)))
    linear_grad = jnp.concatenate(
        [
            linear_grad[:1] * above_edge,
            linear_grad[1 : rows + 1],
            linear_grad[rows + 1 :] * below_edge,
        ],
        axis=0,
    )
    out_ref[0] = linear_grad.astype(BF16)
    first = column_sum(linear_grad)
    second = column_sum(linear_grad * centred)
    vector_ref[0:1] += second
    vector_ref[1:2] += first
    store_sums(sums_ref, date, dates, first * gain, second * gain)


def block_grad_kernel(
    date,
    dates,
    edge_ref,
    conv_ref,
    up_ref,
    down_ref,
    norm_ref,
    gain_ref,
    shift_ref,
    pre_ref,
    key_ref,
    out_ref,
    total,
    hidden_ref,
    *,
    row_devs,
):
    rows, cols, width = pre_ref.shape[1:]

    if date == 0:
        total[...] = jnp.zeros_like(total)

    activate_rows(
        date,
        dates,
        edges(edge_ref, row_devs),
        (conv_ref, up_ref, down_ref),
        (norm_ref, gain_ref, shift_ref),
        hidden_ref,
    )
    grads = pre_ref[0].astype(F32)
    grads = jnp.concatenate(
        [from_right(grads).astype(BF16), pre_ref[0], from_left(grads).astype(BF16)], axis=-1
    ).reshape(rows * cols, 3 * width)
    taps = jnp.concatenate(
        [hidden_ref[0, tap : tap + rows] for tap in range(3)], axis=-1
    ).reshape(rows * cols, 3 * width)
    total[...] += product(taps, grads, 0, 0)

    if date == dates - 1:
        for row_tap in range(3):
            for col_tap in range(3):
                base = (row_tap * 3 + col_tap) * width
                out_ref[base : base + width] = total[
                    row_tap * width : (row_tap + 1) * width, col_tap * width : (col_tap + 1) * width
                ].astype(BF16)
        key_part = key_ref[...]
        rest = key_part - key_part.astype(BF16).astype(F32)
        lanes = width // 16
        place = lax.broadcasted_iota(jnp.int32, key_part.shape, 1) % lanes
        rest = pltpu.roll(rest, lanes // 2, 1)
        key_rows = jnp.where(place < lanes // 2, key_part, rest).astype(BF16)
        out_ref[9 * width : 10 * width] = key_rows
        if out_ref.shape[0] > 10 * width:
            out_ref[10 * width :] = jnp.zeros_like(out_ref[10 * width :])


def conv_grad_kernel(
    date,
    dates,
    img_ref,
    above_ref,
    inner_ref,
    outer_ref,
    place_ref,
    conv_ref,
    grad_ref,
    tails_ref,
    norm_ref,
    gain_ref,
    vector_ref,
    other_ref,
    block_rows_ref,
    turn_ref,
    keep_ref,
    give_ref,
    factors,
    total,
    out_ref,
    high_ref,
    below_ref,
    *,
    norm_count,
):
    rows, cols, width = conv_ref.shape[1:]
    half = width // 2

    if date == 0:
        sort_halos(place_ref, inner_ref, outer_ref, high_ref, below_ref)
        tails = group_sum(jnp.sum(tails_ref[...], axis=0)) / norm_count
        mean, inverse = norm_ref[:dates], norm_ref[dates:]
        slope = -inverse * inverse * tails[dates:]
        factors[0:dates] = slope
        factors[dates : 2 * dates] = -inverse * tails[:dates] - mean * slope
        total[...] = jnp.zeros_like(total)

    scale = norm_ref[pl.ds(dates + date, 1), :] * gain_ref[...]
    slope = factors[pl.ds(date, 1), :]
    constant = factors[pl.ds(dates + date, 1), :]
    own = conv_ref[0].astype(F32) * slope + constant
    scaled = grad_ref[0].astype(F32) * scale
    stored = jnp.concatenate(
        [scaled[:1], scaled[1 : rows + 1] + own, scaled[rows + 1 :]], axis=0
    ).astype(BF16)
    moved = from_right(stored.astype(F32)).astype(BF16)
    reach = rows + 2
    grads = jnp.concatenate([stored, moved], axis=-1).reshape(reach * cols, 2 * width)
    even, odd = img_ref[0, :, 0], img_ref[0, :, 1]
    above = above_ref[0][None]
    taps = [
        jnp.concatenate([high_ref[date, :1], above, odd], axis=0),
        jnp.concatenate([high_ref[date, 1:], even, below_ref[date, :1]], axis=0),
        jnp.concatenate([above, odd, below_ref[date, 1:]], axis=0),
    ]
    taps = jnp.concatenate(taps, axis=-1).reshape(reach * cols, 3 * width)
    total[...] += product(taps, grads, 0, 0)

    if date == dates - 1:
        begin = block_rows_ref.shape[0]
        out_ref[:begin] = block_rows_ref[...]
        for tap in range(3):
            base = tap * width
            pair = total[base : base + width, :width].astype(BF16)
            left = total[base + half : base + width, width:].astype(BF16)
            start = begin + tap * 3 * half
            out_ref[start : start + half] = left
            out_ref[start + half : start + 3 * half] = pair
        start = begin + 9 * half
        for source in (vector_ref, other_ref):
            high, low = split(source[...])
            out_ref[start : start + 16] = jnp.concatenate([high, low], axis=0)
            start += 16
        if out_ref.shape[0] > start:
            out_ref[start:] = jnp.zeros_like(out_ref[start:])
        half_rows = keep_ref.shape[0]
        core = turn_ref[0] % 2
        start = pl.multiple_of(core * half_rows, half_rows)
        keep_ref[...] = out_ref[pl.ds(start, half_rows), :]
        start = pl.multiple_of((1 - core) * half_rows, half_rows)
        give_ref[...] = out_ref[pl.ds(start, half_rows), :]


def total_kernel(in_ref, out_ref):
    total = jnp.sum(in_ref[...].astype(F32), axis=0).astype(BF16)
    for copy in range(out_ref.shape[0]):
        out_ref[copy] = total


def final_kernel(
    depth,
    turn_ref,
    own_ref,
    other_ref,
    conv_ref,
    block_ref,
    key_ref,
    query_ref,
    *refs,
):
    vector_refs, rows_ref = refs[:-1], refs[-1]
    half_rows = own_ref.shape[0]
    core = turn_ref[0] % 2
    rows_ref[pl.ds(pl.multiple_of(core * half_rows, half_rows), half_rows), :] = own_ref[...]
    start = pl.multiple_of((1 - core) * half_rows, half_rows)
    rows_ref[pl.ds(start, half_rows), :] = other_ref[...]
    conv_end, block_end, width = conv_ref.shape[0], block_ref.shape[0], block_ref.shape[1]
    block_ref[...] = rows_ref[:block_end].astype(F32)
    wide = key_ref.shape[0]
    heads = wide // depth
    lanes = width // heads
    row = lax.broadcasted_iota(jnp.int32, (wide, width), 0)
    lane = lax.broadcasted_iota(jnp.int32, (wide, width), 1)
    narrow = (row // depth == lane // lanes) & (row % depth == lane % depth)
    narrow = narrow.astype(F32).astype(BF16)
    key_ref[...] = product(narrow, rows_ref[block_end : block_end + width], 1, 1)
    start = block_end + width
    conv_ref[...] = rows_ref[start : start + conv_end].astype(F32)
    start += conv_end
    for index in range(2):
        both = rows_ref[start : start + 16].astype(F32)
        both = both[:8] + both[8:]
        vector_refs[2 * index][...] = both[0:1]
        vector_refs[2 * index + 1][...] = both[1:2]
        start += 16
    both = rows_ref[start - 16 : start]
    row = lax.broadcasted_iota(jnp.int32, (heads, width), 0)
    lane = lax.broadcasted_iota(jnp.int32, (heads, width), 1)
    inside = row == lane // lanes
    step = lax.broadcasted_iota(jnp.int32, (8, width), 0)
    place = lax.broadcasted_iota(jnp.int32, (8, width), 1) % lanes
    steps = step == place
    query = jnp.zeros((8, heads), F32)
    for index in (2, 10):
        picked = jnp.where(steps, both[index : index + 1].astype(F32), 0.0).astype(BF16)
        query = query + product(picked, inside.astype(F32).astype(BF16), 1, 1)
    query_ref[...] = query[:depth]


def call(kernel, dates, inputs, outputs, scratch, flops):
    in_specs, out_specs, arrays, out_shape, buffers = [], [], [], [], []
    in_vmem, in_hbm = pl.BlockSpec(memory_space=pltpu.VMEM), pl.BlockSpec(memory_space=pltpu.HBM)
    loads, stores = [], []
    for place, (kind, array) in enumerate(inputs):
        if kind == "scalar":
            in_specs.append(pl.BlockSpec(memory_space=pltpu.SMEM))
        elif "far" in kind:
            array = pltpu.with_memory_space_constraint(array, pltpu.HBM)
            in_specs.append(in_hbm)
            loads.append(place)
            buffers.append(pltpu.VMEM(array.shape, array.dtype))
        else:
            in_specs.append(in_vmem)
        arrays.append(array)
    for place, (kind, shape, dtype) in enumerate(outputs):
        if "far" in kind:
            out_shape.append(pltpu.HBM(shape, dtype))
            out_specs.append(in_hbm)
            stores.append(place)
            buffers.append(pltpu.VMEM(shape, dtype))
        else:
            out_shape.append(jax.ShapeDtypeStruct(shape, dtype))
            out_specs.append(in_vmem)
    copies = len(loads) + len(stores)
    kinds = [kind for kind, _ in inputs] + [kind for kind, _, _ in outputs]

    def body(*refs):
        views, rest = list(refs[: len(kinds)]), refs[len(kinds) :]
        buffer_refs, ready, rest = rest[:copies], rest[copies], rest[copies + 1 :]

        def copies_of(place, index, inward):
            outside, inside = views[place], buffer_refs[index]
            made = []
            for date in range(dates if "date" in kinds[place] else 1):
                here = pl.ds(date, 1) if "date" in kinds[place] else slice(None)
                pair = (outside.at[here], inside.at[here])
                source, target = pair if inward else pair[::-1]
                made.append(pltpu.make_async_copy(source, target, ready.at[index, date]))
            return made

        incoming = [copies_of(place, index, True) for index, place in enumerate(loads)]
        outgoing = [
            copies_of(len(inputs) + place, len(loads) + index, False)
            for index, place in enumerate(stores)
        ]
        def fetch(date):
            for moves in incoming:
                if date < len(moves):
                    moves[date].start()

        fetch(0)
        fetch(1)
        for index, place in enumerate(loads):
            views[place] = buffer_refs[index]
        for index, place in enumerate(stores):
            views[len(inputs) + place] = buffer_refs[len(loads) + index]
        for date in range(dates):
            for moves in incoming:
                if date < len(moves):
                    moves[date].wait()
            fetch(date + 2)
            here = [
                view.at[pl.ds(date, 1)] if "date" in kind else view
                for view, kind in zip(views, kinds)
            ]
            kernel(date, dates, *here, *rest)
            for moves in outgoing:
                if len(moves) == dates:
                    moves[date].start()
                elif date == dates - 1:
                    moves[0].start()
        for moves in outgoing:
            for move in moves:
                move.wait()

    moved = sum(array.size * array.dtype.itemsize for _, array in inputs)
    return pl.pallas_call(
        body,
        in_specs=in_specs,
        out_specs=out_specs,
        out_shape=out_shape,
        scratch_shapes=buffers + [pltpu.SemaphoreType.DMA((max(copies, 1), dates))] + scratch,
        compiler_params=pltpu.CompilerParams(vmem_limit_bytes=40 * MIB),
        cost_estimate=pl.CostEstimate(flops=flops, bytes_accessed=2 * moved, transcendentals=0),
    )(*arrays)


def shifted(array, by):
    devices = lax.axis_size("rows")
    pairs = [(i, i + by) for i in range(devices) if 0 <= i + by < devices]
    return lax.ppermute(array, "rows", pairs)


def same_core(array):
    devices = lax.axis_size("dates")
    pieces = [array]
    for step in range(2, devices, 2):
        pairs = [((i + step) % devices, i) for i in range(devices)]
        pieces.append(lax.ppermute(array, "dates", pairs))
    return pieces


def sum_of_parts(parts):
    devices = lax.axis_size("dates")
    place = lax.axis_index("dates")
    total = lax.dynamic_index_in_dim(parts, place, 0, keepdims=False).astype(F32)
    for step in range(1, devices):
        piece = lax.dynamic_index_in_dim(parts, (place + step) % devices, 0, keepdims=False)
        pairs = [(i, (i + step) % devices) for i in range(devices)]
        total = total + lax.ppermute(piece, "dates", pairs).astype(F32)
    return total.astype(BF16)


def exchange(pieces, axes):
    return lax.all_to_all(pieces, axes, split_axis=0, concat_axis=0, tiled=True)


def gather(array, axis):
    return lax.all_gather(array, axis, axis=0, tiled=True)


def other_core(array):
    devices = lax.axis_size("dates")
    return lax.ppermute(array, "dates", [(i, i + 1 - 2 * (i % 2)) for i in range(devices)])


def exchange_cores(pieces):
    axes = ("rows", "dates")
    devices = lax.axis_size(axes)
    groups = [list(range(core, devices, 2)) for core in range(2)]
    return lax.all_to_all(
        pieces, axes, split_axis=0, concat_axis=0, axis_index_groups=groups, tiled=True
    )


def scatter(rows_array):
    devices = lax.axis_size(("rows", "dates")) // 2
    count, width = rows_array.shape
    return exchange_cores(rows_array.reshape(devices, count // devices, width))


def collect(pieces):
    spread = pl.pallas_call(
        total_kernel,
        out_shape=jax.ShapeDtypeStruct(pieces.shape, BF16),
        compiler_params=pltpu.CompilerParams(vmem_limit_bytes=16 * MIB),
    )(pieces)
    count, rows, width = pieces.shape
    return exchange_cores(spread).reshape(count * rows, width)


def padded_count(count, devices):
    step = 8 * devices
    return -(-count // step) * step


def local(
    images,
    day_index,
    valid,
    out_grad,
    conv_weight,
    first_gain,
    first_shift,
    block_weight,
    gn_gain,
    gn_shift,
    key_weight,
    queries,
):
    dates, rows_here, cols, pair_width = images.shape
    width = conv_weight.shape[-1]
    row_devs, date_devs = lax.axis_size("rows"), lax.axis_size("dates")
    devices = row_devs * date_devs
    rows = rows_here // 2
    heads, depth = queries.shape
    norm_count = float(rows * row_devs * cols * (width // GROUPS))
    grad_scale = float(rows * row_devs * cols) ** (-0.5)
    date_start = lax.axis_index("dates") * dates
    frame = (dates, rows, cols, width)
    edge_rows = (dates, cols, width)
    flops = 2 * dates * rows * cols * width * width

    rows_of = lambda vector: vector.reshape(1, width)
    first_gain, first_shift = rows_of(first_gain), rows_of(first_shift)
    gn_gain, gn_shift = rows_of(gn_gain), rows_of(gn_shift)
    last = images[:, -1]
    above = shifted(last, 1)
    grad_rows = out_grad.size // width
    row_place = lax.axis_index("rows")
    place = row_place.reshape(1)
    valid_count = valid.shape[0] * rows
    piece = out_grad.shape[1]
    packed_shape = ((grad_rows + valid_count) // piece, piece, width)
    in_hbm, in_vmem = pl.BlockSpec(memory_space=pltpu.HBM), pl.BlockSpec(memory_space=pltpu.VMEM)
    images_near, inner, outer, packed = pl.pallas_call(
        load_kernel,
        in_specs=[pl.BlockSpec(memory_space=pltpu.SMEM), in_vmem, in_hbm, in_hbm, in_hbm],
        out_specs=[in_vmem] * 4,
        out_shape=[
            jax.ShapeDtypeStruct(shape, BF16)
            for shape in (images.shape,) + ((dates, 2, cols, pair_width),) * 2 + (packed_shape,)
        ],
        scratch_shapes=[pltpu.VMEM(valid.shape, valid.dtype), pltpu.SemaphoreType.DMA((3,))],
        compiler_params=pltpu.CompilerParams(vmem_limit_bytes=16 * MIB),
    )(
        place,
        last,
        *[pltpu.with_memory_space_constraint(x, pltpu.HBM) for x in (images, out_grad, valid)],
    )
    packed = packed.reshape(grad_rows + valid_count, width)
    inner, outer, above, packed = lax.optimization_barrier((inner, outer, above, packed))
    inner = lax.ppermute(inner, "rows", [(i, i ^ 1) for i in range(row_devs)])
    pairs = [(i, i + 1) for i in range(1, row_devs - 1, 2)]
    outer = lax.ppermute(outer, "rows", pairs + [(j, i) for i, j in pairs])
    paired = images.reshape(dates, rows, 2, cols, pair_width)
    conv_out, sums = call(
        down_kernel,
        dates,
        [
            ("date", images_near.reshape(paired.shape)),
            ("date", above),
            ("all", conv_weight),
        ],
        [("date far", frame, BF16), ("all", (row_devs, 2 * dates, width), F32)],
        [pltpu.VMEM((3 * pair_width, 2 * width), BF16)],
        6 * flops,
    )
    stats = exchange(sums, "rows")
    inner, outer, last, _ = lax.optimization_barrier((inner, outer, last, sums))
    halo_up, halo_down = call(
        edge_kernel,
        1,
        [
            ("scalar", place),
            ("all", inner),
            ("all", outer),
            ("all", above),
            ("all", last),
            ("all", conv_weight),
        ],
        [("all", edge_rows, BF16)] * 2,
        [
            pltpu.VMEM((3 * pair_width, 2 * width), BF16),
            pltpu.VMEM(inner.shape, BF16),
            pltpu.VMEM(inner.shape, BF16),
        ],
        6 * flops // rows,
    )
    turn = lax.axis_index("dates").reshape(1)
    packed, _ = lax.optimization_barrier((packed, halo_up))
    pieces = same_core(packed)
    block_out, first_norm, sums = call(
        functools.partial(block_kernel, norm_count=norm_count, row_devs=row_devs),
        dates,
        [
            ("scalar", place),
            ("date far", conv_out),
            ("date", halo_up),
            ("date", halo_down),
            ("all", stats),
            ("all", first_gain),
            ("all", first_shift),
            ("all far", block_weight),
        ],
        [
            ("date far", frame, BF16),
            ("all", (2 * dates, width), F32),
            ("all", (row_devs, 2 * dates, width), F32),
        ],
        [
            pltpu.VMEM((3 * width, 3 * width), BF16),
            pltpu.VMEM((1, rows + 2, cols, width), BF16),
        ],
        9 * flops,
    )
    stats = exchange(sums, "rows")
    pieces, _ = lax.optimization_barrier((pieces, sums))
    sources = jnp.stack(pieces + [other_core(piece) for piece in pieces])
    clear = lax.dynamic_slice_in_dim(sources, grad_rows + date_start * rows, dates * rows, 1)
    clear = clear.astype(F32)
    features, exponent, attn, norm, packed, own_total, key_wide, query_wide = call(
        functools.partial(score_kernel, norm_count=norm_count, grad_scale=grad_scale),
        dates,
        [
            ("scalar", day_index),
            ("date far", block_out),
            ("all", stats),
            ("all", gn_gain),
            ("all", gn_shift),
            ("all", sources),
            ("all", clear),
            ("scalar", turn),
            ("all", key_weight.T),
            ("all", queries.T),
        ],
        [
            ("date", frame, BF16),
            ("date", frame, F32),
            ("date", frame, F32),
            ("all", (2 * dates, width), F32),
            ("all", (1, 3, cols, width), BF16),
            ("all", (cols, width), F32),
            ("all", (width, width), BF16),
            ("all", (8, width), F32),
        ],
        [
            pltpu.VMEM(frame[1:], F32),
            pltpu.VMEM(frame[1:], F32),
            pltpu.VMEM((2 * width, width), BF16),
            pltpu.VMEM((width, 2 * width), BF16),
        ],
        5 * flops,
    )
    packed = gather(packed, "dates")
    block_grad, attended, key_part, vectors, sums = call(
        functools.partial(attend_kernel, grad_scale=grad_scale),
        dates,
        [
            ("all", packed),
            ("all", own_total),
            ("date", features),
            ("date", exponent),
            ("date", attn),
            ("date", block_out),
            ("all", norm),
            ("all", gn_gain),
            ("all", gn_shift),
            ("all", query_wide),
            ("all", sources),
            ("scalar", turn),
            ("all", key_wide),
        ],
        [
            ("date far", frame, BF16),
            ("all far", (date_devs, rows, cols // date_devs, width), BF16),
            ("all far", (width, width), F32),
            ("all", (8, width), F32),
            ("all", (row_devs, 2 * dates, width), F32),
        ],
        [pltpu.VMEM(frame[1:], F32)] * 3,
        5 * flops,
    )
    tails = exchange(sums, "rows")
    pre_grad, linear_grad, first_vectors, sums = call(
        functools.partial(hidden_kernel, norm_count=norm_count, row_devs=row_devs),
        dates,
        [
            ("scalar", place),
            ("date far", block_grad),
            ("date far", block_out),
            ("all", tails),
            ("all", norm),
            ("all far", block_weight),
            ("date far", conv_out),
            ("date", halo_up),
            ("date", halo_down),
            ("all", first_norm),
            ("all", first_gain),
            ("all", first_shift),
        ],
        [
            ("date far", frame, BF16),
            ("date far", (dates, rows + 2, cols, width), BF16),
            ("all", (8, width), F32),
            ("all", (row_devs, 2 * dates, width), F32),
        ],
        [
            pltpu.VMEM((3 * width, 3 * width), BF16),
            pltpu.VMEM((2 * dates, width), F32),
            pltpu.VMEM((rows + 4, cols, width), BF16),
        ],
        9 * flops,
    )
    tails = exchange(sums, "rows")
    (block_rows,) = call(
        functools.partial(block_grad_kernel, row_devs=row_devs),
        dates,
        [
            ("scalar", place),
            ("date far", conv_out),
            ("date", halo_up),
            ("date", halo_down),
            ("all", first_norm),
            ("all", first_gain),
            ("all", first_shift),
            ("date far", pre_grad),
            ("all far", key_part),
        ],
        [("all far", (10 * width, width), BF16)],
        [
            pltpu.VMEM((3 * width, 3 * width), F32),
            pltpu.VMEM((1, rows + 2, cols, width), BF16),
        ],
        9 * flops,
    )
    tails, block_rows = lax.optimization_barrier((tails, block_rows))
    conv_count = 9 * pair_width // 2 + 32
    half_rows = padded_count(10 * width + conv_count, devices) // 2
    keep, give = call(
        functools.partial(conv_grad_kernel, norm_count=norm_count),
        dates,
        [
            ("date far", paired),
            ("date", above),
            ("all", inner),
            ("all", outer),
            ("scalar", place),
            ("date far", conv_out),
            ("date far", linear_grad),
            ("all", tails),
            ("all", first_norm),
            ("all", first_gain),
            ("all", first_vectors),
            ("all", vectors),
            ("all far", block_rows),
            ("scalar", turn),
        ],
        [("all", (half_rows, width), BF16)] * 2,
        [
            pltpu.VMEM((2 * dates, width), F32),
            pltpu.VMEM((3 * pair_width, 2 * width), F32),
            pltpu.VMEM((2 * half_rows, width), BF16),
            pltpu.VMEM(inner.shape, BF16),
            pltpu.VMEM(inner.shape, BF16),
        ],
        6 * flops,
    )
    rows_half = (keep.astype(F32) + other_core(give).astype(F32)).astype(BF16)
    pieces = scatter(rows_half)
    attended, _ = lax.optimization_barrier((attended, rows_half))
    attended = sum_of_parts(attended)
    rows_half = collect(pieces)
    rows_other = other_core(rows_half)
    shapes = [
        (9 * pair_width // 2, width),
        (9 * width, width),
        (heads * depth, width),
        (depth, heads),
    ] + [(1, width)] * 4
    conv_total, block_total, key_total, query_total, *totals = pl.pallas_call(
        functools.partial(final_kernel, depth),
        in_specs=[
            pl.BlockSpec(memory_space=pltpu.SMEM),
            pl.BlockSpec(memory_space=pltpu.VMEM),
            pl.BlockSpec(memory_space=pltpu.VMEM),
        ],
        out_shape=[jax.ShapeDtypeStruct(shape, F32) for shape in shapes],
        scratch_shapes=[pltpu.VMEM((2 * half_rows, width), BF16)],
        compiler_params=pltpu.CompilerParams(vmem_limit_bytes=16 * MIB),
    )(turn, rows_half, rows_other)
    totals = [total.reshape(width) for total in totals]
    return (
        attended,
        conv_total.reshape(conv_weight.shape),
        totals[0],
        totals[1],
        block_total.reshape(block_weight.shape),
        totals[2],
        totals[3],
        key_total.T,
        query_total.T,
    )


def solution(mesh):
    return jax.shard_map(
        local,
        mesh=mesh,
        in_specs=(
            P("dates", "rows", None, None),
            P(),
            P(None, "rows", "dates"),
            P("rows", "dates", None),
            P(),
            P(),
            P(),
            P(),
            P(),
            P(),
            P(),
            P(),
        ),
        out_specs=(P("rows", "dates", None), P(), P(), P(), P(), P(), P(), P(), P()),
        check_vma=False,
    )
```

```python
import functools
import math

import jax
import jax.numpy as jnp
from jax import lax
from jax.experimental import pallas as pl
from jax.experimental.pallas import tpu as pltpu
from jax.sharding import PartitionSpec as P

GROUPS = 4


EPS = 1e-05


MIB = 1 << 20


F32 = jnp.float32


BF16 = jnp.bfloat16


def product(left, right, left_dim, right_dim):
    return lax.dot_general(
        left, right, (((left_dim,), (right_dim,)), ((), ())), preferred_element_type=F32
    )


def group_sum(values):
    width = values.shape[-1]
    lane_group = lax.broadcasted_iota(jnp.int32, values.shape, 1) // (width // GROUPS)
    spread = jnp.zeros_like(values)
    for group in range(GROUPS):
        inside = lane_group == group
        total = jnp.sum(jnp.where(inside, values, 0.0), axis=1, keepdims=True)
        spread = spread + jnp.where(inside, total, 0.0)
    return spread


def sigmoid(values):
    return 0.5 * jnp.tanh(0.5 * values) + 0.5


def from_left(values):
    moved = pltpu.roll(values, 1, 1)
    first = moved[:, :8]
    column = lax.broadcasted_iota(jnp.int32, first.shape, 1)
    return jnp.concatenate([jnp.where(column > 0, first, 0.0), moved[:, 8:]], axis=1)


def from_right(values):
    count = values.shape[1]
    moved = pltpu.roll(values, count - 1, 1)
    last = moved[:, count - 8 :]
    column = lax.broadcasted_iota(jnp.int32, last.shape, 1)
    return jnp.concatenate([moved[:, : count - 8], jnp.where(column < 7, last, 0.0)], axis=1)


def tap_table(weight_ref, table, backward):
    width = weight_ref.shape[-1]
    for row_tap in range(3):
        for col_tap in range(3):
            deep = slice(row_tap * width, (row_tap + 1) * width)
            wide = slice(col_tap * width, (col_tap + 1) * width)
            if backward:
                table[wide, deep] = weight_ref[2 - row_tap, col_tap]
            else:
                table[deep, wide] = weight_ref[row_tap, col_tap]


def tap_rows(padded, table, backward):
    rows, cols, width = padded.shape[0] - 2, *padded.shape[1:]
    taps = jnp.concatenate([padded[tap : tap + rows] for tap in range(3)], axis=-1)
    taps = taps.reshape(rows * cols, 3 * width)
    terms = product(taps, table[...], 1, 1 if backward else 0).reshape(rows, cols, 3 * width)
    first, last = (from_right, from_left) if backward else (from_left, from_right)
    return (
        terms[..., width : 2 * width]
        + first(terms[..., :width])
        + last(terms[..., 2 * width :])
    )


def column_sum(values):
    return jnp.sum(jnp.sum(values, axis=0), axis=0, keepdims=True)


def edges(place_ref, row_devs):
    place = place_ref[0]
    return (place > 0).astype(F32), (place < row_devs - 1).astype(F32)


def head_spread(width):
    lane = lax.broadcasted_iota(jnp.int32, (2 * width, width), 1) // (width // 16)
    head = lax.broadcasted_iota(jnp.int32, (2 * width, width), 0) % width // (width // 16)
    return (lane == head).astype(F32).astype(BF16)


def split(values):
    high = values.astype(BF16)
    return high, (values - high.astype(F32)).astype(BF16)


def store_sums(sums_ref, date, dates, first, second):
    for copy in range(sums_ref.shape[0]):
        sums_ref[copy, pl.ds(date, 1), :] = first
        sums_ref[copy, pl.ds(dates + date, 1), :] = second


def norm_table(sums_ref, table_ref, dates, norm_count):
    means = group_sum(jnp.sum(sums_ref[...], axis=0)) / norm_count
    mean = means[:dates]
    table_ref[:dates] = mean
    table_ref[dates:] = 1.0 / jnp.sqrt(means[dates:] - mean * mean + EPS)


def down_table(weight_ref, table):
    half = weight_ref.shape[2]
    for tap in range(3):
        base = tap * 2 * half
        table[base : base + half, : 2 * half] = weight_ref[tap, 1]
        table[base + half : base + 2 * half, : 2 * half] = weight_ref[tap, 2]
        table[base : base + half, 2 * half :] = jnp.zeros_like(weight_ref[tap, 0])
        table[base + half : base + 2 * half, 2 * half :] = weight_ref[tap, 0]


def down_rows(taps, table):
    rows, cols, width = taps[0].shape
    taps = jnp.concatenate(taps, axis=-1).reshape(rows * cols, 3 * width)
    both = product(taps, table[...], 1, 0).reshape(rows, cols, 2 * width)
    return (both[..., :width] + from_left(both[..., width:])).astype(BF16)


def down_kernel(
    date, dates, img_ref, above_ref, weight_ref, out_ref, sums_ref, table
):

    if date is None:
        down_table(weight_ref, table)
        return

    even, odd = img_ref[0, :, 0], img_ref[0, :, 1]
    above = jnp.concatenate([above_ref[0][None], odd[:-1]], axis=0)
    stored = down_rows([above, even, odd], table)
    out_ref[0] = stored
    values = stored.astype(F32)
    store_sums(sums_ref, date, dates, column_sum(values), column_sum(values * values))


def sort_halos(place_ref, inner_ref, outer_ref, high_ref, below_ref):
    odd = place_ref[0] % 2 == 1

    @pl.when(odd)
    def _():
        high_ref[...] = inner_ref[...]
        below_ref[...] = outer_ref[...]

    @pl.when(jnp.logical_not(odd))
    def _():
        high_ref[...] = outer_ref[...]
        below_ref[...] = inner_ref[...]


def load_kernel(
    place_ref,
    last_ref,
    img_hbm,
    grad_hbm,
    valid_hbm,
    img_ref,
    inner_ref,
    outer_ref,
    packed_ref,
    valid_ref,
    ready,
):
    blocks = grad_hbm.shape[0]
    moves = [
        pltpu.make_async_copy(grad_hbm, packed_ref.at[pl.ds(0, blocks)], ready.at[0]),
        pltpu.make_async_copy(valid_hbm, valid_ref, ready.at[1]),
        pltpu.make_async_copy(img_hbm, img_ref, ready.at[2]),
    ]
    for move in moves:
        move.start()
    for move in moves:
        move.wait()
    rows = img_ref.shape[1]
    odd = place_ref[0] % 2 == 1

    @pl.when(odd)
    def _():
        inner_ref[...] = img_ref[:, :2]
        outer_ref[...] = img_ref[:, rows - 3 : rows - 1]

    @pl.when(jnp.logical_not(odd))
    def _():
        inner_ref[...] = img_ref[:, rows - 3 : rows - 1]
        outer_ref[...] = img_ref[:, :2]

    piece, width = packed_ref.shape[1:]
    dates, rows, cols = valid_ref.shape
    values = valid_ref[...].astype(F32).reshape(dates * rows, cols)
    values = jnp.concatenate([values, jnp.zeros((dates * rows, width - cols), F32)], axis=1)
    packed_ref[blocks:] = values.astype(BF16).reshape(-1, piece, width)


def edge_kernel(
    step,
    steps,
    place_ref,
    inner_ref,
    outer_ref,
    above_ref,
    last_ref,
    weight_ref,
    up_ref,
    down_ref,
    table,
    high_ref,
    below_ref,
):
    if step is None:
        return
    dates = above_ref.shape[0]
    sort_halos(place_ref, inner_ref, outer_ref, high_ref, below_ref)
    down_table(weight_ref, table)
    taps = [
        jnp.concatenate([high_ref[:, 0], last_ref[...]], axis=0),
        jnp.concatenate([high_ref[:, 1], below_ref[:, 0]], axis=0),
        jnp.concatenate([above_ref[...], below_ref[:, 1]], axis=0),
    ]
    stored = down_rows(taps, table)
    up_ref[...] = stored[:dates]
    down_ref[...] = stored[dates:]


def activate_rows(date, dates, edge_flags, conv_refs, norm_refs, hidden_ref):
    conv_ref, up_ref, down_ref = conv_refs
    norm_ref, gain_ref, shift_ref = norm_refs
    scale = norm_ref[pl.ds(dates + date, 1), :] * gain_ref[...]
    shift = shift_ref[...] - norm_ref[pl.ds(date, 1), :] * scale

    def activate(values):
        linear = values.astype(F32) * scale + shift
        return linear * sigmoid(linear)

    rows = conv_ref.shape[1]
    hidden_ref[0, 0] = (activate(up_ref[0]) * edge_flags[0]).astype(BF16)
    hidden_ref[0, rows + 1] = (activate(down_ref[0]) * edge_flags[1]).astype(BF16)
    hidden_ref[0, 1 : rows + 1] = activate(conv_ref[0]).astype(BF16)


def block_kernel(
    date,
    dates,
    edge_ref,
    conv_ref,
    up_ref,
    down_ref,
    stats_ref,
    gain_ref,
    shift_ref,
    weight_ref,
    out_ref,
    norm_ref,
    sums_ref,
    table,
    hidden_ref,
    *,
    norm_count,
    row_devs,
):

    if date is None:
        norm_table(stats_ref, norm_ref, dates, norm_count)
        tap_table(weight_ref, table, False)
        return

    activate_rows(
        date,
        dates,
        edges(edge_ref, row_devs),
        (conv_ref, up_ref, down_ref),
        (norm_ref, gain_ref, shift_ref),
        hidden_ref,
    )
    stored = tap_rows(hidden_ref[0], table, False).astype(BF16)
    out_ref[0] = stored
    values = stored.astype(F32)
    store_sums(sums_ref, date, dates, column_sum(values), column_sum(values * values))


def encoding(day, width):
    lane = lax.broadcasted_iota(jnp.int32, (1, width), 1)
    frequency = jnp.exp((lane // 2).astype(F32) * (-2.0 * math.log(1000.0) / width))
    angles = day.astype(F32) * frequency
    return jnp.where(lane % 2 == 0, jnp.sin(angles), jnp.cos(angles))


def fold_keys(key_ref, query_ref, wide_ref, vector_ref, spread_ref, score_ref):
    depth, heads = query_ref.shape
    width = key_ref.shape[1]
    lanes = width // heads
    spread_ref[...] = head_spread(width)
    row = lax.broadcasted_iota(jnp.int32, (heads * depth, width), 0)
    lane = lax.broadcasted_iota(jnp.int32, (heads * depth, width), 1)
    widen = (row // depth == lane // lanes) & (row % depth == lane % lanes)
    wide = product(key_ref[...], widen.astype(F32).astype(BF16), 0, 0)
    wide_ref[...] = wide.astype(BF16)
    head = lax.broadcasted_iota(jnp.int32, (heads, width), 0)
    lane = lax.broadcasted_iota(jnp.int32, (heads, width), 1)
    inside = (lane // lanes == head).astype(F32).astype(BF16)
    high, low = split(query_ref[...])
    lower = (query_ref[...] - high.astype(F32) - low.astype(F32)).astype(BF16)
    spread = sum(product(part, inside, 1, 0) for part in (high, low, lower))
    step = lax.broadcasted_iota(jnp.int32, (depth, width), 0)
    place = lax.broadcasted_iota(jnp.int32, (depth, width), 1) % lanes
    queries = jnp.sum(jnp.where(step == place, spread * depth**-0.5, 0.0), axis=0, keepdims=True)
    place = lax.broadcasted_iota(jnp.int32, (1, width), 1) % lanes
    queries = queries + jnp.where((place == depth) | (place == depth + 1), 1.0, 0.0)
    vector_ref[...] = jnp.broadcast_to(queries, vector_ref.shape)
    folded = jnp.concatenate(split(wide * queries), axis=-1)
    folded = product(folded, spread_ref[...], 1, 0)
    score_ref[...] = jnp.concatenate(split(folded), axis=-1)


def source_of(turn_ref, device, devices):
    half = devices // 2
    core = (device + turn_ref[0]) % 2
    return core * half + (device // 2 + half - turn_ref[0] // 2) % half


def upstream_rows(grad_ref, turn_ref, rows, cols):
    devices = grad_ref.shape[0]
    piece = cols // devices
    parts = [
        grad_ref[source_of(turn_ref, device, devices), : rows * piece].reshape(rows, piece, -1)
        for device in range(devices)
    ]
    return jnp.concatenate(parts, axis=1)


def score_kernel(
    date,
    dates,
    day_ref,
    block_ref,
    stats_ref,
    gain_ref,
    shift_ref,
    grad_ref,
    valid_ref,
    turn_ref,
    key_ref,
    query_ref,
    feat_ref,
    exp_ref,
    attn_ref,
    norm_ref,
    packed_ref,
    own_ref,
    wide_ref,
    vector_ref,
    total,
    mean,
    spread_ref,
    score_ref,
    *,
    norm_count,
    grad_scale,
):
    rows, cols, width = block_ref.shape[1:]

    if date is None:
        norm_table(stats_ref, norm_ref, dates, norm_count)
        fold_keys(key_ref, query_ref, wide_ref, vector_ref, spread_ref, score_ref)
        total[...] = jnp.zeros_like(total)
        mean[...] = jnp.zeros_like(mean)
        return

    scale = norm_ref[pl.ds(dates + date, 1), :] * gain_ref[...]
    shift = shift_ref[...] - norm_ref[pl.ds(date, 1), :] * scale
    linear = block_ref[0].astype(F32) * scale + shift
    features = (linear * sigmoid(linear) + encoding(day_ref[turn_ref[0] * dates + date], width)).astype(BF16)
    feat_ref[0] = features
    upstream = upstream_rows(grad_ref, turn_ref, rows, cols)
    parts = split(upstream.astype(F32) * features.astype(F32))
    parts = jnp.concatenate(parts, axis=-1).reshape(rows * cols, 2 * width)
    attn = product(parts, spread_ref[...], 1, 0).reshape(rows, cols, width) * grad_scale
    both = product(features.reshape(rows * cols, width), score_ref[...], 1, 0)
    scores = (both[:, :width] + both[:, width:]).reshape(rows, cols, width)
    devices = grad_ref.shape[0]
    valid = jnp.zeros((rows, width), F32)
    for device in range(devices):
        piece = valid_ref[
            source_of(turn_ref, device, devices), pl.ds(date * rows, rows), :
        ]
        valid = valid + pltpu.roll(piece, device * (cols // devices), 1)
    diagonal = lax.broadcasted_iota(jnp.int32, (cols, cols), 0) == lax.broadcasted_iota(
        jnp.int32, (cols, cols), 1
    )
    ones = jnp.ones((cols, width), BF16)
    clear = jnp.concatenate(
        [jnp.where(diagonal, valid[row : row + 1], 0.0) for row in range(rows)], axis=0
    ).astype(BF16)
    clear = product(clear, ones, 1, 0).reshape(rows, cols, width)
    exponent = clear * jnp.exp(scores)
    running = total[...] + exponent
    share = jnp.where(running > 0.0, exponent / running, 0.0)
    total[...] = running
    mean[...] += share * (attn - mean[...])
    exp_ref[0] = exponent
    attn_ref[0] = attn

    if date == dates - 1:
        place = lax.broadcasted_iota(jnp.int32, (cols, width), 1) % rows
        for index, source in enumerate((total, mean)):
            dense = jnp.zeros((cols, width), F32)
            for row in range(rows):
                dense = dense + jnp.where(place == row, source[row], 0.0)
            if index == 0:
                packed_ref[0, 0] = dense.astype(BF16)
                own_ref[...] = dense
            else:
                packed_ref[0, 1], packed_ref[0, 2] = split(dense)


def attend_kernel(
    date,
    dates,
    packed_ref,
    own_ref,
    feat_ref,
    exp_ref,
    attn_ref,
    block_ref,
    norm_ref,
    gain_ref,
    shift_ref,
    query_ref,
    grad_ref,
    turn_ref,
    key_ref,
    grad_out_ref,
    part_ref,
    key_out_ref,
    vector_ref,
    sums_ref,
    inverse,
    average,
    attended,
    *,
    grad_scale,
):
    rows, cols, width = block_ref.shape[1:]

    if date is None:
        totals = packed_ref[:, 0].astype(F32)
        reciprocal = 1.0 / jnp.sum(totals, axis=0)
        means = packed_ref[:, 1].astype(F32) + packed_ref[:, 2].astype(F32)
        mean = jnp.sum(totals * reciprocal * means, axis=0)
        own = own_ref[...]
        sent = own.astype(BF16).astype(F32)
        reciprocal = reciprocal * jnp.where(own > 0.0, sent / own, 0.0)
        place = lax.broadcasted_iota(jnp.int32, (cols, width), 1) % rows
        for values, target in ((reciprocal, inverse), (mean, average)):
            parts = jnp.concatenate(split(values), axis=-1)
            wide_place = jnp.concatenate([place, place], axis=-1)
            picked = jnp.concatenate(
                [jnp.where(wide_place == row, parts, jnp.zeros_like(parts)) for row in range(rows)], axis=0
            )
            target[...] = product(picked, head_spread(width), 1, 0).reshape(rows, cols, width)
        attended[...] = jnp.zeros_like(attended)
        key_out_ref[...] = jnp.zeros_like(key_out_ref)
        vector_ref[...] = jnp.zeros_like(vector_ref)
        return

    features = feat_ref[0]
    weights = exp_ref[0] * inverse[...]
    rounded = weights.astype(BF16).astype(F32)
    attended[...] += rounded * features.astype(F32)
    score_grad = weights * (attn_ref[0] - average[...])
    spread_grad = score_grad * query_ref[0:1]
    rest = spread_grad - spread_grad.astype(BF16).astype(F32)
    lane = lax.broadcasted_iota(jnp.int32, spread_grad.shape, 2) % (width // 16)
    key_grads = jnp.where(lane == 5, rest, spread_grad).astype(BF16).reshape(rows * cols, width)
    key_out_ref[...] += product(features.reshape(rows * cols, width), key_grads, 0, 0)
    upstream = upstream_rows(grad_ref, turn_ref, rows, cols)
    feat_grad = rounded * (upstream.astype(F32) * grad_scale) + product(
        key_grads, key_ref[...], 1, 1
    ).reshape(rows, cols, width)
    gain = gain_ref[...]
    centred = (block_ref[0].astype(F32) - norm_ref[pl.ds(date, 1), :]) * norm_ref[
        pl.ds(dates + date, 1), :
    ]
    linear = centred * gain + shift_ref[...]
    part = sigmoid(linear)
    linear_grad = feat_grad * (part * (1.0 + linear * (1.0 - part)))
    first = column_sum(linear_grad)
    second = column_sum(linear_grad * centred)
    vector_ref[0:1] += second
    vector_ref[1:2] += first
    store_sums(sums_ref, date, dates, first * gain, second * gain)
    grad_out_ref[0] = (linear_grad * gain).astype(BF16)

    if date == dates - 1:
        devices, piece = part_ref.shape[0], part_ref.shape[2]
        for device in range(devices):
            part_ref[device] = attended[:, device * piece : (device + 1) * piece].astype(BF16)
        key_part = key_out_ref[...]
        place = lax.broadcasted_iota(jnp.int32, (width, width), 1) % (width // 16)
        both = pltpu.roll(key_part, width - 4, 1) + pltpu.roll(key_part, width - 5, 1)
        both = jnp.where(place == 0, both, 0.0)
        both = both + pltpu.roll(both, 1, 1)
        both = both + pltpu.roll(both, 2, 1)
        vector_ref[2:3] = 0.5 * jnp.sum(key_ref[...].astype(F32) * both, axis=0, keepdims=True)


def hidden_kernel(
    date,
    dates,
    edge_ref,
    grad_ref,
    block_ref,
    tails_ref,
    norm_ref,
    weight_ref,
    conv_ref,
    up_ref,
    down_ref,
    first_norm_ref,
    gain_ref,
    shift_ref,
    pre_ref,
    out_ref,
    vector_ref,
    sums_ref,
    table,
    factors,
    padded,
    *,
    norm_count,
    row_devs,
):
    rows, cols, width = block_ref.shape[1:]

    if date is None:
        tails = group_sum(jnp.sum(tails_ref[...], axis=0)) / norm_count
        mean, inverse = norm_ref[:dates], norm_ref[dates:]
        slope = -inverse * inverse * tails[dates:]
        factors[0:dates] = slope
        factors[dates : 2 * dates] = -inverse * tails[:dates] - mean * slope
        vector_ref[...] = jnp.zeros_like(vector_ref)
        padded[:2] = jnp.zeros_like(padded[:2])
        padded[rows + 2 :] = jnp.zeros_like(padded[rows + 2 :])
        tap_table(weight_ref, table, True)
        return

    inverse = norm_ref[pl.ds(dates + date, 1), :]
    slope = factors[pl.ds(date, 1), :]
    constant = factors[pl.ds(dates + date, 1), :]

    above_edge, below_edge = edges(edge_ref, row_devs)
    stored = (
        grad_ref[0].astype(F32) * inverse + (block_ref[0].astype(F32) * slope + constant)
    ).astype(BF16)
    pre_ref[0] = stored
    padded[2 : rows + 2] = stored
    hidden_grad = tap_rows(padded[...], table, True)
    gain = gain_ref[...]
    conv = jnp.concatenate([up_ref[0][None], conv_ref[0], down_ref[0][None]], axis=0)
    centred = (conv.astype(F32) - first_norm_ref[pl.ds(date, 1), :]) * first_norm_ref[
        pl.ds(dates + date, 1), :
    ]
    linear = centred * gain + shift_ref[...]
    part = sigmoid(linear)
    linear_grad = hidden_grad * (part * (1.0 + linear * (1.0 - part)))
    linear_grad = jnp.concatenate(
        [
            linear_grad[:1] * above_edge,
            linear_grad[1 : rows + 1],
            linear_grad[rows + 1 :] * below_edge,
        ],
        axis=0,
    )
    out_ref[0] = linear_grad.astype(BF16)
    first = column_sum(linear_grad)
    second = column_sum(linear_grad * centred)
    vector_ref[0:1] += second
    vector_ref[1:2] += first
    store_sums(sums_ref, date, dates, first * gain, second * gain)


def block_grad_kernel(
    date,
    dates,
    edge_ref,
    conv_ref,
    up_ref,
    down_ref,
    norm_ref,
    gain_ref,
    shift_ref,
    pre_ref,
    key_ref,
    out_ref,
    total,
    hidden_ref,
    *,
    row_devs,
):
    rows, cols, width = pre_ref.shape[1:]

    if date is None:
        total[...] = jnp.zeros_like(total)
        return

    activate_rows(
        date,
        dates,
        edges(edge_ref, row_devs),
        (conv_ref, up_ref, down_ref),
        (norm_ref, gain_ref, shift_ref),
        hidden_ref,
    )
    grads = pre_ref[0].astype(F32)
    grads = jnp.concatenate(
        [from_right(grads).astype(BF16), pre_ref[0], from_left(grads).astype(BF16)], axis=-1
    ).reshape(rows * cols, 3 * width)
    taps = jnp.concatenate(
        [hidden_ref[0, tap : tap + rows] for tap in range(3)], axis=-1
    ).reshape(rows * cols, 3 * width)
    total[...] += product(taps, grads, 0, 0)

    if date == dates - 1:
        for row_tap in range(3):
            for col_tap in range(3):
                base = (row_tap * 3 + col_tap) * width
                out_ref[base : base + width] = total[
                    row_tap * width : (row_tap + 1) * width, col_tap * width : (col_tap + 1) * width
                ].astype(BF16)
        key_part = key_ref[...]
        rest = key_part - key_part.astype(BF16).astype(F32)
        lanes = width // 16
        place = lax.broadcasted_iota(jnp.int32, key_part.shape, 1) % lanes
        rest = pltpu.roll(rest, lanes // 2, 1)
        key_rows = jnp.where(place < lanes // 2, key_part, rest).astype(BF16)
        out_ref[9 * width : 10 * width] = key_rows
        if out_ref.shape[0] > 10 * width:
            out_ref[10 * width :] = jnp.zeros_like(out_ref[10 * width :])


def conv_grad_kernel(
    date,
    dates,
    img_ref,
    above_ref,
    inner_ref,
    outer_ref,
    place_ref,
    conv_ref,
    grad_ref,
    tails_ref,
    norm_ref,
    gain_ref,
    vector_ref,
    other_ref,
    block_rows_ref,
    turn_ref,
    keep_ref,
    give_ref,
    factors,
    total,
    out_ref,
    high_ref,
    below_ref,
    *,
    norm_count,
):
    rows, cols, width = conv_ref.shape[1:]
    half = width // 2

    if date is None:
        sort_halos(place_ref, inner_ref, outer_ref, high_ref, below_ref)
        tails = group_sum(jnp.sum(tails_ref[...], axis=0)) / norm_count
        mean, inverse = norm_ref[:dates], norm_ref[dates:]
        slope = -inverse * inverse * tails[dates:]
        factors[0:dates] = slope
        factors[dates : 2 * dates] = -inverse * tails[:dates] - mean * slope
        total[...] = jnp.zeros_like(total)
        return

    scale = norm_ref[pl.ds(dates + date, 1), :] * gain_ref[...]
    slope = factors[pl.ds(date, 1), :]
    constant = factors[pl.ds(dates + date, 1), :]
    own = conv_ref[0].astype(F32) * slope + constant
    scaled = grad_ref[0].astype(F32) * scale
    stored = jnp.concatenate(
        [scaled[:1], scaled[1 : rows + 1] + own, scaled[rows + 1 :]], axis=0
    ).astype(BF16)
    moved = from_right(stored.astype(F32)).astype(BF16)
    reach = rows + 2
    grads = jnp.concatenate([stored, moved], axis=-1).reshape(reach * cols, 2 * width)
    even, odd = img_ref[0, :, 0], img_ref[0, :, 1]
    above = above_ref[0][None]
    taps = [
        jnp.concatenate([high_ref[date, :1], above, odd], axis=0),
        jnp.concatenate([high_ref[date, 1:], even, below_ref[date, :1]], axis=0),
        jnp.concatenate([above, odd, below_ref[date, 1:]], axis=0),
    ]
    taps = jnp.concatenate(taps, axis=-1).reshape(reach * cols, 3 * width)
    total[...] += product(taps, grads, 0, 0)

    if date == dates - 1:
        begin = block_rows_ref.shape[0]
        out_ref[:begin] = block_rows_ref[...]
        for tap in range(3):
            base = tap * width
            pair = total[base : base + width, :width].astype(BF16)
            left = total[base + half : base + width, width:].astype(BF16)
            start = begin + tap * 3 * half
            out_ref[start : start + half] = left
            out_ref[start + half : start + 3 * half] = pair
        start = begin + 9 * half
        for source in (vector_ref, other_ref):
            high, low = split(source[...])
            out_ref[start : start + 16] = jnp.concatenate([high, low], axis=0)
            start += 16
        if out_ref.shape[0] > start:
            out_ref[start:] = jnp.zeros_like(out_ref[start:])
        half_rows = keep_ref.shape[0]
        core = turn_ref[0] % 2
        start = pl.multiple_of(core * half_rows, half_rows)
        keep_ref[...] = out_ref[pl.ds(start, half_rows), :]
        start = pl.multiple_of((1 - core) * half_rows, half_rows)
        give_ref[...] = out_ref[pl.ds(start, half_rows), :]


def total_kernel(in_ref, out_ref):
    total = jnp.sum(in_ref[...].astype(F32), axis=0).astype(BF16)
    for copy in range(out_ref.shape[0]):
        out_ref[copy] = total


def final_kernel(
    depth,
    turn_ref,
    own_ref,
    other_ref,
    conv_ref,
    block_ref,
    key_ref,
    query_ref,
    *refs,
):
    vector_refs, rows_ref = refs[:-1], refs[-1]
    half_rows = own_ref.shape[0]
    core = turn_ref[0] % 2
    rows_ref[pl.ds(pl.multiple_of(core * half_rows, half_rows), half_rows), :] = own_ref[...]
    start = pl.multiple_of((1 - core) * half_rows, half_rows)
    rows_ref[pl.ds(start, half_rows), :] = other_ref[...]
    conv_end, block_end, width = conv_ref.shape[0], block_ref.shape[0], block_ref.shape[1]
    block_ref[...] = rows_ref[:block_end].astype(F32)
    wide = key_ref.shape[0]
    heads = wide // depth
    lanes = width // heads
    row = lax.broadcasted_iota(jnp.int32, (wide, width), 0)
    lane = lax.broadcasted_iota(jnp.int32, (wide, width), 1)
    narrow = (row // depth == lane // lanes) & (row % depth == lane % depth)
    narrow = narrow.astype(F32).astype(BF16)
    key_ref[...] = product(narrow, rows_ref[block_end : block_end + width], 1, 1)
    start = block_end + width
    conv_ref[...] = rows_ref[start : start + conv_end].astype(F32)
    start += conv_end
    for index in range(2):
        both = rows_ref[start : start + 16].astype(F32)
        both = both[:8] + both[8:]
        vector_refs[2 * index][...] = both[0:1]
        vector_refs[2 * index + 1][...] = both[1:2]
        start += 16
    both = rows_ref[start - 16 : start]
    row = lax.broadcasted_iota(jnp.int32, (heads, width), 0)
    lane = lax.broadcasted_iota(jnp.int32, (heads, width), 1)
    inside = row == lane // lanes
    step = lax.broadcasted_iota(jnp.int32, (8, width), 0)
    place = lax.broadcasted_iota(jnp.int32, (8, width), 1) % lanes
    steps = step == place
    query = jnp.zeros((8, heads), F32)
    for index in (2, 10):
        picked = jnp.where(steps, both[index : index + 1].astype(F32), 0.0).astype(BF16)
        query = query + product(picked, inside.astype(F32).astype(BF16), 1, 1)
    query_ref[...] = query[:depth]


def call(kernel, dates, inputs, outputs, scratch, flops):
    in_specs, out_specs, arrays, out_shape, buffers = [], [], [], [], []
    in_vmem, in_hbm = pl.BlockSpec(memory_space=pltpu.VMEM), pl.BlockSpec(memory_space=pltpu.HBM)
    loads, stores = [], []
    for place, (kind, array) in enumerate(inputs):
        if kind == "scalar":
            in_specs.append(pl.BlockSpec(memory_space=pltpu.SMEM))
        elif "far" in kind:
            array = pltpu.with_memory_space_constraint(array, pltpu.HBM)
            in_specs.append(in_hbm)
            loads.append(place)
            buffers.append(pltpu.VMEM(array.shape, array.dtype))
        else:
            in_specs.append(in_vmem)
        arrays.append(array)
    for place, (kind, shape, dtype) in enumerate(outputs):
        if "far" in kind:
            out_shape.append(pltpu.HBM(shape, dtype))
            out_specs.append(in_hbm)
            stores.append(place)
            buffers.append(pltpu.VMEM(shape, dtype))
        else:
            out_shape.append(jax.ShapeDtypeStruct(shape, dtype))
            out_specs.append(in_vmem)
    copies = len(loads) + len(stores)
    kinds = [kind for kind, _ in inputs] + [kind for kind, _, _ in outputs]

    def body(*refs):
        views, rest = list(refs[: len(kinds)]), refs[len(kinds) :]
        buffer_refs, ready, rest = rest[:copies], rest[copies], rest[copies + 1 :]

        def copies_of(place, index, inward):
            outside, inside = views[place], buffer_refs[index]
            made = []
            for date in range(dates if "date" in kinds[place] else 1):
                here = pl.ds(date, 1) if "date" in kinds[place] else slice(None)
                pair = (outside.at[here], inside.at[here])
                source, target = pair if inward else pair[::-1]
                made.append(pltpu.make_async_copy(source, target, ready.at[index, date]))
            return made

        incoming = [copies_of(place, index, True) for index, place in enumerate(loads)]
        outgoing = [
            copies_of(len(inputs) + place, len(loads) + index, False)
            for index, place in enumerate(stores)
        ]
        def per_date(date):
            for place, moves in zip(loads, incoming):
                if date < len(moves) and "date" in kinds[place]:
                    yield moves[date]

        early = [m[0] for p, m in zip(loads, incoming) if kinds[p] == "all far"]
        late = [m[0] for p, m in zip(loads, incoming) if kinds[p] == "late far"]
        for move in early + list(per_date(0)) + list(per_date(1)) + late:
            move.start()
        for index, place in enumerate(loads):
            views[place] = buffer_refs[index]
        for index, place in enumerate(stores):
            views[len(inputs) + place] = buffer_refs[len(loads) + index]
        for move in early:
            move.wait()
        kernel(None, dates, *views, *rest)
        for date in range(dates):
            for move in per_date(date):
                move.wait()
            for move in per_date(date + 2):
                move.start()
            if date == dates - 1:
                for move in late:
                    move.wait()
            here = [
                view.at[pl.ds(date, 1)] if "date" in kind else view
                for view, kind in zip(views, kinds)
            ]
            kernel(date, dates, *here, *rest)
            for moves in outgoing:
                if len(moves) == dates:
                    moves[date].start()
                elif date == dates - 1:
                    moves[0].start()
        for moves in outgoing:
            for move in moves:
                move.wait()

    moved = sum(array.size * array.dtype.itemsize for _, array in inputs)
    return pl.pallas_call(
        body,
        in_specs=in_specs,
        out_specs=out_specs,
        out_shape=out_shape,
        scratch_shapes=buffers + [pltpu.SemaphoreType.DMA((max(copies, 1), dates))] + scratch,
        compiler_params=pltpu.CompilerParams(vmem_limit_bytes=40 * MIB),
        cost_estimate=pl.CostEstimate(flops=flops, bytes_accessed=2 * moved, transcendentals=0),
    )(*arrays)


def shifted(array, by):
    devices = lax.axis_size("rows")
    pairs = [(i, i + by) for i in range(devices) if 0 <= i + by < devices]
    return lax.ppermute(array, "rows", pairs)


def same_core(array):
    devices = lax.axis_size("dates")
    pieces = [array]
    for step in range(2, devices, 2):
        pairs = [((i + step) % devices, i) for i in range(devices)]
        pieces.append(lax.ppermute(array, "dates", pairs))
    return pieces


def sum_of_parts(parts):
    devices = lax.axis_size("dates")
    place = lax.axis_index("dates")
    total = lax.dynamic_index_in_dim(parts, place, 0, keepdims=False).astype(F32)
    for step in range(1, devices):
        piece = lax.dynamic_index_in_dim(parts, (place + step) % devices, 0, keepdims=False)
        pairs = [(i, (i + step) % devices) for i in range(devices)]
        total = total + lax.ppermute(piece, "dates", pairs).astype(F32)
    return total.astype(BF16)


def exchange(pieces, axes):
    return lax.all_to_all(pieces, axes, split_axis=0, concat_axis=0, tiled=True)


def gather(array, axis):
    return lax.all_gather(array, axis, axis=0, tiled=True)


def other_core(array):
    devices = lax.axis_size("dates")
    return lax.ppermute(array, "dates", [(i, i + 1 - 2 * (i % 2)) for i in range(devices)])


def exchange_cores(pieces):
    axes = ("rows", "dates")
    devices = lax.axis_size(axes)
    groups = [list(range(core, devices, 2)) for core in range(2)]
    return lax.all_to_all(
        pieces, axes, split_axis=0, concat_axis=0, axis_index_groups=groups, tiled=True
    )


def scatter(rows_array):
    devices = lax.axis_size(("rows", "dates")) // 2
    count, width = rows_array.shape
    return exchange_cores(rows_array.reshape(devices, count // devices, width))


def collect(pieces):
    spread = pl.pallas_call(
        total_kernel,
        out_shape=jax.ShapeDtypeStruct(pieces.shape, BF16),
        compiler_params=pltpu.CompilerParams(vmem_limit_bytes=16 * MIB),
    )(pieces)
    count, rows, width = pieces.shape
    return exchange_cores(spread).reshape(count * rows, width)


def padded_count(count, devices):
    step = 8 * devices
    return -(-count // step) * step


def local(
    images,
    day_index,
    valid,
    out_grad,
    conv_weight,
    first_gain,
    first_shift,
    block_weight,
    gn_gain,
    gn_shift,
    key_weight,
    queries,
):
    dates, rows_here, cols, pair_width = images.shape
    width = conv_weight.shape[-1]
    row_devs, date_devs = lax.axis_size("rows"), lax.axis_size("dates")
    devices = row_devs * date_devs
    rows = rows_here // 2
    heads, depth = queries.shape
    norm_count = float(rows * row_devs * cols * (width // GROUPS))
    grad_scale = float(rows * row_devs * cols) ** (-0.5)
    date_start = lax.axis_index("dates") * dates
    frame = (dates, rows, cols, width)
    edge_rows = (dates, cols, width)
    flops = 2 * dates * rows * cols * width * width

    rows_of = lambda vector: vector.reshape(1, width)
    first_gain, first_shift = rows_of(first_gain), rows_of(first_shift)
    gn_gain, gn_shift = rows_of(gn_gain), rows_of(gn_shift)
    last = images[:, -1]
    above = shifted(last, 1)
    grad_rows = out_grad.size // width
    row_place = lax.axis_index("rows")
    place = row_place.reshape(1)
    valid_count = valid.shape[0] * rows
    piece = out_grad.shape[1]
    packed_shape = ((grad_rows + valid_count) // piece, piece, width)
    in_hbm, in_vmem = pl.BlockSpec(memory_space=pltpu.HBM), pl.BlockSpec(memory_space=pltpu.VMEM)
    images_near, inner, outer, packed = pl.pallas_call(
        load_kernel,
        in_specs=[pl.BlockSpec(memory_space=pltpu.SMEM), in_vmem, in_hbm, in_hbm, in_hbm],
        out_specs=[in_vmem] * 4,
        out_shape=[
            jax.ShapeDtypeStruct(shape, BF16)
            for shape in (images.shape,) + ((dates, 2, cols, pair_width),) * 2 + (packed_shape,)
        ],
        scratch_shapes=[pltpu.VMEM(valid.shape, valid.dtype), pltpu.SemaphoreType.DMA((3,))],
        compiler_params=pltpu.CompilerParams(vmem_limit_bytes=16 * MIB),
    )(
        place,
        last,
        *[pltpu.with_memory_space_constraint(x, pltpu.HBM) for x in (images, out_grad, valid)],
    )
    packed = packed.reshape(grad_rows + valid_count, width)
    inner, outer, above, packed = lax.optimization_barrier((inner, outer, above, packed))
    inner = lax.ppermute(inner, "rows", [(i, i ^ 1) for i in range(row_devs)])
    pairs = [(i, i + 1) for i in range(1, row_devs - 1, 2)]
    outer = lax.ppermute(outer, "rows", pairs + [(j, i) for i, j in pairs])
    paired = images.reshape(dates, rows, 2, cols, pair_width)
    conv_out, sums = call(
        down_kernel,
        dates,
        [
            ("date", images_near.reshape(paired.shape)),
            ("date", above),
            ("all", conv_weight),
        ],
        [("date far", frame, BF16), ("all", (row_devs, 2 * dates, width), F32)],
        [pltpu.VMEM((3 * pair_width, 2 * width), BF16)],
        6 * flops,
    )
    stats = exchange(sums, "rows")
    inner, outer, last, _ = lax.optimization_barrier((inner, outer, last, sums))
    halo_up, halo_down = call(
        edge_kernel,
        1,
        [
            ("scalar", place),
            ("all", inner),
            ("all", outer),
            ("all", above),
            ("all", last),
            ("all", conv_weight),
        ],
        [("all", edge_rows, BF16)] * 2,
        [
            pltpu.VMEM((3 * pair_width, 2 * width), BF16),
            pltpu.VMEM(inner.shape, BF16),
            pltpu.VMEM(inner.shape, BF16),
        ],
        6 * flops // rows,
    )
    turn = lax.axis_index("dates").reshape(1)
    packed, _ = lax.optimization_barrier((packed, halo_up))
    pieces = same_core(packed)
    block_out, first_norm, sums = call(
        functools.partial(block_kernel, norm_count=norm_count, row_devs=row_devs),
        dates,
        [
            ("scalar", place),
            ("date far", conv_out),
            ("date", halo_up),
            ("date", halo_down),
            ("all", stats),
            ("all", first_gain),
            ("all", first_shift),
            ("all far", block_weight),
        ],
        [
            ("date far", frame, BF16),
            ("all", (2 * dates, width), F32),
            ("all", (row_devs, 2 * dates, width), F32),
        ],
        [
            pltpu.VMEM((3 * width, 3 * width), BF16),
            pltpu.VMEM((1, rows + 2, cols, width), BF16),
        ],
        9 * flops,
    )
    stats = exchange(sums, "rows")
    pieces, _ = lax.optimization_barrier((pieces, sums))
    sources = jnp.stack(pieces + [other_core(piece) for piece in pieces])
    clear = lax.dynamic_slice_in_dim(sources, grad_rows + date_start * rows, dates * rows, 1)
    clear = clear.astype(F32)
    features, exponent, attn, norm, packed, own_total, key_wide, query_wide = call(
        functools.partial(score_kernel, norm_count=norm_count, grad_scale=grad_scale),
        dates,
        [
            ("scalar", day_index),
            ("date far", block_out),
            ("all", stats),
            ("all", gn_gain),
            ("all", gn_shift),
            ("all", sources),
            ("all", clear),
            ("scalar", turn),
            ("all", key_weight.T),
            ("all", queries.T),
        ],
        [
            ("date", frame, BF16),
            ("date", frame, F32),
            ("date", frame, F32),
            ("all", (2 * dates, width), F32),
            ("all", (1, 3, cols, width), BF16),
            ("all", (cols, width), F32),
            ("all", (width, width), BF16),
            ("all", (8, width), F32),
        ],
        [
            pltpu.VMEM(frame[1:], F32),
            pltpu.VMEM(frame[1:], F32),
            pltpu.VMEM((2 * width, width), BF16),
            pltpu.VMEM((width, 2 * width), BF16),
        ],
        5 * flops,
    )
    packed = gather(packed, "dates")
    block_grad, attended, key_part, vectors, sums = call(
        functools.partial(attend_kernel, grad_scale=grad_scale),
        dates,
        [
            ("all", packed),
            ("all", own_total),
            ("date", features),
            ("date", exponent),
            ("date", attn),
            ("date", block_out),
            ("all", norm),
            ("all", gn_gain),
            ("all", gn_shift),
            ("all", query_wide),
            ("all", sources),
            ("scalar", turn),
            ("all", key_wide),
        ],
        [
            ("date far", frame, BF16),
            ("all far", (date_devs, rows, cols // date_devs, width), BF16),
            ("all far", (width, width), F32),
            ("all", (8, width), F32),
            ("all", (row_devs, 2 * dates, width), F32),
        ],
        [pltpu.VMEM(frame[1:], F32)] * 3,
        5 * flops,
    )
    tails = exchange(sums, "rows")
    pre_grad, linear_grad, first_vectors, sums = call(
        functools.partial(hidden_kernel, norm_count=norm_count, row_devs=row_devs),
        dates,
        [
            ("scalar", place),
            ("date far", block_grad),
            ("date far", block_out),
            ("all", tails),
            ("all", norm),
            ("all far", block_weight),
            ("date far", conv_out),
            ("date", halo_up),
            ("date", halo_down),
            ("all", first_norm),
            ("all", first_gain),
            ("all", first_shift),
        ],
        [
            ("date far", frame, BF16),
            ("date far", (dates, rows + 2, cols, width), BF16),
            ("all", (8, width), F32),
            ("all", (row_devs, 2 * dates, width), F32),
        ],
        [
            pltpu.VMEM((3 * width, 3 * width), BF16),
            pltpu.VMEM((2 * dates, width), F32),
            pltpu.VMEM((rows + 4, cols, width), BF16),
        ],
        9 * flops,
    )
    tails = exchange(sums, "rows")
    (block_rows,) = call(
        functools.partial(block_grad_kernel, row_devs=row_devs),
        dates,
        [
            ("scalar", place),
            ("date far", conv_out),
            ("date", halo_up),
            ("date", halo_down),
            ("all", first_norm),
            ("all", first_gain),
            ("all", first_shift),
            ("date far", pre_grad),
            ("late far", key_part),
        ],
        [("all far", (10 * width, width), BF16)],
        [
            pltpu.VMEM((3 * width, 3 * width), F32),
            pltpu.VMEM((1, rows + 2, cols, width), BF16),
        ],
        9 * flops,
    )
    tails, block_rows = lax.optimization_barrier((tails, block_rows))
    conv_count = 9 * pair_width // 2 + 32
    half_rows = padded_count(10 * width + conv_count, devices) // 2
    keep, give = call(
        functools.partial(conv_grad_kernel, norm_count=norm_count),
        dates,
        [
            ("date far", paired),
            ("date", above),
            ("all", inner),
            ("all", outer),
            ("scalar", place),
            ("date far", conv_out),
            ("date far", linear_grad),
            ("all", tails),
            ("all", first_norm),
            ("all", first_gain),
            ("all", first_vectors),
            ("all", vectors),
            ("late far", block_rows),
            ("scalar", turn),
        ],
        [("all", (half_rows, width), BF16)] * 2,
        [
            pltpu.VMEM((2 * dates, width), F32),
            pltpu.VMEM((3 * pair_width, 2 * width), F32),
            pltpu.VMEM((2 * half_rows, width), BF16),
            pltpu.VMEM(inner.shape, BF16),
            pltpu.VMEM(inner.shape, BF16),
        ],
        6 * flops,
    )
    rows_half = (keep.astype(F32) + other_core(give).astype(F32)).astype(BF16)
    pieces = scatter(rows_half)
    attended, _ = lax.optimization_barrier((attended, rows_half))
    attended = sum_of_parts(attended)
    rows_half = collect(pieces)
    rows_other = other_core(rows_half)
    shapes = [
        (9 * pair_width // 2, width),
        (9 * width, width),
        (heads * depth, width),
        (depth, heads),
    ] + [(1, width)] * 4
    conv_total, block_total, key_total, query_total, *totals = pl.pallas_call(
        functools.partial(final_kernel, depth),
        in_specs=[
            pl.BlockSpec(memory_space=pltpu.SMEM),
            pl.BlockSpec(memory_space=pltpu.VMEM),
            pl.BlockSpec(memory_space=pltpu.VMEM),
        ],
        out_shape=[jax.ShapeDtypeStruct(shape, F32) for shape in shapes],
        scratch_shapes=[pltpu.VMEM((2 * half_rows, width), BF16)],
        compiler_params=pltpu.CompilerParams(vmem_limit_bytes=16 * MIB),
    )(turn, rows_half, rows_other)
    totals = [total.reshape(width) for total in totals]
    return (
        attended,
        conv_total.reshape(conv_weight.shape),
        totals[0],
        totals[1],
        block_total.reshape(block_weight.shape),
        totals[2],
        totals[3],
        key_total.T,
        query_total.T,
    )


def solution(mesh):
    return jax.shard_map(
        local,
        mesh=mesh,
        in_specs=(
            P("dates", "rows", None, None),
            P(),
            P(None, "rows", "dates"),
            P("rows", "dates", None),
            P(),
            P(),
            P(),
            P(),
            P(),
            P(),
            P(),
            P(),
        ),
        out_specs=(P("rows", "dates", None), P(), P(), P(), P(), P(), P(), P(), P()),
        check_vma=False,
    )
```

```python
import functools
import math

import jax
import jax.numpy as jnp
from jax import lax
from jax.experimental import pallas as pl
from jax.experimental.pallas import tpu as pltpu
from jax.sharding import PartitionSpec as P

GROUPS = 4


EPS = 1e-05


MIB = 1 << 20


F32 = jnp.float32


BF16 = jnp.bfloat16


def product(left, right, left_dim, right_dim):
    return lax.dot_general(
        left, right, (((left_dim,), (right_dim,)), ((), ())), preferred_element_type=F32
    )


def group_sum(values):
    width = values.shape[-1]
    lane_group = lax.broadcasted_iota(jnp.int32, values.shape, 1) // (width // GROUPS)
    spread = jnp.zeros_like(values)
    for group in range(GROUPS):
        inside = lane_group == group
        total = jnp.sum(jnp.where(inside, values, 0.0), axis=1, keepdims=True)
        spread = spread + jnp.where(inside, total, 0.0)
    return spread


def sigmoid(values):
    return 0.5 * jnp.tanh(0.5 * values) + 0.5


def from_left(values):
    moved = pltpu.roll(values, 1, 1)
    first = moved[:, :8]
    column = lax.broadcasted_iota(jnp.int32, first.shape, 1)
    return jnp.concatenate([jnp.where(column > 0, first, 0.0), moved[:, 8:]], axis=1)


def from_right(values):
    count = values.shape[1]
    moved = pltpu.roll(values, count - 1, 1)
    last = moved[:, count - 8 :]
    column = lax.broadcasted_iota(jnp.int32, last.shape, 1)
    return jnp.concatenate([moved[:, : count - 8], jnp.where(column < 7, last, 0.0)], axis=1)


def tap_table(weight_ref, table, backward):
    width = weight_ref.shape[-1]
    for row_tap in range(3):
        for col_tap in range(3):
            deep = slice(row_tap * width, (row_tap + 1) * width)
            wide = slice(col_tap * width, (col_tap + 1) * width)
            if backward:
                table[wide, deep] = weight_ref[2 - row_tap, col_tap]
            else:
                table[deep, wide] = weight_ref[row_tap, col_tap]


def tap_rows(padded, table, backward):
    rows, cols, width = padded.shape[0] - 2, *padded.shape[1:]
    taps = jnp.concatenate([padded[tap : tap + rows] for tap in range(3)], axis=-1)
    taps = taps.reshape(rows * cols, 3 * width)
    terms = product(taps, table[...], 1, 1 if backward else 0).reshape(rows, cols, 3 * width)
    first, last = (from_right, from_left) if backward else (from_left, from_right)
    return (
        terms[..., width : 2 * width]
        + first(terms[..., :width])
        + last(terms[..., 2 * width :])
    )


def column_sum(values):
    return jnp.sum(jnp.sum(values, axis=0), axis=0, keepdims=True)


def edges(place_ref, row_devs):
    place = place_ref[0]
    return (place > 0).astype(F32), (place < row_devs - 1).astype(F32)


def head_spread(width):
    lane = lax.broadcasted_iota(jnp.int32, (2 * width, width), 1) // (width // 16)
    head = lax.broadcasted_iota(jnp.int32, (2 * width, width), 0) % width // (width // 16)
    return (lane == head).astype(F32).astype(BF16)


def split(values):
    high = values.astype(BF16)
    return high, (values - high.astype(F32)).astype(BF16)


def store_sums(sums_ref, date, dates, first, second):
    for copy in range(sums_ref.shape[0]):
        sums_ref[copy, pl.ds(date, 1), :] = first
        sums_ref[copy, pl.ds(dates + date, 1), :] = second


def norm_table(sums_ref, table_ref, dates, norm_count):
    means = group_sum(jnp.sum(sums_ref[...], axis=0)) / norm_count
    mean = means[:dates]
    table_ref[:dates] = mean
    table_ref[dates:] = 1.0 / jnp.sqrt(means[dates:] - mean * mean + EPS)


def down_table(weight_ref, table):
    half = weight_ref.shape[2]
    for tap in range(3):
        base = tap * 2 * half
        table[base : base + half, : 2 * half] = weight_ref[tap, 1]
        table[base + half : base + 2 * half, : 2 * half] = weight_ref[tap, 2]
        table[base : base + half, 2 * half :] = jnp.zeros_like(weight_ref[tap, 0])
        table[base + half : base + 2 * half, 2 * half :] = weight_ref[tap, 0]


def down_rows(taps, table):
    rows, cols, width = taps[0].shape
    taps = jnp.concatenate(taps, axis=-1).reshape(rows * cols, 3 * width)
    both = product(taps, table[...], 1, 0).reshape(rows, cols, 2 * width)
    return (both[..., :width] + from_left(both[..., width:])).astype(BF16)


def inner_kernel(date, dates, img_ref, weight_ref, main_ref, sums_ref, table):
    if date is None:
        down_table(weight_ref, table)
        return

    even, odd = img_ref[0, :, 0], img_ref[0, :, 1]
    stored = down_rows([odd[:-1], even[1:], odd[1:]], table)
    main_ref[0, 1:] = stored
    values = stored.astype(F32)
    store_sums(sums_ref, date, dates, column_sum(values), column_sum(values * values))


def first_row_kernel(
    img_ref,
    above_ref,
    weight_ref,
    main_ref,
    part_ref,
    out_hbm,
    sums_ref,
    table,
    row_ref,
    ready,
):
    rows = main_ref.shape[1]
    rest = pl.ds(1, rows - 1)
    main_move = pltpu.make_async_copy(main_ref.at[:, rest], out_hbm.at[:, rest], ready.at[0])
    main_move.start()
    down_table(weight_ref, table)
    stored = down_rows([above_ref[...], img_ref[:, 0], img_ref[:, 1]], table)
    row_ref[:, 0] = stored
    row_move = pltpu.make_async_copy(row_ref, out_hbm.at[:, pl.ds(0, 1)], ready.at[1])
    row_move.start()
    values = stored.astype(F32)
    both = [jnp.sum(values, axis=1), jnp.sum(values * values, axis=1)]
    total = part_ref[0] + jnp.concatenate(both, axis=0)
    for copy in range(sums_ref.shape[0]):
        sums_ref[copy] = total
    main_move.wait()
    row_move.wait()


def sort_halos(place_ref, inner_ref, outer_ref, high_ref, below_ref):
    odd = place_ref[0] % 2 == 1

    @pl.when(odd)
    def _():
        high_ref[...] = inner_ref[...]
        below_ref[...] = outer_ref[...]

    @pl.when(jnp.logical_not(odd))
    def _():
        high_ref[...] = outer_ref[...]
        below_ref[...] = inner_ref[...]


def load_kernel(
    place_ref,
    last_ref,
    img_hbm,
    grad_hbm,
    valid_hbm,
    img_ref,
    inner_ref,
    outer_ref,
    packed_ref,
    valid_ref,
    ready,
):
    blocks = grad_hbm.shape[0]
    moves = [
        pltpu.make_async_copy(grad_hbm, packed_ref.at[pl.ds(0, blocks)], ready.at[0]),
        pltpu.make_async_copy(valid_hbm, valid_ref, ready.at[1]),
        pltpu.make_async_copy(img_hbm, img_ref, ready.at[2]),
    ]
    for move in moves:
        move.start()
    for move in moves:
        move.wait()
    rows = img_ref.shape[1]
    odd = place_ref[0] % 2 == 1

    @pl.when(odd)
    def _():
        inner_ref[...] = img_ref[:, :2]
        outer_ref[...] = img_ref[:, rows - 3 : rows - 1]

    @pl.when(jnp.logical_not(odd))
    def _():
        inner_ref[...] = img_ref[:, rows - 3 : rows - 1]
        outer_ref[...] = img_ref[:, :2]

    piece, width = packed_ref.shape[1:]
    dates, rows, cols = valid_ref.shape
    values = valid_ref[...].astype(F32).reshape(dates * rows, cols)
    values = jnp.concatenate([values, jnp.zeros((dates * rows, width - cols), F32)], axis=1)
    packed_ref[blocks:] = values.astype(BF16).reshape(-1, piece, width)


def edge_kernel(
    step,
    steps,
    place_ref,
    inner_ref,
    outer_ref,
    above_ref,
    last_ref,
    weight_ref,
    up_ref,
    down_ref,
    table,
    high_ref,
    below_ref,
):
    if step is None:
        return
    dates = above_ref.shape[0]
    sort_halos(place_ref, inner_ref, outer_ref, high_ref, below_ref)
    down_table(weight_ref, table)
    taps = [
        jnp.concatenate([high_ref[:, 0], last_ref[...]], axis=0),
        jnp.concatenate([high_ref[:, 1], below_ref[:, 0]], axis=0),
        jnp.concatenate([above_ref[...], below_ref[:, 1]], axis=0),
    ]
    stored = down_rows(taps, table)
    up_ref[...] = stored[:dates]
    down_ref[...] = stored[dates:]


def activate_rows(date, dates, edge_flags, conv_refs, norm_refs, hidden_ref):
    conv_ref, up_ref, down_ref = conv_refs
    norm_ref, gain_ref, shift_ref = norm_refs
    scale = norm_ref[pl.ds(dates + date, 1), :] * gain_ref[...]
    shift = shift_ref[...] - norm_ref[pl.ds(date, 1), :] * scale

    def activate(values):
        linear = values.astype(F32) * scale + shift
        return linear * sigmoid(linear)

    rows = conv_ref.shape[1]
    hidden_ref[0, 0] = (activate(up_ref[0]) * edge_flags[0]).astype(BF16)
    hidden_ref[0, rows + 1] = (activate(down_ref[0]) * edge_flags[1]).astype(BF16)
    hidden_ref[0, 1 : rows + 1] = activate(conv_ref[0]).astype(BF16)


def block_kernel(
    date,
    dates,
    edge_ref,
    conv_ref,
    up_ref,
    down_ref,
    stats_ref,
    gain_ref,
    shift_ref,
    weight_ref,
    out_ref,
    norm_ref,
    sums_ref,
    table,
    hidden_ref,
    *,
    norm_count,
    row_devs,
):

    if date is None:
        norm_table(stats_ref, norm_ref, dates, norm_count)
        tap_table(weight_ref, table, False)
        return

    activate_rows(
        date,
        dates,
        edges(edge_ref, row_devs),
        (conv_ref, up_ref, down_ref),
        (norm_ref, gain_ref, shift_ref),
        hidden_ref,
    )
    stored = tap_rows(hidden_ref[0], table, False).astype(BF16)
    out_ref[0] = stored
    values = stored.astype(F32)
    store_sums(sums_ref, date, dates, column_sum(values), column_sum(values * values))


def encoding(day, width):
    lane = lax.broadcasted_iota(jnp.int32, (1, width), 1)
    frequency = jnp.exp((lane // 2).astype(F32) * (-2.0 * math.log(1000.0) / width))
    angles = day.astype(F32) * frequency
    return jnp.where(lane % 2 == 0, jnp.sin(angles), jnp.cos(angles))


def fold_keys(key_ref, query_ref, wide_ref, vector_ref, spread_ref, score_ref):
    depth, heads = query_ref.shape
    width = key_ref.shape[1]
    lanes = width // heads
    spread_ref[...] = head_spread(width)
    row = lax.broadcasted_iota(jnp.int32, (heads * depth, width), 0)
    lane = lax.broadcasted_iota(jnp.int32, (heads * depth, width), 1)
    widen = (row // depth == lane // lanes) & (row % depth == lane % lanes)
    wide = product(key_ref[...], widen.astype(F32).astype(BF16), 0, 0)
    wide_ref[...] = wide.astype(BF16)
    head = lax.broadcasted_iota(jnp.int32, (heads, width), 0)
    lane = lax.broadcasted_iota(jnp.int32, (heads, width), 1)
    inside = (lane // lanes == head).astype(F32).astype(BF16)
    high, low = split(query_ref[...])
    lower = (query_ref[...] - high.astype(F32) - low.astype(F32)).astype(BF16)
    spread = sum(product(part, inside, 1, 0) for part in (high, low, lower))
    step = lax.broadcasted_iota(jnp.int32, (depth, width), 0)
    place = lax.broadcasted_iota(jnp.int32, (depth, width), 1) % lanes
    queries = jnp.sum(jnp.where(step == place, spread * depth**-0.5, 0.0), axis=0, keepdims=True)
    place = lax.broadcasted_iota(jnp.int32, (1, width), 1) % lanes
    queries = queries + jnp.where((place == depth) | (place == depth + 1), 1.0, 0.0)
    vector_ref[...] = jnp.broadcast_to(queries, vector_ref.shape)
    folded = jnp.concatenate(split(wide * queries), axis=-1)
    folded = product(folded, spread_ref[...], 1, 0)
    score_ref[...] = jnp.concatenate(split(folded), axis=-1)


def source_of(turn_ref, device, devices):
    half = devices // 2
    core = (device + turn_ref[0]) % 2
    return core * half + (device // 2 + half - turn_ref[0] // 2) % half


def upstream_rows(grad_ref, turn_ref, rows, cols):
    devices = grad_ref.shape[0]
    piece = cols // devices
    parts = [
        grad_ref[source_of(turn_ref, device, devices), : rows * piece].reshape(rows, piece, -1)
        for device in range(devices)
    ]
    return jnp.concatenate(parts, axis=1)


def score_kernel(
    date,
    dates,
    day_ref,
    block_ref,
    stats_ref,
    gain_ref,
    shift_ref,
    grad_ref,
    valid_ref,
    turn_ref,
    key_ref,
    query_ref,
    feat_ref,
    exp_ref,
    attn_ref,
    norm_ref,
    packed_ref,
    own_ref,
    wide_ref,
    vector_ref,
    total,
    mean,
    spread_ref,
    score_ref,
    *,
    norm_count,
    grad_scale,
):
    rows, cols, width = block_ref.shape[1:]

    if date is None:
        norm_table(stats_ref, norm_ref, dates, norm_count)
        fold_keys(key_ref, query_ref, wide_ref, vector_ref, spread_ref, score_ref)
        total[...] = jnp.zeros_like(total)
        mean[...] = jnp.zeros_like(mean)
        return

    scale = norm_ref[pl.ds(dates + date, 1), :] * gain_ref[...]
    shift = shift_ref[...] - norm_ref[pl.ds(date, 1), :] * scale
    linear = block_ref[0].astype(F32) * scale + shift
    features = (linear * sigmoid(linear) + encoding(day_ref[turn_ref[0] * dates + date], width)).astype(BF16)
    feat_ref[0] = features
    upstream = upstream_rows(grad_ref, turn_ref, rows, cols)
    parts = split(upstream.astype(F32) * features.astype(F32))
    parts = jnp.concatenate(parts, axis=-1).reshape(rows * cols, 2 * width)
    attn = product(parts, spread_ref[...], 1, 0).reshape(rows, cols, width) * grad_scale
    both = product(features.reshape(rows * cols, width), score_ref[...], 1, 0)
    scores = (both[:, :width] + both[:, width:]).reshape(rows, cols, width)
    devices = grad_ref.shape[0]
    valid = jnp.zeros((rows, width), F32)
    for device in range(devices):
        piece = valid_ref[
            source_of(turn_ref, device, devices), pl.ds(date * rows, rows), :
        ]
        valid = valid + pltpu.roll(piece, device * (cols // devices), 1)
    diagonal = lax.broadcasted_iota(jnp.int32, (cols, cols), 0) == lax.broadcasted_iota(
        jnp.int32, (cols, cols), 1
    )
    ones = jnp.ones((cols, width), BF16)
    clear = jnp.concatenate(
        [jnp.where(diagonal, valid[row : row + 1], 0.0) for row in range(rows)], axis=0
    ).astype(BF16)
    clear = product(clear, ones, 1, 0).reshape(rows, cols, width)
    exponent = clear * jnp.exp(scores)
    running = total[...] + exponent
    share = jnp.where(running > 0.0, exponent / running, 0.0)
    total[...] = running
    mean[...] += share * (attn - mean[...])
    exp_ref[0] = exponent
    attn_ref[0] = attn

    if date == dates - 1:
        place = lax.broadcasted_iota(jnp.int32, (cols, width), 1) % rows
        for index, source in enumerate((total, mean)):
            dense = jnp.zeros((cols, width), F32)
            for row in range(rows):
                dense = dense + jnp.where(place == row, source[row], 0.0)
            if index == 0:
                packed_ref[0, 0] = dense.astype(BF16)
                own_ref[...] = dense
            else:
                packed_ref[0, 1], packed_ref[0, 2] = split(dense)


def attend_kernel(
    date,
    dates,
    packed_ref,
    own_ref,
    feat_ref,
    exp_ref,
    attn_ref,
    block_ref,
    norm_ref,
    gain_ref,
    shift_ref,
    query_ref,
    grad_ref,
    turn_ref,
    key_ref,
    grad_out_ref,
    part_ref,
    key_out_ref,
    vector_ref,
    sums_ref,
    inverse,
    average,
    attended,
    *,
    grad_scale,
):
    rows, cols, width = block_ref.shape[1:]

    if date is None:
        totals = packed_ref[:, 0].astype(F32)
        reciprocal = 1.0 / jnp.sum(totals, axis=0)
        means = packed_ref[:, 1].astype(F32) + packed_ref[:, 2].astype(F32)
        mean = jnp.sum(totals * reciprocal * means, axis=0)
        own = own_ref[...]
        sent = own.astype(BF16).astype(F32)
        reciprocal = reciprocal * jnp.where(own > 0.0, sent / own, 0.0)
        place = lax.broadcasted_iota(jnp.int32, (cols, width), 1) % rows
        for values, target in ((reciprocal, inverse), (mean, average)):
            parts = jnp.concatenate(split(values), axis=-1)
            wide_place = jnp.concatenate([place, place], axis=-1)
            picked = jnp.concatenate(
                [jnp.where(wide_place == row, parts, jnp.zeros_like(parts)) for row in range(rows)], axis=0
            )
            target[...] = product(picked, head_spread(width), 1, 0).reshape(rows, cols, width)
        attended[...] = jnp.zeros_like(attended)
        key_out_ref[...] = jnp.zeros_like(key_out_ref)
        vector_ref[...] = jnp.zeros_like(vector_ref)
        return

    features = feat_ref[0]
    weights = exp_ref[0] * inverse[...]
    rounded = weights.astype(BF16).astype(F32)
    attended[...] += rounded * features.astype(F32)
    score_grad = weights * (attn_ref[0] - average[...])
    spread_grad = score_grad * query_ref[0:1]
    rest = spread_grad - spread_grad.astype(BF16).astype(F32)
    lane = lax.broadcasted_iota(jnp.int32, spread_grad.shape, 2) % (width // 16)
    key_grads = jnp.where(lane == 5, rest, spread_grad).astype(BF16).reshape(rows * cols, width)
    key_out_ref[...] += product(features.reshape(rows * cols, width), key_grads, 0, 0)
    upstream = upstream_rows(grad_ref, turn_ref, rows, cols)
    feat_grad = rounded * (upstream.astype(F32) * grad_scale) + product(
        key_grads, key_ref[...], 1, 1
    ).reshape(rows, cols, width)
    gain = gain_ref[...]
    centred = (block_ref[0].astype(F32) - norm_ref[pl.ds(date, 1), :]) * norm_ref[
        pl.ds(dates + date, 1), :
    ]
    linear = centred * gain + shift_ref[...]
    part = sigmoid(linear)
    linear_grad = feat_grad * (part * (1.0 + linear * (1.0 - part)))
    first = column_sum(linear_grad)
    second = column_sum(linear_grad * centred)
    vector_ref[0:1] += second
    vector_ref[1:2] += first
    store_sums(sums_ref, date, dates, first * gain, second * gain)
    grad_out_ref[0] = (linear_grad * gain).astype(BF16)

    if date == dates - 1:
        devices, piece = part_ref.shape[0], part_ref.shape[2]
        for device in range(devices):
            part_ref[device] = attended[:, device * piece : (device + 1) * piece].astype(BF16)
        key_part = key_out_ref[...]
        place = lax.broadcasted_iota(jnp.int32, (width, width), 1) % (width // 16)
        both = pltpu.roll(key_part, width - 4, 1) + pltpu.roll(key_part, width - 5, 1)
        both = jnp.where(place == 0, both, 0.0)
        both = both + pltpu.roll(both, 1, 1)
        both = both + pltpu.roll(both, 2, 1)
        vector_ref[2:3] = 0.5 * jnp.sum(key_ref[...].astype(F32) * both, axis=0, keepdims=True)


def hidden_kernel(
    date,
    dates,
    edge_ref,
    grad_ref,
    block_ref,
    tails_ref,
    norm_ref,
    weight_ref,
    conv_ref,
    up_ref,
    down_ref,
    first_norm_ref,
    gain_ref,
    shift_ref,
    pre_ref,
    out_ref,
    vector_ref,
    sums_ref,
    table,
    factors,
    padded,
    *,
    norm_count,
    row_devs,
):
    rows, cols, width = block_ref.shape[1:]

    if date is None:
        tails = group_sum(jnp.sum(tails_ref[...], axis=0)) / norm_count
        mean, inverse = norm_ref[:dates], norm_ref[dates:]
        slope = -inverse * inverse * tails[dates:]
        factors[0:dates] = slope
        factors[dates : 2 * dates] = -inverse * tails[:dates] - mean * slope
        vector_ref[...] = jnp.zeros_like(vector_ref)
        padded[:2] = jnp.zeros_like(padded[:2])
        padded[rows + 2 :] = jnp.zeros_like(padded[rows + 2 :])
        tap_table(weight_ref, table, True)
        return

    inverse = norm_ref[pl.ds(dates + date, 1), :]
    slope = factors[pl.ds(date, 1), :]
    constant = factors[pl.ds(dates + date, 1), :]

    above_edge, below_edge = edges(edge_ref, row_devs)
    stored = (
        grad_ref[0].astype(F32) * inverse + (block_ref[0].astype(F32) * slope + constant)
    ).astype(BF16)
    pre_ref[0] = stored
    padded[2 : rows + 2] = stored
    hidden_grad = tap_rows(padded[...], table, True)
    gain = gain_ref[...]
    conv = jnp.concatenate([up_ref[0][None], conv_ref[0], down_ref[0][None]], axis=0)
    centred = (conv.astype(F32) - first_norm_ref[pl.ds(date, 1), :]) * first_norm_ref[
        pl.ds(dates + date, 1), :
    ]
    linear = centred * gain + shift_ref[...]
    part = sigmoid(linear)
    linear_grad = hidden_grad * (part * (1.0 + linear * (1.0 - part)))
    linear_grad = jnp.concatenate(
        [
            linear_grad[:1] * above_edge,
            linear_grad[1 : rows + 1],
            linear_grad[rows + 1 :] * below_edge,
        ],
        axis=0,
    )
    out_ref[0] = linear_grad.astype(BF16)
    first = column_sum(linear_grad)
    second = column_sum(linear_grad * centred)
    vector_ref[0:1] += second
    vector_ref[1:2] += first
    store_sums(sums_ref, date, dates, first * gain, second * gain)


def block_grad_kernel(
    date,
    dates,
    edge_ref,
    conv_ref,
    up_ref,
    down_ref,
    norm_ref,
    gain_ref,
    shift_ref,
    pre_ref,
    key_ref,
    out_ref,
    total,
    hidden_ref,
    *,
    row_devs,
):
    rows, cols, width = pre_ref.shape[1:]

    if date is None:
        total[...] = jnp.zeros_like(total)
        return

    activate_rows(
        date,
        dates,
        edges(edge_ref, row_devs),
        (conv_ref, up_ref, down_ref),
        (norm_ref, gain_ref, shift_ref),
        hidden_ref,
    )
    grads = pre_ref[0].astype(F32)
    grads = jnp.concatenate(
        [from_right(grads).astype(BF16), pre_ref[0], from_left(grads).astype(BF16)], axis=-1
    ).reshape(rows * cols, 3 * width)
    taps = jnp.concatenate(
        [hidden_ref[0, tap : tap + rows] for tap in range(3)], axis=-1
    ).reshape(rows * cols, 3 * width)
    total[...] += product(taps, grads, 0, 0)

    if date == dates - 1:
        for row_tap in range(3):
            for col_tap in range(3):
                base = (row_tap * 3 + col_tap) * width
                out_ref[base : base + width] = total[
                    row_tap * width : (row_tap + 1) * width, col_tap * width : (col_tap + 1) * width
                ].astype(BF16)
        key_part = key_ref[...]
        rest = key_part - key_part.astype(BF16).astype(F32)
        lanes = width // 16
        place = lax.broadcasted_iota(jnp.int32, key_part.shape, 1) % lanes
        rest = pltpu.roll(rest, lanes // 2, 1)
        key_rows = jnp.where(place < lanes // 2, key_part, rest).astype(BF16)
        out_ref[9 * width : 10 * width] = key_rows
        if out_ref.shape[0] > 10 * width:
            out_ref[10 * width :] = jnp.zeros_like(out_ref[10 * width :])


def conv_grad_kernel(
    date,
    dates,
    img_ref,
    above_ref,
    inner_ref,
    outer_ref,
    place_ref,
    conv_ref,
    grad_ref,
    tails_ref,
    norm_ref,
    gain_ref,
    vector_ref,
    other_ref,
    block_rows_ref,
    turn_ref,
    keep_ref,
    give_ref,
    factors,
    total,
    out_ref,
    high_ref,
    below_ref,
    *,
    norm_count,
):
    rows, cols, width = conv_ref.shape[1:]
    half = width // 2

    if date is None:
        sort_halos(place_ref, inner_ref, outer_ref, high_ref, below_ref)
        tails = group_sum(jnp.sum(tails_ref[...], axis=0)) / norm_count
        mean, inverse = norm_ref[:dates], norm_ref[dates:]
        slope = -inverse * inverse * tails[dates:]
        factors[0:dates] = slope
        factors[dates : 2 * dates] = -inverse * tails[:dates] - mean * slope
        total[...] = jnp.zeros_like(total)
        return

    scale = norm_ref[pl.ds(dates + date, 1), :] * gain_ref[...]
    slope = factors[pl.ds(date, 1), :]
    constant = factors[pl.ds(dates + date, 1), :]
    own = conv_ref[0].astype(F32) * slope + constant
    scaled = grad_ref[0].astype(F32) * scale
    stored = jnp.concatenate(
        [scaled[:1], scaled[1 : rows + 1] + own, scaled[rows + 1 :]], axis=0
    ).astype(BF16)
    moved = from_right(stored.astype(F32)).astype(BF16)
    reach = rows + 2
    grads = jnp.concatenate([stored, moved], axis=-1).reshape(reach * cols, 2 * width)
    even, odd = img_ref[0, :, 0], img_ref[0, :, 1]
    above = above_ref[0][None]
    taps = [
        jnp.concatenate([high_ref[date, :1], above, odd], axis=0),
        jnp.concatenate([high_ref[date, 1:], even, below_ref[date, :1]], axis=0),
        jnp.concatenate([above, odd, below_ref[date, 1:]], axis=0),
    ]
    taps = jnp.concatenate(taps, axis=-1).reshape(reach * cols, 3 * width)
    total[...] += product(taps, grads, 0, 0)

    if date == dates - 1:
        begin = block_rows_ref.shape[0]
        out_ref[:begin] = block_rows_ref[...]
        for tap in range(3):
            base = tap * width
            pair = total[base : base + width, :width].astype(BF16)
            left = total[base + half : base + width, width:].astype(BF16)
            start = begin + tap * 3 * half
            out_ref[start : start + half] = left
            out_ref[start + half : start + 3 * half] = pair
        start = begin + 9 * half
        for source in (vector_ref, other_ref):
            high, low = split(source[...])
            out_ref[start : start + 16] = jnp.concatenate([high, low], axis=0)
            start += 16
        if out_ref.shape[0] > start:
            out_ref[start:] = jnp.zeros_like(out_ref[start:])
        half_rows = keep_ref.shape[0]
        core = turn_ref[0] % 2
        start = pl.multiple_of(core * half_rows, half_rows)
        keep_ref[...] = out_ref[pl.ds(start, half_rows), :]
        start = pl.multiple_of((1 - core) * half_rows, half_rows)
        give_ref[...] = out_ref[pl.ds(start, half_rows), :]


def total_kernel(in_ref, out_ref):
    total = jnp.sum(in_ref[...].astype(F32), axis=0).astype(BF16)
    for copy in range(out_ref.shape[0]):
        out_ref[copy] = total


def final_kernel(
    depth,
    turn_ref,
    own_ref,
    other_ref,
    conv_ref,
    block_ref,
    key_ref,
    query_ref,
    *refs,
):
    vector_refs, rows_ref = refs[:-1], refs[-1]
    half_rows = own_ref.shape[0]
    core = turn_ref[0] % 2
    rows_ref[pl.ds(pl.multiple_of(core * half_rows, half_rows), half_rows), :] = own_ref[...]
    start = pl.multiple_of((1 - core) * half_rows, half_rows)
    rows_ref[pl.ds(start, half_rows), :] = other_ref[...]
    conv_end, block_end, width = conv_ref.shape[0], block_ref.shape[0], block_ref.shape[1]
    block_ref[...] = rows_ref[:block_end].astype(F32)
    wide = key_ref.shape[0]
    heads = wide // depth
    lanes = width // heads
    row = lax.broadcasted_iota(jnp.int32, (wide, width), 0)
    lane = lax.broadcasted_iota(jnp.int32, (wide, width), 1)
    narrow = (row // depth == lane // lanes) & (row % depth == lane % depth)
    narrow = narrow.astype(F32).astype(BF16)
    key_ref[...] = product(narrow, rows_ref[block_end : block_end + width], 1, 1)
    start = block_end + width
    conv_ref[...] = rows_ref[start : start + conv_end].astype(F32)
    start += conv_end
    for index in range(2):
        both = rows_ref[start : start + 16].astype(F32)
        both = both[:8] + both[8:]
        vector_refs[2 * index][...] = both[0:1]
        vector_refs[2 * index + 1][...] = both[1:2]
        start += 16
    both = rows_ref[start - 16 : start]
    row = lax.broadcasted_iota(jnp.int32, (heads, width), 0)
    lane = lax.broadcasted_iota(jnp.int32, (heads, width), 1)
    inside = row == lane // lanes
    step = lax.broadcasted_iota(jnp.int32, (8, width), 0)
    place = lax.broadcasted_iota(jnp.int32, (8, width), 1) % lanes
    steps = step == place
    query = jnp.zeros((8, heads), F32)
    for index in (2, 10):
        picked = jnp.where(steps, both[index : index + 1].astype(F32), 0.0).astype(BF16)
        query = query + product(picked, inside.astype(F32).astype(BF16), 1, 1)
    query_ref[...] = query[:depth]


def call(kernel, dates, inputs, outputs, scratch, flops):
    in_specs, out_specs, arrays, out_shape, buffers = [], [], [], [], []
    in_vmem, in_hbm = pl.BlockSpec(memory_space=pltpu.VMEM), pl.BlockSpec(memory_space=pltpu.HBM)
    loads, stores = [], []
    for place, (kind, array) in enumerate(inputs):
        if kind == "scalar":
            in_specs.append(pl.BlockSpec(memory_space=pltpu.SMEM))
        elif "far" in kind:
            array = pltpu.with_memory_space_constraint(array, pltpu.HBM)
            in_specs.append(in_hbm)
            loads.append(place)
            buffers.append(pltpu.VMEM(array.shape, array.dtype))
        else:
            in_specs.append(in_vmem)
        arrays.append(array)
    for place, (kind, shape, dtype) in enumerate(outputs):
        if "far" in kind:
            out_shape.append(pltpu.HBM(shape, dtype))
            out_specs.append(in_hbm)
            stores.append(place)
            buffers.append(pltpu.VMEM(shape, dtype))
        else:
            out_shape.append(jax.ShapeDtypeStruct(shape, dtype))
            out_specs.append(in_vmem)
    copies = len(loads) + len(stores)
    kinds = [kind for kind, _ in inputs] + [kind for kind, _, _ in outputs]

    def body(*refs):
        views, rest = list(refs[: len(kinds)]), refs[len(kinds) :]
        buffer_refs, ready, rest = rest[:copies], rest[copies], rest[copies + 1 :]

        def copies_of(place, index, inward):
            outside, inside = views[place], buffer_refs[index]
            made = []
            for date in range(dates if "date" in kinds[place] else 1):
                here = pl.ds(date, 1) if "date" in kinds[place] else slice(None)
                pair = (outside.at[here], inside.at[here])
                source, target = pair if inward else pair[::-1]
                made.append(pltpu.make_async_copy(source, target, ready.at[index, date]))
            return made

        incoming = [copies_of(place, index, True) for index, place in enumerate(loads)]
        outgoing = [
            copies_of(len(inputs) + place, len(loads) + index, False)
            for index, place in enumerate(stores)
        ]
        def per_date(date):
            for place, moves in zip(loads, incoming):
                if date < len(moves) and "date" in kinds[place]:
                    yield moves[date]

        early = [m[0] for p, m in zip(loads, incoming) if kinds[p] == "all far"]
        late = [m[0] for p, m in zip(loads, incoming) if kinds[p] == "late far"]
        for move in early + list(per_date(0)) + list(per_date(1)) + late:
            move.start()
        for index, place in enumerate(loads):
            views[place] = buffer_refs[index]
        for index, place in enumerate(stores):
            views[len(inputs) + place] = buffer_refs[len(loads) + index]
        for move in early:
            move.wait()
        kernel(None, dates, *views, *rest)
        for date in range(dates):
            for move in per_date(date):
                move.wait()
            for move in per_date(date + 2):
                move.start()
            if date == dates - 1:
                for move in late:
                    move.wait()
            here = [
                view.at[pl.ds(date, 1)] if "date" in kind else view
                for view, kind in zip(views, kinds)
            ]
            kernel(date, dates, *here, *rest)
            for moves in outgoing:
                if len(moves) == dates:
                    moves[date].start()
                elif date == dates - 1:
                    moves[0].start()
        for moves in outgoing:
            for move in moves:
                move.wait()

    moved = sum(array.size * array.dtype.itemsize for _, array in inputs)
    return pl.pallas_call(
        body,
        in_specs=in_specs,
        out_specs=out_specs,
        out_shape=out_shape,
        scratch_shapes=buffers + [pltpu.SemaphoreType.DMA((max(copies, 1), dates))] + scratch,
        compiler_params=pltpu.CompilerParams(vmem_limit_bytes=40 * MIB),
        cost_estimate=pl.CostEstimate(flops=flops, bytes_accessed=2 * moved, transcendentals=0),
    )(*arrays)


def shifted(array, by):
    devices = lax.axis_size("rows")
    pairs = [(i, i + by) for i in range(devices) if 0 <= i + by < devices]
    return lax.ppermute(array, "rows", pairs)


def same_core(array):
    devices = lax.axis_size("dates")
    pieces = [array]
    for step in range(2, devices, 2):
        pairs = [((i + step) % devices, i) for i in range(devices)]
        pieces.append(lax.ppermute(array, "dates", pairs))
    return pieces


def sum_of_parts(parts):
    devices = lax.axis_size("dates")
    place = lax.axis_index("dates")
    total = lax.dynamic_index_in_dim(parts, place, 0, keepdims=False).astype(F32)
    for step in range(1, devices):
        piece = lax.dynamic_index_in_dim(parts, (place + step) % devices, 0, keepdims=False)
        pairs = [(i, (i + step) % devices) for i in range(devices)]
        total = total + lax.ppermute(piece, "dates", pairs).astype(F32)
    return total.astype(BF16)


def exchange(pieces, axes):
    return lax.all_to_all(pieces, axes, split_axis=0, concat_axis=0, tiled=True)


def gather(array, axis):
    return lax.all_gather(array, axis, axis=0, tiled=True)


def other_core(array):
    devices = lax.axis_size("dates")
    return lax.ppermute(array, "dates", [(i, i + 1 - 2 * (i % 2)) for i in range(devices)])


def exchange_cores(pieces):
    axes = ("rows", "dates")
    devices = lax.axis_size(axes)
    groups = [list(range(core, devices, 2)) for core in range(2)]
    return lax.all_to_all(
        pieces, axes, split_axis=0, concat_axis=0, axis_index_groups=groups, tiled=True
    )


def scatter(rows_array):
    devices = lax.axis_size(("rows", "dates")) // 2
    count, width = rows_array.shape
    return exchange_cores(rows_array.reshape(devices, count // devices, width))


def collect(pieces):
    spread = pl.pallas_call(
        total_kernel,
        out_shape=jax.ShapeDtypeStruct(pieces.shape, BF16),
        compiler_params=pltpu.CompilerParams(vmem_limit_bytes=16 * MIB),
    )(pieces)
    count, rows, width = pieces.shape
    return exchange_cores(spread).reshape(count * rows, width)


def padded_count(count, devices):
    step = 8 * devices
    return -(-count // step) * step


def local(
    images,
    day_index,
    valid,
    out_grad,
    conv_weight,
    first_gain,
    first_shift,
    block_weight,
    gn_gain,
    gn_shift,
    key_weight,
    queries,
):
    dates, rows_here, cols, pair_width = images.shape
    width = conv_weight.shape[-1]
    row_devs, date_devs = lax.axis_size("rows"), lax.axis_size("dates")
    devices = row_devs * date_devs
    rows = rows_here // 2
    heads, depth = queries.shape
    norm_count = float(rows * row_devs * cols * (width // GROUPS))
    grad_scale = float(rows * row_devs * cols) ** (-0.5)
    date_start = lax.axis_index("dates") * dates
    frame = (dates, rows, cols, width)
    edge_rows = (dates, cols, width)
    flops = 2 * dates * rows * cols * width * width

    rows_of = lambda vector: vector.reshape(1, width)
    first_gain, first_shift = rows_of(first_gain), rows_of(first_shift)
    gn_gain, gn_shift = rows_of(gn_gain), rows_of(gn_shift)
    last = images[:, -1]
    above = shifted(last, 1)
    grad_rows = out_grad.size // width
    row_place = lax.axis_index("rows")
    place = row_place.reshape(1)
    valid_count = valid.shape[0] * rows
    piece = out_grad.shape[1]
    packed_shape = ((grad_rows + valid_count) // piece, piece, width)
    in_hbm, in_vmem = pl.BlockSpec(memory_space=pltpu.HBM), pl.BlockSpec(memory_space=pltpu.VMEM)
    images_near, inner, outer, packed = pl.pallas_call(
        load_kernel,
        in_specs=[pl.BlockSpec(memory_space=pltpu.SMEM), in_vmem, in_hbm, in_hbm, in_hbm],
        out_specs=[in_vmem] * 4,
        out_shape=[
            jax.ShapeDtypeStruct(shape, BF16)
            for shape in (images.shape,) + ((dates, 2, cols, pair_width),) * 2 + (packed_shape,)
        ],
        scratch_shapes=[pltpu.VMEM(valid.shape, valid.dtype), pltpu.SemaphoreType.DMA((3,))],
        compiler_params=pltpu.CompilerParams(vmem_limit_bytes=16 * MIB),
    )(
        place,
        last,
        *[pltpu.with_memory_space_constraint(x, pltpu.HBM) for x in (images, out_grad, valid)],
    )
    packed = packed.reshape(grad_rows + valid_count, width)
    paired = images.reshape(dates, rows, 2, cols, pair_width)
    conv_main, part = call(
        inner_kernel,
        dates,
        [("date", images_near.reshape(paired.shape)), ("all", conv_weight)],
        [("date", frame, BF16), ("all", (1, 2 * dates, width), F32)],
        [pltpu.VMEM((3 * pair_width, 2 * width), BF16)],
        6 * flops,
    )
    inner, outer, above, packed, part = lax.optimization_barrier(
        (inner, outer, above, packed, part)
    )
    inner = lax.ppermute(inner, "rows", [(i, i ^ 1) for i in range(row_devs)])
    pairs = [(i, i + 1) for i in range(1, row_devs - 1, 2)]
    outer = lax.ppermute(outer, "rows", pairs + [(j, i) for i, j in pairs])
    conv_out, sums = pl.pallas_call(
        first_row_kernel,
        in_specs=[in_vmem] * 5,
        out_specs=[in_hbm, in_vmem],
        out_shape=[
            pltpu.HBM(frame, BF16),
            jax.ShapeDtypeStruct((row_devs, 2 * dates, width), F32),
        ],
        scratch_shapes=[
            pltpu.VMEM((3 * pair_width, 2 * width), BF16),
            pltpu.VMEM((dates, 1, cols, width), BF16),
            pltpu.SemaphoreType.DMA((2,)),
        ],
        compiler_params=pltpu.CompilerParams(vmem_limit_bytes=16 * MIB),
    )(images_near, above, conv_weight, conv_main, part)
    stats = exchange(sums, "rows")
    inner, outer, last, _ = lax.optimization_barrier((inner, outer, last, sums))
    halo_up, halo_down = call(
        edge_kernel,
        1,
        [
            ("scalar", place),
            ("all", inner),
            ("all", outer),
            ("all", above),
            ("all", last),
            ("all", conv_weight),
        ],
        [("all", edge_rows, BF16)] * 2,
        [
            pltpu.VMEM((3 * pair_width, 2 * width), BF16),
            pltpu.VMEM(inner.shape, BF16),
            pltpu.VMEM(inner.shape, BF16),
        ],
        6 * flops // rows,
    )
    turn = lax.axis_index("dates").reshape(1)
    packed, _ = lax.optimization_barrier((packed, halo_up))
    pieces = same_core(packed)
    block_out, first_norm, sums = call(
        functools.partial(block_kernel, norm_count=norm_count, row_devs=row_devs),
        dates,
        [
            ("scalar", place),
            ("date far", conv_out),
            ("date", halo_up),
            ("date", halo_down),
            ("all", stats),
            ("all", first_gain),
            ("all", first_shift),
            ("all far", block_weight),
        ],
        [
            ("date far", frame, BF16),
            ("all", (2 * dates, width), F32),
            ("all", (row_devs, 2 * dates, width), F32),
        ],
        [
            pltpu.VMEM((3 * width, 3 * width), BF16),
            pltpu.VMEM((1, rows + 2, cols, width), BF16),
        ],
        9 * flops,
    )
    stats = exchange(sums, "rows")
    pieces, _ = lax.optimization_barrier((pieces, sums))
    sources = jnp.stack(pieces + [other_core(piece) for piece in pieces])
    clear = lax.dynamic_slice_in_dim(sources, grad_rows + date_start * rows, dates * rows, 1)
    clear = clear.astype(F32)
    features, exponent, attn, norm, packed, own_total, key_wide, query_wide = call(
        functools.partial(score_kernel, norm_count=norm_count, grad_scale=grad_scale),
        dates,
        [
            ("scalar", day_index),
            ("date far", block_out),
            ("all", stats),
            ("all", gn_gain),
            ("all", gn_shift),
            ("all", sources),
            ("all", clear),
            ("scalar", turn),
            ("all", key_weight.T),
            ("all", queries.T),
        ],
        [
            ("date", frame, BF16),
            ("date", frame, F32),
            ("date", frame, F32),
            ("all", (2 * dates, width), F32),
            ("all", (1, 3, cols, width), BF16),
            ("all", (cols, width), F32),
            ("all", (width, width), BF16),
            ("all", (8, width), F32),
        ],
        [
            pltpu.VMEM(frame[1:], F32),
            pltpu.VMEM(frame[1:], F32),
            pltpu.VMEM((2 * width, width), BF16),
            pltpu.VMEM((width, 2 * width), BF16),
        ],
        5 * flops,
    )
    packed = gather(packed, "dates")
    block_grad, attended, key_part, vectors, sums = call(
        functools.partial(attend_kernel, grad_scale=grad_scale),
        dates,
        [
            ("all", packed),
            ("all", own_total),
            ("date", features),
            ("date", exponent),
            ("date", attn),
            ("date", block_out),
            ("all", norm),
            ("all", gn_gain),
            ("all", gn_shift),
            ("all", query_wide),
            ("all", sources),
            ("scalar", turn),
            ("all", key_wide),
        ],
        [
            ("date far", frame, BF16),
            ("all far", (date_devs, rows, cols // date_devs, width), BF16),
            ("all far", (width, width), F32),
            ("all", (8, width), F32),
            ("all", (row_devs, 2 * dates, width), F32),
        ],
        [pltpu.VMEM(frame[1:], F32)] * 3,
        5 * flops,
    )
    tails = exchange(sums, "rows")
    pre_grad, linear_grad, first_vectors, sums = call(
        functools.partial(hidden_kernel, norm_count=norm_count, row_devs=row_devs),
        dates,
        [
            ("scalar", place),
            ("date far", block_grad),
            ("date far", block_out),
            ("all", tails),
            ("all", norm),
            ("all far", block_weight),
            ("date far", conv_out),
            ("date", halo_up),
            ("date", halo_down),
            ("all", first_norm),
            ("all", first_gain),
            ("all", first_shift),
        ],
        [
            ("date far", frame, BF16),
            ("date far", (dates, rows + 2, cols, width), BF16),
            ("all", (8, width), F32),
            ("all", (row_devs, 2 * dates, width), F32),
        ],
        [
            pltpu.VMEM((3 * width, 3 * width), BF16),
            pltpu.VMEM((2 * dates, width), F32),
            pltpu.VMEM((rows + 4, cols, width), BF16),
        ],
        9 * flops,
    )
    tails = exchange(sums, "rows")
    (block_rows,) = call(
        functools.partial(block_grad_kernel, row_devs=row_devs),
        dates,
        [
            ("scalar", place),
            ("date far", conv_out),
            ("date", halo_up),
            ("date", halo_down),
            ("all", first_norm),
            ("all", first_gain),
            ("all", first_shift),
            ("date far", pre_grad),
            ("late far", key_part),
        ],
        [("all far", (10 * width, width), BF16)],
        [
            pltpu.VMEM((3 * width, 3 * width), F32),
            pltpu.VMEM((1, rows + 2, cols, width), BF16),
        ],
        9 * flops,
    )
    tails, block_rows = lax.optimization_barrier((tails, block_rows))
    conv_count = 9 * pair_width // 2 + 32
    half_rows = padded_count(10 * width + conv_count, devices) // 2
    keep, give = call(
        functools.partial(conv_grad_kernel, norm_count=norm_count),
        dates,
        [
            ("date far", paired),
            ("date", above),
            ("all", inner),
            ("all", outer),
            ("scalar", place),
            ("date far", conv_out),
            ("date far", linear_grad),
            ("all", tails),
            ("all", first_norm),
            ("all", first_gain),
            ("all", first_vectors),
            ("all", vectors),
            ("late far", block_rows),
            ("scalar", turn),
        ],
        [("all", (half_rows, width), BF16)] * 2,
        [
            pltpu.VMEM((2 * dates, width), F32),
            pltpu.VMEM((3 * pair_width, 2 * width), F32),
            pltpu.VMEM((2 * half_rows, width), BF16),
            pltpu.VMEM(inner.shape, BF16),
            pltpu.VMEM(inner.shape, BF16),
        ],
        6 * flops,
    )
    rows_half = (keep.astype(F32) + other_core(give).astype(F32)).astype(BF16)
    pieces = scatter(rows_half)
    attended, _ = lax.optimization_barrier((attended, rows_half))
    attended = sum_of_parts(attended)
    rows_half = collect(pieces)
    rows_other = other_core(rows_half)
    shapes = [
        (9 * pair_width // 2, width),
        (9 * width, width),
        (heads * depth, width),
        (depth, heads),
    ] + [(1, width)] * 4
    conv_total, block_total, key_total, query_total, *totals = pl.pallas_call(
        functools.partial(final_kernel, depth),
        in_specs=[
            pl.BlockSpec(memory_space=pltpu.SMEM),
            pl.BlockSpec(memory_space=pltpu.VMEM),
            pl.BlockSpec(memory_space=pltpu.VMEM),
        ],
        out_shape=[jax.ShapeDtypeStruct(shape, F32) for shape in shapes],
        scratch_shapes=[pltpu.VMEM((2 * half_rows, width), BF16)],
        compiler_params=pltpu.CompilerParams(vmem_limit_bytes=16 * MIB),
    )(turn, rows_half, rows_other)
    totals = [total.reshape(width) for total in totals]
    return (
        attended,
        conv_total.reshape(conv_weight.shape),
        totals[0],
        totals[1],
        block_total.reshape(block_weight.shape),
        totals[2],
        totals[3],
        key_total.T,
        query_total.T,
    )


def solution(mesh):
    return jax.shard_map(
        local,
        mesh=mesh,
        in_specs=(
            P("dates", "rows", None, None),
            P(),
            P(None, "rows", "dates"),
            P("rows", "dates", None),
            P(),
            P(),
            P(),
            P(),
            P(),
            P(),
            P(),
            P(),
        ),
        out_specs=(P("rows", "dates", None), P(), P(), P(), P(), P(), P(), P(), P()),
        check_vma=False,
    )
```
